32 devices in a mesh: seq: 2 (over core), ctx: 4 (over z), fsdp: 4 (over y, x).
Axes of the slice: x: 2, y: 2, z: 4, core: 2. Of those that a mesh axis runs over, the one named last changes fastest.
Arguments:
- tokens: bfloat16 [8, 512, 2048], P(('seq', 'fsdp'), 'ctx'), may hold values from -6 to 6
- stretch_order: int32 [8], replicated, may hold values from 0 to 7, as said below
- expert_ids: int32 [8, 512, 8], P(('seq', 'fsdp'), 'ctx'), may hold values from 0 to 31, as said below
- slot_index: int32 [8, 512, 8], P(('seq', 'fsdp'), 'ctx'), may hold values from 0 to 33, as said below
- norm_attn: bfloat16 [2048], P(('seq', 'ctx', 'fsdp')), may hold values from 0.5 to 1.5
- head_gains: bfloat16 [2, 128], replicated, may hold values from 0.5 to 1.5
- w_query: bfloat16 [2048, 4096], P(('seq', 'ctx', 'fsdp')), may hold values from -0.125 to 0.125
- key_projection_weight: bfloat16 [2048, 512], P(('seq', 'ctx', 'fsdp')), may hold values from -0.125 to 0.125
- value_projection_weight: bfloat16 [2048, 512], P(('seq', 'ctx', 'fsdp')), may hold values from -0.125 to 0.125
- w_out: bfloat16 [4096, 2048], P(('seq', 'ctx', 'fsdp')), may hold values from -0.375 to 0.375
- norm_moe: bfloat16 [2048], P(('seq', 'ctx', 'fsdp')), may hold values from 0.5 to 1.5
- w_router: bfloat16 [2048, 32], P(('seq', 'ctx', 'fsdp')), may hold values from -0.06591797 to 0.06591797
- w_gate: bfloat16 [32, 2048, 768], P(('seq', 'ctx', 'fsdp')), may hold values from -0.125 to 0.125
- w_up: bfloat16 [32, 2048, 768], P(('seq', 'ctx', 'fsdp')), may hold values from -0.125 to 0.125
- w_down: bfloat16 [32, 768, 2048], P(('seq', 'ctx', 'fsdp')), may hold values from -0.625 to 0.625
- cotangent: bfloat16 [8, 512, 2048], P(('seq', 'fsdp'), 'ctx'), may hold values from -6 to 6
Outputs:
- layer_out: bfloat16 [8, 512, 2048], P(('seq', 'fsdp'), 'ctx')
- grad_tokens: bfloat16 [8, 512, 2048], P(('seq', 'fsdp'), 'ctx')
- grad_norm_attn: float32 [2048], P(('seq', 'ctx', 'fsdp'))
- grad_head_gains: float32 [2, 128], replicated
- grad_w_query: float32 [2048, 4096], P(('seq', 'ctx', 'fsdp'))
- grad_w_key: float32 [2048, 512], P(('seq', 'ctx', 'fsdp'))
- grad_w_value: float32 [2048, 512], P(('seq', 'ctx', 'fsdp'))
- grad_w_out: float32 [4096, 2048], P(('seq', 'ctx', 'fsdp'))
- grad_norm_moe: float32 [2048], P(('seq', 'ctx', 'fsdp'))
- grad_w_router: float32 [2048, 32], P(('seq', 'ctx', 'fsdp'))
- grad_w_gate: float32 [32, 2048, 768], P(('seq', 'ctx', 'fsdp'))
- grad_w_up: float32 [32, 2048, 768], P(('seq', 'ctx', 'fsdp'))
- grad_w_down: float32 [32, 768, 2048], P(('seq', 'ctx', 'fsdp'))
The draws below stay inside these ranges and needn't reach their ends.
Inputs may be any that keep to these rules, and one draw needn't show every extreme that they name: `stretch_order`: A permutation; stored block 2 i and block 2 i + 1 of 64 rows hold block numbers that add to 7. `expert_ids`: each token names 8 different experts; expert e is held by index e of the seq+ctx+fsdp axes. `slot_index`: over the 128 rows of one device, tokens in order, a choice's slot is the number of earlier choices of that device naming the same expert, or 33 where that number is 33 or more (the choice is dropped); some expert has more than 33 choices from every device.
All inputs are finite; a program needn't handle non-finite values.
Results may differ from the reference program's by a relative error of at most 0.025.
Values may be sent and summed in bfloat16 or wider, within the bound.
A program may use at most 256 MiB of HBM per device.

```python
import jax
import jax.numpy as jnp
from jax import lax

MODEL_DIM = 2048
QUERY_HEADS = 32
KEY_VALUE_HEADS = 4
HEAD_DIM = 128
FFE = 768
TOP = 8
TOK_DEV = 128
SEQS = 8
SEQ_LEN = 512
STRETCH = 64
NCHUNK = 8
EXPERTS = 32
CAP = 33
N_CTX = 4
N_FSDP = 4
DEVICES = 32


def routing_tables(key):
    score_key, hot_key = jax.random.split(key)
    scores = jax.random.randint(score_key, (SEQS, SEQ_LEN, EXPERTS), 0, 2 ** 20) * EXPERTS + jnp.arange(EXPERTS, dtype=jnp.int32)
    hot_expert = jax.random.randint(hot_key, (), 0, EXPERTS)
    early_rows = jnp.arange(SEQ_LEN, dtype=jnp.int32) % TOK_DEV < CAP + 4
    boost_table = (early_rows[:, None] & (jnp.arange(EXPERTS, dtype=jnp.int32) == hot_expert)[None, :]).astype(jnp.int32) * 2 ** 28
    unused_values, route_ids = lax.top_k(scores + boost_table[None], TOP)
    route_ids = route_ids.astype(jnp.int32)
    onehot = (route_ids[..., None] == jnp.arange(EXPERTS, dtype=jnp.int32)).astype(jnp.int32)
    blocks = onehot.reshape(SEQS, SEQ_LEN // TOK_DEV, TOK_DEV * TOP, EXPERTS)
    earlier = jnp.cumsum(blocks, axis=2) - blocks
    slot_ids = jnp.sum(earlier * blocks, axis=-1).reshape(SEQS, SEQ_LEN, TOP)
    return (route_ids, jnp.minimum(slot_ids, CAP).astype(jnp.int32))


def draw_expert_ids(key, part):
    return routing_tables(key)[0]


def draw_slot_index(key, part):
    return routing_tables(key)[1]


def draw_stretch_order(key, part):
    key = jax.random.fold_in(key, 5)
    pair_key, flip_key = jax.random.split(key)
    pair_count = NCHUNK // 2
    pair_ids = jax.random.permutation(pair_key, pair_count).astype(jnp.int32)
    flip_bits = jax.random.randint(flip_key, (pair_count,), 0, 2)
    lower_block = jnp.where(flip_bits == 1, pair_ids, NCHUNK - 1 - pair_ids)
    upper_block = NCHUNK - 1 - lower_block
    return jnp.stack([lower_block, upper_block], axis=1).reshape(-1).astype(jnp.int32)


def block_scale(key, shape, pieces, low, high):
    loudness, own = 1.0, jax.random.fold_in(key, 6)
    for axis_at, shards_of in pieces:
        steps = jnp.exp(jax.random.uniform(jax.random.fold_in(own, axis_at), (shards_of,), jnp.float32, low / len(pieces), high / len(pieces)))
        loudness = loudness * jnp.repeat(steps, shape[axis_at] // shards_of).reshape([-1 if axis == axis_at else 1 for axis in range(len(shape))])
    return loudness


def noise(key, shape, spread, limit, cuts=(), kind=jnp.bfloat16):
    loudness = block_scale(key, shape, cuts, -0.22, 0.18) if cuts else 1.0
    values = jax.random.normal(key, shape, jnp.float32) * spread * loudness
    return jnp.minimum(jnp.maximum(values, -limit), limit).astype(kind)


def setup_inputs(seed: int = 0) -> dict:
    streams_of = jax.random.split(jax.random.key(seed), 17)
    return {
        "tokens": noise(streams_of[0], (SEQS, SEQ_LEN, MODEL_DIM), 1.0, 6.0, ((0, 8), (1, 4))),
        "stretch_order": draw_stretch_order(jax.random.fold_in(streams_of[16], 71), 0),
        "expert_ids": draw_expert_ids(jax.random.fold_in(streams_of[16], 71), 0),
        "slot_index": draw_slot_index(jax.random.fold_in(streams_of[16], 71), 0),
        "norm_attn": jnp.clip(1.0 + 0.1 * jax.random.normal(streams_of[4], (MODEL_DIM,), jnp.float32), 0.5, 1.5).astype(jnp.bfloat16),
        "head_gains": jnp.clip(1.0 + 0.1 * jax.random.normal(streams_of[5], (2, HEAD_DIM), jnp.float32), 0.5, 1.5).astype(jnp.bfloat16),
        "w_query": noise(streams_of[6], (MODEL_DIM, QUERY_HEADS * HEAD_DIM), MODEL_DIM ** -0.5, 0.125, ((0, 32),)),
        "key_projection_weight": noise(streams_of[7], (MODEL_DIM, KEY_VALUE_HEADS * HEAD_DIM), MODEL_DIM ** -0.5, 0.125, ((0, 32),)),
        "value_projection_weight": noise(streams_of[8], (MODEL_DIM, KEY_VALUE_HEADS * HEAD_DIM), MODEL_DIM ** -0.5, 0.125, ((0, 32),)),
        "w_out": noise(streams_of[9], (QUERY_HEADS * HEAD_DIM, MODEL_DIM), (QUERY_HEADS * HEAD_DIM // 16) ** -0.5, 0.375, ((0, 32),)),
        "norm_moe": jnp.clip(1.0 + 0.1 * jax.random.normal(streams_of[10], (MODEL_DIM,), jnp.float32), 0.5, 1.5).astype(jnp.bfloat16),
        "w_router": noise(streams_of[11], (MODEL_DIM, EXPERTS), (0.5 * MODEL_DIM ** -0.5), 0.06591797, ((0, 32),)),
        "w_gate": noise(streams_of[12], (EXPERTS, MODEL_DIM, FFE), MODEL_DIM ** -0.5, 0.125, ((0, 32),)),
        "w_up": noise(streams_of[13], (EXPERTS, MODEL_DIM, FFE), MODEL_DIM ** -0.5, 0.125, ((0, 32),)),
        "w_down": noise(streams_of[14], (EXPERTS, FFE, MODEL_DIM), (FFE // 8) ** -0.5, 0.625, ((0, 32),)),
        "cotangent": noise(streams_of[15], (SEQS, SEQ_LEN, MODEL_DIM), 1.0, 6.0, ((0, 8), (1, 4))),
    }


@jax.custom_vjp
def lowered_input(v):
    return lax.optimization_barrier(v.astype(jnp.bfloat16)).astype(jnp.float32)

@jax.custom_vjp
def lowered_backward(v):
    return v

def low_keep(v):
    return (lowered_input(v), None)

def low_pass(kept, grad):
    return (grad,)

def back_keep(v):
    return (v, None)

def back_low(kept, grad):
    return (lowered_input(grad),)
lowered_input.defvjp(low_keep, low_pass)
lowered_backward.defvjp(back_keep, back_low)
highest = lax.Precision.HIGHEST
epsilon = 1e-06
rope_base = 1000000.0

def matrix_multiply(left, right):
    return jnp.dot(left, right, precision=highest, preferred_element_type=jnp.float32)

def rms_scale(value_rows, norm_gain):
    factor = lax.rsqrt(lax.optimization_barrier(jnp.mean(value_rows * value_rows, axis=-1, keepdims=True)) + epsilon)
    return value_rows * factor * norm_gain

def rotate(value_rows, cosine, sine_table):
    half_width = value_rows.shape[-1] // 2
    first_half = value_rows[..., :half_width]
    second_half = value_rows[..., half_width:]
    return jnp.concatenate([first_half * cosine - second_half * sine_table, second_half * cosine + first_half * sine_table], axis=-1)

def rope_tables(positions, head_width):
    frequency = jnp.power(rope_base, -jnp.arange(head_width // 2, dtype=jnp.float32) * 2.0 / head_width)
    angles = positions.astype(jnp.float32)[:, None] * frequency[None, :]
    return (jnp.cos(angles), jnp.sin(angles))

def attend(seq_rows, params, cosine, sine_table, causal):
    gain_attn, head_gain, query_weight, key_matrix, value_matrix, out_weight = params
    sequence_count = seq_rows.shape[0]
    normalized_input = lowered_input(rms_scale(seq_rows, gain_attn))
    query_proj = lowered_backward(matrix_multiply(normalized_input, query_weight)).reshape(sequence_count, QUERY_HEADS, HEAD_DIM)
    key_projected = lowered_backward(matrix_multiply(normalized_input, key_matrix)).reshape(sequence_count, KEY_VALUE_HEADS, HEAD_DIM)
    value_projected = lowered_input(lowered_backward(matrix_multiply(normalized_input, value_matrix))).reshape(sequence_count, KEY_VALUE_HEADS, HEAD_DIM)
    query_rotated = lowered_input(rotate(rms_scale(query_proj, head_gain[0]), cosine[:, None, :], sine_table[:, None, :]))
    key_rot = lowered_input(rotate(rms_scale(key_projected, head_gain[1]), cosine[:, None, :], sine_table[:, None, :]))
    grouped_rows = query_rotated.reshape(sequence_count, KEY_VALUE_HEADS, QUERY_HEADS // KEY_VALUE_HEADS, HEAD_DIM)
    scores = lowered_backward(jnp.einsum('qhgd,khd->hgqk', grouped_rows, key_rot, precision=highest) * HEAD_DIM ** (-0.5))
    scores = jnp.where(causal[None, None], scores, -jnp.inf)
    attn_probs = lowered_input(jax.nn.softmax(scores, axis=-1))
    mixed_heads = jnp.einsum('hgqk,khd->qhgd', attn_probs, value_projected, precision=highest)
    mixed_heads = lowered_input(lowered_backward(mixed_heads.reshape(sequence_count, QUERY_HEADS * HEAD_DIM)))
    return seq_rows + lowered_backward(matrix_multiply(mixed_heads, out_weight))

def reference(tokens, stretch_order, expert_ids, slot_index, norm_attn, head_gains, w_query, key_projection_weight, value_projection_weight, w_out, norm_moe, w_router, w_gate, w_up, w_down, cotangent):
    positions = (stretch_order[:, None] * STRETCH + jnp.arange(STRETCH, dtype=jnp.int32)[None, :]).reshape(-1).astype(jnp.int32)
    cosine, sine_table = rope_tables(positions, HEAD_DIM)
    causal = positions[:, None] >= positions[None, :]
    token_count = SEQS * SEQ_LEN
    seq_index = jnp.arange(SEQS, dtype=jnp.int32)[:, None]
    row_index = jnp.arange(SEQ_LEN, dtype=jnp.int32)[None, :]
    source = seq_index // N_FSDP * (N_CTX * N_FSDP) + row_index // TOK_DEV * N_FSDP + seq_index % N_FSDP
    source = jnp.broadcast_to(source[:, :, None], expert_ids.shape).reshape(token_count, TOP).astype(jnp.int32)
    route_ids = expert_ids.reshape(token_count, TOP).astype(jnp.int32)
    slot_ids = slot_index.reshape(token_count, TOP).astype(jnp.int32)
    kept_mask = (slot_ids < CAP).astype(jnp.float32)
    buffer_size = EXPERTS * DEVICES * CAP
    target = jnp.where(slot_ids < CAP, (route_ids * DEVICES + source) * CAP + slot_ids, buffer_size).reshape(-1).astype(jnp.int32)
    owner_token = jnp.repeat(jnp.arange(token_count, dtype=jnp.int32), TOP)
    slot_table = jnp.full((buffer_size + 1,), token_count, jnp.int32).at[target].set(owner_token)[:buffer_size]
    slot_table = slot_table.reshape(EXPERTS, DEVICES * CAP).astype(jnp.int32)
    read_index = ((route_ids * DEVICES + source) * CAP + jnp.minimum(slot_ids, CAP - 1)).astype(jnp.int32)

    def forward(inputs, gain_attn, head_gain, query_weight, key_matrix, value_matrix, out_weight, gain_moe, router_weight, gate_weight, up_weight, down_weight):
        params = (gain_attn, head_gain, query_weight, key_matrix, value_matrix, out_weight)

        def one_sequence(seq_rows):
            return attend(seq_rows, params, cosine, sine_table, causal)
        hidden_one = lax.map(jax.checkpoint(one_sequence), inputs)
        flat_rows = hidden_one.reshape(token_count, MODEL_DIM)
        normed_moe = lowered_input(rms_scale(flat_rows, gain_moe))
        router_logits = lowered_backward(matrix_multiply(normed_moe, router_weight))
        chosen_logits = jnp.take_along_axis(router_logits, route_ids, axis=1)
        route_weight = jax.nn.softmax(chosen_logits, axis=-1) * kept_mask
        padded = jnp.concatenate([normed_moe, jnp.zeros((1, MODEL_DIM), normed_moe.dtype)], axis=0)

        def run_expert(operands):
            table_row, gate_part, up_part, down_part = operands
            buffer_rows = lowered_backward(padded[table_row])
            gate_pre = lowered_backward(matrix_multiply(buffer_rows, gate_part))
            up_pre = lowered_backward(matrix_multiply(buffer_rows, up_part))
            hidden = lowered_input(jax.nn.silu(gate_pre) * up_pre)
            return lowered_input(lowered_backward(matrix_multiply(hidden, down_part)))
        produced = lax.map(jax.checkpoint(run_expert), (slot_table, gate_weight, up_weight, down_weight))
        picked = produced.reshape(buffer_size, MODEL_DIM)[read_index]
        expert_sum = lax.optimization_barrier(jnp.sum(route_weight[:, :, None] * picked, axis=1))
        return (flat_rows + expert_sum).reshape(SEQS, SEQ_LEN, MODEL_DIM)
    arrays = (tokens, norm_attn, head_gains, w_query, key_projection_weight, value_projection_weight, w_out, norm_moe, w_router, w_gate, w_up, w_down)
    arrays = tuple((piece_array.astype(jnp.float32) for piece_array in arrays))
    layer_out, pullback = jax.vjp(forward, *arrays)
    all_grads = pullback(cotangent.astype(jnp.float32))
    return (layer_out.astype(jnp.bfloat16), all_grads[0].astype(jnp.bfloat16), all_grads[1], all_grads[2], all_grads[3], all_grads[4], all_grads[5], all_grads[6], all_grads[7], all_grads[8], all_grads[9], all_grads[10], all_grads[11])
```

```python
import functools

import jax
import jax.numpy as jnp
from jax import lax
from jax.experimental import pallas as pl
from jax.experimental.pallas import tpu as pltpu
from jax.sharding import PartitionSpec as P

QUERY_HEADS = 32
KEY_VALUE_HEADS = 4
HEAD_DIM = 128
TOP = 8
AXES = ("seq", "ctx", "fsdp")
MESH = pl.DeviceIdType.MESH
epsilon = 1e-06
rope_base = 1000000.0
VMEM_LIMIT = 56 * 2**20
f32 = jnp.float32
bf16 = jnp.bfloat16


def round_up(value, step):
    return (value + step - 1) // step * step


def place():
    return tuple(lax.axis_index(name) for name in AXES)


def sizes():
    return tuple(lax.axis_size(name) for name in AXES)


def signal(device):
    pl.semaphore_signal(
        pltpu.get_barrier_semaphore(), inc=1, device_id=device, device_id_type=MESH
    )


def remote(src, dst, send, recv, device):
    return pltpu.make_async_remote_copy(
        src_ref=src,
        dst_ref=dst,
        send_sem=send,
        recv_sem=recv,
        device_id=device,
        device_id_type=MESH,
    )


def params(cid, limit=VMEM_LIMIT):
    return pltpu.CompilerParams(
        collective_id=cid, has_side_effects=True, vmem_limit_bytes=limit
    )


ANY = pl.BlockSpec(memory_space=pl.ANY)
DMA = pltpu.SemaphoreType.DMA


def exchange(name, cid, items):
    S, C, F = sizes()
    Q = S * F
    count = len(items)
    kinds = [kind for kind, _ in items]
    use_z = any(kind[0] == "z" for kind in kinds)
    use_p = any(kind[0] == "p" for kind in kinds)

    def kernel(*refs):
        ins, outs = refs[:count], refs[count : 2 * count]
        local, zsend, zrecv, psend, precv = refs[2 * count :]
        s, c, f = place()
        q = s * F + f
        z_peers = [(s, lax.rem(c + k, C), f) for k in range(1, C)]
        p_peers = []
        for k in range(1, Q):
            other = lax.rem(q + k, Q)
            p_peers.append((other // F, c, lax.rem(other, F)))
        expected = 0
        if use_z:
            for peer in z_peers:
                signal(peer)
            expected += C - 1
        if use_p:
            for peer in p_peers:
                signal(peer)
            expected += Q - 1
        pl.semaphore_wait(pltpu.get_barrier_semaphore(), expected)
        waits = []
        for i, kind in enumerate(kinds):
            x, o = ins[i], outs[i]
            if kind[0] == "z":
                for k, peer in enumerate(z_peers):
                    src = x if kind == "zag" else x.at[peer[1]]
                    copy = remote(src, o.at[c], zsend.at[i, k], zrecv.at[i, k], peer)
                    copy.start()
                    waits.append(copy)
            else:
                for k, peer in enumerate(p_peers):
                    src = x.at[peer[0] * F + peer[2]]
                    copy = remote(src, o.at[q], psend.at[i, k], precv.at[i, k], peer)
                    copy.start()
                    waits.append(copy)
            if kind == "zag":
                own = pltpu.make_async_copy(x, o.at[c], local.at[i])
            elif kind == "za2a":
                own = pltpu.make_async_copy(x.at[c], o.at[c], local.at[i])
            else:
                own = pltpu.make_async_copy(x.at[q], o.at[q], local.at[i])
            own.start()
            waits.append(own)
        for copy in waits:
            copy.wait()

    shapes = []
    for kind, array in items:
        shape = ((C,) + array.shape) if kind == "zag" else array.shape
        shapes.append(jax.ShapeDtypeStruct(shape, array.dtype))
    return pl.pallas_call(
        kernel,
        out_shape=shapes,
        in_specs=[ANY] * count,
        out_specs=[ANY] * count,
        scratch_shapes=[
            DMA((count,)),
            DMA((count, max(C - 1, 1))),
            DMA((count, max(C - 1, 1))),
            DMA((count, max(Q - 1, 1))),
            DMA((count, max(Q - 1, 1))),
        ],
        name=name,
        compiler_params=params(cid),
    )(*[array for _, array in items])


def gather_kernel(tokens, wq, wk, wv, wo, pack, cot, slots, X, W, WO, PK, G, SM, *sems):
    local, zsend, zrecv, fsend, frecv, csend, crecv, wsend, wrecv = sems
    S, C, F = sizes()
    s, c, f = place()
    head_width = wq.shape[1] // C
    z_peers = [(s, lax.rem(c + k, C), f) for k in range(1, C)]
    f_peers = [(s, c, lax.rem(f + k, F)) for k in range(1, F)]
    sibling = (1 - s, c, f)
    pair = s * C + c
    out_dst = (lax.rem(pair, S), pair // S, f)
    pair_in = c * S + s
    out_src = (pair_in // C, lax.rem(pair_in, C), f)
    stays = jnp.logical_and(out_dst[0] == s, out_dst[1] == c)
    moves = jnp.logical_not(stays)
    greet = (
        jnp.where(stays, 1 - s, out_src[0]),
        jnp.where(stays, C - 1 - c, out_src[1]),
        f,
    )
    for peer in z_peers + f_peers + [sibling, greet]:
        signal(peer)
    pl.semaphore_wait(pltpu.get_barrier_semaphore(), C + F)

    def pieces(target):
        kv = (target * KEY_VALUE_HEADS) // C
        q_cols = pl.ds(pl.multiple_of(target * head_width, 128), head_width)
        kv_cols = pl.ds(pl.multiple_of(kv * HEAD_DIM, 128), HEAD_DIM)
        mine = W.at[s, c, f]
        return [
            (wq.at[:, q_cols], mine.at[:, pl.ds(0, head_width)]),
            (wk.at[:, kv_cols], mine.at[:, pl.ds(head_width, HEAD_DIM)]),
            (wv.at[:, kv_cols], mine.at[:, pl.ds(head_width + HEAD_DIM, HEAD_DIM)]),
            (pack, PK.at[s, c, f]),
            (tokens, X.at[c]),
            (slots, SM.at[c]),
            (cot, G.at[c]),
        ]

    own = []
    for i, (src, dst) in enumerate(pieces(c)):
        own.append(pltpu.make_async_copy(src, dst, local.at[i]))
        own[-1].start()
    z_copies = []
    for k, peer in enumerate(z_peers):
        z_copies.append(
            [
                remote(src, dst, zsend.at[i, k], zrecv.at[i, k], peer)
                for i, (src, dst) in enumerate(pieces(peer[1]))
            ]
        )
    for i in range(5):
        for row in z_copies:
            row[i].start()
    out_copy = remote(wo, WO.at[out_dst[0], f], wsend.at[0], wrecv.at[0], out_dst)
    out_stay = pltpu.make_async_copy(wo, WO.at[s, f], wsend.at[1])

    @pl.when(moves)
    def _():
        out_copy.start()

    @pl.when(stays)
    def _():
        out_stay.start()

    for i in range(5, 7):
        for row in z_copies:
            row[i].start()
    for copy in own[:4]:
        copy.wait()
    for row in z_copies:
        for copy in row[:4]:
            copy.wait_recv()
    f_copies = []

    def forward(array, index, block):
        for k, peer in enumerate(f_peers):
            copy = remote(block, block, fsend.at[index, k], frecv.at[index, k], peer)
            copy.start()
            f_copies.append((index, k, array, copy))
        copy = remote(block, block, csend.at[index, 0], crecv.at[index, 0], sibling)
        copy.start()
        return copy

    c_copies = [forward("W", 0, W.at[s, :, f]), forward("P", 1, PK.at[s, :, f])]

    @pl.when(moves)
    def _():
        out_copy.wait()

    @pl.when(stays)
    def _():
        out_stay.wait()

    c_copies.append(forward("O", 2, WO.at[s, f]))
    for index, k, array, copy in f_copies:
        copy.wait_recv()
        came = lax.rem(f + F - (k + 1), F)
        block = {"W": lambda: W.at[s, :, came], "P": lambda: PK.at[s, :, came], "O": lambda: WO.at[s, came]}[array]()
        copy = remote(block, block, csend.at[index, k + 1], crecv.at[index, k + 1], sibling)
        copy.start()
        c_copies.append(copy)
    for index, k, array, copy in f_copies:
        copy.wait_send()
    for copy in c_copies:
        copy.wait()
    for row in z_copies:
        for copy in row[:4]:
            copy.wait_send()
        for copy in row[4:]:
            copy.wait()
    for copy in own[4:]:
        copy.wait()


def gather_all(tokens, wq, wk, wv, wo, pack, cot, slots):
    S, C, F = sizes()
    rows, width = tokens.shape
    head_width = wq.shape[1] // C
    out_shape = [
        jax.ShapeDtypeStruct((C, rows, width), bf16),
        jax.ShapeDtypeStruct((S, C, F, wq.shape[0], head_width + 2 * HEAD_DIM), bf16),
        jax.ShapeDtypeStruct((S, F) + wo.shape, bf16),
        jax.ShapeDtypeStruct((S, C, F) + pack.shape, bf16),
        jax.ShapeDtypeStruct((C, rows, width), bf16),
        jax.ShapeDtypeStruct((C,) + slots.shape, slots.dtype),
    ]
    return pl.pallas_call(
        gather_kernel,
        out_shape=out_shape,
        in_specs=[ANY] * 8,
        out_specs=[ANY] * 6,
        scratch_shapes=[
            DMA((7,)),
            DMA((7, C - 1)),
            DMA((7, C - 1)),
            DMA((3, F - 1)),
            DMA((3, F - 1)),
            DMA((3, F)),
            DMA((3, F)),
            DMA((2,)),
            DMA((1,)),
        ],
        name="gather_weights_tokens",
        compiler_params=params(1),
    )(tokens, wq, wk, wv, wo, pack, cot, slots)


def grads_kernel(gq, go, sp, hg, Q3, O3, S3, H3, *scratch):
    (
        q_own, q_in, q_plane, q_sum,
        o_own, o_in, o_plane, o_sum,
        s_own, s_in, s_plane, s_sum,
        h_in, h_plane, h_acc, h_z,
        local, csend, crecv, fsend, frecv, zsend, zrecv,
    ) = scratch
    S, C, F = sizes()
    s, c, f = place()
    z_peers = [(s, lax.rem(c + k, C), f) for k in range(1, C)]
    f_peers = [(s, c, lax.rem(f + k, F)) for k in range(1, F)]
    sibling = (1 - s, c, f)
    pair = c * S + s
    out_dst = (pair // C, lax.rem(pair, C), f)
    pair_in = s * C + c
    out_src = (lax.rem(pair_in, S), pair_in // S, f)
    stays = jnp.logical_and(out_dst[0] == s, out_dst[1] == c)
    moves = jnp.logical_not(stays)
    greet = (
        jnp.where(stays, 1 - s, out_src[0]),
        jnp.where(stays, C - 1 - c, out_src[1]),
        f,
    )
    for peer in z_peers + f_peers + [sibling, greet]:
        signal(peer)
    pl.semaphore_wait(pltpu.get_barrier_semaphore(), C + F)

    first = [
        remote(go.at[1 - s], o_in, csend.at[0], crecv.at[0], sibling),
        remote(gq.at[1 - s], q_in, csend.at[1], crecv.at[1], sibling),
        remote(sp.at[1 - s], s_in, csend.at[2], crecv.at[2], sibling),
        remote(hg, h_in, csend.at[3], crecv.at[3], sibling),
    ]
    loads = [
        pltpu.make_async_copy(go.at[s], o_own, local.at[0]),
        pltpu.make_async_copy(gq.at[s], q_own, local.at[1]),
        pltpu.make_async_copy(sp.at[s], s_own, local.at[2]),
        pltpu.make_async_copy(hg, h_acc, local.at[3]),
    ]
    for copy in first + loads:
        copy.start()

    def add_into(total, term):
        lead = total.shape[:-2]
        flat = 1
        for size in lead:
            flat *= size

        def body(i, carry):
            index = []
            rest = i
            for size in reversed(lead):
                index.append(lax.rem(rest, size))
                rest = rest // size
            index = tuple(reversed(index))
            total[index] = (total[index].astype(f32) + term[index].astype(f32)).astype(total.dtype)
            return carry

        lax.fori_loop(0, flat, body, 0)

    second = []

    def plane(index, total, part, landing):
        row = []
        for k, peer in enumerate(f_peers):
            copy = remote(part(peer[2]), landing.at[k], fsend.at[index, k], frecv.at[index, k], peer)
            copy.start()
            row.append(copy)
        second.append(row)

    first[0].wait()
    loads[0].wait()
    add_into(o_own, o_in)
    plane(0, o_own, lambda at: o_own.at[at], o_plane)
    first[1].wait()
    loads[1].wait()
    add_into(q_own, q_in)
    plane(1, q_own, lambda at: q_own.at[:, at], q_plane)
    first[2].wait()
    loads[2].wait()
    add_into(s_own, s_in)
    plane(2, s_own, lambda at: s_own.at[:, at], s_plane)
    first[3].wait()
    loads[3].wait()
    h_acc[...] = h_acc[...] + h_in[...]
    plane(3, h_acc, lambda at: h_acc, h_plane)
    for copy in second[0]:
        copy.wait()
    total = o_own[f].astype(f32)
    for k in range(F - 1):
        total = total + o_plane[k].astype(f32)
    o_sum[...] = total.astype(bf16)
    out_copy = remote(o_sum, O3, zsend.at[0, 0], zrecv.at[0, 0], out_dst)
    out_stay = pltpu.make_async_copy(o_sum, O3, local.at[0])

    @pl.when(moves)
    def _():
        out_copy.start()

    @pl.when(stays)
    def _():
        out_stay.start()

    for copy in second[1]:
        copy.wait()

    def q_body(i, carry):
        total = q_own[i, f].astype(f32)
        for k in range(F - 1):
            total = total + q_plane[k, i].astype(f32)
        q_sum[i] = total.astype(bf16)
        return carry

    lax.fori_loop(0, C, q_body, 0)
    third = []
    for k, peer in enumerate(z_peers):
        third.append(remote(q_sum.at[peer[1]], Q3.at[c], zsend.at[1, k], zrecv.at[1, k], peer))
        third[-1].start()
    q_keep = pltpu.make_async_copy(q_sum.at[c], Q3.at[c], local.at[1])
    q_keep.start()
    for copy in second[2]:
        copy.wait()

    def s_body(i, carry):
        total = s_own[i, f]
        for k in range(F - 1):
            total = total + s_plane[k, i]
        s_sum[i] = total
        return carry

    lax.fori_loop(0, C, s_body, 0)
    for k, peer in enumerate(z_peers):
        third.append(remote(s_sum.at[peer[1]], S3.at[c], zsend.at[2, k], zrecv.at[2, k], peer))
        third[-1].start()
    s_keep = pltpu.make_async_copy(s_sum.at[c], S3.at[c], local.at[2])
    s_keep.start()
    for copy in second[3]:
        copy.wait()
    total = h_acc[...]
    order = []
    for g in range(F):
        term = jnp.zeros_like(total)
        for k in range(F - 1):
            came = lax.rem(f + F - (k + 1), F)
            term = term + jnp.where(came == g, h_plane[k], 0.0)
        order.append(term + jnp.where(f == g, h_acc[...], 0.0))
    total = order[0]
    for term in order[1:]:
        total = total + term
    h_z[...] = total
    for k, peer in enumerate(z_peers):
        third.append(remote(h_z, H3.at[c], zsend.at[3, k], zrecv.at[3, k], peer))
        third[-1].start()
    h_keep = pltpu.make_async_copy(h_z, H3.at[c], local.at[3])
    h_keep.start()

    @pl.when(moves)
    def _():
        out_copy.wait()

    @pl.when(stays)
    def _():
        out_stay.wait()

    for copy in third + [q_keep, s_keep, h_keep]:
        copy.wait()


def reduce_grads(gq, go, sp, hg):
    S, C, F = sizes()
    q_block, o_block, s_block = gq.shape[3:], go.shape[2:], sp.shape[3:]
    V = pltpu.VMEM
    return pl.pallas_call(
        grads_kernel,
        out_shape=[
            jax.ShapeDtypeStruct((C,) + q_block, bf16),
            jax.ShapeDtypeStruct(o_block, bf16),
            jax.ShapeDtypeStruct((C,) + s_block, f32),
            jax.ShapeDtypeStruct((C,) + hg.shape, f32),
        ],
        in_specs=[ANY] * 4,
        out_specs=[ANY] * 4,
        scratch_shapes=[
            V((C, F) + q_block, bf16), V((C, F) + q_block, bf16), V((F - 1, C) + q_block, bf16), V((C,) + q_block, bf16),
            V((F,) + o_block, bf16), V((F,) + o_block, bf16), V((F - 1,) + o_block, bf16), V(o_block, bf16),
            V((C, F) + s_block, f32), V((C, F) + s_block, f32), V((F - 1, C) + s_block, f32), V((C,) + s_block, f32),
            V(hg.shape, f32), V((F - 1,) + hg.shape, f32), V(hg.shape, f32), V(hg.shape, f32),
            DMA((4,)), DMA((4,)), DMA((4,)), DMA((4, F - 1)), DMA((4, F - 1)), DMA((4, C - 1)), DMA((4, C - 1)),
        ],
        name="reduce_gradients",
        compiler_params=params(9),
    )(gq, go, sp, hg)


def rms_unit(rows):
    factor = lax.rsqrt(jnp.mean(rows * rows, axis=-1, keepdims=True) + epsilon)
    return rows * factor, factor


def norm_backward(grad_scaled, normed, factor, gain):
    grad_normed = grad_scaled * gain
    inner = jnp.mean(grad_normed * normed, axis=-1, keepdims=True)
    return factor * (grad_normed - normed * inner)


def half_turn(rows, cosine, sine):
    return rows * cosine + pltpu.roll(rows, HEAD_DIM // 2, 1) * sine


def score_block(qr, kr, pos_col, pos_row):
    scores = lax.dot_general(
        qr, kr, (((1,), (1,)), ((), ())), preferred_element_type=f32
    ) * (HEAD_DIM**-0.5)
    scores = jnp.where(pos_col >= pos_row, scores, -jnp.inf)
    peak = jnp.max(scores, axis=-1, keepdims=True)
    weight = jnp.exp(scores - peak)
    return weight * (1.0 / jnp.sum(weight, axis=-1, keepdims=True))


def attend_kernel(block, q, k, v, cosine, sine, pos_col, pos_row, gains, mixed, kr):
    head, part = pl.program_id(0), pl.program_id(1)

    @pl.when(jnp.logical_and(head == 0, part == 0))
    def _():
        unit, _ = rms_unit(k[...])
        kr[...] = half_turn(unit * gains[1:2, :], cosine[...], sine[...]).astype(bf16)

    rows = pl.ds(part * block, block)
    unit, _ = rms_unit(q[...])
    qr = half_turn(unit * gains[0:1, :], cosine[rows, :], sine[rows, :]).astype(bf16)
    probs = score_block(qr, kr[...], pos_col[rows, :], pos_row[...])
    mixed[...] = jnp.dot(probs.astype(bf16), v[...], preferred_element_type=f32).astype(bf16)


def attend(q, k, v, cosine, sine, pos_col, pos_row, gains):
    length, width = q.shape
    heads = width // HEAD_DIM
    block = min(length, 512)
    whole = lambda array: pl.BlockSpec(array.shape, lambda h, i: (0, 0))
    return pl.pallas_call(
        functools.partial(attend_kernel, block),
        out_shape=jax.ShapeDtypeStruct((length, width), bf16),
        grid=(heads, length // block),
        in_specs=[pl.BlockSpec((block, HEAD_DIM), lambda h, i: (i, h))]
        + [whole(array) for array in (k, v, cosine, sine, pos_col, pos_row, gains)],
        out_specs=pl.BlockSpec((block, HEAD_DIM), lambda h, i: (i, h)),
        scratch_shapes=[pltpu.VMEM((length, HEAD_DIM), bf16)],
        name="attention_forward",
        compiler_params=pltpu.CompilerParams(vmem_limit_bytes=VMEM_LIMIT),
    )(q, k, v, cosine, sine, pos_col, pos_row, gains)


def attend_back_kernel(
    heads, block, q, dmixed, k, v, cosine, sine, pos_col, pos_row, gains, out, head_grad, kr, dkr, dv
):
    head, part = pl.program_id(0), pl.program_id(1)
    rows = pl.ds(part * block, block)

    @pl.when(jnp.logical_and(head == 0, part == 0))
    def _():
        unit, _ = rms_unit(k[...])
        kr[...] = half_turn(unit * gains[1:2, :], cosine[...], sine[...]).astype(bf16)
        dkr[...] = jnp.zeros_like(dkr)
        dv[...] = jnp.zeros_like(dv)
        head_grad[...] = jnp.zeros_like(head_grad)

    @pl.when(head < heads)
    def _():
        unit, factor = rms_unit(q[...])
        cos, sin = cosine[rows, :], sine[rows, :]
        qr = half_turn(unit * gains[0:1, :], cos, sin).astype(bf16)
        keys = kr[...]
        probs = score_block(qr, keys, pos_col[rows, :], pos_row[...])
        dm = dmixed[...]
        dprobs = lax.dot_general(dm, v[...], (((1,), (1,)), ((), ())), preferred_element_type=f32)
        delta = jnp.sum(probs * dprobs, axis=-1, keepdims=True)
        dscores = (probs * (dprobs - delta)).astype(bf16)
        dqr = jnp.dot(dscores, keys, preferred_element_type=f32) * (HEAD_DIM**-0.5)
        rows_in = (((0,), (0,)), ((), ()))
        dkr[...] += lax.dot_general(dscores, qr, rows_in, preferred_element_type=f32) * (HEAD_DIM**-0.5)
        dv[...] += lax.dot_general(probs.astype(bf16), dm, rows_in, preferred_element_type=f32)
        dqs = half_turn(dqr, cos, -sin)
        head_grad[0:1, :] += jnp.sum(dqs * unit, axis=0, keepdims=True)
        out[...] = norm_backward(dqs, unit, factor, gains[0:1, :]).astype(bf16)

    @pl.when(head == heads)
    def _():
        unit, factor = rms_unit(k[rows, :])
        dks = half_turn(dkr[rows, :], cosine[rows, :], -sine[rows, :])
        head_grad[1:2, :] += jnp.sum(dks * unit, axis=0, keepdims=True)
        out[...] = norm_backward(dks, unit, factor, gains[1:2, :]).astype(bf16)

    @pl.when(head == heads + 1)
    def _():
        out[...] = dv[rows, :].astype(bf16)


def attend_back(q, dmixed, k, v, cosine, sine, pos_col, pos_row, gains):
    length, width = q.shape
    heads = width // HEAD_DIM
    block = min(length, 512)
    whole = lambda array: pl.BlockSpec(array.shape, lambda h, i: (0, 0))
    per_head = pl.BlockSpec((block, HEAD_DIM), lambda h, i: (i, jnp.minimum(h, heads - 1)))
    return pl.pallas_call(
        functools.partial(attend_back_kernel, heads, block),
        out_shape=[
            jax.ShapeDtypeStruct((length, width + 2 * HEAD_DIM), bf16),
            jax.ShapeDtypeStruct((8, HEAD_DIM), f32),
        ],
        grid=(heads + 2, length // block),
        in_specs=[per_head, per_head]
        + [whole(array) for array in (k, v, cosine, sine, pos_col, pos_row, gains)],
        out_specs=[
            pl.BlockSpec((block, HEAD_DIM), lambda h, i: (i, h)),
            pl.BlockSpec((8, HEAD_DIM), lambda h, i: (0, 0)),
        ],
        scratch_shapes=[
            pltpu.VMEM((length, HEAD_DIM), bf16),
            pltpu.VMEM((length, HEAD_DIM), f32),
            pltpu.VMEM((length, HEAD_DIM), f32),
        ],
        name="attention_backward",
        compiler_params=pltpu.CompilerParams(vmem_limit_bytes=VMEM_LIMIT),
    )(q, dmixed, k, v, cosine, sine, pos_col, pos_row, gains)


def dot(left, right):
    return jnp.dot(left, right, preferred_element_type=f32)


def contract_rows(left, right):
    return lax.dot_general(left, right, (((0,), (0,)), ((), ())), preferred_element_type=f32)


def times_transpose(left, right):
    return lax.dot_general(left, right, (((1,), (1,)), ((), ())), preferred_element_type=f32)


def on_device(
    tokens,
    stretch_order,
    expert_ids,
    slot_index,
    norm_attn,
    head_gains,
    w_query,
    w_key,
    w_value,
    w_out,
    norm_moe,
    w_router,
    w_gate,
    w_up,
    w_down,
    cotangent,
):
    S, C, F = sizes()
    Q = S * F
    seq_at, ctx_at, fsdp_at = place()
    rows, width = tokens.shape[1:]
    length = C * rows
    experts = w_router.shape[1]
    capacity = rows * TOP // (Q * C) + 1
    packed = round_up(C * capacity, 16)
    lanes = round_up(packed, 128)
    head_width = w_query.shape[1] // C
    shard = w_router.shape[0]
    stretch_rows = rows // 2
    route_ids, slot_ids = expert_ids[0], slot_index[0]
    picker = route_ids[:, :, None] == jnp.arange(experts, dtype=jnp.int32)
    kept = slot_ids < capacity
    slot_map = jnp.max(
        jnp.where(picker & kept[:, :, None], slot_ids[:, :, None], -1), axis=1
    ).astype(f32)
    slot_map = jnp.pad(slot_map, ((0, 0), (0, round_up(experts, 128) - experts)))
    pack_width = round_up(experts + 2, 128)
    pack = jnp.concatenate(
        [
            w_router,
            norm_attn[:, None],
            norm_moe[:, None],
            jnp.zeros((shard, pack_width - experts - 2), bf16),
        ],
        axis=1,
    )
    X, W, WO, PK, G, SM = gather_all(
        tokens[0], w_query, w_key, w_value, w_out, pack, cotangent[0], slot_map
    )
    W = W.reshape(width, head_width + 2 * HEAD_DIM)
    WO = WO.reshape(head_width, width)
    PK = PK.reshape(width, pack_width)
    router = PK[:, :experts]
    gain_attn = PK[:, experts].astype(f32)
    gain_moe = PK[:, experts + 1].astype(f32)
    gains = head_gains.astype(f32)
    positions = (
        stretch_order[:, None] * stretch_rows + jnp.arange(stretch_rows, dtype=jnp.int32)[None, :]
    ).reshape(-1)
    frequency = jnp.power(rope_base, -jnp.arange(HEAD_DIM // 2, dtype=f32) * 2.0 / HEAD_DIM)
    angles = positions.astype(f32)[:, None] * frequency[None, :]
    cosine, sine = jnp.cos(angles), jnp.sin(angles)
    cosine = jnp.concatenate([cosine, cosine], axis=1)
    sine = jnp.concatenate([-sine, sine], axis=1)
    pos_col, pos_row = positions[:, None], positions[None, :]
    inputs_all = X.reshape(length, width).astype(f32)
    normed_one, _ = rms_unit(inputs_all)
    xn = (normed_one * gain_attn).astype(bf16)
    qkv = dot(xn, W)
    q, k = qkv[:, :head_width], qkv[:, head_width : head_width + HEAD_DIM]
    v = qkv[:, head_width + HEAD_DIM :].astype(bf16)
    mixed = attend(q, k, v, cosine, sine, pos_col, pos_row, gains)
    out_part = dot(mixed, WO).astype(bf16).reshape(C, rows, width)
    slot_plane = lax.dynamic_index_in_dim(
        SM[:, :, :experts].reshape(length, S, C, F), ctx_at, axis=2, keepdims=False
    ).reshape(length, Q)
    source = jnp.repeat(jnp.arange(C, dtype=jnp.int32), rows)[:, None]
    slot_plane = slot_plane.astype(jnp.int32)
    target = jnp.where(slot_plane >= 0, slot_plane + source * capacity, -1).T
    select = target[:, None, :] == jnp.arange(packed, dtype=jnp.int32)[None, :, None]
    select_low = select.astype(bf16).reshape(Q * packed, length)

    def to_slots(array):
        return dot(select_low, array.reshape(length, width)).astype(bf16).reshape(Q, packed, width)

    def from_slots(array):
        return contract_rows(select_low, array.reshape(Q * packed, width)).astype(bf16)

    out_parts, dispatched_grad = exchange(
        "sum_out_projection", 2, [("za2a", out_part), ("pa2a", to_slots(G))]
    )
    h1 = tokens[0].astype(f32) + jnp.sum(out_parts.astype(f32), axis=0)
    normed_two, factor_two = rms_unit(h1)
    xm = (normed_two * gain_moe).astype(bf16)
    logits = dot(xm, router)
    picker_f = picker.astype(f32)
    chosen = jnp.sum(picker_f * logits[:, None, :], axis=-1)
    gates = jax.nn.softmax(chosen, axis=-1)
    weight = gates * kept.astype(f32)
    weight_map = jnp.sum(picker_f * weight[:, :, None], axis=1)
    weight_map = jnp.pad(weight_map, ((0, 0), (0, round_up(experts, 128) - experts)))
    XM, WM = exchange("gather_moe_rows", 3, [("zag", xm), ("zag", weight_map)])
    weight_plane = lax.dynamic_index_in_dim(
        WM[:, :, :experts].reshape(length, S, C, F), ctx_at, axis=2, keepdims=False
    ).reshape(length, Q)
    slot_weight = jnp.sum(jnp.where(select, weight_plane.T[:, None, :], 0.0), axis=-1)
    slot_weight = jnp.broadcast_to(
        jnp.pad(slot_weight, ((0, 0), (0, lanes - packed)))[:, None, :], (Q, 8, lanes)
    )
    buffer, slot_weight = exchange(
        "dispatch_moe_rows", 4, [("pa2a", to_slots(XM)), ("pa2a", slot_weight)]
    )
    buffer = buffer.reshape(Q * packed, width)
    slot_weight = slot_weight[:, 0, :packed].reshape(Q * packed, 1)
    slot_grad = dispatched_grad.reshape(Q * packed, width).astype(f32)
    gate_pre = dot(buffer, w_gate[0])
    up_pre = dot(buffer, w_up[0])
    sigmoid_gp = jax.nn.sigmoid(gate_pre)
    silu_gp = gate_pre * sigmoid_gp
    hidden = (silu_gp * up_pre).astype(bf16)
    y = dot(hidden, w_down[0])
    weighted_y = (slot_weight * y).astype(bf16).reshape(Q, packed, width)
    slot_dgate = jnp.sum(slot_grad * y, axis=-1).reshape(Q, packed)
    dy = (slot_weight * slot_grad).astype(bf16)
    dhid = times_transpose(dy, w_down[0])
    dgp = (dhid * up_pre * sigmoid_gp * (1.0 + gate_pre * (1.0 - sigmoid_gp))).astype(bf16)
    dup = (dhid * silu_gp).astype(bf16)
    din = (times_transpose(dgp, w_gate[0]) + times_transpose(dup, w_up[0])).astype(bf16)
    slot_dgate = jnp.broadcast_to(
        jnp.pad(slot_dgate, ((0, 0), (0, lanes - packed)))[:, None, :], (Q, 8, lanes)
    )
    back_in, back_dgate = exchange(
        "return_moe_grads", 5, [("pa2a", din.reshape(Q, packed, width)), ("pa2a", slot_dgate)]
    )
    grad_wgate = contract_rows(buffer, dgp)
    grad_wup = contract_rows(buffer, dup)
    grad_wdown = contract_rows(hidden, dy)
    dxm_part = from_slots(back_in).reshape(C, rows, width)
    dgate_part = jnp.sum(
        jnp.where(select, back_dgate[:, 0, :packed, None], 0.0), axis=1
    ).T.reshape(C, rows, Q)
    dgate_part = jnp.pad(dgate_part, ((0, 0), (0, 0), (0, round_up(Q, 128) - Q)))
    dxm_parts, dgate_parts, back_y = exchange(
        "sum_moe_grads", 6, [("za2a", dxm_part), ("za2a", dgate_part), ("pa2a", weighted_y)]
    )
    dgate_map = (
        dgate_parts[:, :, :Q].reshape(C, rows, S, F).transpose(1, 2, 0, 3).reshape(rows, experts)
    )
    dgate = jnp.sum(picker_f * dgate_map[:, None, :], axis=-1)
    dchosen = gates * (dgate - jnp.sum(gates * dgate, axis=-1, keepdims=True))
    dlogits = jnp.sum(picker_f * dchosen[:, :, None], axis=1).astype(bf16)
    dxm = jnp.sum(dxm_parts.astype(f32), axis=0) + times_transpose(dlogits, router)
    grad_router = contract_rows(xm, dlogits)
    grad_norm_moe = jnp.sum(dxm * normed_two, axis=0)
    dh1 = cotangent[0].astype(f32) + norm_backward(dxm, normed_two, factor_two, gain_moe)
    (DA,) = exchange("gather_attention_grads", 7, [("zag", dh1.astype(bf16))])
    DA = DA.reshape(length, width)
    dmixed = times_transpose(DA, WO).astype(bf16)
    grad_out_part = contract_rows(mixed, DA).astype(bf16)
    dqkv, head_grad = attend_back(q, dmixed, k, v, cosine, sine, pos_col, pos_row, gains)
    grad_qkv_part = contract_rows(xn, dqkv).astype(bf16)
    dxn_part = times_transpose(dqkv, W)
    grad_norm_attn = jnp.sum(dxn_part * normed_one, axis=0)
    y_part = from_slots(back_y).reshape(C, rows, width)
    dxn_parts, y_parts = exchange(
        "sum_input_grads", 8, [("za2a", dxn_part.astype(bf16).reshape(C, rows, width)), ("za2a", y_part)]
    )
    small = jnp.concatenate(
        [
            grad_router,
            grad_norm_attn[:, None],
            grad_norm_moe[:, None],
            jnp.zeros((width, pack_width - experts - 2), f32),
        ],
        axis=1,
    )
    q_sums, o_sum, small_sums, head_sums = reduce_grads(
        grad_qkv_part.reshape(S, C, F, shard, head_width + 2 * HEAD_DIM),
        grad_out_part.reshape(S, F, head_width // Q, width),
        small.reshape(S, C, F, shard, pack_width),
        head_grad,
    )
    layer_out = (h1 + jnp.sum(y_parts.astype(f32), axis=0)).astype(bf16)
    inputs = tokens[0].astype(f32)
    unit, factor = rms_unit(inputs)
    dxn = jnp.sum(dxn_parts.astype(f32), axis=0)
    grad_tokens = (dh1 + norm_backward(dxn, unit, factor, gain_attn)).astype(bf16)
    q_sums = q_sums.astype(f32)
    grad_query = q_sums[:, :, :head_width].transpose(1, 0, 2).reshape(shard, C * head_width)

    def key_columns(block):
        pieces = block.reshape(KEY_VALUE_HEADS, C // KEY_VALUE_HEADS, shard, HEAD_DIM).sum(axis=1)
        return pieces.transpose(1, 0, 2).reshape(shard, KEY_VALUE_HEADS * HEAD_DIM)

    grad_key = key_columns(q_sums[:, :, head_width : head_width + HEAD_DIM])
    grad_value = key_columns(q_sums[:, :, head_width + HEAD_DIM :])
    small_sum = jnp.sum(small_sums, axis=0)
    return (
        layer_out[None],
        grad_tokens[None],
        small_sum[:, experts],
        jnp.sum(head_sums, axis=0)[:2],
        grad_query,
        grad_key,
        grad_value,
        o_sum.astype(f32),
        small_sum[:, experts + 1],
        small_sum[:, :experts],
        grad_wgate[None],
        grad_wup[None],
        grad_wdown[None],
    )


def solution(mesh):
    rows = P(("seq", "fsdp"), "ctx", None)
    vector = P(AXES)
    matrix = P(AXES, None)
    cube = P(AXES, None, None)
    return jax.shard_map(
        on_device,
        mesh=mesh,
        in_specs=(
            rows, P(), rows, rows, vector, P(), matrix, matrix, matrix, matrix,
            vector, matrix, cube, cube, cube, rows,
        ),
        out_specs=(
            rows, rows, vector, P(), matrix, matrix, matrix, matrix, vector, matrix,
            cube, cube, cube,
        ),
        check_vma=False,
    )
```

```python
import functools

import jax
import jax.numpy as jnp
from jax import lax
from jax.experimental import pallas as pl
from jax.experimental.pallas import tpu as pltpu
from jax.sharding import PartitionSpec as P

QUERY_HEADS = 32
KEY_VALUE_HEADS = 4
HEAD_DIM = 128
TOP = 8
AXES = ("seq", "ctx", "fsdp")
MESH = pl.DeviceIdType.MESH
epsilon = 1e-06
rope_base = 1000000.0
VMEM_LIMIT = 56 * 2**20
f32 = jnp.float32
bf16 = jnp.bfloat16


def round_up(value, step):
    return (value + step - 1) // step * step


def place():
    return tuple(lax.axis_index(name) for name in AXES)


def sizes():
    return tuple(lax.axis_size(name) for name in AXES)


def signal(device):
    pl.semaphore_signal(
        pltpu.get_barrier_semaphore(), inc=1, device_id=device, device_id_type=MESH
    )


def remote(src, dst, send, recv, device):
    return pltpu.make_async_remote_copy(
        src_ref=src,
        dst_ref=dst,
        send_sem=send,
        recv_sem=recv,
        device_id=device,
        device_id_type=MESH,
    )


def params(cid, limit=VMEM_LIMIT):
    return pltpu.CompilerParams(
        collective_id=cid, has_side_effects=True, vmem_limit_bytes=limit
    )


ANY = pl.BlockSpec(memory_space=pl.ANY)
DMA = pltpu.SemaphoreType.DMA


def gather_kernel(tokens, wq, wk, wv, wo, pack, slots, X, W, WO, PK, SM, *sems):
    local, zsend, zrecv, fsend, frecv, csend, crecv, wsend, wrecv = sems
    S, C, F = sizes()
    s, c, f = place()
    head_width = wq.shape[1] // C
    z_peers = [(s, lax.rem(c + k, C), f) for k in range(1, C)]
    f_peers = [(s, c, lax.rem(f + k, F)) for k in range(1, F)]
    sibling = (1 - s, c, f)
    pair = s * C + c
    out_dst = (lax.rem(pair, S), pair // S, f)
    pair_in = c * S + s
    out_src = (pair_in // C, lax.rem(pair_in, C), f)
    stays = jnp.logical_and(out_dst[0] == s, out_dst[1] == c)
    moves = jnp.logical_not(stays)
    greet = (
        jnp.where(stays, 1 - s, out_src[0]),
        jnp.where(stays, C - 1 - c, out_src[1]),
        f,
    )
    for peer in z_peers + f_peers + [sibling, greet]:
        signal(peer)
    pl.semaphore_wait(pltpu.get_barrier_semaphore(), C + F)

    def pieces(target):
        kv = (target * KEY_VALUE_HEADS) // C
        q_cols = pl.ds(pl.multiple_of(target * head_width, 128), head_width)
        kv_cols = pl.ds(pl.multiple_of(kv * HEAD_DIM, 128), HEAD_DIM)
        mine = W.at[s, c, f]
        return [
            (wq.at[:, q_cols], mine.at[:, pl.ds(0, head_width)]),
            (wk.at[:, kv_cols], mine.at[:, pl.ds(head_width, HEAD_DIM)]),
            (wv.at[:, kv_cols], mine.at[:, pl.ds(head_width + HEAD_DIM, HEAD_DIM)]),
            (pack, PK.at[s, c, f]),
            (tokens, X.at[c]),
            (slots, SM.at[c]),
        ]

    own = []
    for i, (src, dst) in enumerate(pieces(c)):
        own.append(pltpu.make_async_copy(src, dst, local.at[i]))
        own[-1].start()
    z_copies = []
    for k, peer in enumerate(z_peers):
        z_copies.append(
            [
                remote(src, dst, zsend.at[i, k], zrecv.at[i, k], peer)
                for i, (src, dst) in enumerate(pieces(peer[1]))
            ]
        )
    for i in range(4):
        for row in z_copies:
            row[i].start()
    out_copy = remote(wo, WO.at[out_dst[0], f], wsend.at[0], wrecv.at[0], out_dst)
    out_stay = pltpu.make_async_copy(wo, WO.at[s, f], wsend.at[1])

    @pl.when(moves)
    def _():
        out_copy.start()

    @pl.when(stays)
    def _():
        out_stay.start()

    for i in range(4, 6):
        for row in z_copies:
            row[i].start()
    for copy in own[:4]:
        copy.wait()
    for row in z_copies:
        for copy in row[:4]:
            copy.wait_recv()
    f_copies = []

    def forward(array, index, block):
        for k, peer in enumerate(f_peers):
            copy = remote(block, block, fsend.at[index, k], frecv.at[index, k], peer)
            copy.start()
            f_copies.append((index, k, array, copy))
        copy = remote(block, block, csend.at[index, 0], crecv.at[index, 0], sibling)
        copy.start()
        return copy

    c_copies = [forward("W", 0, W.at[s, :, f]), forward("P", 1, PK.at[s, :, f])]

    @pl.when(moves)
    def _():
        out_copy.wait()

    @pl.when(stays)
    def _():
        out_stay.wait()

    c_copies.append(forward("O", 2, WO.at[s, f]))
    for index, k, array, copy in f_copies:
        copy.wait_recv()
        came = lax.rem(f + F - (k + 1), F)
        block = {"W": lambda: W.at[s, :, came], "P": lambda: PK.at[s, :, came], "O": lambda: WO.at[s, came]}[array]()
        copy = remote(block, block, csend.at[index, k + 1], crecv.at[index, k + 1], sibling)
        copy.start()
        c_copies.append(copy)
    for index, k, array, copy in f_copies:
        copy.wait_send()
    for copy in c_copies:
        copy.wait()
    for row in z_copies:
        for copy in row[:4]:
            copy.wait_send()
        for copy in row[4:]:
            copy.wait()
    for copy in own[4:]:
        copy.wait()


def gather_all(tokens, wq, wk, wv, wo, pack, slots):
    S, C, F = sizes()
    rows, width = tokens.shape
    head_width = wq.shape[1] // C
    out_shape = [
        jax.ShapeDtypeStruct((C, rows, width), bf16),
        jax.ShapeDtypeStruct((S, C, F, wq.shape[0], head_width + 2 * HEAD_DIM), bf16),
        jax.ShapeDtypeStruct((S, F) + wo.shape, bf16),
        jax.ShapeDtypeStruct((S, C, F) + pack.shape, bf16),
        jax.ShapeDtypeStruct((C,) + slots.shape, slots.dtype),
    ]
    return pl.pallas_call(
        gather_kernel,
        out_shape=out_shape,
        in_specs=[ANY] * 7,
        out_specs=[ANY] * 5,
        scratch_shapes=[
            DMA((6,)),
            DMA((6, C - 1)),
            DMA((6, C - 1)),
            DMA((3, F - 1)),
            DMA((3, F - 1)),
            DMA((3, F)),
            DMA((3, F)),
            DMA((2,)),
            DMA((1,)),
        ],
        name="gather_weights_tokens",
        compiler_params=params(1),
    )(tokens, wq, wk, wv, wo, pack, slots)


def grads_kernel(gq, go, sp, hg, dx, yp, Q3, O3, S3, H3, DX, YP, *scratch):
    (
        q_own, q_in, q_plane, q_sum,
        o_own, o_in, o_plane, o_sum,
        s_own, s_in, s_plane, s_sum,
        h_in, h_plane, h_acc, h_z,
        local, csend, crecv, fsend, frecv, zsend, zrecv, tsend, trecv,
    ) = scratch
    S, C, F = sizes()
    s, c, f = place()
    z_peers = [(s, lax.rem(c + k, C), f) for k in range(1, C)]
    f_peers = [(s, c, lax.rem(f + k, F)) for k in range(1, F)]
    sibling = (1 - s, c, f)
    pair = c * S + s
    out_dst = (pair // C, lax.rem(pair, C), f)
    pair_in = s * C + c
    out_src = (lax.rem(pair_in, S), pair_in // S, f)
    stays = jnp.logical_and(out_dst[0] == s, out_dst[1] == c)
    moves = jnp.logical_not(stays)
    greet = (
        jnp.where(stays, 1 - s, out_src[0]),
        jnp.where(stays, C - 1 - c, out_src[1]),
        f,
    )
    for peer in z_peers + f_peers + [sibling, greet]:
        signal(peer)
    pl.semaphore_wait(pltpu.get_barrier_semaphore(), C + F)

    first = [
        remote(go.at[1 - s], o_in, csend.at[0], crecv.at[0], sibling),
        remote(gq.at[1 - s], q_in, csend.at[1], crecv.at[1], sibling),
        remote(sp.at[1 - s], s_in, csend.at[2], crecv.at[2], sibling),
        remote(hg, h_in, csend.at[3], crecv.at[3], sibling),
    ]
    loads = [
        pltpu.make_async_copy(go.at[s], o_own, local.at[0]),
        pltpu.make_async_copy(gq.at[s], q_own, local.at[1]),
        pltpu.make_async_copy(sp.at[s], s_own, local.at[2]),
        pltpu.make_async_copy(hg, h_acc, local.at[3]),
    ]
    for copy in first + loads:
        copy.start()
    tokens_back = []
    for i, (src, dst) in enumerate(((dx, DX), (yp, YP))):
        for k, peer in enumerate(z_peers):
            tokens_back.append(
                remote(src.at[peer[1]], dst.at[c], tsend.at[i, k], trecv.at[i, k], peer)
            )
        tokens_back.append(pltpu.make_async_copy(src.at[c], dst.at[c], local.at[4 + i]))
    for copy in tokens_back:
        copy.start()

    def add_into(total, term):
        lead = total.shape[:-2]
        flat = 1
        for size in lead:
            flat *= size

        def body(i, carry):
            index = []
            rest = i
            for size in reversed(lead):
                index.append(lax.rem(rest, size))
                rest = rest // size
            index = tuple(reversed(index))
            total[index] = (total[index].astype(f32) + term[index].astype(f32)).astype(total.dtype)
            return carry

        lax.fori_loop(0, flat, body, 0)

    second = []

    def plane(index, total, part, landing):
        row = []
        for k, peer in enumerate(f_peers):
            copy = remote(part(peer[2]), landing.at[k], fsend.at[index, k], frecv.at[index, k], peer)
            copy.start()
            row.append(copy)
        second.append(row)

    first[0].wait()
    loads[0].wait()
    add_into(o_own, o_in)
    plane(0, o_own, lambda at: o_own.at[at], o_plane)
    first[1].wait()
    loads[1].wait()
    add_into(q_own, q_in)
    plane(1, q_own, lambda at: q_own.at[:, at], q_plane)
    first[2].wait()
    loads[2].wait()
    add_into(s_own, s_in)
    plane(2, s_own, lambda at: s_own.at[:, at], s_plane)
    first[3].wait()
    loads[3].wait()
    h_acc[...] = h_acc[...] + h_in[...]
    plane(3, h_acc, lambda at: h_acc, h_plane)
    for copy in second[0]:
        copy.wait()
    total = o_own[f].astype(f32)
    for k in range(F - 1):
        total = total + o_plane[k].astype(f32)
    o_sum[...] = total.astype(bf16)
    out_copy = remote(o_sum, O3, zsend.at[0, 0], zrecv.at[0, 0], out_dst)
    out_stay = pltpu.make_async_copy(o_sum, O3, local.at[0])

    @pl.when(moves)
    def _():
        out_copy.start()

    @pl.when(stays)
    def _():
        out_stay.start()

    for copy in second[1]:
        copy.wait()

    def q_body(i, carry):
        total = q_own[i, f].astype(f32)
        for k in range(F - 1):
            total = total + q_plane[k, i].astype(f32)
        q_sum[i] = total.astype(bf16)
        return carry

    lax.fori_loop(0, C, q_body, 0)
    third = []
    for k, peer in enumerate(z_peers):
        third.append(remote(q_sum.at[peer[1]], Q3.at[c], zsend.at[1, k], zrecv.at[1, k], peer))
        third[-1].start()
    q_keep = pltpu.make_async_copy(q_sum.at[c], Q3.at[c], local.at[1])
    q_keep.start()
    for copy in second[2]:
        copy.wait()

    def s_body(i, carry):
        total = s_own[i, f]
        for k in range(F - 1):
            total = total + s_plane[k, i]
        s_sum[i] = total
        return carry

    lax.fori_loop(0, C, s_body, 0)
    for k, peer in enumerate(z_peers):
        third.append(remote(s_sum.at[peer[1]], S3.at[c], zsend.at[2, k], zrecv.at[2, k], peer))
        third[-1].start()
    s_keep = pltpu.make_async_copy(s_sum.at[c], S3.at[c], local.at[2])
    s_keep.start()
    for copy in second[3]:
        copy.wait()
    total = h_acc[...]
    order = []
    for g in range(F):
        term = jnp.zeros_like(total)
        for k in range(F - 1):
            came = lax.rem(f + F - (k + 1), F)
            term = term + jnp.where(came == g, h_plane[k], 0.0)
        order.append(term + jnp.where(f == g, h_acc[...], 0.0))
    total = order[0]
    for term in order[1:]:
        total = total + term
    h_z[...] = total
    for k, peer in enumerate(z_peers):
        third.append(remote(h_z, H3.at[c], zsend.at[3, k], zrecv.at[3, k], peer))
        third[-1].start()
    h_keep = pltpu.make_async_copy(h_z, H3.at[c], local.at[3])
    h_keep.start()

    @pl.when(moves)
    def _():
        out_copy.wait()

    @pl.when(stays)
    def _():
        out_stay.wait()

    for copy in third + [q_keep, s_keep, h_keep] + tokens_back:
        copy.wait()


def reduce_grads(gq, go, sp, hg, dx, yp):
    S, C, F = sizes()
    q_block, o_block, s_block = gq.shape[3:], go.shape[2:], sp.shape[3:]
    V = pltpu.VMEM
    return pl.pallas_call(
        grads_kernel,
        out_shape=[
            jax.ShapeDtypeStruct((C,) + q_block, bf16),
            jax.ShapeDtypeStruct(o_block, bf16),
            jax.ShapeDtypeStruct((C,) + s_block, f32),
            jax.ShapeDtypeStruct((C,) + hg.shape, f32),
            jax.ShapeDtypeStruct(dx.shape, bf16),
            jax.ShapeDtypeStruct(yp.shape, bf16),
        ],
        in_specs=[ANY] * 6,
        out_specs=[ANY] * 6,
        scratch_shapes=[
            V((C, F) + q_block, bf16), V((C, F) + q_block, bf16), V((F - 1, C) + q_block, bf16), V((C,) + q_block, bf16),
            V((F,) + o_block, bf16), V((F,) + o_block, bf16), V((F - 1,) + o_block, bf16), V(o_block, bf16),
            V((C, F) + s_block, f32), V((C, F) + s_block, f32), V((F - 1, C) + s_block, f32), V((C,) + s_block, f32),
            V(hg.shape, f32), V((F - 1,) + hg.shape, f32), V(hg.shape, f32), V(hg.shape, f32),
            DMA((6,)), DMA((4,)), DMA((4,)), DMA((4, F - 1)), DMA((4, F - 1)), DMA((4, C - 1)), DMA((4, C - 1)),
            DMA((2, C - 1)), DMA((2, C - 1)),
        ],
        name="reduce_gradients",
        compiler_params=params(9),
    )(gq, go, sp, hg, dx, yp)


def rms_unit(rows):
    factor = lax.rsqrt(jnp.mean(rows * rows, axis=-1, keepdims=True) + epsilon)
    return rows * factor, factor


def norm_backward(grad_scaled, normed, factor, gain):
    grad_normed = grad_scaled * gain
    inner = jnp.mean(grad_normed * normed, axis=-1, keepdims=True)
    return factor * (grad_normed - normed * inner)


def half_turn(rows, cosine, sine):
    return rows * cosine + pltpu.roll(rows, HEAD_DIM // 2, 1) * sine


def score_block(qr, kr, pos_col, pos_row):
    scores = lax.dot_general(
        qr, kr, (((1,), (1,)), ((), ())), preferred_element_type=f32
    ) * (HEAD_DIM**-0.5)
    scores = jnp.where(pos_col >= pos_row, scores, -jnp.inf)
    peak = jnp.max(scores, axis=-1, keepdims=True)
    weight = jnp.exp(scores - peak)
    return weight * (1.0 / jnp.sum(weight, axis=-1, keepdims=True))


def z_neighbours():
    _, C, _ = sizes()
    s, c, f = place()
    return [(s, lax.rem(c + k, C), f) for k in range(1, C)]


def plane_neighbours():
    S, _, F = sizes()
    s, c, f = place()
    Q = S * F
    at = [lax.rem(s * F + f + k, Q) for k in range(1, Q)]
    return at, [(q // F, c, lax.rem(q, F)) for q in at]


def greet_all(peers):
    for peer in peers:
        signal(peer)
    pl.semaphore_wait(pltpu.get_barrier_semaphore(), len(peers))


def forward_kernel(
    block, x, w, wo, gain, cosine, sine, pos_col, pos_row, gains, cot,
    out, q_out, k_out, v_out, mixed, xn, G, kr, acc, local, zsend, zrecv,
):
    step = pl.program_id(0)
    length = x.shape[0]
    head_width = wo.shape[0]
    c = lax.axis_index("ctx")
    peers = z_neighbours()
    copies = [
        remote(cot, G.at[c], zsend.at[k], zrecv.at[k], peer) for k, peer in enumerate(peers)
    ]
    copies.append(pltpu.make_async_copy(cot, G.at[c], local))

    @pl.when(step == 0)
    def _():
        greet_all(peers)
        for copy in copies:
            copy.start()

        def norm_rows(i, carry):
            rows = pl.ds(i * 64, 64)
            unit, _ = rms_unit(x[rows, :].astype(f32))
            xn[rows, :] = (unit * gain[...]).astype(bf16)
            return carry

        lax.fori_loop(0, length // 64, norm_rows, 0)
        kv = jnp.dot(xn[...], w[:, head_width:], preferred_element_type=f32)
        k = kv[:, :HEAD_DIM]
        k_out[...] = k
        v_out[...] = kv[:, HEAD_DIM:].astype(bf16)
        unit, _ = rms_unit(k)
        kr[...] = half_turn(unit * gains[1:2, :], cosine[...], sine[...]).astype(bf16)

    pair = pl.ds(pl.multiple_of(step * 2 * HEAD_DIM, 2 * HEAD_DIM), 2 * HEAD_DIM)
    q_out[...] = jnp.dot(xn[...], w[:, pair], preferred_element_type=f32)
    for half in range(2):
        lanes = slice(half * HEAD_DIM, (half + 1) * HEAD_DIM)
        for part in range(length // block):
            rows = slice(part * block, (part + 1) * block)
            unit, _ = rms_unit(q_out[rows, lanes])
            qr = half_turn(unit * gains[0:1, :], cosine[rows, :], sine[rows, :]).astype(bf16)
            probs = score_block(qr, kr[...], pos_col[rows, :], pos_row[...])
            mixed[rows, lanes] = jnp.dot(
                probs.astype(bf16), v_out[...], preferred_element_type=f32
            ).astype(bf16)
    term = jnp.dot(mixed[...], wo[pair, :], preferred_element_type=f32)

    @pl.when(step == 0)
    def _():
        acc[...] = term

    @pl.when(step > 0)
    def _():
        acc[...] += term

    @pl.when(step == pl.num_programs(0) - 1)
    def _():
        out[...] = acc[...].astype(bf16)
        for copy in copies:
            copy.wait()


def forward(x, w, wo, gain, cosine, sine, pos_col, pos_row, gains, cot):
    S, C, F = sizes()
    length, width = x.shape
    head_width = wo.shape[0]
    block = min(length, 512)
    whole = lambda array: pl.BlockSpec(array.shape, lambda i: (0, 0))
    full = lambda shape: pl.BlockSpec(shape, lambda i: (0, 0))
    pair = pl.BlockSpec((length, 2 * HEAD_DIM), lambda i: (0, i))
    sds = jax.ShapeDtypeStruct
    return pl.pallas_call(
        functools.partial(forward_kernel, block),
        out_shape=[
            sds((length, width), bf16),
            sds((length, head_width), f32),
            sds((length, HEAD_DIM), f32),
            sds((length, HEAD_DIM), bf16),
            sds((length, head_width), bf16),
            sds((length, width), bf16),
            sds((C,) + cot.shape, bf16),
        ],
        grid=(head_width // (2 * HEAD_DIM),),
        in_specs=[
            whole(array) for array in (x, w, wo, gain, cosine, sine, pos_col, pos_row, gains)
        ]
        + [ANY],
        out_specs=[
            full((length, width)), pair, full((length, HEAD_DIM)), full((length, HEAD_DIM)), pair,
            full((length, width)), ANY,
        ],
        scratch_shapes=[
            pltpu.VMEM((length, HEAD_DIM), bf16),
            pltpu.VMEM((length, width), f32),
            DMA,
            DMA((C - 1,)),
            DMA((C - 1,)),
        ],
        name="attention_forward",
        compiler_params=params(2),
    )(x, w, wo, gain, cosine, sine, pos_col, pos_row, gains, cot)


CHUNKS = 4


def columns(width, j):
    step = width // CHUNKS
    return pl.ds(j * step, step)


def dispatch_kernel(
    packed, out_part, gslots, tokens, pack, gain, chosen, kept, select,
    buffer, gbuf, wrow, h1, xm, gates,
    RO, XM, SL, WM, WS,
    local, osend, orecv, gsend, grecv, xsend, xrecv, msend, mrecv, bsend, brecv, wsend, wrecv,
):
    S, C, F = sizes()
    s, c, f = place()
    Q = S * F
    q = s * F + f
    rows, width = tokens.shape
    z_peers = z_neighbours()
    p_at, p_peers = plane_neighbours()
    greet_all(z_peers + p_peers)
    mine = pl.ds(pl.multiple_of(q * packed, 16), packed)
    own_rows = pl.ds(pl.multiple_of(c * rows, 16), rows)
    first = []
    for k, peer in enumerate(z_peers):
        first.append(remote(out_part.at[peer[1]], RO.at[k], osend.at[k], orecv.at[k], peer))
    first.append(pltpu.make_async_copy(out_part.at[c], RO.at[C - 1], local.at[0]))
    later = []
    for k, peer in enumerate(p_peers):
        theirs = pl.ds(pl.multiple_of(p_at[k] * packed, 16), packed)
        later.append(remote(gslots.at[theirs], gbuf.at[mine], gsend.at[k], grecv.at[k], peer))
    later.append(pltpu.make_async_copy(gslots.at[mine], gbuf.at[mine], local.at[1]))
    for copy in first + later:
        copy.start()
    for copy in first:
        copy.wait()

    def head_rows(i, carry):
        part = pl.ds(i * 32, 32)
        total = tokens[part, :].astype(f32)
        for k in range(C):
            total = total + RO[k, part, :].astype(f32)
        h1[part, :] = total
        unit, _ = rms_unit(total)
        xm[part, :] = (unit * gain[...]).astype(bf16)
        return carry

    lax.fori_loop(0, rows // 32, head_rows, 0)
    XM[own_rows, :] = xm[...]
    chunks = []
    for j in range(CHUNKS):
        cols = columns(width, j)
        row = []
        for k, peer in enumerate(z_peers):
            piece = XM.at[own_rows, cols]
            row.append(remote(piece, piece, xsend.at[j, k], xrecv.at[j, k], peer))
            row[-1].start()
        chunks.append(row)
    logits = jnp.dot(xm[...], pack[...], preferred_element_type=f32)[:, : chosen.shape[1]]
    logits = jnp.where(chosen[...] > 0.0, logits, -jnp.inf)
    power = jnp.exp(logits - jnp.max(logits, axis=-1, keepdims=True))
    gates[...] = power / jnp.sum(power, axis=-1, keepdims=True)
    WM[own_rows, :] = gates[...] * kept[...]
    row = []
    for k, peer in enumerate(z_peers):
        piece = WM.at[own_rows, :]
        row.append(remote(piece, piece, msend.at[k], mrecv.at[k], peer))
        row[-1].start()
    sent = []
    for j in range(CHUNKS):
        cols = columns(width, j)
        for copy in chunks[j]:
            copy.wait_recv()

        def slots(p, carry):
            at = pl.ds(pl.multiple_of(p * packed, 16), packed)
            SL[at, cols] = jnp.dot(
                select[at, :], XM[:, cols], preferred_element_type=f32
            ).astype(bf16)
            return carry

        lax.fori_loop(0, Q, slots, 0)
        for k, peer in enumerate(p_peers):
            theirs = pl.ds(pl.multiple_of(p_at[k] * packed, 16), packed)
            sent.append(
                remote(SL.at[theirs, cols], buffer.at[mine, cols], bsend.at[j, k], brecv.at[j, k], peer)
            )
            sent[-1].start()
        sent.append(pltpu.make_async_copy(SL.at[mine, cols], buffer.at[mine, cols], local.at[2 + j]))
        sent[-1].start()
    for copy in row:
        copy.wait_recv()
    WS[...] = jnp.zeros_like(WS)

    def weights(p, carry):
        at = pl.ds(pl.multiple_of(p * packed, 16), packed)
        every = lax.dot_general(
            WM[...], select[at, :].astype(f32), (((0,), (1,)), ((), ())),
            precision=lax.Precision.HIGHEST, preferred_element_type=f32,
        )
        expert = (p // F * C + c) * F + lax.rem(p, F)
        hit = lax.broadcasted_iota(jnp.int32, every.shape, 0) == expert
        line = jnp.sum(jnp.where(hit, every, 0.0), axis=0, keepdims=True)
        WS[p, :, pl.ds(0, packed)] = jnp.broadcast_to(line, (8, packed))
        return carry

    lax.fori_loop(0, Q, weights, 0)
    for k, peer in enumerate(p_peers):
        sent.append(remote(WS.at[p_at[k]], wrow.at[q], wsend.at[k], wrecv.at[k], peer))
        sent[-1].start()
    sent.append(pltpu.make_async_copy(WS.at[q], wrow.at[q], local.at[2 + CHUNKS]))
    sent[-1].start()
    for copy in sent + later:
        copy.wait()
    for line in chunks + [row]:
        for copy in line:
            copy.wait_send()


def dispatch(packed, out_part, gslots, tokens, pack, gain, chosen, kept, select):
    S, C, F = sizes()
    Q = S * F
    rows, width = tokens.shape
    lanes = round_up(packed, 128)
    wide = chosen.shape[1]
    V = pltpu.VMEM
    sds = jax.ShapeDtypeStruct
    vm = pl.BlockSpec(memory_space=pltpu.VMEM)
    return pl.pallas_call(
        functools.partial(dispatch_kernel, packed),
        out_shape=[
            sds((Q * packed, width), bf16),
            sds((Q * packed, width), bf16),
            sds((Q, 8, lanes), f32),
            sds((rows, width), f32),
            sds((rows, width), bf16),
            sds((rows, wide), f32),
        ],
        in_specs=[ANY, ANY] + [vm] * 6,
        out_specs=[ANY, ANY, ANY, vm, vm, vm],
        scratch_shapes=[
            V((C, rows, width), bf16),
            V((C * rows, width), bf16),
            V((Q * packed, width), bf16),
            V((C * rows, wide), f32),
            V((Q, 8, lanes), f32),
            DMA((3 + CHUNKS,)),
            DMA((C - 1,)), DMA((C - 1,)),
            DMA((Q - 1,)), DMA((Q - 1,)),
            DMA((CHUNKS, C - 1)), DMA((CHUNKS, C - 1)),
            DMA((C - 1,)), DMA((C - 1,)),
            DMA((CHUNKS, Q - 1)), DMA((CHUNKS, Q - 1)),
            DMA((Q - 1,)), DMA((Q - 1,)),
        ],
        name="dispatch_rows",
        compiler_params=params(3),
    )(out_part, gslots, tokens, pack, gain, chosen, kept, select)


def return_kernel(
    packed, din, dgr, wy, select, select_t, gates, pack, h1, gain, cot,
    DA, y_part, dh1, dlog, gnorm,
    RD, YB, PART, RX, DG, DGP, RG, DL,
    local, dsend, drecv, gsend, grecv, ysend, yrecv, xsend, xrecv, msend, mrecv, asend, arecv,
):
    S, C, F = sizes()
    s, c, f = place()
    Q = S * F
    q = s * F + f
    rows, width = h1.shape
    z_peers = z_neighbours()
    p_at, p_peers = plane_neighbours()
    greet_all(z_peers + p_peers)
    mine = pl.ds(pl.multiple_of(q * packed, 16), packed)
    theirs = [pl.ds(pl.multiple_of(at * packed, 16), packed) for at in p_at]
    small = [
        remote(dgr.at[p_at[k]], DG.at[q], gsend.at[k], grecv.at[k], peer)
        for k, peer in enumerate(p_peers)
    ]
    small.append(pltpu.make_async_copy(dgr.at[q], DG.at[q], local.at[0]))
    for copy in small:
        copy.start()
    chunks = []
    for j in range(CHUNKS):
        cols = columns(width, j)
        line = [
            remote(din.at[theirs[k], cols], RD.at[mine, cols], dsend.at[j, k], drecv.at[j, k], peer)
            for k, peer in enumerate(p_peers)
        ]
        line.append(pltpu.make_async_copy(din.at[mine, cols], RD.at[mine, cols], local.at[2 + j]))
        for copy in line:
            copy.start()
        chunks.append(line)
    sums = []
    for j in range(CHUNKS):
        cols = columns(width, j)
        for copy in chunks[j]:
            copy.wait()

        def combine(i, carry):
            at = pl.ds(pl.multiple_of(i * rows, 16), rows)
            PART[at, cols] = jnp.dot(
                select_t[at, :], RD[:, cols], preferred_element_type=f32
            ).astype(bf16)
            return carry

        lax.fori_loop(0, C, combine, 0)
        for k, peer in enumerate(z_peers):
            src = PART.at[pl.ds(pl.multiple_of(peer[1] * rows, 16), rows), cols]
            sums.append(remote(src, RX.at[k, :, cols], xsend.at[j, k], xrecv.at[j, k], peer))
            sums[-1].start()
    ys = [
        remote(wy.at[theirs[k]], YB.at[mine], ysend.at[k], yrecv.at[k], peer)
        for k, peer in enumerate(p_peers)
    ]
    ys.append(pltpu.make_async_copy(wy.at[mine], YB.at[mine], local.at[1]))
    for copy in ys:
        copy.start()
    for copy in small:
        copy.wait()
    wide = gates.shape[1]
    place_of = lax.broadcasted_iota(jnp.int32, (Q, wide), 0)
    expert = (place_of // F * C + c) * F + lax.rem(place_of, F)
    spread = (lax.broadcasted_iota(jnp.int32, (Q, wide), 1) == expert).astype(f32)

    for p in range(Q):
        at = pl.ds(p * packed, packed)
        line = jnp.dot(
            DG[p, :, pl.ds(0, packed)], select[at, :].astype(f32),
            precision=lax.Precision.HIGHEST, preferred_element_type=f32,
        )
        DL[pl.ds(p, 1), :] = line[0:1, :]
    DGP[...] = lax.dot_general(
        DL[...], spread, (((0,), (0,)), ((), ())),
        precision=lax.Precision.HIGHEST, preferred_element_type=f32,
    ).reshape(DGP.shape)
    more = []
    for k, peer in enumerate(z_peers):
        more.append(remote(DGP.at[peer[1]], RG.at[k], msend.at[k], mrecv.at[k], peer))
        more[-1].start()
    for copy in more:
        copy.wait()
    total = DGP[c]
    for k in range(C - 1):
        total = total + RG[k]
    dlogits = gates[...] * (total - jnp.sum(gates[...] * total, axis=-1, keepdims=True))
    dlog[...] = dlogits.astype(bf16)
    gnorm[...] = jnp.zeros_like(gnorm)
    for copy in sums:
        copy.wait()

    def head_rows(i, carry):
        part = pl.ds(i * 32, 32)
        mine_part = pl.ds(pl.multiple_of(c * rows + i * 32, 16), 32)
        dxm = PART[mine_part, :].astype(f32)
        for k in range(C - 1):
            dxm = dxm + RX[k, part, :].astype(f32)
        dxm = dxm + lax.dot_general(
            dlog[part, :], pack[:, pl.ds(0, wide)], (((1,), (1,)), ((), ())), preferred_element_type=f32
        )
        unit, factor = rms_unit(h1[part, :])
        gnorm[...] += jnp.sum(dxm * unit, axis=0, keepdims=True)
        grad = cot[part, :].astype(f32) + norm_backward(dxm, unit, factor, gain[...])
        dh1[part, :] = grad
        RX[0, part, :] = grad.astype(bf16)
        return carry

    lax.fori_loop(0, rows // 32, head_rows, 0)
    last = []
    for k, peer in enumerate(z_peers):
        last.append(remote(RX.at[0], DA.at[c], asend.at[k], arecv.at[k], peer))
    last.append(pltpu.make_async_copy(RX.at[0], DA.at[c], local.at[2 + CHUNKS]))
    for copy in last:
        copy.start()
    for copy in ys:
        copy.wait()

    def combine_y(i, carry):
        at = pl.ds(pl.multiple_of(i * 32, 32), 32)
        y_part[at, :] = jnp.dot(
            select_t[at, :], YB[...], preferred_element_type=f32
        ).astype(bf16)
        return carry

    lax.fori_loop(0, C * rows // 32, combine_y, 0)
    for copy in last:
        copy.wait()


def give_back(packed, din, dgr, wy, select, select_t, gates, pack, h1, gain, cot):
    S, C, F = sizes()
    Q = S * F
    rows, width = h1.shape
    wide = gates.shape[1]
    V = pltpu.VMEM
    sds = jax.ShapeDtypeStruct
    vm = pl.BlockSpec(memory_space=pltpu.VMEM)
    return pl.pallas_call(
        functools.partial(return_kernel, packed),
        out_shape=[
            sds((C, rows, width), bf16),
            sds((C * rows, width), bf16),
            sds((rows, width), f32),
            sds((rows, wide), bf16),
            sds((1, width), f32),
        ],
        in_specs=[ANY] * 3 + [vm] * 7,
        out_specs=[ANY] + [vm] * 4,
        scratch_shapes=[
            V((Q * packed, width), bf16),
            V((Q * packed, width), bf16),
            V((C * rows, width), bf16),
            V((C - 1, rows, width), bf16),
            V(dgr.shape, f32),
            V((C, rows, wide), f32),
            V((C - 1, rows, wide), f32),
            V((Q, C * rows), f32),
            DMA((3 + CHUNKS,)),
            DMA((CHUNKS, Q - 1)), DMA((CHUNKS, Q - 1)),
            DMA((Q - 1,)), DMA((Q - 1,)),
            DMA((Q - 1,)), DMA((Q - 1,)),
            DMA((CHUNKS, C - 1)), DMA((CHUNKS, C - 1)),
            DMA((C - 1,)), DMA((C - 1,)),
            DMA((C - 1,)), DMA((C - 1,)),
        ],
        name="return_grads",
        compiler_params=params(5),
    )(din, dgr, wy, select, select_t, gates, pack, h1, gain, cot)


def attend_back_kernel(
    heads, block, q, dmixed, k, v, cosine, sine, pos_col, pos_row, gains, out, head_grad, kr, dkr, dv
):
    head, part = pl.program_id(0), pl.program_id(1)
    rows = pl.ds(part * block, block)

    @pl.when(jnp.logical_and(head == 0, part == 0))
    def _():
        unit, _ = rms_unit(k[...])
        kr[...] = half_turn(unit * gains[1:2, :], cosine[...], sine[...]).astype(bf16)
        dkr[...] = jnp.zeros_like(dkr)
        dv[...] = jnp.zeros_like(dv)
        head_grad[...] = jnp.zeros_like(head_grad)

    @pl.when(head < heads)
    def _():
        unit, factor = rms_unit(q[...])
        cos, sin = cosine[rows, :], sine[rows, :]
        qr = half_turn(unit * gains[0:1, :], cos, sin).astype(bf16)
        keys = kr[...]
        probs = score_block(qr, keys, pos_col[rows, :], pos_row[...])
        dm = dmixed[...]
        dprobs = lax.dot_general(dm, v[...], (((1,), (1,)), ((), ())), preferred_element_type=f32)
        delta = jnp.sum(probs * dprobs, axis=-1, keepdims=True)
        dscores = (probs * (dprobs - delta)).astype(bf16)
        dqr = jnp.dot(dscores, keys, preferred_element_type=f32) * (HEAD_DIM**-0.5)
        rows_in = (((0,), (0,)), ((), ()))
        dkr[...] += lax.dot_general(dscores, qr, rows_in, preferred_element_type=f32) * (HEAD_DIM**-0.5)
        dv[...] += lax.dot_general(probs.astype(bf16), dm, rows_in, preferred_element_type=f32)
        dqs = half_turn(dqr, cos, -sin)
        head_grad[0:1, :] += jnp.sum(dqs * unit, axis=0, keepdims=True)
        out[...] = norm_backward(dqs, unit, factor, gains[0:1, :]).astype(bf16)

    @pl.when(head == heads)
    def _():
        unit, factor = rms_unit(k[rows, :])
        dks = half_turn(dkr[rows, :], cosine[rows, :], -sine[rows, :])
        head_grad[1:2, :] += jnp.sum(dks * unit, axis=0, keepdims=True)
        out[...] = norm_backward(dks, unit, factor, gains[1:2, :]).astype(bf16)

    @pl.when(head == heads + 1)
    def _():
        out[...] = dv[rows, :].astype(bf16)


def attend_back(q, dmixed, k, v, cosine, sine, pos_col, pos_row, gains):
    length, width = q.shape
    heads = width // HEAD_DIM
    block = min(length, 512)
    whole = lambda array: pl.BlockSpec(array.shape, lambda h, i: (0, 0))
    per_head = pl.BlockSpec((block, HEAD_DIM), lambda h, i: (i, jnp.minimum(h, heads - 1)))
    return pl.pallas_call(
        functools.partial(attend_back_kernel, heads, block),
        out_shape=[
            jax.ShapeDtypeStruct((length, width + 2 * HEAD_DIM), bf16),
            jax.ShapeDtypeStruct((8, HEAD_DIM), f32),
        ],
        grid=(heads + 2, length // block),
        in_specs=[per_head, per_head]
        + [whole(array) for array in (k, v, cosine, sine, pos_col, pos_row, gains)],
        out_specs=[
            pl.BlockSpec((block, HEAD_DIM), lambda h, i: (i, h)),
            pl.BlockSpec((8, HEAD_DIM), lambda h, i: (0, 0)),
        ],
        scratch_shapes=[
            pltpu.VMEM((length, HEAD_DIM), bf16),
            pltpu.VMEM((length, HEAD_DIM), f32),
            pltpu.VMEM((length, HEAD_DIM), f32),
        ],
        name="attention_backward",
        compiler_params=pltpu.CompilerParams(vmem_limit_bytes=VMEM_LIMIT),
    )(q, dmixed, k, v, cosine, sine, pos_col, pos_row, gains)


def dot(left, right):
    return jnp.dot(left, right, preferred_element_type=f32)


def contract_rows(left, right):
    return lax.dot_general(left, right, (((0,), (0,)), ((), ())), preferred_element_type=f32)


def times_transpose(left, right):
    return lax.dot_general(left, right, (((1,), (1,)), ((), ())), preferred_element_type=f32)


def on_device(
    tokens,
    stretch_order,
    expert_ids,
    slot_index,
    norm_attn,
    head_gains,
    w_query,
    w_key,
    w_value,
    w_out,
    norm_moe,
    w_router,
    w_gate,
    w_up,
    w_down,
    cotangent,
):
    S, C, F = sizes()
    Q = S * F
    seq_at, ctx_at, fsdp_at = place()
    rows, width = tokens.shape[1:]
    length = C * rows
    experts = w_router.shape[1]
    capacity = rows * TOP // (Q * C) + 1
    packed = round_up(C * capacity, 16)
    lanes = round_up(packed, 128)
    head_width = w_query.shape[1] // C
    shard = w_router.shape[0]
    stretch_rows = rows // 2
    route_ids, slot_ids = expert_ids[0], slot_index[0]
    picker = route_ids[:, :, None] == jnp.arange(experts, dtype=jnp.int32)
    kept = slot_ids < capacity
    wide = round_up(experts, 128)
    side = ((0, 0), (0, wide - experts))
    slot_map = jnp.max(
        jnp.where(picker & kept[:, :, None], slot_ids[:, :, None], -1), axis=1
    ).astype(f32)
    chosen = jnp.pad(jnp.any(picker, axis=1).astype(f32), side)
    slot_map = jnp.pad(slot_map, side, constant_values=-1.0)
    kept_map = (slot_map >= 0.0).astype(f32)
    pack_width = round_up(experts + 2, 128)
    pack = jnp.concatenate(
        [
            w_router,
            norm_attn[:, None],
            norm_moe[:, None],
            jnp.zeros((shard, pack_width - experts - 2), bf16),
        ],
        axis=1,
    )
    X, W, WO, PK, SM = gather_all(tokens[0], w_query, w_key, w_value, w_out, pack, slot_map)
    W = W.reshape(width, head_width + 2 * HEAD_DIM)
    WO = WO.reshape(head_width, width)
    PK = PK.reshape(width, pack_width)
    gain_attn = PK[:, experts].astype(f32)[None]
    gain_moe = PK[:, experts + 1].astype(f32)[None]
    gains = head_gains.astype(f32)
    positions = (
        stretch_order[:, None] * stretch_rows + jnp.arange(stretch_rows, dtype=jnp.int32)[None, :]
    ).reshape(-1)
    frequency = jnp.power(rope_base, -jnp.arange(HEAD_DIM // 2, dtype=f32) * 2.0 / HEAD_DIM)
    angles = positions.astype(f32)[:, None] * frequency[None, :]
    cosine, sine = jnp.cos(angles), jnp.sin(angles)
    cosine = jnp.concatenate([cosine, cosine], axis=1)
    sine = jnp.concatenate([-sine, sine], axis=1)
    pos_col, pos_row = positions[:, None], positions[None, :]
    out_part, q, k, v, mixed, xn, G = forward(
        X.reshape(length, width), W, WO, gain_attn, cosine, sine, pos_col, pos_row, gains, cotangent[0]
    )
    slot_plane = lax.dynamic_index_in_dim(
        SM[:, :, :experts].reshape(length, S, C, F), ctx_at, axis=2, keepdims=False
    ).reshape(length, Q)
    source = jnp.repeat(jnp.arange(C, dtype=jnp.int32), rows)[:, None]
    slot_plane = slot_plane.astype(jnp.int32)
    target = jnp.where(slot_plane >= 0, slot_plane + source * capacity, -1).T
    slots = jnp.arange(packed, dtype=jnp.int32)
    select = (target[:, None, :] == slots[None, :, None]).astype(bf16).reshape(Q * packed, length)
    select_t = (
        (target.T[:, :, None] == slots[None, None, :]).astype(bf16).reshape(length, Q * packed)
    )
    gslots = dot(select, G.reshape(length, width)).astype(bf16)
    buffer, slot_grad, slot_weight, h1, xm, gates = dispatch(
        packed, out_part.reshape(C, rows, width), gslots, tokens[0], PK, gain_moe, chosen, kept_map, select
    )
    slot_weight = slot_weight[:, 0, :packed].reshape(Q * packed, 1)
    slot_grad = slot_grad.astype(f32)
    gate_pre = dot(buffer, w_gate[0])
    up_pre = dot(buffer, w_up[0])
    sigmoid_gp = jax.nn.sigmoid(gate_pre)
    silu_gp = gate_pre * sigmoid_gp
    hidden = (silu_gp * up_pre).astype(bf16)
    y = dot(hidden, w_down[0])
    weighted_y = (slot_weight * y).astype(bf16)
    slot_dgate = jnp.sum(slot_grad * y, axis=-1).reshape(Q, packed)
    dy = (slot_weight * slot_grad).astype(bf16)
    dhid = times_transpose(dy, w_down[0])
    dgp = (dhid * up_pre * sigmoid_gp * (1.0 + gate_pre * (1.0 - sigmoid_gp))).astype(bf16)
    dup = (dhid * silu_gp).astype(bf16)
    din = (times_transpose(dgp, w_gate[0]) + times_transpose(dup, w_up[0])).astype(bf16)
    slot_dgate = jnp.broadcast_to(
        jnp.pad(slot_dgate, ((0, 0), (0, lanes - packed)))[:, None, :], (Q, 8, lanes)
    )
    grad_wgate = contract_rows(buffer, dgp)
    grad_wup = contract_rows(buffer, dup)
    grad_wdown = contract_rows(hidden, dy)
    DA, y_part, dh1, dlogits, grad_norm_moe = give_back(
        packed, din, slot_dgate, weighted_y, select, select_t, gates, PK, h1, gain_moe, cotangent[0]
    )
    grad_router = contract_rows(xm, dlogits[:, :experts])
    DA = DA.reshape(length, width)
    dmixed = times_transpose(DA, WO).astype(bf16)
    grad_out_part = contract_rows(mixed, DA).astype(bf16)
    dqkv, head_grad = attend_back(q, dmixed, k, v, cosine, sine, pos_col, pos_row, gains)
    grad_qkv_part = contract_rows(xn, dqkv).astype(bf16)
    dxn_part = times_transpose(dqkv, W)
    normed_one, _ = rms_unit(X.reshape(length, width).astype(f32))
    grad_norm_attn = jnp.sum(dxn_part * normed_one, axis=0)
    small = jnp.concatenate(
        [
            grad_router,
            grad_norm_attn[:, None],
            grad_norm_moe.T,
            jnp.zeros((width, pack_width - experts - 2), f32),
        ],
        axis=1,
    )
    q_sums, o_sum, small_sums, head_sums, dxn_parts, y_parts = reduce_grads(
        grad_qkv_part.reshape(S, C, F, shard, head_width + 2 * HEAD_DIM),
        grad_out_part.reshape(S, F, head_width // Q, width),
        small.reshape(S, C, F, shard, pack_width),
        head_grad,
        dxn_part.astype(bf16).reshape(C, rows, width),
        y_part.reshape(C, rows, width),
    )
    layer_out = (h1 + jnp.sum(y_parts.astype(f32), axis=0)).astype(bf16)
    inputs = tokens[0].astype(f32)
    unit, factor = rms_unit(inputs)
    dxn = jnp.sum(dxn_parts.astype(f32), axis=0)
    grad_tokens = (dh1 + norm_backward(dxn, unit, factor, gain_attn)).astype(bf16)
    q_sums = q_sums.astype(f32)
    grad_query = q_sums[:, :, :head_width].transpose(1, 0, 2).reshape(shard, C * head_width)

    def key_columns(block):
        pieces = block.reshape(KEY_VALUE_HEADS, C // KEY_VALUE_HEADS, shard, HEAD_DIM).sum(axis=1)
        return pieces.transpose(1, 0, 2).reshape(shard, KEY_VALUE_HEADS * HEAD_DIM)

    grad_key = key_columns(q_sums[:, :, head_width : head_width + HEAD_DIM])
    grad_value = key_columns(q_sums[:, :, head_width + HEAD_DIM :])
    small_sum = jnp.sum(small_sums, axis=0)
    return (
        layer_out[None],
        grad_tokens[None],
        small_sum[:, experts],
        jnp.sum(head_sums, axis=0)[:2],
        grad_query,
        grad_key,
        grad_value,
        o_sum.astype(f32),
        small_sum[:, experts + 1],
        small_sum[:, :experts],
        grad_wgate[None],
        grad_wup[None],
        grad_wdown[None],
    )


def solution(mesh):
    rows = P(("seq", "fsdp"), "ctx", None)
    vector = P(AXES)
    matrix = P(AXES, None)
    cube = P(AXES, None, None)
    return jax.shard_map(
        on_device,
        mesh=mesh,
        in_specs=(
            rows, P(), rows, rows, vector, P(), matrix, matrix, matrix, matrix,
            vector, matrix, cube, cube, cube, rows,
        ),
        out_specs=(
            rows, rows, vector, P(), matrix, matrix, matrix, matrix, vector, matrix,
            cube, cube, cube,
        ),
        check_vma=False,
    )
```

```python
import functools

import jax
import jax.numpy as jnp
from jax import lax
from jax.experimental import pallas as pl
from jax.experimental.pallas import tpu as pltpu
from jax.sharding import PartitionSpec as P

QUERY_HEADS = 32
KEY_VALUE_HEADS = 4
HEAD_DIM = 128
TOP = 8
AXES = ("seq", "ctx", "fsdp")
MESH = pl.DeviceIdType.MESH
epsilon = 1e-06
rope_base = 1000000.0
VMEM_LIMIT = 56 * 2**20
f32 = jnp.float32
bf16 = jnp.bfloat16


def round_up(value, step):
    return (value + step - 1) // step * step


def place():
    return tuple(lax.axis_index(name) for name in AXES)


def sizes():
    return tuple(lax.axis_size(name) for name in AXES)


def signal(device):
    pl.semaphore_signal(
        pltpu.get_barrier_semaphore(), inc=1, device_id=device, device_id_type=MESH
    )


def remote(src, dst, send, recv, device):
    return pltpu.make_async_remote_copy(
        src_ref=src,
        dst_ref=dst,
        send_sem=send,
        recv_sem=recv,
        device_id=device,
        device_id_type=MESH,
    )


def params(cid, limit=VMEM_LIMIT):
    return pltpu.CompilerParams(
        collective_id=cid, has_side_effects=True, vmem_limit_bytes=limit
    )


ANY = pl.BlockSpec(memory_space=pl.ANY)
DMA = pltpu.SemaphoreType.DMA


def rms_unit(rows):
    factor = lax.rsqrt(jnp.mean(rows * rows, axis=-1, keepdims=True) + epsilon)
    return rows * factor, factor


def norm_backward(grad_scaled, normed, factor, gain):
    grad_normed = grad_scaled * gain
    inner = jnp.mean(grad_normed * normed, axis=-1, keepdims=True)
    return factor * (grad_normed - normed * inner)


def half_turn(rows, cosine, sine):
    return rows * cosine + pltpu.roll(rows, HEAD_DIM // 2, 1) * sine


def score_block(qr, kr, pos_col, pos_row):
    scores = lax.dot_general(
        qr, kr, (((1,), (1,)), ((), ())), preferred_element_type=f32
    ) * (HEAD_DIM**-0.5)
    scores = jnp.where(pos_col >= pos_row, scores, -jnp.inf)
    peak = jnp.max(scores, axis=-1, keepdims=True)
    weight = jnp.exp(scores - peak)
    return weight * (1.0 / jnp.sum(weight, axis=-1, keepdims=True))


def z_neighbours():
    _, C, _ = sizes()
    s, c, f = place()
    return [(s, lax.rem(c + k, C), f) for k in range(1, C)]


def plane_neighbours():
    S, _, F = sizes()
    s, c, f = place()
    Q = S * F
    at = [lax.rem(s * F + f + k, Q) for k in range(1, Q)]
    return at, [(q // F, c, lax.rem(q, F)) for q in at]


def greet_all(peers):
    for peer in peers:
        signal(peer)
    pl.semaphore_wait(pltpu.get_barrier_semaphore(), len(peers))


class Line:
    def __init__(self, own, block, rsend, rrecv, lsend, lrecv):
        s, self.c, f = place()
        self.C = lax.axis_size("ctx")
        self.own, self.block = own, block
        self.sems = (rsend, rrecv, lsend, lrecv)
        self.right = (s, lax.rem(self.c + 1, self.C), f)
        self.left = (s, lax.rem(self.c + self.C - 1, self.C), f)

    def copy(self, rightward, h):
        origin = self.c - h if rightward else self.c + h
        src = self.own if h == 0 else self.block(origin)
        send, recv = self.sems[:2] if rightward else self.sems[2:]
        return remote(
            src, self.block(origin), send.at[h], recv.at[h], self.right if rightward else self.left
        )

    def sends(self, rightward, h):
        if rightward:
            return jnp.logical_and(self.c >= h, self.c < self.C - 1)
        return jnp.logical_and(self.c + h < self.C, self.c > 0)

    def start(self):
        for way in (True, False):
            pl.when(self.sends(way, 0))(self.copy(way, 0).start)

    def hop(self, h):
        for way in (True, False):
            origin = self.c - h if way else self.c + h
            there = origin >= 0 if way else origin < self.C
            landed = remote(
                self.block(origin), self.block(origin),
                self.sems[0 if way else 2].at[h - 1], self.sems[1 if way else 3].at[h - 1],
                self.left if way else self.right,
            )
            pl.when(there)(landed.wait_recv)
            if h < self.C - 1:
                pl.when(self.sends(way, h))(self.copy(way, h).start)

    def finish(self):
        for way in (True, False):
            for h in range(self.C - 1):
                pl.when(self.sends(way, h))(self.copy(way, h).wait_send)


def line_sems(C):
    return [DMA((C - 1,)) for _ in range(4)]


def front_kernel(
    block, capacity, packed, experts,
    order, ids, slot_ids, tokens, wq, wk, wv, wo, pack, cot, gains, frequency,
    X_out, W_out, WO_out, PK, SM, G, out, q, k_out, v, mixed, xnt, row_gains,
    cosine, sine, pos_col, pos_row, select, select_t, chosen, kept,
    X, W, WO, xn, kr,
    local, save, zsend, zrecv, fsend, frecv, csend, crecv, wsend, wrecv,
    xrs, xrr, xls, xlr, grs, grr, gls, glr,
):
    S, C, F = sizes()
    s, c, f = place()
    Q = S * F
    rows, width = tokens.shape
    length = C * rows
    head_width = wq.shape[1] // C
    shard = wq.shape[0]
    wide = chosen.shape[1]
    z_peers = z_neighbours()
    f_peers = [(s, c, lax.rem(f + k, F)) for k in range(1, F)]
    sibling = (1 - s, c, f)
    pair = s * C + c
    out_dst = (lax.rem(pair, S), pair // S, f)
    pair_in = c * S + s
    out_src = (pair_in // C, lax.rem(pair_in, C), f)
    stays = jnp.logical_and(out_dst[0] == s, out_dst[1] == c)
    moves = jnp.logical_not(stays)
    greet = (
        jnp.where(stays, 1 - s, out_src[0]),
        jnp.where(stays, C - 1 - c, out_src[1]),
        f,
    )
    lane = lax.broadcasted_iota(jnp.int32, (rows, wide), 1)
    hits = jnp.zeros((rows, wide), f32)
    slot_map = jnp.full((rows, wide), -1, jnp.int32)
    for j in range(TOP):
        here = lane == ids[:, j : j + 1]
        slot = jnp.broadcast_to(slot_ids[:, j : j + 1], (rows, wide))
        hits = jnp.where(here, 1.0, hits)
        slot_map = jnp.where(jnp.logical_and(here, slot < capacity), slot, slot_map)
    chosen[...] = hits
    kept[...] = (slot_map >= 0).astype(f32)
    SM[c] = slot_map.astype(f32)
    greet_all(z_peers + f_peers + [sibling, greet])

    def pieces(target):
        kv = (target * KEY_VALUE_HEADS) // C
        q_cols = pl.ds(pl.multiple_of(target * head_width, 128), head_width)
        kv_cols = pl.ds(pl.multiple_of(kv * HEAD_DIM, 128), HEAD_DIM)
        mine = W.at[s, c, f]
        return [
            (wq.at[:, q_cols], mine.at[:, pl.ds(0, head_width)]),
            (wk.at[:, kv_cols], mine.at[:, pl.ds(head_width, HEAD_DIM)]),
            (wv.at[:, kv_cols], mine.at[:, pl.ds(head_width + HEAD_DIM, HEAD_DIM)]),
            (pack, PK.at[s, c, f]),
        ]

    def token_rows(at):
        return X.at[pl.ds(pl.multiple_of(at * rows, 16), rows)]

    own = [
        pltpu.make_async_copy(src, dst, local.at[i])
        for i, (src, dst) in enumerate(pieces(c) + [(tokens, token_rows(c)), (cot, G.at[c])])
    ]
    z_copies = [
        remote(src, dst, zsend.at[i, k], zrecv.at[i, k], peer)
        for k, peer in enumerate(z_peers)
        for i, (src, dst) in enumerate(pieces(peer[1]))
    ]
    slot_copies = [
        remote(SM.at[c], SM.at[c], zsend.at[4, k], zrecv.at[4, k], peer)
        for k, peer in enumerate(z_peers)
    ]
    x_line = Line(tokens, token_rows, xrs, xrr, xls, xlr)
    g_line = Line(cot, lambda at: G.at[at], grs, grr, gls, glr)
    out_copy = remote(wo, WO.at[out_dst[0], f], wsend.at[0], wrecv.at[0], out_dst)
    out_stay = pltpu.make_async_copy(wo, WO.at[s, f], wsend.at[1])
    for copy in own + z_copies + slot_copies:
        copy.start()
    x_line.start()
    pl.when(moves)(out_copy.start)
    pl.when(stays)(out_stay.start)

    where = lax.broadcasted_iota(jnp.int32, (1, length), 1)
    where_col = lax.broadcasted_iota(jnp.int32, (length, 1), 0)
    stretch_rows = rows // 2

    def position(at):
        total = jnp.zeros_like(at)
        for j in range(2 * C):
            base = order[j] * stretch_rows - j * stretch_rows
            total = jnp.where(at // stretch_rows == j, at + base, total)
        return total

    pos_row[...] = position(where)
    pos_col[...] = position(where_col)
    angles = pos_col[...].astype(f32) * frequency[...]
    cosine[...] = jnp.cos(angles)
    turned = jnp.sin(angles)
    sine[...] = jnp.where(
        lax.broadcasted_iota(jnp.int32, turned.shape, 1) < HEAD_DIM // 2, -turned, turned
    )

    for copy in own[:5] + z_copies:
        copy.wait()

    def weight_block(index, at):
        return (W.at[s, :, at], PK.at[s, :, at], WO.at[s, at])[index]

    f_copies = [
        [
            remote(weight_block(i, f), weight_block(i, f), fsend.at[i, k], frecv.at[i, k], peer)
            for k, peer in enumerate(f_peers)
        ]
        for i in range(3)
    ]

    def to_sibling(i, k):
        at = lax.rem(f + F - k, F)
        return remote(weight_block(i, at), weight_block(i, at), csend.at[i, k], crecv.at[i, k], sibling)

    c_copies = [[to_sibling(i, k) for k in range(F)] for i in range(3)]
    for i in range(2):
        for copy in f_copies[i] + c_copies[i][:1]:
            copy.start()
    x_line.hop(1)
    pl.when(moves)(out_copy.wait)
    pl.when(stays)(out_stay.wait)
    for copy in f_copies[2] + c_copies[2][:1]:
        copy.start()
    for h in range(2, C - 1):
        x_line.hop(h)
    g_line.start()
    for k in range(F - 1):
        for i in range(2):
            f_copies[i][k].wait_recv()
            c_copies[i][k + 1].start()
    for copy in slot_copies:
        copy.wait()
    at = lax.broadcasted_iota(jnp.int32, (wide, Q * packed), 1) // packed
    expert = (at // F * C + c) * F + lax.rem(at, F)
    spread = (lax.broadcasted_iota(jnp.int32, (wide, Q * packed), 0) == expert).astype(bf16)
    slot_rows = SM[...].reshape(length, wide).astype(bf16)
    by_token = jnp.dot(slot_rows, spread, preferred_element_type=f32)
    base = (lax.broadcasted_iota(jnp.int32, by_token.shape, 0) // rows * capacity).astype(f32)
    number = lax.rem(lax.broadcasted_iota(jnp.int32, by_token.shape, 1), packed).astype(f32)
    select_t[...] = jnp.where(
        jnp.logical_and(by_token >= 0.0, by_token + base == number), 1.0, 0.0
    ).astype(bf16)
    at = lax.broadcasted_iota(jnp.int32, (Q, wide), 0)
    expert = (at // F * C + c) * F + lax.rem(at, F)
    spread = (lax.broadcasted_iota(jnp.int32, (Q, wide), 1) == expert).astype(bf16)
    by_slot = lax.dot_general(
        spread, slot_rows, (((1,), (1,)), ((), ())), preferred_element_type=f32
    )
    base = (where // rows * capacity).astype(f32)
    by_slot = jnp.where(by_slot >= 0.0, by_slot + base, -1.0)
    number = lax.broadcasted_iota(jnp.int32, (packed, length), 0).astype(f32)
    for p in range(Q):
        select[p * packed : (p + 1) * packed, :] = jnp.where(
            number == by_slot[p : p + 1, :], 1.0, 0.0
        ).astype(bf16)

    x_line.hop(C - 1)
    for i in range(2):
        for copy in c_copies[i]:
            copy.wait()
    saves = [
        pltpu.make_async_copy(X, X_out, save.at[0]),
        pltpu.make_async_copy(W, W_out, save.at[1]),
        pltpu.make_async_copy(WO, WO_out, save.at[2]),
    ]
    saves[0].start()
    saves[1].start()
    across = lax.broadcasted_iota(jnp.int32, (HEAD_DIM, HEAD_DIM), 0)
    diagonal = across == lax.broadcasted_iota(jnp.int32, (HEAD_DIM, HEAD_DIM), 1)
    flat = PK[...].reshape(width, PK.shape[-1]).astype(f32)
    for j in range(width // HEAD_DIM):
        part = slice(j * HEAD_DIM, (j + 1) * HEAD_DIM)
        for i in range(2):
            line = flat[part, experts + i : experts + i + 1]
            row_gains[i : i + 1, part] = jnp.sum(jnp.where(diagonal, line, 0.0), axis=0, keepdims=True)

    def norm_rows(i, carry):
        part = pl.ds(i * 64, 64)
        unit, _ = rms_unit(X[part, :].astype(f32))
        xn[part, :] = (unit * row_gains[0:1, :]).astype(bf16)
        return carry

    lax.fori_loop(0, length // 64, norm_rows, 0)

    def weights(cols):
        return W[:, :, :, :, cols].reshape(width, 2 * HEAD_DIM)

    kv = jnp.dot(xn[...], weights(pl.ds(head_width, 2 * HEAD_DIM)), preferred_element_type=f32)
    k_out[...] = kv[:, :HEAD_DIM]
    v[...] = kv[:, HEAD_DIM:].astype(bf16)
    unit, _ = rms_unit(k_out[...])
    kr[...] = half_turn(unit * gains[1:2, :], cosine[...], sine[...]).astype(bf16)

    def head_pair(i, carry):
        cols = pl.ds(pl.multiple_of(i * 2 * HEAD_DIM, 2 * HEAD_DIM), 2 * HEAD_DIM)
        both = jnp.dot(xn[...], weights(cols), preferred_element_type=f32)
        q[:, cols] = both
        for half in range(2):
            lanes = pl.ds(pl.multiple_of((2 * i + half) * HEAD_DIM, HEAD_DIM), HEAD_DIM)
            for part in range(length // block):
                at = slice(part * block, (part + 1) * block)
                unit, _ = rms_unit(both[at, half * HEAD_DIM : (half + 1) * HEAD_DIM])
                qr = half_turn(unit * gains[0:1, :], cosine[at, :], sine[at, :]).astype(bf16)
                probs = score_block(qr, kr[...], pos_col[at, :], pos_row[...])
                mixed[at, lanes] = jnp.dot(
                    probs.astype(bf16), v[...], preferred_element_type=f32
                ).astype(bf16)
        return carry

    pairs = head_width // (2 * HEAD_DIM)
    half_way = pairs // 2
    g_line.hop(1)
    lax.fori_loop(0, half_way, head_pair, 0)
    for k in range(F - 1):
        f_copies[2][k].wait_recv()
        c_copies[2][k + 1].start()
    for h in range(2, C - 1):
        g_line.hop(h)
    lax.fori_loop(half_way, pairs, head_pair, 0)
    for copy in c_copies[2]:
        copy.wait()
    saves[2].start()

    def project(j, carry):
        cols = pl.ds(pl.multiple_of(j * 256, 256), 256)
        out[:, cols] = jnp.dot(
            mixed[...], WO[:, :, :, cols].reshape(head_width, 256), preferred_element_type=f32
        ).astype(bf16)
        return carry

    lax.fori_loop(0, width // 256, project, 0)

    def turn(j, carry):
        cols = pl.ds(pl.multiple_of(j * 256, 256), 256)
        xnt[cols, :] = xn[:, cols].T
        return carry

    lax.fori_loop(0, width // 256, turn, 0)
    g_line.hop(C - 1)
    x_line.finish()
    g_line.finish()
    for line in f_copies:
        for copy in line:
            copy.wait_send()
    for copy in saves + own[5:]:
        copy.wait()


def front(capacity, packed, experts, order, ids, slot_ids, tokens, wq, wk, wv, wo, pack, cot, gains):
    S, C, F = sizes()
    Q = S * F
    rows, width = tokens.shape
    length = C * rows
    shard = wq.shape[0]
    head_width = wq.shape[1] // C
    wide = round_up(experts, 128)
    frequency = jnp.power(rope_base, -jnp.arange(HEAD_DIM // 2, dtype=f32) * 2.0 / HEAD_DIM)
    frequency = jnp.concatenate([frequency, frequency])[None]
    block = min(length, 512)
    sds = jax.ShapeDtypeStruct
    V = pltpu.VMEM
    vm = pl.BlockSpec(memory_space=pltpu.VMEM)
    w_shape = (S, C, F, shard, head_width + 2 * HEAD_DIM)
    wo_shape = (S, F) + wo.shape
    pack_shape = (S, C, F) + pack.shape
    return pl.pallas_call(
        functools.partial(front_kernel, block, capacity, packed, experts),
        out_shape=[
            sds((length, width), bf16),
            sds(w_shape, bf16),
            sds(wo_shape, bf16),
            sds(pack_shape, bf16),
            sds((C, rows, wide), f32),
            sds((C, rows, width), bf16),
            sds((length, width), bf16),
            sds((length, head_width), f32),
            sds((length, HEAD_DIM), f32),
            sds((length, HEAD_DIM), bf16),
            sds((length, head_width), bf16),
            sds((width, length), bf16),
            sds((2, width), f32),
            sds((length, HEAD_DIM), f32),
            sds((length, HEAD_DIM), f32),
            sds((length, 1), jnp.int32),
            sds((1, length), jnp.int32),
            sds((Q * packed, length), bf16),
            sds((length, Q * packed), bf16),
            sds((rows, wide), f32),
            sds((rows, wide), f32),
        ],
        in_specs=[pl.BlockSpec(memory_space=pltpu.SMEM), vm, vm] + [ANY] * 7 + [vm, vm],
        out_specs=[ANY, ANY, ANY, vm, vm, ANY] + [vm] * 15,
        scratch_shapes=[
            V((length, width), bf16),
            V(w_shape, bf16),
            V(wo_shape, bf16),
            V((length, width), bf16),
            V((length, HEAD_DIM), bf16),
            DMA((6,)), DMA((3,)),
            DMA((5, C - 1)), DMA((5, C - 1)),
            DMA((3, F - 1)), DMA((3, F - 1)),
            DMA((3, F)), DMA((3, F)),
            DMA((2,)), DMA((1,)),
        ]
        + line_sems(C)
        + line_sems(C),
        name="gather_and_attend",
        compiler_params=params(1, 60 * 2**20),
    )(order, ids, slot_ids, tokens, wq, wk, wv, wo, pack, cot, gains, frequency)


CHUNKS = 4


def columns(width, j):
    step = width // CHUNKS
    return pl.ds(j * step, step)


def dispatch_kernel(
    packed, out_part, G_in, tokens, pack, gain, chosen, kept, select,
    buffer, gbuf, wrow, h1, xm, gates,
    RO, XM, SL, WM, WS, G, SG,
    local, osend, orecv, gsend, grecv, xsend, xrecv, msend, mrecv, bsend, brecv, wsend, wrecv,
):
    S, C, F = sizes()
    s, c, f = place()
    Q = S * F
    q = s * F + f
    rows, width = tokens.shape
    z_peers = z_neighbours()
    p_at, p_peers = plane_neighbours()
    greet_all(z_peers + p_peers)
    mine = pl.ds(pl.multiple_of(q * packed, 16), packed)
    own_rows = pl.ds(pl.multiple_of(c * rows, 16), rows)
    first = []
    for k, peer in enumerate(z_peers):
        first.append(remote(out_part.at[peer[1]], RO.at[k], osend.at[k], orecv.at[k], peer))
    first.append(pltpu.make_async_copy(out_part.at[c], RO.at[C - 1], local.at[0]))
    load = pltpu.make_async_copy(G_in, G, local.at[1])
    for copy in first + [load]:
        copy.start()
    load.wait()

    def grad_slots(p):
        at = pl.ds(pl.multiple_of(p * packed, 16), packed)

        def body(j, carry):
            cols = pl.ds(pl.multiple_of(j * 512, 512), 512)
            SG[at, cols] = jnp.dot(select[at, :], G[:, cols], preferred_element_type=f32).astype(bf16)
            return carry

        lax.fori_loop(0, width // 512, body, 0)

    later = []
    for k, peer in enumerate(p_peers):
        theirs = pl.ds(pl.multiple_of(p_at[k] * packed, 16), packed)
        later.append(remote(SG.at[theirs], gbuf.at[mine], gsend.at[k], grecv.at[k], peer))
        grad_slots(p_at[k])
        later[-1].start()
    grad_slots(q)
    later.append(pltpu.make_async_copy(SG.at[mine], gbuf.at[mine], local.at[3 + CHUNKS]))
    later[-1].start()
    for copy in first:
        copy.wait()

    def head_rows(i, carry):
        part = pl.ds(i * 32, 32)
        total = tokens[part, :].astype(f32)
        for k in range(C):
            total = total + RO[k, part, :].astype(f32)
        h1[part, :] = total
        unit, _ = rms_unit(total)
        xm[part, :] = (unit * gain[...]).astype(bf16)
        return carry

    lax.fori_loop(0, rows // 32, head_rows, 0)
    XM[own_rows, :] = xm[...]
    chunks = []
    for j in range(CHUNKS):
        cols = columns(width, j)
        row = []
        for k, peer in enumerate(z_peers):
            piece = XM.at[own_rows, cols]
            row.append(remote(piece, piece, xsend.at[j, k], xrecv.at[j, k], peer))
            row[-1].start()
        chunks.append(row)
    logits = jnp.dot(xm[...], pack[...], preferred_element_type=f32)[:, : chosen.shape[1]]
    logits = jnp.where(chosen[...] > 0.0, logits, -jnp.inf)
    power = jnp.exp(logits - jnp.max(logits, axis=-1, keepdims=True))
    gates[...] = power / jnp.sum(power, axis=-1, keepdims=True)
    WM[own_rows, :] = gates[...] * kept[...]
    row = []
    for k, peer in enumerate(z_peers):
        piece = WM.at[own_rows, :]
        row.append(remote(piece, piece, msend.at[k], mrecv.at[k], peer))
        row[-1].start()
    sent = []
    for j in range(CHUNKS):
        cols = columns(width, j)
        for copy in chunks[j]:
            copy.wait_recv()

        def slots(p, carry):
            at = pl.ds(pl.multiple_of(p * packed, 16), packed)
            SL[at, cols] = jnp.dot(
                select[at, :], XM[:, cols], preferred_element_type=f32
            ).astype(bf16)
            return carry

        lax.fori_loop(0, Q, slots, 0)
        for k, peer in enumerate(p_peers):
            theirs = pl.ds(pl.multiple_of(p_at[k] * packed, 16), packed)
            sent.append(
                remote(SL.at[theirs, cols], buffer.at[mine, cols], bsend.at[j, k], brecv.at[j, k], peer)
            )
            sent[-1].start()
        sent.append(pltpu.make_async_copy(SL.at[mine, cols], buffer.at[mine, cols], local.at[2 + j]))
        sent[-1].start()
    for copy in row:
        copy.wait_recv()
    WS[...] = jnp.zeros_like(WS)

    def weights(p, carry):
        at = pl.ds(pl.multiple_of(p * packed, 16), packed)
        every = lax.dot_general(
            WM[...], select[at, :].astype(f32), (((0,), (1,)), ((), ())),
            precision=lax.Precision.HIGHEST, preferred_element_type=f32,
        )
        expert = (p // F * C + c) * F + lax.rem(p, F)
        hit = lax.broadcasted_iota(jnp.int32, every.shape, 0) == expert
        line = jnp.sum(jnp.where(hit, every, 0.0), axis=0, keepdims=True)
        WS[p, :, pl.ds(0, packed)] = jnp.broadcast_to(line, (8, packed))
        return carry

    lax.fori_loop(0, Q, weights, 0)
    for k, peer in enumerate(p_peers):
        sent.append(remote(WS.at[p_at[k]], wrow.at[q], wsend.at[k], wrecv.at[k], peer))
        sent[-1].start()
    sent.append(pltpu.make_async_copy(WS.at[q], wrow.at[q], local.at[2 + CHUNKS]))
    sent[-1].start()
    for copy in sent + later:
        copy.wait()
    for line in chunks + [row]:
        for copy in line:
            copy.wait_send()


def dispatch(packed, out_part, G, tokens, pack, gain, chosen, kept, select):
    S, C, F = sizes()
    Q = S * F
    rows, width = tokens.shape
    lanes = round_up(packed, 128)
    wide = chosen.shape[1]
    V = pltpu.VMEM
    sds = jax.ShapeDtypeStruct
    vm = pl.BlockSpec(memory_space=pltpu.VMEM)
    return pl.pallas_call(
        functools.partial(dispatch_kernel, packed),
        out_shape=[
            sds((Q * packed, width), bf16),
            sds((Q * packed, width), bf16),
            sds((Q, 8, lanes), f32),
            sds((rows, width), f32),
            sds((rows, width), bf16),
            sds((rows, wide), f32),
        ],
        in_specs=[ANY, ANY] + [vm] * 6,
        out_specs=[ANY, ANY, ANY, vm, vm, vm],
        scratch_shapes=[
            V((C, rows, width), bf16),
            V((C * rows, width), bf16),
            V((Q * packed, width), bf16),
            V((C * rows, wide), f32),
            V((Q, 8, lanes), f32),
            V((C * rows, width), bf16),
            V((Q * packed, width), bf16),
            DMA((4 + CHUNKS,)),
            DMA((C - 1,)), DMA((C - 1,)),
            DMA((Q - 1,)), DMA((Q - 1,)),
            DMA((CHUNKS, C - 1)), DMA((CHUNKS, C - 1)),
            DMA((C - 1,)), DMA((C - 1,)),
            DMA((CHUNKS, Q - 1)), DMA((CHUNKS, Q - 1)),
            DMA((Q - 1,)), DMA((Q - 1,)),
        ],
        name="dispatch_rows",
        compiler_params=params(3),
    )(out_part, G, tokens, pack, gain, chosen, kept, select)


def return_kernel(
    packed, din, dgr, wy, select, select_t, gates, pack, h1, gain, cot,
    DA, y_part, dh1, dlog, gnorm,
    RD, YB, PART, RX, DG, DGP, RG, DL,
    local, dsend, drecv, gsend, grecv, ysend, yrecv, xsend, xrecv, msend, mrecv, asend, arecv,
):
    S, C, F = sizes()
    s, c, f = place()
    Q = S * F
    q = s * F + f
    rows, width = h1.shape
    z_peers = z_neighbours()
    p_at, p_peers = plane_neighbours()
    greet_all(z_peers + p_peers)
    mine = pl.ds(pl.multiple_of(q * packed, 16), packed)
    theirs = [pl.ds(pl.multiple_of(at * packed, 16), packed) for at in p_at]
    small = [
        remote(dgr.at[p_at[k]], DG.at[q], gsend.at[k], grecv.at[k], peer)
        for k, peer in enumerate(p_peers)
    ]
    small.append(pltpu.make_async_copy(dgr.at[q], DG.at[q], local.at[0]))
    for copy in small:
        copy.start()
    chunks = []
    for j in range(CHUNKS):
        cols = columns(width, j)
        line = [
            remote(din.at[theirs[k], cols], RD.at[mine, cols], dsend.at[j, k], drecv.at[j, k], peer)
            for k, peer in enumerate(p_peers)
        ]
        line.append(pltpu.make_async_copy(din.at[mine, cols], RD.at[mine, cols], local.at[2 + j]))
        for copy in line:
            copy.start()
        chunks.append(line)
    sums = []
    for j in range(CHUNKS):
        cols = columns(width, j)
        for copy in chunks[j]:
            copy.wait()

        def combine(i, carry):
            at = pl.ds(pl.multiple_of(i * rows, 16), rows)
            PART[at, cols] = jnp.dot(
                select_t[at, :], RD[:, cols], preferred_element_type=f32
            ).astype(bf16)
            return carry

        lax.fori_loop(0, C, combine, 0)
        for k, peer in enumerate(z_peers):
            src = PART.at[pl.ds(pl.multiple_of(peer[1] * rows, 16), rows), cols]
            sums.append(remote(src, RX.at[k, :, cols], xsend.at[j, k], xrecv.at[j, k], peer))
            sums[-1].start()
    ys = [
        remote(wy.at[theirs[k]], YB.at[mine], ysend.at[k], yrecv.at[k], peer)
        for k, peer in enumerate(p_peers)
    ]
    ys.append(pltpu.make_async_copy(wy.at[mine], YB.at[mine], local.at[1]))
    for copy in ys:
        copy.start()
    for copy in small:
        copy.wait()
    wide = gates.shape[1]
    place_of = lax.broadcasted_iota(jnp.int32, (Q, wide), 0)
    expert = (place_of // F * C + c) * F + lax.rem(place_of, F)
    spread = (lax.broadcasted_iota(jnp.int32, (Q, wide), 1) == expert).astype(f32)

    for p in range(Q):
        at = pl.ds(p * packed, packed)
        line = jnp.dot(
            DG[p, :, pl.ds(0, packed)], select[at, :].astype(f32),
            precision=lax.Precision.HIGHEST, preferred_element_type=f32,
        )
        DL[pl.ds(p, 1), :] = line[0:1, :]
    DGP[...] = lax.dot_general(
        DL[...], spread, (((0,), (0,)), ((), ())),
        precision=lax.Precision.HIGHEST, preferred_element_type=f32,
    ).reshape(DGP.shape)
    more = []
    for k, peer in enumerate(z_peers):
        more.append(remote(DGP.at[peer[1]], RG.at[k], msend.at[k], mrecv.at[k], peer))
        more[-1].start()
    for copy in more:
        copy.wait()
    total = DGP[c]
    for k in range(C - 1):
        total = total + RG[k]
    dlogits = gates[...] * (total - jnp.sum(gates[...] * total, axis=-1, keepdims=True))
    dlog[...] = dlogits.astype(bf16)
    gnorm[...] = jnp.zeros_like(gnorm)
    for copy in sums:
        copy.wait()

    def head_rows(i, carry):
        part = pl.ds(i * 32, 32)
        mine_part = pl.ds(pl.multiple_of(c * rows + i * 32, 16), 32)
        dxm = PART[mine_part, :].astype(f32)
        for k in range(C - 1):
            dxm = dxm + RX[k, part, :].astype(f32)
        dxm = dxm + lax.dot_general(
            dlog[part, :], pack[:, pl.ds(0, wide)], (((1,), (1,)), ((), ())), preferred_element_type=f32
        )
        unit, factor = rms_unit(h1[part, :])
        gnorm[...] += jnp.sum(dxm * unit, axis=0, keepdims=True)
        grad = cot[part, :].astype(f32) + norm_backward(dxm, unit, factor, gain[...])
        dh1[part, :] = grad
        RX[0, part, :] = grad.astype(bf16)
        return carry

    lax.fori_loop(0, rows // 32, head_rows, 0)
    last = []
    for k, peer in enumerate(z_peers):
        last.append(remote(RX.at[0], DA.at[c], asend.at[k], arecv.at[k], peer))
    last.append(pltpu.make_async_copy(RX.at[0], DA.at[c], local.at[2 + CHUNKS]))
    for copy in last:
        copy.start()
    for copy in ys:
        copy.wait()

    def combine_y(i, carry):
        at = pl.ds(pl.multiple_of(i * 32, 32), 32)
        y_part[at, :] = jnp.dot(
            select_t[at, :], YB[...], preferred_element_type=f32
        ).astype(bf16)
        return carry

    lax.fori_loop(0, C * rows // 32, combine_y, 0)
    for copy in last:
        copy.wait()


def give_back(packed, din, dgr, wy, select, select_t, gates, pack, h1, gain, cot):
    S, C, F = sizes()
    Q = S * F
    rows, width = h1.shape
    wide = gates.shape[1]
    V = pltpu.VMEM
    sds = jax.ShapeDtypeStruct
    vm = pl.BlockSpec(memory_space=pltpu.VMEM)
    return pl.pallas_call(
        functools.partial(return_kernel, packed),
        out_shape=[
            sds((C, rows, width), bf16),
            sds((C * rows, width), bf16),
            sds((rows, width), f32),
            sds((rows, wide), bf16),
            sds((1, width), f32),
        ],
        in_specs=[ANY] * 3 + [vm] * 7,
        out_specs=[ANY] + [vm] * 4,
        scratch_shapes=[
            V((Q * packed, width), bf16),
            V((Q * packed, width), bf16),
            V((C * rows, width), bf16),
            V((C - 1, rows, width), bf16),
            V(dgr.shape, f32),
            V((C, rows, wide), f32),
            V((C - 1, rows, wide), f32),
            V((Q, C * rows), f32),
            DMA((3 + CHUNKS,)),
            DMA((CHUNKS, Q - 1)), DMA((CHUNKS, Q - 1)),
            DMA((Q - 1,)), DMA((Q - 1,)),
            DMA((Q - 1,)), DMA((Q - 1,)),
            DMA((CHUNKS, C - 1)), DMA((CHUNKS, C - 1)),
            DMA((C - 1,)), DMA((C - 1,)),
            DMA((C - 1,)), DMA((C - 1,)),
        ],
        name="return_grads",
        compiler_params=params(5),
    )(din, dgr, wy, select, select_t, gates, pack, h1, gain, cot)


def backward_kernel(
    block, da, w, wo, q, k, v, xnt, x, cosine, sine, pos_col, pos_row, gains, go, sp, yp,
    dxn, Q3, O3, S3, T3, YP,
    kr, dkr, dv, acc, DQ, head_grad,
    GQ, Q1, Q2, QS, o_own, o_in, o_plane, o_sum, s_own, s_in, s_plane, s_sum, T, t_in, t_plane, t_sum,
    local, qlocal, csend, crecv, fsend, frecv, zsend, zrecv, qcs, qcr, qfs, qfr, qzs, qzr, ysend, yrecv,
):
    S, C, F = sizes()
    s, c, f = place()
    step = pl.program_id(0)
    units = GQ.shape[0]
    pairs = units - 1
    length, width = x.shape
    wide = 2 * HEAD_DIM
    z_peers = z_neighbours()
    f_peers = [(s, c, lax.rem(f + k, F)) for k in range(1, F)]
    sibling = (1 - s, c, f)
    pair = c * S + s
    out_dst = (pair // C, lax.rem(pair, C), f)
    pair_in = s * C + c
    out_src = (lax.rem(pair_in, S), pair_in // S, f)
    stays = jnp.logical_and(out_dst[0] == s, out_dst[1] == c)
    moves = jnp.logical_not(stays)
    at_once = lambda copy: copy.start()
    cols = pl.ds(pl.multiple_of(step * wide, wide), wide)

    o_first = remote(go.at[1 - s], o_in, csend.at[0], crecv.at[0], sibling)
    s_first = remote(sp.at[1 - s], s_in, csend.at[1], crecv.at[1], sibling)
    t_first = remote(T, t_in, csend.at[2], crecv.at[2], sibling)
    o_load = pltpu.make_async_copy(go.at[s], o_own, local.at[0])
    s_load = pltpu.make_async_copy(sp.at[s], s_own, local.at[1])
    f_at = list(enumerate(f_peers))
    z_at = list(enumerate(z_peers))
    o_second = [remote(o_own.at[p[2]], o_plane.at[k], fsend.at[0, k], frecv.at[0, k], p) for k, p in f_at]
    s_second = [remote(s_own.at[:, p[2]], s_plane.at[k], fsend.at[1, k], frecv.at[1, k], p) for k, p in f_at]
    t_second = [remote(T, t_plane.at[k], fsend.at[2, k], frecv.at[2, k], p) for k, p in f_at]
    o_third = remote(o_sum, O3, zsend.at[0, 0], zrecv.at[0, 0], out_dst)
    o_stay = pltpu.make_async_copy(o_sum, O3, local.at[2])
    s_third = [remote(s_sum.at[p[1]], S3.at[c], zsend.at[1, k], zrecv.at[1, k], p) for k, p in z_at]
    s_third.append(pltpu.make_async_copy(s_sum.at[c], S3.at[c], local.at[3]))
    t_third = [remote(t_sum, T3.at[c], zsend.at[2, k], zrecv.at[2, k], p) for k, p in z_at]
    t_third.append(pltpu.make_async_copy(t_sum, T3.at[c], local.at[4]))
    y_copies = [remote(yp.at[p[1]], YP.at[c], ysend.at[k], yrecv.at[k], p) for k, p in z_at]
    y_copies.append(pltpu.make_async_copy(yp.at[c], YP.at[c], local.at[5]))

    def q_first(u):
        return remote(GQ.at[u, 1 - s], Q1.at[u], qcs.at[u], qcr.at[u], sibling)

    def q_second(u):
        return [remote(GQ.at[u, s, :, p[2]], Q2.at[u, k], qfs.at[u, k], qfr.at[u, k], p) for k, p in f_at]

    def q_third(u):
        lanes = pl.ds(pl.multiple_of(u * wide, wide), wide)
        copies = [
            remote(QS.at[u, p[1]], Q3.at[c, :, lanes], qzs.at[u, k], qzr.at[u, k], p) for k, p in z_at
        ]
        copies.append(pltpu.make_async_copy(QS.at[u, c], Q3.at[c, :, lanes], qlocal.at[u]))
        return copies

    def to_plane(u):
        q_first(u).wait()

        def body(i, carry):
            at = (u, s, i // F, lax.rem(i, F))
            GQ[at] = (GQ[at].astype(f32) + Q1[u, i // F, lax.rem(i, F)].astype(f32)).astype(bf16)
            return carry

        lax.fori_loop(0, C * F, body, 0)
        for copy in q_second(u):
            copy.start()

    def to_ctx(u):
        for copy in q_second(u):
            copy.wait()

        def body(i, carry):
            total = GQ[u, s, i, f].astype(f32)
            for k in range(F - 1):
                total = total + Q2[u, k, i].astype(f32)
            QS[u, i] = total.astype(bf16)
            return carry

        lax.fori_loop(0, C, body, 0)
        for copy in q_third(u):
            copy.start()

    @pl.when(step == 0)
    def _():
        greet = (
            jnp.where(stays, 1 - s, out_src[0]),
            jnp.where(stays, C - 1 - c, out_src[1]),
            f,
        )
        greet_all(z_peers + f_peers + [sibling, greet])
        for copy in [o_first, s_first, o_load, s_load] + y_copies:
            copy.start()
        unit, _ = rms_unit(k[...])
        kr[...] = half_turn(unit * gains[1:2, :], cosine[...], sine[...]).astype(bf16)
        dkr[...] = jnp.zeros_like(dkr)
        dv[...] = jnp.zeros_like(dv)
        head_grad[...] = jnp.zeros_like(head_grad)
        acc[...] = jnp.zeros_like(acc)

    @pl.when(step >= 1)
    def _():
        to_plane(step - 1)

    @pl.when(step == 1)
    def _():
        o_first.wait()
        o_load.wait()

        def o_body(i, carry):
            o_own[i] = (o_own[i].astype(f32) + o_in[i].astype(f32)).astype(bf16)
            return carry

        lax.fori_loop(0, F, o_body, 0)
        for copy in o_second:
            copy.start()
        s_first.wait()
        s_load.wait()

        def s_body(i, carry):
            at = (i // F, lax.rem(i, F))
            s_own[at] = s_own[at] + s_in[at]
            return carry

        lax.fori_loop(0, C * F, s_body, 0)
        for copy in s_second:
            copy.start()

    @pl.when(step >= 2)
    def _():
        to_ctx(step - 2)

    @pl.when(step == 2)
    def _():
        for copy in o_second + s_second:
            copy.wait()
        total = o_own[f].astype(f32)
        for k in range(F - 1):
            total = total + o_plane[k].astype(f32)
        o_sum[...] = total.astype(bf16)

        def s_body(i, carry):
            total = s_own[i, f]
            for k in range(F - 1):
                total = total + s_plane[k, i]
            s_sum[i] = total
            return carry

        lax.fori_loop(0, C, s_body, 0)
        for copy in s_third:
            copy.start()

    @pl.when(jnp.logical_and(step == 2, moves))
    def _():
        o_third.start()

    @pl.when(jnp.logical_and(step == 2, stays))
    def _():
        o_stay.start()

    @pl.when(step < pairs)
    def _():
        dm = lax.dot_general(
            da[...], wo[cols, :], (((1,), (1,)), ((), ())), preferred_element_type=f32
        ).astype(bf16)
        for half in range(2):
            lanes = slice(half * HEAD_DIM, (half + 1) * HEAD_DIM)
            for part in range(length // block):
                rows = slice(part * block, (part + 1) * block)
                unit, factor = rms_unit(q[rows, lanes])
                cos, sin = cosine[rows, :], sine[rows, :]
                qr = half_turn(unit * gains[0:1, :], cos, sin).astype(bf16)
                keys = kr[...]
                probs = score_block(qr, keys, pos_col[rows, :], pos_row[...])
                dmh = dm[rows, lanes]
                dprobs = lax.dot_general(
                    dmh, v[...], (((1,), (1,)), ((), ())), preferred_element_type=f32
                )
                delta = jnp.sum(probs * dprobs, axis=-1, keepdims=True)
                dscores = (probs * (dprobs - delta)).astype(bf16)
                dqr = jnp.dot(dscores, keys, preferred_element_type=f32) * (HEAD_DIM**-0.5)
                rows_in = (((0,), (0,)), ((), ()))
                dkr[...] += lax.dot_general(dscores, qr, rows_in, preferred_element_type=f32) * (
                    HEAD_DIM**-0.5
                )
                dv[...] += lax.dot_general(
                    probs.astype(bf16), dmh, rows_in, preferred_element_type=f32
                )
                dqs = half_turn(dqr, cos, -sin)
                head_grad[0:1, :] += jnp.sum(dqs * unit, axis=0, keepdims=True)
                DQ[rows, lanes] = norm_backward(dqs, unit, factor, gains[0:1, :]).astype(bf16)

    @pl.when(step == pairs)
    def _():
        unit, factor = rms_unit(k[...])
        dks = half_turn(dkr[...], cosine[...], -sine[...])
        head_grad[1:2, :] += jnp.sum(dks * unit, axis=0, keepdims=True)
        DQ[:, :HEAD_DIM] = norm_backward(dks, unit, factor, gains[1:2, :]).astype(bf16)
        DQ[:, HEAD_DIM:] = dv[...].astype(bf16)

    def weight_rows(i, carry):
        part = F * GQ.shape[4]
        rows = pl.ds(pl.multiple_of(i * part, 16), part)
        piece = jnp.dot(xnt[rows, :], DQ[...], preferred_element_type=f32)
        GQ[step, i // C, lax.rem(i, C)] = piece.astype(bf16).reshape(GQ.shape[3:])
        return carry

    lax.fori_loop(0, S * C, weight_rows, 0)
    q_first(step).start()
    for j in range(4):
        part = pl.ds(j * (width // 4), width // 4)
        acc[:, part] += lax.dot_general(
            DQ[...], w[part, cols], (((1,), (1,)), ((), ())), preferred_element_type=f32
        )

    @pl.when(step == pairs)
    def _():
        to_plane(pairs)
        rows_of = width // HEAD_DIM
        total = jnp.zeros((1, width), f32)

        def finish(i, total):
            rows = pl.ds(i * 64, 64)
            unit, _ = rms_unit(x[rows, :].astype(f32))
            term = acc[rows, :]
            dxn[rows, :] = term.astype(bf16)
            return total + jnp.sum(term * unit, axis=0, keepdims=True)

        total = lax.fori_loop(0, length // 64, finish, total)
        for r in range(rows_of):
            T[r : r + 1, :] = total[:, r * HEAD_DIM : (r + 1) * HEAD_DIM]
        T[rows_of:, :] = head_grad[...]
        t_first.start()
        to_ctx(pairs - 1)
        t_first.wait()
        T[...] = T[...] + t_in[...]
        for copy in t_second:
            copy.start()
        to_ctx(pairs)
        for copy in t_second:
            copy.wait()
        order = []
        for g in range(F):
            term = jnp.zeros_like(T)
            for k in range(F - 1):
                came = lax.rem(f + F - (k + 1), F)
                term = term + jnp.where(came == g, t_plane[k], 0.0)
            order.append(term + jnp.where(f == g, T[...], 0.0))
        total = order[0]
        for term in order[1:]:
            total = total + term
        t_sum[...] = total
        for copy in t_third:
            copy.start()
        for copy in s_third + y_copies:
            copy.wait()
        for u in range(units):
            for copy in q_third(u):
                copy.wait()
        for copy in t_third:
            copy.wait()

    @pl.when(jnp.logical_and(step == pairs, moves))
    def _():
        o_third.wait()

    @pl.when(jnp.logical_and(step == pairs, stays))
    def _():
        o_stay.wait()


def backward(da, w, wo, q, k, v, xnt, x, cosine, sine, pos_col, pos_row, gains, go, sp, yp):
    S, C, F = sizes()
    length, width = x.shape
    head_width = wo.shape[0]
    pairs = head_width // (2 * HEAD_DIM)
    units = pairs + 1
    shard = sp.shape[3]
    block = min(length, 512)
    wide = 2 * HEAD_DIM
    once = pl.Buffered(buffer_count=1)
    whole = lambda array: pl.BlockSpec(array.shape, lambda i: (0, 0), pipeline_mode=once)
    sds = jax.ShapeDtypeStruct
    V = pltpu.VMEM
    q_block, o_block, s_block = (shard, wide), go.shape[2:], sp.shape[3:]
    t_block = (width // HEAD_DIM + 8, HEAD_DIM)
    return pl.pallas_call(
        functools.partial(backward_kernel, block),
        out_shape=[
            sds((length, width), bf16),
            sds((C, shard, head_width + wide), bf16),
            sds(o_block, bf16),
            sds((C,) + s_block, f32),
            sds((C,) + t_block, f32),
            sds(yp.shape, bf16),
        ],
        grid=(units,),
        in_specs=[whole(da), whole(w), whole(wo)]
        + [pl.BlockSpec((length, wide), lambda i: (0, jnp.minimum(i, pairs - 1)))]
        + [whole(array) for array in (k, v, xnt, x, cosine, sine, pos_col, pos_row, gains)]
        + [ANY] * 3,
        out_specs=[pl.BlockSpec((length, width), lambda i: (0, 0), pipeline_mode=once)] + [ANY] * 5,
        scratch_shapes=[
            V((length, HEAD_DIM), bf16), V((length, HEAD_DIM), f32), V((length, HEAD_DIM), f32),
            V((length, width), f32), V((length, wide), bf16), V((8, HEAD_DIM), f32),
            V((units, S, C, F) + q_block, bf16), V((units, C, F) + q_block, bf16),
            V((units, F - 1, C) + q_block, bf16), V((units, C) + q_block, bf16),
            V((F,) + o_block, bf16), V((F,) + o_block, bf16), V((F - 1,) + o_block, bf16), V(o_block, bf16),
            V((C, F) + s_block, f32), V((C, F) + s_block, f32), V((F - 1, C) + s_block, f32), V((C,) + s_block, f32),
            V(t_block, f32), V(t_block, f32), V((F - 1,) + t_block, f32), V(t_block, f32),
            DMA((6,)), DMA((units,)),
            DMA((3,)), DMA((3,)), DMA((3, F - 1)), DMA((3, F - 1)), DMA((3, C - 1)), DMA((3, C - 1)),
            DMA((units,)), DMA((units,)), DMA((units, F - 1)), DMA((units, F - 1)),
            DMA((units, C - 1)), DMA((units, C - 1)), DMA((C - 1,)), DMA((C - 1,)),
        ],
        name="attention_backward",
        compiler_params=params(7, 60 * 2**20),
    )(da, w, wo, q, k, v, xnt, x, cosine, sine, pos_col, pos_row, gains, go, sp, yp)


def dot(left, right):
    return jnp.dot(left, right, preferred_element_type=f32)


def contract_rows(left, right):
    return lax.dot_general(left, right, (((0,), (0,)), ((), ())), preferred_element_type=f32)


def times_transpose(left, right):
    return lax.dot_general(left, right, (((1,), (1,)), ((), ())), preferred_element_type=f32)


def on_device(
    tokens,
    stretch_order,
    expert_ids,
    slot_index,
    norm_attn,
    head_gains,
    w_query,
    w_key,
    w_value,
    w_out,
    norm_moe,
    w_router,
    w_gate,
    w_up,
    w_down,
    cotangent,
):
    S, C, F = sizes()
    Q = S * F
    seq_at, ctx_at, fsdp_at = place()
    rows, width = tokens.shape[1:]
    length = C * rows
    experts = w_router.shape[1]
    capacity = rows * TOP // (Q * C) + 1
    packed = round_up(C * capacity, 16)
    lanes = round_up(packed, 128)
    head_width = w_query.shape[1] // C
    shard = w_router.shape[0]
    pack_width = round_up(experts + 2, 128)
    pack = jnp.concatenate(
        [
            w_router,
            norm_attn[:, None],
            norm_moe[:, None],
            jnp.zeros((shard, pack_width - experts - 2), bf16),
        ],
        axis=1,
    )
    gains = head_gains.astype(f32)
    (
        X, W, WO, PK, _, G, out_part, q, k, v, mixed, xnt, row_gains,
        cosine, sine, pos_col, pos_row, select, select_t, chosen, kept_map,
    ) = front(
        capacity, packed, experts, stretch_order, expert_ids[0], slot_index[0],
        tokens[0], w_query, w_key, w_value, w_out, pack, cotangent[0], gains,
    )
    W = W.reshape(width, head_width + 2 * HEAD_DIM)
    WO = WO.reshape(head_width, width)
    PK = PK.reshape(width, pack_width)
    gain_attn, gain_moe = row_gains[0:1], row_gains[1:2]
    buffer, slot_grad, slot_weight, h1, xm, gates = dispatch(
        packed, out_part.reshape(C, rows, width), G.reshape(length, width), tokens[0], PK, gain_moe, chosen, kept_map, select
    )
    slot_weight = slot_weight[:, 0, :packed].reshape(Q * packed, 1)
    slot_grad = slot_grad.astype(f32)
    gate_pre = dot(buffer, w_gate[0])
    up_pre = dot(buffer, w_up[0])
    sigmoid_gp = jax.nn.sigmoid(gate_pre)
    silu_gp = gate_pre * sigmoid_gp
    hidden = (silu_gp * up_pre).astype(bf16)
    y = dot(hidden, w_down[0])
    weighted_y = (slot_weight * y).astype(bf16)
    slot_dgate = jnp.sum(slot_grad * y, axis=-1).reshape(Q, packed)
    dy = (slot_weight * slot_grad).astype(bf16)
    dhid = times_transpose(dy, w_down[0])
    dgp = (dhid * up_pre * sigmoid_gp * (1.0 + gate_pre * (1.0 - sigmoid_gp))).astype(bf16)
    dup = (dhid * silu_gp).astype(bf16)
    din = (times_transpose(dgp, w_gate[0]) + times_transpose(dup, w_up[0])).astype(bf16)
    slot_dgate = jnp.broadcast_to(
        jnp.pad(slot_dgate, ((0, 0), (0, lanes - packed)))[:, None, :], (Q, 8, lanes)
    )
    DA, y_part, dh1, dlogits, grad_norm_moe = give_back(
        packed, din, slot_dgate, weighted_y, select, select_t, gates, PK, h1, gain_moe, cotangent[0]
    )
    grad_router = contract_rows(xm, dlogits[:, :experts])
    DA = DA.reshape(length, width)
    grad_out_part = contract_rows(mixed, DA).astype(bf16)
    small = jnp.concatenate(
        [grad_router, grad_norm_moe.T, jnp.zeros((width, pack_width - experts - 1), f32)], axis=1
    )
    dxn_part, q_sums, o_sum, small_sums, tiny_sums, y_parts = backward(
        DA, W, WO, q, k, v, xnt, X, cosine, sine, pos_col, pos_row, gains,
        grad_out_part.reshape(S, F, head_width // Q, width),
        small.reshape(S, C, F, shard, pack_width),
        y_part.reshape(C, rows, width),
    )
    dxn_part = dxn_part.reshape(C, rows, width)
    dxn = lax.dynamic_index_in_dim(dxn_part, ctx_at, 0, keepdims=False).astype(f32)
    for k_at in range(1, C):
        theirs = lax.dynamic_index_in_dim(dxn_part, lax.rem(ctx_at + k_at, C), 0, keepdims=False)
        shift = [(i, (i + k_at) % C) for i in range(C)]
        dxn = dxn + lax.ppermute(theirs, "ctx", shift).astype(f32)
    grad_wgate = contract_rows(buffer, dgp)
    grad_wup = contract_rows(buffer, dup)
    grad_wdown = contract_rows(hidden, dy)
    layer_out = (h1 + jnp.sum(y_parts.astype(f32), axis=0)).astype(bf16)
    unit, factor = rms_unit(tokens[0].astype(f32))
    grad_tokens = (dh1 + norm_backward(dxn, unit, factor, gain_attn)).astype(bf16)
    q_sums = q_sums.astype(f32)
    grad_query = q_sums[:, :, :head_width].transpose(1, 0, 2).reshape(shard, C * head_width)

    def key_columns(block):
        pieces = block.reshape(KEY_VALUE_HEADS, C // KEY_VALUE_HEADS, shard, HEAD_DIM).sum(axis=1)
        return pieces.transpose(1, 0, 2).reshape(shard, KEY_VALUE_HEADS * HEAD_DIM)

    grad_key = key_columns(q_sums[:, :, head_width : head_width + HEAD_DIM])
    grad_value = key_columns(q_sums[:, :, head_width + HEAD_DIM :])
    small_sum = jnp.sum(small_sums, axis=0)
    tiny_sum = jnp.sum(tiny_sums, axis=0)
    tiny_rows = width // HEAD_DIM
    device = (seq_at * C + ctx_at) * F + fsdp_at
    grad_norm_attn = lax.dynamic_slice_in_dim(
        tiny_sum[:tiny_rows].reshape(width), device * shard, shard
    )
    return (
        layer_out[None],
        grad_tokens[None],
        grad_norm_attn,
        tiny_sum[tiny_rows : tiny_rows + 2],
        grad_query,
        grad_key,
        grad_value,
        o_sum.astype(f32),
        small_sum[:, experts],
        small_sum[:, :experts],
        grad_wgate[None],
        grad_wup[None],
        grad_wdown[None],
    )


def solution(mesh):
    rows = P(("seq", "fsdp"), "ctx", None)
    vector = P(AXES)
    matrix = P(AXES, None)
    cube = P(AXES, None, None)
    return jax.shard_map(
        on_device,
        mesh=mesh,
        in_specs=(
            rows, P(), rows, rows, vector, P(), matrix, matrix, matrix, matrix,
            vector, matrix, cube, cube, cube, rows,
        ),
        out_specs=(
            rows, rows, vector, P(), matrix, matrix, matrix, matrix, vector, matrix,
            cube, cube, cube,
        ),
        check_vma=False,
    )
```

```python
import functools

import jax
import jax.numpy as jnp
from jax import lax
from jax.experimental import pallas as pl
from jax.experimental.pallas import tpu as pltpu
from jax.sharding import PartitionSpec as P

QUERY_HEADS = 32
KEY_VALUE_HEADS = 4
HEAD_DIM = 128
TOP = 8
AXES = ("seq", "ctx", "fsdp")
MESH = pl.DeviceIdType.MESH
epsilon = 1e-06
rope_base = 1000000.0
VMEM_LIMIT = 56 * 2**20
f32 = jnp.float32
bf16 = jnp.bfloat16


def round_up(value, step):
    return (value + step - 1) // step * step


def place():
    return tuple(lax.axis_index(name) for name in AXES)


def sizes():
    return tuple(lax.axis_size(name) for name in AXES)


def signal(device):
    pl.semaphore_signal(
        pltpu.get_barrier_semaphore(), inc=1, device_id=device, device_id_type=MESH
    )


def remote(src, dst, send, recv, device):
    return pltpu.make_async_remote_copy(
        src_ref=src,
        dst_ref=dst,
        send_sem=send,
        recv_sem=recv,
        device_id=device,
        device_id_type=MESH,
    )


def params(cid, limit=VMEM_LIMIT):
    return pltpu.CompilerParams(
        collective_id=cid, has_side_effects=True, vmem_limit_bytes=limit
    )


ANY = pl.BlockSpec(memory_space=pl.ANY)
DMA = pltpu.SemaphoreType.DMA


def rms_unit(rows):
    factor = lax.rsqrt(jnp.mean(rows * rows, axis=-1, keepdims=True) + epsilon)
    return rows * factor, factor


def norm_backward(grad_scaled, normed, factor, gain):
    grad_normed = grad_scaled * gain
    inner = jnp.mean(grad_normed * normed, axis=-1, keepdims=True)
    return factor * (grad_normed - normed * inner)


def half_turn(rows, cosine, sine):
    return rows * cosine + pltpu.roll(rows, HEAD_DIM // 2, 1) * sine


def score_block(qr, kr, pos_col, pos_row):
    scores = lax.dot_general(
        qr, kr, (((1,), (1,)), ((), ())), preferred_element_type=f32
    ) * (HEAD_DIM**-0.5)
    scores = jnp.where(pos_col >= pos_row, scores, -jnp.inf)
    peak = jnp.max(scores, axis=-1, keepdims=True)
    weight = jnp.exp(scores - peak)
    return weight * (1.0 / jnp.sum(weight, axis=-1, keepdims=True))


def z_neighbours():
    _, C, _ = sizes()
    s, c, f = place()
    return [(s, lax.rem(c + k, C), f) for k in range(1, C)]


def plane_neighbours():
    S, _, F = sizes()
    s, c, f = place()
    Q = S * F
    at = [lax.rem(s * F + f + k, Q) for k in range(1, Q)]
    return at, [(q // F, c, lax.rem(q, F)) for q in at]


def greet_all(peers):
    for peer in peers:
        signal(peer)
    pl.semaphore_wait(pltpu.get_barrier_semaphore(), len(peers))


class Line:
    def __init__(self, own, block, rsend, rrecv, lsend, lrecv):
        s, self.c, f = place()
        self.C = lax.axis_size("ctx")
        self.own, self.block = own, block
        self.sems = (rsend, rrecv, lsend, lrecv)
        self.right = (s, lax.rem(self.c + 1, self.C), f)
        self.left = (s, lax.rem(self.c + self.C - 1, self.C), f)

    def copy(self, rightward, h):
        origin = self.c - h if rightward else self.c + h
        src = self.own if h == 0 else self.block(origin)
        send, recv = self.sems[:2] if rightward else self.sems[2:]
        return remote(
            src, self.block(origin), send.at[h], recv.at[h], self.right if rightward else self.left
        )

    def sends(self, rightward, h):
        if rightward:
            return jnp.logical_and(self.c >= h, self.c < self.C - 1)
        return jnp.logical_and(self.c + h < self.C, self.c > 0)

    def start(self):
        for way in (True, False):
            pl.when(self.sends(way, 0))(self.copy(way, 0).start)

    def hop(self, h):
        for way in (True, False):
            origin = self.c - h if way else self.c + h
            there = origin >= 0 if way else origin < self.C
            landed = remote(
                self.block(origin), self.block(origin),
                self.sems[0 if way else 2].at[h - 1], self.sems[1 if way else 3].at[h - 1],
                self.left if way else self.right,
            )
            pl.when(there)(landed.wait_recv)
            if h < self.C - 1:
                pl.when(self.sends(way, h))(self.copy(way, h).start)

    def finish(self):
        for way in (True, False):
            for h in range(self.C - 1):
                pl.when(self.sends(way, h))(self.copy(way, h).wait_send)


def line_sems(C):
    return [DMA((C - 1,)) for _ in range(4)]


def front_kernel(
    block, capacity, packed, experts,
    order, ids, slot_ids, tokens, wq, wk, wv, wo, pack, cot, gains, frequency,
    X_out, W_out, WO_out, PK, SM, G, out, q, k_out, v, mixed, xnt, row_gains,
    cosine, sine, pos_col, pos_row, select, select_t, chosen, kept,
    X, W, WO, xn, kr,
    local, save, zsend, zrecv, fsend, frecv, csend, crecv, wsend, wrecv,
    xrs, xrr, xls, xlr, grs, grr, gls, glr,
):
    S, C, F = sizes()
    s, c, f = place()
    Q = S * F
    rows, width = tokens.shape
    length = C * rows
    head_width = wq.shape[1] // C
    shard = wq.shape[0]
    wide = chosen.shape[1]
    z_peers = z_neighbours()
    f_peers = [(s, c, lax.rem(f + k, F)) for k in range(1, F)]
    sibling = (1 - s, c, f)
    pair = s * C + c
    out_dst = (lax.rem(pair, S), pair // S, f)
    pair_in = c * S + s
    out_src = (pair_in // C, lax.rem(pair_in, C), f)
    stays = jnp.logical_and(out_dst[0] == s, out_dst[1] == c)
    moves = jnp.logical_not(stays)
    greet = (
        jnp.where(stays, 1 - s, out_src[0]),
        jnp.where(stays, C - 1 - c, out_src[1]),
        f,
    )
    lane = lax.broadcasted_iota(jnp.int32, (rows, wide), 1)
    hits = jnp.zeros((rows, wide), f32)
    slot_map = jnp.full((rows, wide), -1, jnp.int32)
    for j in range(TOP):
        here = lane == ids[:, j : j + 1]
        slot = jnp.broadcast_to(slot_ids[:, j : j + 1], (rows, wide))
        hits = jnp.where(here, 1.0, hits)
        slot_map = jnp.where(jnp.logical_and(here, slot < capacity), slot, slot_map)
    chosen[...] = hits
    kept[...] = (slot_map >= 0).astype(f32)
    SM[c] = slot_map.astype(f32)
    greet_all(z_peers + f_peers + [sibling, greet])

    def pieces(target):
        kv = (target * KEY_VALUE_HEADS) // C
        q_cols = pl.ds(pl.multiple_of(target * head_width, 128), head_width)
        kv_cols = pl.ds(pl.multiple_of(kv * HEAD_DIM, 128), HEAD_DIM)
        mine = W.at[s, c, f]
        return [
            (wq.at[:, q_cols], mine.at[:, pl.ds(0, head_width)]),
            (wk.at[:, kv_cols], mine.at[:, pl.ds(head_width, HEAD_DIM)]),
            (wv.at[:, kv_cols], mine.at[:, pl.ds(head_width + HEAD_DIM, HEAD_DIM)]),
            (pack, PK.at[s, c, f]),
        ]

    def token_rows(at):
        return X.at[pl.ds(pl.multiple_of(at * rows, 16), rows)]

    own = [
        pltpu.make_async_copy(src, dst, local.at[i])
        for i, (src, dst) in enumerate(pieces(c) + [(tokens, token_rows(c)), (cot, G.at[c])])
    ]
    z_copies = [
        remote(src, dst, zsend.at[i, k], zrecv.at[i, k], peer)
        for k, peer in enumerate(z_peers)
        for i, (src, dst) in enumerate(pieces(peer[1]))
    ]
    slot_copies = [
        remote(SM.at[c], SM.at[c], zsend.at[4, k], zrecv.at[4, k], peer)
        for k, peer in enumerate(z_peers)
    ]
    x_line = Line(tokens, token_rows, xrs, xrr, xls, xlr)
    g_line = Line(cot, lambda at: G.at[at], grs, grr, gls, glr)
    out_copy = remote(wo, WO.at[out_dst[0], f], wsend.at[0], wrecv.at[0], out_dst)
    out_stay = pltpu.make_async_copy(wo, WO.at[s, f], wsend.at[1])
    for copy in own + z_copies + slot_copies:
        copy.start()
    x_line.start()
    pl.when(moves)(out_copy.start)
    pl.when(stays)(out_stay.start)

    where = lax.broadcasted_iota(jnp.int32, (1, length), 1)
    where_col = lax.broadcasted_iota(jnp.int32, (length, 1), 0)
    stretch_rows = rows // 2

    def position(at):
        total = jnp.zeros_like(at)
        for j in range(2 * C):
            base = order[j] * stretch_rows - j * stretch_rows
            total = jnp.where(at // stretch_rows == j, at + base, total)
        return total

    pos_row[...] = position(where)
    pos_col[...] = position(where_col)
    angles = pos_col[...].astype(f32) * frequency[...]
    cosine[...] = jnp.cos(angles)
    turned = jnp.sin(angles)
    sine[...] = jnp.where(
        lax.broadcasted_iota(jnp.int32, turned.shape, 1) < HEAD_DIM // 2, -turned, turned
    )

    for copy in own[:5] + z_copies:
        copy.wait()

    def weight_block(index, at):
        return (W.at[s, :, at], PK.at[s, :, at], WO.at[s, at])[index]

    f_copies = [
        [
            remote(weight_block(i, f), weight_block(i, f), fsend.at[i, k], frecv.at[i, k], peer)
            for k, peer in enumerate(f_peers)
        ]
        for i in range(3)
    ]

    def to_sibling(i, k):
        at = lax.rem(f + F - k, F)
        return remote(weight_block(i, at), weight_block(i, at), csend.at[i, k], crecv.at[i, k], sibling)

    c_copies = [[to_sibling(i, k) for k in range(F)] for i in range(3)]
    for i in range(2):
        for copy in f_copies[i] + c_copies[i][:1]:
            copy.start()
    x_line.hop(1)
    pl.when(moves)(out_copy.wait)
    pl.when(stays)(out_stay.wait)
    for copy in f_copies[2] + c_copies[2][:1]:
        copy.start()
    for h in range(2, C - 1):
        x_line.hop(h)
    g_line.start()
    for k in range(F - 1):
        for i in range(2):
            f_copies[i][k].wait_recv()
            c_copies[i][k + 1].start()
    for copy in slot_copies:
        copy.wait()
    at = lax.broadcasted_iota(jnp.int32, (wide, Q * packed), 1) // packed
    expert = (at // F * C + c) * F + lax.rem(at, F)
    spread = (lax.broadcasted_iota(jnp.int32, (wide, Q * packed), 0) == expert).astype(bf16)
    slot_rows = SM[...].reshape(length, wide).astype(bf16)
    by_token = jnp.dot(slot_rows, spread, preferred_element_type=f32)
    base = (lax.broadcasted_iota(jnp.int32, by_token.shape, 0) // rows * capacity).astype(f32)
    number = lax.rem(lax.broadcasted_iota(jnp.int32, by_token.shape, 1), packed).astype(f32)
    select_t[...] = jnp.where(
        jnp.logical_and(by_token >= 0.0, by_token + base == number), 1.0, 0.0
    ).astype(bf16)
    at = lax.broadcasted_iota(jnp.int32, (Q, wide), 0)
    expert = (at // F * C + c) * F + lax.rem(at, F)
    spread = (lax.broadcasted_iota(jnp.int32, (Q, wide), 1) == expert).astype(bf16)
    by_slot = lax.dot_general(
        spread, slot_rows, (((1,), (1,)), ((), ())), preferred_element_type=f32
    )
    base = (where // rows * capacity).astype(f32)
    by_slot = jnp.where(by_slot >= 0.0, by_slot + base, -1.0)
    number = lax.broadcasted_iota(jnp.int32, (packed, length), 0).astype(f32)
    for p in range(Q):
        select[p * packed : (p + 1) * packed, :] = jnp.where(
            number == by_slot[p : p + 1, :], 1.0, 0.0
        ).astype(bf16)

    x_line.hop(C - 1)
    for i in range(2):
        for copy in c_copies[i]:
            copy.wait()
    saves = [
        pltpu.make_async_copy(X, X_out, save.at[0]),
        pltpu.make_async_copy(W, W_out, save.at[1]),
        pltpu.make_async_copy(WO, WO_out, save.at[2]),
    ]
    saves[0].start()
    saves[1].start()
    across = lax.broadcasted_iota(jnp.int32, (HEAD_DIM, HEAD_DIM), 0)
    diagonal = across == lax.broadcasted_iota(jnp.int32, (HEAD_DIM, HEAD_DIM), 1)
    flat = PK[...].reshape(width, PK.shape[-1]).astype(f32)
    for j in range(width // HEAD_DIM):
        part = slice(j * HEAD_DIM, (j + 1) * HEAD_DIM)
        for i in range(2):
            line = flat[part, experts + i : experts + i + 1]
            row_gains[i : i + 1, part] = jnp.sum(jnp.where(diagonal, line, 0.0), axis=0, keepdims=True)

    def norm_rows(i, carry):
        part = pl.ds(i * 64, 64)
        unit, _ = rms_unit(X[part, :].astype(f32))
        xn[part, :] = (unit * row_gains[0:1, :]).astype(bf16)
        return carry

    lax.fori_loop(0, length // 64, norm_rows, 0)

    def weights(cols):
        return W[:, :, :, :, cols].reshape(width, 2 * HEAD_DIM)

    kv = jnp.dot(xn[...], weights(pl.ds(head_width, 2 * HEAD_DIM)), preferred_element_type=f32)
    k_out[...] = kv[:, :HEAD_DIM]
    v[...] = kv[:, HEAD_DIM:].astype(bf16)
    unit, _ = rms_unit(k_out[...])
    kr[...] = half_turn(unit * gains[1:2, :], cosine[...], sine[...]).astype(bf16)

    def head_pair(i, carry):
        cols = pl.ds(pl.multiple_of(i * 2 * HEAD_DIM, 2 * HEAD_DIM), 2 * HEAD_DIM)
        both = jnp.dot(xn[...], weights(cols), preferred_element_type=f32)
        q[:, cols] = both
        for half in range(2):
            lanes = pl.ds(pl.multiple_of((2 * i + half) * HEAD_DIM, HEAD_DIM), HEAD_DIM)
            for part in range(length // block):
                at = slice(part * block, (part + 1) * block)
                unit, _ = rms_unit(both[at, half * HEAD_DIM : (half + 1) * HEAD_DIM])
                qr = half_turn(unit * gains[0:1, :], cosine[at, :], sine[at, :]).astype(bf16)
                probs = score_block(qr, kr[...], pos_col[at, :], pos_row[...])
                mixed[at, lanes] = jnp.dot(
                    probs.astype(bf16), v[...], preferred_element_type=f32
                ).astype(bf16)
        return carry

    pairs = head_width // (2 * HEAD_DIM)
    half_way = pairs // 2
    g_line.hop(1)
    lax.fori_loop(0, half_way, head_pair, 0)
    for k in range(F - 1):
        f_copies[2][k].wait_recv()
        c_copies[2][k + 1].start()
    for h in range(2, C - 1):
        g_line.hop(h)
    lax.fori_loop(half_way, pairs, head_pair, 0)
    for copy in c_copies[2]:
        copy.wait()
    saves[2].start()

    def project(j, carry):
        cols = pl.ds(pl.multiple_of(j * 256, 256), 256)
        out[:, cols] = jnp.dot(
            mixed[...], WO[:, :, :, cols].reshape(head_width, 256), preferred_element_type=f32
        ).astype(bf16)
        return carry

    lax.fori_loop(0, width // 256, project, 0)

    def turn(j, carry):
        cols = pl.ds(pl.multiple_of(j * 256, 256), 256)
        xnt[cols, :] = xn[:, cols].T
        return carry

    lax.fori_loop(0, width // 256, turn, 0)
    g_line.hop(C - 1)
    x_line.finish()
    g_line.finish()
    for line in f_copies:
        for copy in line:
            copy.wait_send()
    for copy in saves + own[5:]:
        copy.wait()


def front(capacity, packed, experts, order, ids, slot_ids, tokens, wq, wk, wv, wo, pack, cot, gains):
    S, C, F = sizes()
    Q = S * F
    rows, width = tokens.shape
    length = C * rows
    shard = wq.shape[0]
    head_width = wq.shape[1] // C
    wide = round_up(experts, 128)
    frequency = jnp.power(rope_base, -jnp.arange(HEAD_DIM // 2, dtype=f32) * 2.0 / HEAD_DIM)
    frequency = jnp.concatenate([frequency, frequency])[None]
    block = min(length, 512)
    sds = jax.ShapeDtypeStruct
    V = pltpu.VMEM
    vm = pl.BlockSpec(memory_space=pltpu.VMEM)
    w_shape = (S, C, F, shard, head_width + 2 * HEAD_DIM)
    wo_shape = (S, F) + wo.shape
    pack_shape = (S, C, F) + pack.shape
    return pl.pallas_call(
        functools.partial(front_kernel, block, capacity, packed, experts),
        out_shape=[
            sds((length, width), bf16),
            sds(w_shape, bf16),
            sds(wo_shape, bf16),
            sds(pack_shape, bf16),
            sds((C, rows, wide), f32),
            sds((C, rows, width), bf16),
            sds((length, width), bf16),
            sds((length, head_width), f32),
            sds((length, HEAD_DIM), f32),
            sds((length, HEAD_DIM), bf16),
            sds((length, head_width), bf16),
            sds((width, length), bf16),
            sds((2, width), f32),
            sds((length, HEAD_DIM), f32),
            sds((length, HEAD_DIM), f32),
            sds((length, 1), jnp.int32),
            sds((1, length), jnp.int32),
            sds((Q * packed, length), bf16),
            sds((length, Q * packed), bf16),
            sds((rows, wide), f32),
            sds((rows, wide), f32),
        ],
        in_specs=[pl.BlockSpec(memory_space=pltpu.SMEM), vm, vm] + [ANY] * 7 + [vm, vm],
        out_specs=[ANY, ANY, ANY, vm, vm, ANY] + [vm] * 15,
        scratch_shapes=[
            V((length, width), bf16),
            V(w_shape, bf16),
            V(wo_shape, bf16),
            V((length, width), bf16),
            V((length, HEAD_DIM), bf16),
            DMA((6,)), DMA((3,)),
            DMA((5, C - 1)), DMA((5, C - 1)),
            DMA((3, F - 1)), DMA((3, F - 1)),
            DMA((3, F)), DMA((3, F)),
            DMA((2,)), DMA((1,)),
        ]
        + line_sems(C)
        + line_sems(C),
        name="gather_and_attend",
        compiler_params=params(1, 60 * 2**20),
    )(order, ids, slot_ids, tokens, wq, wk, wv, wo, pack, cot, gains, frequency)


CHUNKS = 4


def columns(width, j):
    step = width // CHUNKS
    return pl.ds(j * step, step)


def three_parts(line):
    high = line.astype(bf16).astype(f32)
    rest = line - high
    middle = rest.astype(bf16).astype(f32)
    row = lax.broadcasted_iota(jnp.int32, (16, line.shape[1]), 0)
    rows = jnp.where(row == 0, high, jnp.where(row == 1, middle, jnp.where(row == 2, rest - middle, 0.0)))
    return rows.astype(bf16)


def halves(total):
    return total // 2


def dispatch_kernel(
    packed, out_part, G_in, tokens, pack, gain, chosen, kept, select, w_gate, w_up, w_down,
    buffer_out, gbuf, wrow, h1, xm, gates, hidden_out, dgp_out, dup_out, dgr,
    OP, RB, XM, SL, WM, WS, G, SG, buffer, WG, WU, WD, gp, up, gw, dup,
    local, load, saved, osend, orecv, gsend, grecv, xsend, xrecv, msend, mrecv, bsend, brecv, wsend, wrecv,
):
    S, C, F = sizes()
    s, c, f = place()
    Q = S * F
    q = s * F + f
    rows, width = tokens.shape
    total_rows = Q * packed
    half = halves(total_rows)
    z_peers = z_neighbours()
    p_at, p_peers = plane_neighbours()
    loads = [
        pltpu.make_async_copy(G_in, G, load.at[0]),
        pltpu.make_async_copy(w_down.at[0], WD, load.at[1]),
        pltpu.make_async_copy(w_gate.at[0], WG, load.at[2]),
        pltpu.make_async_copy(w_up.at[0], WU, load.at[3]),
    ]
    for copy in loads:
        copy.start()
    greet_all(z_peers + p_peers)
    mine = pl.ds(pl.multiple_of(q * packed, 16), packed)
    own_rows = pl.ds(pl.multiple_of(c * rows, 16), rows)
    right = (s, lax.rem(c + 1, C), f)
    left = (s, lax.rem(c + C - 1, C), f)

    def rightward(t):
        return remote(OP.at[t], RB.at[t], osend.at[0, t], orecv.at[0, t], right)

    def leftward(t):
        return remote(OP.at[t], RB.at[jnp.where(c - 1 == t, C, t)], osend.at[1, t], orecv.at[1, t], left)

    def merge(t, way):
        remote(OP.at[t], RB.at[t], osend.at[way, t], orecv.at[way, t], left).wait_recv()

        def add(j, carry):
            part = pl.ds(j * 32, 32)
            OP[t, part, :] = (OP[t, part, :].astype(f32) + RB[t, part, :].astype(f32)).astype(bf16)
            return carry

        lax.fori_loop(0, rows // 32, add, 0)

    def pass_on(step):
        t_right = C - 1 + c - step
        t_left = step - (C - 1 - c)

        @pl.when((t_right > c) & (t_right < C) & (c > 0))
        def _():
            merge(t_right, 0)
            rightward(t_right).start()

        @pl.when((t_left >= 0) & (t_left < c) & (c < C - 1))
        def _():
            merge(t_left, 1)
            leftward(t_left).start()

    fetch = pltpu.make_async_copy(out_part, OP, local.at[0])
    fetch.start()
    fetch.wait()

    @pl.when(c == 0)
    def _():
        for t in range(C - 1, 0, -1):
            rightward(t).start()

    @pl.when(c == C - 1)
    def _():
        for t in range(C - 1):
            leftward(t).start()

    loads[0].wait()

    def grad_slots(p):
        at = pl.ds(pl.multiple_of(p * packed, 16), packed)

        def body(j, carry):
            cols = pl.ds(pl.multiple_of(j * 512, 512), 512)
            SG[at, cols] = jnp.dot(select[at, :], G[:, cols], preferred_element_type=f32).astype(bf16)
            return carry

        lax.fori_loop(0, width // 512, body, 0)

    later = []
    for k, peer in enumerate(p_peers):
        theirs = pl.ds(pl.multiple_of(p_at[k] * packed, 16), packed)
        later.append(remote(SG.at[theirs], gbuf.at[mine], gsend.at[k], grecv.at[k], peer))
        grad_slots(p_at[k])
        later[-1].start()
    grad_slots(q)
    later.append(pltpu.make_async_copy(SG.at[mine], gbuf.at[mine], local.at[1]))
    later[-1].start()
    for step in range(1, C - 1):
        pass_on(step)

    @pl.when(c > 0)
    def _():
        remote(OP.at[0], RB.at[c], osend.at[0, c], orecv.at[0, c], left).wait_recv()

    @pl.when(c < C - 1)
    def _():
        remote(OP.at[0], RB.at[C], osend.at[1, c], orecv.at[1, c], right).wait_recv()


    def head_rows(i, carry):
        part = pl.ds(i * 32, 32)
        total = tokens[part, :].astype(f32) + OP[c, part, :].astype(f32)
        total += jnp.where(c > 0, RB[c, part, :].astype(f32), 0.0)
        total += jnp.where(c < C - 1, RB[C, part, :].astype(f32), 0.0)
        h1[part, :] = total
        unit, _ = rms_unit(total)
        normed = (unit * gain[...]).astype(bf16)
        xm[part, :] = normed
        XM[pl.ds(pl.multiple_of(c * rows + i * 32, 16), 32), :] = normed
        return carry

    lax.fori_loop(0, rows // 32, head_rows, 0)
    chunks = []
    for j in range(CHUNKS):
        piece = XM.at[own_rows, columns(width, j)]
        chunks.append(
            [remote(piece, piece, xsend.at[j, k], xrecv.at[j, k], peer) for k, peer in enumerate(z_peers)]
        )
    for copy in chunks[0]:
        copy.start()
    logits = jnp.dot(xm[...], pack[...], preferred_element_type=f32)[:, : chosen.shape[1]]
    logits = jnp.where(chosen[...] > 0.0, logits, -jnp.inf)
    power = jnp.exp(logits - jnp.max(logits, axis=-1, keepdims=True))
    gates[...] = power / jnp.sum(power, axis=-1, keepdims=True)
    WM[own_rows, :] = gates[...] * kept[...]
    row = []
    for k, peer in enumerate(z_peers):
        piece = WM.at[own_rows, :]
        row.append(remote(piece, piece, msend.at[k], mrecv.at[k], peer))
        row[-1].start()
    for line in chunks[1:]:
        for copy in line:
            copy.start()
    sent = []
    for j in range(CHUNKS):
        cols = columns(width, j)
        for copy in chunks[j]:
            copy.wait_recv()

        def slots(i, carry):
            at = pl.ds(pl.multiple_of(i * half, 16), half)
            SL[at, cols] = jnp.dot(select[at, :], XM[:, cols], preferred_element_type=f32).astype(bf16)
            return carry

        lax.fori_loop(0, 2, slots, 0)
        line = []
        for k, peer in enumerate(p_peers):
            theirs = pl.ds(pl.multiple_of(p_at[k] * packed, 16), packed)
            line.append(
                remote(SL.at[theirs, cols], buffer.at[mine, cols], bsend.at[j, k], brecv.at[j, k], peer)
            )
        line.append(pltpu.make_async_copy(SL.at[mine, cols], buffer.at[mine, cols], local.at[4 + j]))
        for copy in line:
            copy.start()
        sent.append(line)
        if j == 0:
            for copy in row:
                copy.wait_recv()
            WS[...] = jnp.zeros_like(WS)

            place_of = lax.broadcasted_iota(jnp.int32, (Q, WM.shape[1]), 0)
            expert = (place_of // F * C + c) * F + lax.rem(place_of, F)
            spread = (lax.broadcasted_iota(jnp.int32, expert.shape, 1) == expert).astype(f32)
            lines = lax.dot_general(
                spread, WM[...], (((1,), (1,)), ((), ())),
                precision=lax.Precision.HIGHEST, preferred_element_type=f32,
            )
            for p in range(Q):
                line = lax.dot_general(
                    three_parts(lines[p : p + 1, :]), select[p * packed : (p + 1) * packed, :],
                    (((1,), (1,)), ((), ())), preferred_element_type=f32,
                )
                WS[p, :, pl.ds(0, packed)] = jnp.broadcast_to(
                    jnp.sum(line, axis=0, keepdims=True), (8, packed)
                )
            scales = [
                remote(WS.at[p_at[k]], wrow.at[q], wsend.at[k], wrecv.at[k], peer)
                for k, peer in enumerate(p_peers)
            ]
            scales.append(pltpu.make_async_copy(WS.at[q], wrow.at[q], local.at[2]))
            for copy in scales:
                copy.start()
        if j == CHUNKS - 2:
            for copy in later + loads[1:]:
                copy.wait()
            reload = pltpu.make_async_copy(gbuf, SG, local.at[3])
            reload.start()
            reload.wait()

            def through_down(i, carry):
                at = pl.ds(pl.multiple_of(i * half, 16), half)
                gw[at, :] = lax.dot_general(
                    SG[at, :], WD[...], (((1,), (1,)), ((), ())), preferred_element_type=f32
                )
                return carry

            lax.fori_loop(0, 2, through_down, 0)
    for j in range(CHUNKS - 1):
        cols = columns(width, j)
        for copy in sent[j]:
            copy.wait()

        def project(i, carry):
            at = pl.ds(pl.multiple_of(i * half, 16), half)
            part = buffer[at, cols]
            one = jnp.dot(part, WG[cols, :], preferred_element_type=f32)
            two = jnp.dot(part, WU[cols, :], preferred_element_type=f32)
            gp[at, :] = one if j == 0 else gp[at, :] + one
            up[at, :] = two if j == 0 else up[at, :] + two
            return carry

        lax.fori_loop(0, 2, project, 0)
    for copy in scales:
        copy.wait()
    diagonal = lax.broadcasted_iota(jnp.int32, (packed, packed), 0) == lax.broadcasted_iota(
        jnp.int32, (packed, packed), 1
    )
    dgr[...] = jnp.zeros_like(dgr)
    cols = columns(width, CHUNKS - 1)
    inner = dup.shape[-1]
    hidden, dgp = SG.at[:, pl.ds(0, inner)], SG.at[:, pl.ds(inner, inner)]

    def saves_of(p):
        at = pl.ds(pl.multiple_of(p * packed, 16), packed)
        pairs = ((buffer, buffer_out), (hidden, hidden_out), (dgp, dgp_out), (dup, dup_out))
        return [
            pltpu.make_async_copy(src.at[at], dst.at[at], saved.at[i, p])
            for i, (src, dst) in enumerate(pairs)
        ]

    def expert_rows(p):
        at = pl.ds(pl.multiple_of(p * packed, 16), packed)
        part = buffer[at, cols]
        gate_pre = gp[at, :] + jnp.dot(part, WG[cols, :], preferred_element_type=f32)
        up_pre = up[at, :] + jnp.dot(part, WU[cols, :], preferred_element_type=f32)
        back = gw[at, :]
        scale = jnp.sum(
            jnp.where(diagonal, wrow[p, 0:1, pl.ds(0, packed)], 0.0), axis=1, keepdims=True
        )
        sigmoid = jax.nn.sigmoid(gate_pre)
        silu = gate_pre * sigmoid
        low = (silu * up_pre).astype(bf16)
        hidden[at, :] = low
        dgate = jnp.sum(back * low.astype(f32), axis=-1, keepdims=True)
        line = jnp.sum(jnp.where(diagonal, dgate, 0.0), axis=0, keepdims=True)
        dgr[p, :, pl.ds(0, packed)] = jnp.broadcast_to(line, (8, packed))
        dhid = scale * back
        dgp[at, :] = (dhid * up_pre * sigmoid * (1.0 + gate_pre * (1.0 - sigmoid))).astype(bf16)
        dup[at, :] = (dhid * silu).astype(bf16)
        for copy in saves_of(p):
            copy.start()

    sent[CHUNKS - 1][Q - 1].wait()
    expert_rows(q)

    def arrival(k, carry):
        p = lax.rem(q + Q - 1 - k, Q)
        at = pl.ds(pl.multiple_of(p * packed, 16), packed)
        came = (p // F, c, lax.rem(p, F))
        remote(
            SL.at[at, cols], buffer.at[at, cols], bsend.at[CHUNKS - 1, k], brecv.at[CHUNKS - 1, k], came
        ).wait_recv()
        expert_rows(p)
        return carry

    lax.fori_loop(0, Q - 1, arrival, 0)
    for copy in sent[CHUNKS - 1][: Q - 1]:
        copy.wait_send()
    for line in chunks + [row]:
        for copy in line:
            copy.wait_send()

    @pl.when(c < C - 1)
    def _():
        def body(t, carry):
            rightward(t).wait_send()
            return carry

        lax.fori_loop(c + 1, C, body, 0)

    @pl.when(c > 0)
    def _():
        def body(t, carry):
            leftward(t).wait_send()
            return carry

        lax.fori_loop(0, c, body, 0)

    for p in range(Q):
        for copy in saves_of(p):
            copy.wait()


def dispatch(packed, out_part, G, tokens, pack, gain, chosen, kept, select, w_gate, w_up, w_down):
    S, C, F = sizes()
    Q = S * F
    rows, width = tokens.shape
    inner = w_gate.shape[-1]
    lanes = round_up(packed, 128)
    wide = chosen.shape[1]
    V = pltpu.VMEM
    sds = jax.ShapeDtypeStruct
    vm = pl.BlockSpec(memory_space=pltpu.VMEM)
    slots = Q * packed
    return pl.pallas_call(
        functools.partial(dispatch_kernel, packed),
        out_shape=[
            sds((slots, width), bf16),
            sds((slots, width), bf16),
            sds((Q, 8, lanes), f32),
            sds((rows, width), f32),
            sds((rows, width), bf16),
            sds((rows, wide), f32),
            sds((slots, inner), bf16),
            sds((slots, inner), bf16),
            sds((slots, inner), bf16),
            sds((Q, 8, lanes), f32),
        ],
        in_specs=[ANY, ANY] + [vm] * 6 + [ANY] * 3,
        out_specs=[ANY, ANY, vm, vm, vm, vm, ANY, ANY, ANY, vm],
        scratch_shapes=[
            V((C, rows, width), bf16),
            V((C + 1, rows, width), bf16),
            V((C * rows, width), bf16),
            V((slots, width), bf16),
            V((C * rows, wide), f32),
            V((Q, 8, lanes), f32),
            V((C * rows, width), bf16),
            V((slots, width), bf16),
            V((slots, width), bf16),
            V((width, inner), bf16), V((width, inner), bf16), V((inner, width), bf16),
            V((slots, inner), f32), V((slots, inner), f32), V((slots, inner), f32),
            V((slots, inner), bf16),
            DMA((4 + CHUNKS,)),
            DMA((4,)),
            DMA((4, Q)),
            DMA((2, C)), DMA((2, C)),
            DMA((Q - 1,)), DMA((Q - 1,)),
            DMA((CHUNKS, C - 1)), DMA((CHUNKS, C - 1)),
            DMA((C - 1,)), DMA((C - 1,)),
            DMA((CHUNKS, Q - 1)), DMA((CHUNKS, Q - 1)),
            DMA((Q - 1,)), DMA((Q - 1,)),
        ],
        name="dispatch_rows",
        compiler_params=params(3, 62 * 2**20),
    )(out_part, G, tokens, pack, gain, chosen, kept, select, w_gate, w_up, w_down)


def return_kernel(
    packed, dgr, select, select_t, gates, pack, h1, gain, cot, wrow, hidden, dgp, dup,
    w_gate, w_up, w_down,
    DA, y_part, dh1, dlog, gnorm,
    RD, YB, PART, RX, DG, DGP, RG, DL, din, wy, WG, WU, WD, SC,
    local, load, dsend, drecv, gsend, grecv, ysend, yrecv, xsend, xrecv, msend, mrecv, *asems,
):
    S, C, F = sizes()
    s, c, f = place()
    Q = S * F
    q = s * F + f
    rows, width = h1.shape
    z_peers = z_neighbours()
    p_at, p_peers = plane_neighbours()
    loads = []
    for j in range(CHUNKS):
        cols = columns(width, j)
        loads.append(
            [
                pltpu.make_async_copy(w_gate.at[0, cols], WG.at[cols], load.at[0, j]),
                pltpu.make_async_copy(w_up.at[0, cols], WU.at[cols], load.at[1, j]),
            ]
        )
    load_down = pltpu.make_async_copy(w_down.at[0], WD, load.at[2, 0])
    for line in loads:
        for copy in line:
            copy.start()
    load_down.start()
    greet_all(z_peers + p_peers)
    half = halves(Q * packed)
    mine = pl.ds(pl.multiple_of(q * packed, 16), packed)
    theirs = [pl.ds(pl.multiple_of(at * packed, 16), packed) for at in p_at]
    small = [
        remote(dgr.at[p_at[k]], DG.at[q], gsend.at[k], grecv.at[k], peer)
        for k, peer in enumerate(p_peers)
    ]
    small.append(pltpu.make_async_copy(dgr.at[q], DG.at[q], local.at[0]))
    for copy in small:
        copy.start()
    chunks = []
    for j in range(CHUNKS):
        cols = columns(width, j)
        for copy in loads[j]:
            copy.wait()

        def expert_in(i, carry):
            at = pl.ds(pl.multiple_of(i * half, 16), half)
            across = (((1,), (1,)), ((), ()))
            total = lax.dot_general(dgp[at, :], WG[cols, :], across, preferred_element_type=f32)
            total += lax.dot_general(dup[at, :], WU[cols, :], across, preferred_element_type=f32)
            din[at, cols] = total.astype(bf16)
            return carry

        lax.fori_loop(0, 2, expert_in, 0)
        line = [
            remote(din.at[theirs[k], cols], RD.at[mine, cols], dsend.at[j, k], drecv.at[j, k], peer)
            for k, peer in enumerate(p_peers)
        ]
        line.append(pltpu.make_async_copy(din.at[mine, cols], RD.at[mine, cols], local.at[2 + j]))
        for copy in line:
            copy.start()
        chunks.append(line)
    load_down.wait()
    diagonal = lax.broadcasted_iota(jnp.int32, (packed, packed), 0) == lax.broadcasted_iota(
        jnp.int32, (packed, packed), 1
    )

    for p in range(Q):
        scale = jnp.sum(
            jnp.where(diagonal, wrow[p, 0:1, pl.ds(0, packed)], 0.0), axis=1, keepdims=True
        )
        SC[p * packed : (p + 1) * packed, :] = jnp.broadcast_to(scale, (packed, HEAD_DIM))

    def expert_out(i, carry):
        at = pl.ds(pl.multiple_of(i * half, 16), half)

        def body(j, carry):
            cols = pl.ds(pl.multiple_of(j * 512, 512), 512)
            y = jnp.dot(hidden[at, :], WD[:, cols], preferred_element_type=f32)
            wy[at, cols] = (SC[at, 0:1] * y).astype(bf16)
            return carry

        return lax.fori_loop(0, width // 512, body, carry)

    lax.fori_loop(0, 2, expert_out, 0)
    sums = []
    for j in range(CHUNKS):
        cols = columns(width, j)
        for copy in chunks[j]:
            copy.wait()

        def combine(i, carry):
            lanes = pl.ds(pl.multiple_of(j * (width // CHUNKS) + i * 256, 256), 256)
            PART[:, lanes] = jnp.dot(
                select_t[...], RD[:, lanes], preferred_element_type=f32
            ).astype(bf16)
            return carry

        lax.fori_loop(0, width // CHUNKS // 256, combine, 0)
        for k, peer in enumerate(z_peers):
            src = PART.at[pl.ds(pl.multiple_of(peer[1] * rows, 16), rows), cols]
            sums.append(remote(src, RX.at[k, :, cols], xsend.at[j, k], xrecv.at[j, k], peer))
            sums[-1].start()
    ys = [
        remote(wy.at[theirs[k]], YB.at[mine], ysend.at[k], yrecv.at[k], peer)
        for k, peer in enumerate(p_peers)
    ]
    ys.append(pltpu.make_async_copy(wy.at[mine], YB.at[mine], local.at[1]))
    for copy in ys:
        copy.start()
    for copy in small:
        copy.wait()
    wide = gates.shape[1]
    place_of = lax.broadcasted_iota(jnp.int32, (Q, wide), 0)
    expert = (place_of // F * C + c) * F + lax.rem(place_of, F)
    spread = (lax.broadcasted_iota(jnp.int32, (Q, wide), 1) == expert).astype(f32)

    for p in range(Q):
        at = pl.ds(p * packed, packed)
        line = jnp.dot(
            three_parts(DG[p, 0:1, pl.ds(0, packed)]), select[at, :], preferred_element_type=f32
        )
        DL[pl.ds(p, 1), :] = jnp.sum(line, axis=0, keepdims=True)
    DGP[...] = lax.dot_general(
        DL[...], spread, (((0,), (0,)), ((), ())),
        precision=lax.Precision.HIGHEST, preferred_element_type=f32,
    ).reshape(DGP.shape)
    more = []
    for k, peer in enumerate(z_peers):
        more.append(remote(DGP.at[peer[1]], RG.at[k], msend.at[k], mrecv.at[k], peer))
        more[-1].start()
    for copy in more:
        copy.wait()
    total = DGP[c]
    for k in range(C - 1):
        total = total + RG[k]
    dlogits = gates[...] * (total - jnp.sum(gates[...] * total, axis=-1, keepdims=True))
    dlog[...] = dlogits.astype(bf16)
    gnorm[...] = jnp.zeros_like(gnorm)
    for copy in sums:
        copy.wait()

    def head_rows(i, carry):
        part = pl.ds(i * 32, 32)
        mine_part = pl.ds(pl.multiple_of(c * rows + i * 32, 16), 32)
        dxm = PART[mine_part, :].astype(f32)
        for k in range(C - 1):
            dxm = dxm + RX[k, part, :].astype(f32)
        dxm = dxm + lax.dot_general(
            dlog[part, :], pack[:, pl.ds(0, wide)], (((1,), (1,)), ((), ())), preferred_element_type=f32
        )
        unit, factor = rms_unit(h1[part, :])
        gnorm[...] += jnp.sum(dxm * unit, axis=0, keepdims=True)
        grad = cot[part, :].astype(f32) + norm_backward(dxm, unit, factor, gain[...])
        dh1[part, :] = grad
        RX[0, part, :] = grad.astype(bf16)
        return carry

    lax.fori_loop(0, rows // 32, head_rows, 0)
    keep = pltpu.make_async_copy(RX.at[0], DA.at[c], local.at[2 + CHUNKS])
    keep.start()
    line = Line(RX.at[0], lambda at: DA.at[at], *asems)
    line.start()
    for h in range(1, C - 1):
        line.hop(h)
    for copy in ys:
        copy.wait()

    def combine_y(i, carry):
        lanes = pl.ds(pl.multiple_of(i * 256, 256), 256)
        y_part[:, lanes] = jnp.dot(
            select_t[...], YB[:, lanes], preferred_element_type=f32
        ).astype(bf16)
        return carry

    lax.fori_loop(0, width // 256, combine_y, 0)
    line.hop(C - 1)
    line.finish()
    keep.wait()


def give_back(
    packed, dgr, select, select_t, gates, pack, h1, gain, cot, wrow, hidden, dgp, dup, w_gate, w_up, w_down
):
    S, C, F = sizes()
    Q = S * F
    rows, width = h1.shape
    wide = gates.shape[1]
    inner = w_gate.shape[-1]
    V = pltpu.VMEM
    sds = jax.ShapeDtypeStruct
    vm = pl.BlockSpec(memory_space=pltpu.VMEM)
    return pl.pallas_call(
        functools.partial(return_kernel, packed),
        out_shape=[
            sds((C, rows, width), bf16),
            sds((C * rows, width), bf16),
            sds((rows, width), f32),
            sds((rows, wide), bf16),
            sds((1, width), f32),
        ],
        in_specs=[vm] * 12 + [ANY] * 3,
        out_specs=[ANY] + [vm] * 4,
        scratch_shapes=[
            V((Q * packed, width), bf16),
            V((Q * packed, width), bf16),
            V((C * rows, width), bf16),
            V((C - 1, rows, width), bf16),
            V(dgr.shape, f32),
            V((C, rows, wide), f32),
            V((C - 1, rows, wide), f32),
            V((Q, C * rows), f32),
            V((Q * packed, width), bf16),
            V((Q * packed, width), bf16),
            V((width, inner), bf16), V((width, inner), bf16), V((inner, width), bf16),
            V((Q * packed, HEAD_DIM), f32),
            DMA((3 + CHUNKS,)),
            DMA((3, CHUNKS)),
            DMA((CHUNKS, Q - 1)), DMA((CHUNKS, Q - 1)),
            DMA((Q - 1,)), DMA((Q - 1,)),
            DMA((Q - 1,)), DMA((Q - 1,)),
            DMA((CHUNKS, C - 1)), DMA((CHUNKS, C - 1)),
            DMA((C - 1,)), DMA((C - 1,)),
        ]
        + line_sems(C),
        name="return_grads",
        compiler_params=params(5, 62 * 2**20),
    )(dgr, select, select_t, gates, pack, h1, gain, cot, wrow, hidden, dgp, dup, w_gate, w_up, w_down)


def backward_kernel(
    block, da, w, wo, q, k, v, xnt, x, cosine, sine, pos_col, pos_row, gains, go, sp, yp,
    dxn, OH, Q3, S3, T3, YP,
    kr, dkr, dv, acc, DQ, head_grad,
    GQ, Q1, Q2, QS, o_own, o_in, s_own, s_in, s_plane, s_sum, T, t_in, t_plane, t_sum,
    local, qlocal, csend, crecv, fsend, frecv, zsend, zrecv, qcs, qcr, qfs, qfr, qzs, qzr, ysend, yrecv,
):
    S, C, F = sizes()
    s, c, f = place()
    step = pl.program_id(0)
    units = GQ.shape[0]
    pairs = units - 1
    length, width = x.shape
    wide = 2 * HEAD_DIM
    z_peers = z_neighbours()
    f_peers = [(s, c, lax.rem(f + k, F)) for k in range(1, F)]
    sibling = (1 - s, c, f)
    cols = pl.ds(pl.multiple_of(step * wide, wide), wide)

    o_first = remote(go.at[1 - s], o_in, csend.at[0], crecv.at[0], sibling)
    t_first = remote(T, t_in, csend.at[2], crecv.at[2], sibling)
    o_load = pltpu.make_async_copy(go.at[s], o_own, local.at[0])
    o_save = pltpu.make_async_copy(o_own, OH, local.at[2])
    s_first = remote(sp.at[1 - s], s_in, csend.at[1], crecv.at[1], sibling)
    s_load = pltpu.make_async_copy(sp.at[s], s_own, local.at[1])
    f_at = list(enumerate(f_peers))
    z_at = list(enumerate(z_peers))
    s_second = [remote(s_own.at[:, p[2]], s_plane.at[k], fsend.at[1, k], frecv.at[1, k], p) for k, p in f_at]
    t_second = [remote(T, t_plane.at[k], fsend.at[2, k], frecv.at[2, k], p) for k, p in f_at]
    s_third = [remote(s_sum.at[p[1]], S3.at[c], zsend.at[1, k], zrecv.at[1, k], p) for k, p in z_at]
    s_third.append(pltpu.make_async_copy(s_sum.at[c], S3.at[c], local.at[3]))
    t_third = [remote(t_sum, T3.at[c], zsend.at[2, k], zrecv.at[2, k], p) for k, p in z_at]
    t_third.append(pltpu.make_async_copy(t_sum, T3.at[c], local.at[4]))
    y_copies = [remote(yp.at[p[1]], YP.at[c], ysend.at[k], yrecv.at[k], p) for k, p in z_at]
    y_copies.append(pltpu.make_async_copy(yp.at[c], YP.at[c], local.at[5]))

    def q_first(u):
        return remote(GQ.at[u, 1 - s], Q1.at[u], qcs.at[u], qcr.at[u], sibling)

    def q_second(u):
        return [remote(GQ.at[u, s, :, p[2]], Q2.at[u, k], qfs.at[u, k], qfr.at[u, k], p) for k, p in f_at]

    def q_third(u):
        copies = [
            remote(QS.at[u, p[1]], Q3.at[u, c], qzs.at[u, k], qzr.at[u, k], p) for k, p in z_at
        ]
        copies.append(pltpu.make_async_copy(QS.at[u, c], Q3.at[u, c], qlocal.at[u]))
        return copies

    def to_plane(u):
        q_first(u).wait()

        def body(i, carry):
            at = (u, s, i // F, lax.rem(i, F))
            GQ[at] = (GQ[at].astype(f32) + Q1[u, i // F, lax.rem(i, F)].astype(f32)).astype(bf16)
            return carry

        lax.fori_loop(0, C * F, body, 0)
        for copy in q_second(u):
            copy.start()

    def to_ctx(u):
        for copy in q_second(u):
            copy.wait()

        def body(i, carry):
            total = GQ[u, s, i, f].astype(f32)
            for k in range(F - 1):
                total = total + Q2[u, k, i].astype(f32)
            QS[u, i] = total.astype(bf16)
            return carry

        lax.fori_loop(0, C, body, 0)
        for copy in q_third(u):
            copy.start()

    @pl.when(step == 0)
    def _():
        greet_all(z_peers + f_peers + [sibling])
        for copy in [s_first, s_load, o_first, o_load] + y_copies:
            copy.start()
        unit, _ = rms_unit(k[...])
        kr[...] = half_turn(unit * gains[1:2, :], cosine[...], sine[...]).astype(bf16)
        dkr[...] = jnp.zeros_like(dkr)
        dv[...] = jnp.zeros_like(dv)
        head_grad[...] = jnp.zeros_like(head_grad)
        acc[...] = jnp.zeros_like(acc)

    @pl.when(step >= 1)
    def _():
        to_plane(step - 1)

    @pl.when(step == 1)
    def _():
        o_first.wait()
        o_load.wait()

        def o_body(i, carry):
            o_own[i] = (o_own[i].astype(f32) + o_in[i].astype(f32)).astype(bf16)
            return carry

        lax.fori_loop(0, F, o_body, 0)
        o_save.start()
        s_first.wait()
        s_load.wait()

        def s_body(i, carry):
            at = (i // F, lax.rem(i, F))
            s_own[at] = (s_own[at].astype(f32) + s_in[at].astype(f32)).astype(bf16)
            return carry

        lax.fori_loop(0, C * F, s_body, 0)
        for copy in s_second:
            copy.start()

    @pl.when(step >= 2)
    def _():
        to_ctx(step - 2)

    @pl.when(step == 2)
    def _():
        for copy in s_second:
            copy.wait()

        def s_body(i, carry):
            total = s_own[i, f].astype(f32)
            for k in range(F - 1):
                total = total + s_plane[k, i].astype(f32)
            s_sum[i] = total.astype(bf16)
            return carry

        lax.fori_loop(0, C, s_body, 0)
        for copy in s_third:
            copy.start()

    @pl.when(step < pairs)
    def _():
        dm = lax.dot_general(
            da[...], wo[cols, :], (((1,), (1,)), ((), ())), preferred_element_type=f32
        ).astype(bf16)
        for half in range(2):
            lanes = slice(half * HEAD_DIM, (half + 1) * HEAD_DIM)
            for part in range(length // block):
                rows = slice(part * block, (part + 1) * block)
                unit, factor = rms_unit(q[rows, lanes])
                cos, sin = cosine[rows, :], sine[rows, :]
                qr = half_turn(unit * gains[0:1, :], cos, sin).astype(bf16)
                keys = kr[...]
                probs = score_block(qr, keys, pos_col[rows, :], pos_row[...])
                dmh = dm[rows, lanes]
                dprobs = lax.dot_general(
                    dmh, v[...], (((1,), (1,)), ((), ())), preferred_element_type=f32
                )
                delta = jnp.sum(probs * dprobs, axis=-1, keepdims=True)
                dscores = (probs * (dprobs - delta)).astype(bf16)
                dqr = jnp.dot(dscores, keys, preferred_element_type=f32) * (HEAD_DIM**-0.5)
                rows_in = (((0,), (0,)), ((), ()))
                dkr[...] += lax.dot_general(dscores, qr, rows_in, preferred_element_type=f32) * (
                    HEAD_DIM**-0.5
                )
                dv[...] += lax.dot_general(
                    probs.astype(bf16), dmh, rows_in, preferred_element_type=f32
                )
                dqs = half_turn(dqr, cos, -sin)
                head_grad[0:1, :] += jnp.sum(dqs * unit, axis=0, keepdims=True)
                DQ[rows, lanes] = norm_backward(dqs, unit, factor, gains[0:1, :]).astype(bf16)

    @pl.when(step == pairs)
    def _():
        unit, factor = rms_unit(k[...])
        dks = half_turn(dkr[...], cosine[...], -sine[...])
        head_grad[1:2, :] += jnp.sum(dks * unit, axis=0, keepdims=True)
        DQ[:, :HEAD_DIM] = norm_backward(dks, unit, factor, gains[1:2, :]).astype(bf16)
        DQ[:, HEAD_DIM:] = dv[...].astype(bf16)

    def weight_rows(i, carry):
        part = F * GQ.shape[4]
        rows = pl.ds(pl.multiple_of(i * part, 16), part)
        piece = jnp.dot(xnt[rows, :], DQ[...], preferred_element_type=f32)
        GQ[step, i // C, lax.rem(i, C)] = piece.astype(bf16).reshape(GQ.shape[3:])
        return carry

    lax.fori_loop(0, S * C, weight_rows, 0)
    q_first(step).start()
    for j in range(4):
        part = pl.ds(j * (width // 4), width // 4)
        acc[:, part] += lax.dot_general(
            DQ[...], w[part, cols], (((1,), (1,)), ((), ())), preferred_element_type=f32
        )

    @pl.when(step == pairs)
    def _():
        to_ctx(pairs - 1)
        to_plane(pairs)
        rows_of = width // HEAD_DIM
        total = jnp.zeros((1, width), f32)

        def finish(i, total):
            rows = pl.ds(i * 64, 64)
            unit, _ = rms_unit(x[rows, :].astype(f32))
            term = acc[rows, :]
            dxn[rows, :] = term.astype(bf16)
            return total + jnp.sum(term * unit, axis=0, keepdims=True)

        total = lax.fori_loop(0, length // 64, finish, total)
        for r in range(rows_of):
            T[r : r + 1, :] = total[:, r * HEAD_DIM : (r + 1) * HEAD_DIM]
        T[rows_of:, :] = head_grad[...]
        t_first.start()
        t_first.wait()
        T[...] = T[...] + t_in[...]
        for copy in t_second:
            copy.start()
        to_ctx(pairs)
        for copy in t_second:
            copy.wait()
        order = []
        for g in range(F):
            term = jnp.zeros_like(T)
            for k in range(F - 1):
                came = lax.rem(f + F - (k + 1), F)
                term = term + jnp.where(came == g, t_plane[k], 0.0)
            order.append(term + jnp.where(f == g, T[...], 0.0))
        total = order[0]
        for term in order[1:]:
            total = total + term
        t_sum[...] = total
        for copy in t_third:
            copy.start()
        for copy in s_third + y_copies + [o_save] + t_third:
            copy.wait()
        for u in range(units):
            for copy in q_third(u):
                copy.wait()


def backward(da, w, wo, q, k, v, xnt, x, cosine, sine, pos_col, pos_row, gains, go, sp, yp):
    S, C, F = sizes()
    length, width = x.shape
    head_width = wo.shape[0]
    pairs = head_width // (2 * HEAD_DIM)
    units = pairs + 1
    shard = sp.shape[3]
    block = min(length, 512)
    wide = 2 * HEAD_DIM
    once = pl.Buffered(buffer_count=1)
    whole = lambda array: pl.BlockSpec(array.shape, lambda i: (0, 0), pipeline_mode=once)
    sds = jax.ShapeDtypeStruct
    V = pltpu.VMEM
    q_block, o_block, s_block = (shard, wide), go.shape[2:], sp.shape[3:]
    t_block = (width // HEAD_DIM + 8, HEAD_DIM)
    return pl.pallas_call(
        functools.partial(backward_kernel, block),
        out_shape=[
            sds((length, width), bf16),
            sds((F,) + o_block, bf16),
            sds((units, C, shard, wide), bf16),
            sds((C,) + s_block, bf16),
            sds((C,) + t_block, f32),
            sds(yp.shape, bf16),
        ],
        grid=(units,),
        in_specs=[whole(da), whole(w), whole(wo)]
        + [pl.BlockSpec((length, wide), lambda i: (0, jnp.minimum(i, pairs - 1)))]
        + [whole(array) for array in (k, v, xnt, x, cosine, sine, pos_col, pos_row, gains)]
        + [ANY] * 3,
        out_specs=[pl.BlockSpec((length, width), lambda i: (0, 0), pipeline_mode=once)] + [ANY] * 5,
        scratch_shapes=[
            V((length, HEAD_DIM), bf16), V((length, HEAD_DIM), f32), V((length, HEAD_DIM), f32),
            V((length, width), f32), V((length, wide), bf16), V((8, HEAD_DIM), f32),
            V((units, S, C, F) + q_block, bf16), V((units, C, F) + q_block, bf16),
            V((units, F - 1, C) + q_block, bf16), V((units, C) + q_block, bf16),
            V((F,) + o_block, bf16), V((F,) + o_block, bf16),
            V((C, F) + s_block, bf16), V((C, F) + s_block, bf16), V((F - 1, C) + s_block, bf16), V((C,) + s_block, bf16),
            V(t_block, f32), V(t_block, f32), V((F - 1,) + t_block, f32), V(t_block, f32),
            DMA((6,)), DMA((units,)),
            DMA((3,)), DMA((3,)), DMA((3, F - 1)), DMA((3, F - 1)), DMA((3, C - 1)), DMA((3, C - 1)),
            DMA((units,)), DMA((units,)), DMA((units, F - 1)), DMA((units, F - 1)),
            DMA((units, C - 1)), DMA((units, C - 1)), DMA((C - 1,)), DMA((C - 1,)),
        ],
        name="attention_backward",
        compiler_params=params(7, 60 * 2**20),
    )(da, w, wo, q, k, v, xnt, x, cosine, sine, pos_col, pos_row, gains, go, sp, yp)


def dot(left, right):
    return jnp.dot(left, right, preferred_element_type=f32)


def contract_rows(left, right):
    return lax.dot_general(left, right, (((0,), (0,)), ((), ())), preferred_element_type=f32)


def times_transpose(left, right):
    return lax.dot_general(left, right, (((1,), (1,)), ((), ())), preferred_element_type=f32)


def on_device(
    tokens,
    stretch_order,
    expert_ids,
    slot_index,
    norm_attn,
    head_gains,
    w_query,
    w_key,
    w_value,
    w_out,
    norm_moe,
    w_router,
    w_gate,
    w_up,
    w_down,
    cotangent,
):
    S, C, F = sizes()
    Q = S * F
    seq_at, ctx_at, fsdp_at = place()
    rows, width = tokens.shape[1:]
    length = C * rows
    experts = w_router.shape[1]
    capacity = rows * TOP // (Q * C) + 1
    packed = round_up(C * capacity, 16)
    lanes = round_up(packed, 128)
    head_width = w_query.shape[1] // C
    shard = w_router.shape[0]
    pack_width = round_up(experts + 2, 128)
    pack = jnp.concatenate(
        [
            w_router,
            norm_attn[:, None],
            norm_moe[:, None],
            jnp.zeros((shard, pack_width - experts - 2), bf16),
        ],
        axis=1,
    )
    gains = head_gains.astype(f32)
    (
        X, W, WO, PK, _, G, out_part, q, k, v, mixed, xnt, row_gains,
        cosine, sine, pos_col, pos_row, select, select_t, chosen, kept_map,
    ) = front(
        capacity, packed, experts, stretch_order, expert_ids[0], slot_index[0],
        tokens[0], w_query, w_key, w_value, w_out, pack, cotangent[0], gains,
    )
    W = W.reshape(width, head_width + 2 * HEAD_DIM)
    WO = WO.reshape(head_width, width)
    PK = PK.reshape(width, pack_width)
    gain_attn, gain_moe = row_gains[0:1], row_gains[1:2]
    buffer, slot_grad, slot_weight, h1, xm, gates, hidden, dgp, dup, slot_dgate = dispatch(
        packed, out_part.reshape(C, rows, width), G.reshape(length, width), tokens[0], PK, gain_moe,
        chosen, kept_map, select, w_gate, w_up, w_down,
    )
    DA, y_part, dh1, dlogits, grad_norm_moe = give_back(
        packed, slot_dgate, select, select_t, gates, PK, h1, gain_moe, cotangent[0],
        slot_weight, hidden, dgp, dup, w_gate, w_up, w_down,
    )
    scale = slot_weight[:, 0, :packed].reshape(Q * packed, 1)
    dy = (scale * slot_grad.astype(f32)).astype(bf16)
    grad_router = contract_rows(xm, dlogits[:, :experts])
    DA = DA.reshape(length, width)
    grad_out_part = contract_rows(mixed, DA).astype(bf16)
    small = jnp.concatenate(
        [grad_router, grad_norm_moe.T, jnp.zeros((width, pack_width - experts - 1), f32)], axis=1
    )
    out_parts = grad_out_part.reshape(S, F, head_width // Q, width)

    def part_of(parts, at):
        return lax.dynamic_index_in_dim(parts, at, 0, keepdims=False)

    dxn_part, out_half, q_sums, small_sums, tiny_sums, y_parts = backward(
        DA, W, WO, q, k, v, xnt, X, cosine, sine, pos_col, pos_row, gains,
        out_parts,
        small.astype(bf16).reshape(S, C, F, shard, pack_width),
        y_part.reshape(C, rows, width),
    )
    dxn_part = dxn_part.reshape(C, rows, width)

    def summed_over(axis, at, count, parts):
        total = part_of(parts, at).astype(f32)
        for k_at in range(1, count):
            shift = [(i, (i + k_at) % count) for i in range(count)]
            total += lax.ppermute(part_of(parts, lax.rem(at + k_at, count)), axis, shift).astype(f32)
        return total

    dxn = summed_over("ctx", ctx_at, C, dxn_part)
    out_sum = out_half
    bit = F // 2
    while bit:
        mine = lax.rem(fsdp_at // bit, 2)
        parts = out_sum.reshape((2, bit) + out_sum.shape[1:])
        came = lax.ppermute(part_of(parts, 1 - mine), "fsdp", [(i, i ^ bit) for i in range(F)])
        out_sum = (part_of(parts, mine).astype(f32) + came.astype(f32)).astype(bf16)
        if bit == F // 2:
            out_sum, hidden, dy = lax.optimization_barrier((out_sum, hidden, dy))
        bit //= 2
    out_sum = out_sum[0]
    turn = [(i * C + j, j * S + i) for i in range(S) for j in range(C)]
    o_sum = lax.ppermute(out_sum, ("seq", "ctx"), turn)
    grad_wgate = contract_rows(buffer, dgp)
    grad_wup = contract_rows(buffer, dup)
    grad_wdown = contract_rows(hidden, dy)
    layer_out = (h1 + jnp.sum(y_parts.astype(f32), axis=0)).astype(bf16)
    unit, factor = rms_unit(tokens[0].astype(f32))
    grad_tokens = (dh1 + norm_backward(dxn, unit, factor, gain_attn)).astype(bf16)
    grad_query = (
        q_sums[:-1].transpose(2, 1, 0, 3).reshape(shard, C * head_width).astype(f32)
    )

    def key_columns(block):
        pieces = block.astype(f32).reshape(KEY_VALUE_HEADS, C // KEY_VALUE_HEADS, shard, HEAD_DIM).sum(axis=1)
        return pieces.transpose(1, 0, 2).reshape(shard, KEY_VALUE_HEADS * HEAD_DIM)

    grad_key = key_columns(q_sums[-1, :, :, :HEAD_DIM])
    grad_value = key_columns(q_sums[-1, :, :, HEAD_DIM:])
    small_sum = jnp.sum(small_sums.astype(f32), axis=0)
    tiny_sum = jnp.sum(tiny_sums, axis=0)
    tiny_rows = width // HEAD_DIM
    device = (seq_at * C + ctx_at) * F + fsdp_at
    grad_norm_attn = lax.dynamic_slice_in_dim(
        tiny_sum[:tiny_rows].reshape(width), device * shard, shard
    )
    return (
        layer_out[None],
        grad_tokens[None],
        grad_norm_attn,
        tiny_sum[tiny_rows : tiny_rows + 2],
        grad_query,
        grad_key,
        grad_value,
        o_sum.astype(f32),
        small_sum[:, experts],
        small_sum[:, :experts],
        grad_wgate[None],
        grad_wup[None],
        grad_wdown[None],
    )


def solution(mesh):
    rows = P(("seq", "fsdp"), "ctx", None)
    vector = P(AXES)
    matrix = P(AXES, None)
    cube = P(AXES, None, None)
    return jax.shard_map(
        on_device,
        mesh=mesh,
        in_specs=(
            rows, P(), rows, rows, vector, P(), matrix, matrix, matrix, matrix,
            vector, matrix, cube, cube, cube, rows,
        ),
        out_specs=(
            rows, rows, vector, P(), matrix, matrix, matrix, matrix, vector, matrix,
            cube, cube, cube,
        ),
        check_vma=False,
    )
```

```python
import functools

import jax
import jax.numpy as jnp
import numpy as np
from jax import lax
from jax.experimental import pallas as pl
from jax.experimental.pallas import tpu as pltpu
from jax.sharding import PartitionSpec as P

QUERY_HEADS = 32
KEY_VALUE_HEADS = 4
HEAD_DIM = 128
TOP = 8
AXES = ("seq", "ctx", "fsdp")
MESH = pl.DeviceIdType.MESH
epsilon = 1e-06
rope_base = 1000000.0
VMEM_LIMIT = 56 * 2**20
f32 = jnp.float32
bf16 = jnp.bfloat16


def round_up(value, step):
    return (value + step - 1) // step * step


def place():
    return tuple(lax.axis_index(name) for name in AXES)


def sizes():
    return tuple(lax.axis_size(name) for name in AXES)


def signal(device):
    pl.semaphore_signal(
        pltpu.get_barrier_semaphore(), inc=1, device_id=device, device_id_type=MESH
    )


def remote(src, dst, send, recv, device):
    return pltpu.make_async_remote_copy(
        src_ref=src,
        dst_ref=dst,
        send_sem=send,
        recv_sem=recv,
        device_id=device,
        device_id_type=MESH,
    )


def params(cid, limit=VMEM_LIMIT):
    return pltpu.CompilerParams(
        collective_id=cid, has_side_effects=True, vmem_limit_bytes=limit
    )


ANY = pl.BlockSpec(memory_space=pl.ANY)
DMA = pltpu.SemaphoreType.DMA


def rms_unit(rows):
    factor = lax.rsqrt(jnp.mean(rows * rows, axis=-1, keepdims=True) + epsilon)
    return rows * factor, factor


def norm_backward(grad_scaled, normed, factor, gain):
    grad_normed = grad_scaled * gain
    inner = jnp.mean(grad_normed * normed, axis=-1, keepdims=True)
    return factor * (grad_normed - normed * inner)


def half_turn(rows, cosine, sine):
    return rows * cosine + pltpu.roll(rows, HEAD_DIM // 2, 1) * sine


def score_block(qr, kr, pos_col, pos_row):
    scores = lax.dot_general(
        qr, kr, (((1,), (1,)), ((), ())), preferred_element_type=f32
    ) * (HEAD_DIM**-0.5)
    scores = jnp.where(pos_col >= pos_row, scores, -jnp.inf)
    peak = jnp.max(scores, axis=-1, keepdims=True)
    weight = jnp.exp(scores - peak)
    return weight * (1.0 / jnp.sum(weight, axis=-1, keepdims=True))


def z_neighbours():
    _, C, _ = sizes()
    s, c, f = place()
    return [(s, lax.rem(c + k, C), f) for k in range(1, C)]


def plane_neighbours():
    S, _, F = sizes()
    s, c, f = place()
    Q = S * F
    at = [lax.rem(s * F + f + k, Q) for k in range(1, Q)]
    return at, [(q // F, c, lax.rem(q, F)) for q in at]


def greet_all(peers):
    for peer in peers:
        signal(peer)
    pl.semaphore_wait(pltpu.get_barrier_semaphore(), len(peers))


class Line:
    def __init__(self, own, block, rsend, rrecv, lsend, lrecv):
        s, self.c, f = place()
        self.C = lax.axis_size("ctx")
        self.own, self.block = own, block
        self.sems = (rsend, rrecv, lsend, lrecv)
        self.right = (s, lax.rem(self.c + 1, self.C), f)
        self.left = (s, lax.rem(self.c + self.C - 1, self.C), f)

    def copy(self, rightward, h):
        origin = self.c - h if rightward else self.c + h
        src = self.own if h == 0 else self.block(origin)
        send, recv = self.sems[:2] if rightward else self.sems[2:]
        return remote(
            src, self.block(origin), send.at[h], recv.at[h], self.right if rightward else self.left
        )

    def sends(self, rightward, h):
        if rightward:
            return jnp.logical_and(self.c >= h, self.c < self.C - 1)
        return jnp.logical_and(self.c + h < self.C, self.c > 0)

    def start(self):
        for way in (True, False):
            pl.when(self.sends(way, 0))(self.copy(way, 0).start)

    def hop(self, h):
        for way in (True, False):
            origin = self.c - h if way else self.c + h
            there = origin >= 0 if way else origin < self.C
            landed = remote(
                self.block(origin), self.block(origin),
                self.sems[0 if way else 2].at[h - 1], self.sems[1 if way else 3].at[h - 1],
                self.left if way else self.right,
            )
            pl.when(there)(landed.wait_recv)
            if h < self.C - 1:
                pl.when(self.sends(way, h))(self.copy(way, h).start)

    def finish(self):
        for way in (True, False):
            for h in range(self.C - 1):
                pl.when(self.sends(way, h))(self.copy(way, h).wait_send)


def line_sems(C):
    return [DMA((C - 1,)) for _ in range(4)]


def front_kernel(
    block, capacity, packed, experts,
    order, ids, slot_ids, tokens, wq, wk, wv, wo, router, norm_attn, norm_moe, cot, low_gains, frequency,
    X_out, W_out, WO_out, PK, SM, G, out, q, k_out, v, mixed, xnt, gain_attn, gain_moe, gains,
    cosine, sine, pos_col, pos_row, select, select_t, chosen, kept,
    X, W, WO, xn, kr, pack,
    local, save, zsend, zrecv, fsend, frecv, csend, crecv, wsend, wrecv,
    xrs, xrr, xls, xlr, grs, grr, gls, glr,
):
    S, C, F = sizes()
    s, c, f = place()
    Q = S * F
    rows, width = tokens.shape
    length = C * rows
    head_width = wq.shape[1] // C
    shard = wq.shape[0]
    wide = chosen.shape[1]
    z_peers = z_neighbours()
    f_peers = [(s, c, lax.rem(f + k, F)) for k in range(1, F)]
    sibling = (1 - s, c, f)
    pair = s * C + c
    out_dst = (lax.rem(pair, S), pair // S, f)
    pair_in = c * S + s
    out_src = (pair_in // C, lax.rem(pair_in, C), f)
    stays = jnp.logical_and(out_dst[0] == s, out_dst[1] == c)
    moves = jnp.logical_not(stays)
    greet = (
        jnp.where(stays, 1 - s, out_src[0]),
        jnp.where(stays, C - 1 - c, out_src[1]),
        f,
    )
    def as_column(line):
        size = line.shape[1]
        square = lax.broadcasted_iota(jnp.int32, (size, size), 0) == lax.broadcasted_iota(
            jnp.int32, (size, size), 1
        )
        return jnp.sum(jnp.where(square, line, 0.0), axis=1, keepdims=True)

    lane = lax.broadcasted_iota(jnp.int32, (rows, wide), 1).astype(f32)
    hits = jnp.zeros((rows, wide), f32)
    slot_map = jnp.full((rows, wide), -1.0, f32)
    for j in range(TOP):
        here = lane == as_column(ids[j : j + 1, :].astype(f32))
        slot = jnp.broadcast_to(as_column(slot_ids[j : j + 1, :].astype(f32)), (rows, wide))
        hits = jnp.where(here, 1.0, hits)
        slot_map = jnp.where(jnp.logical_and(here, slot < capacity), slot, slot_map)
    lane = lax.broadcasted_iota(jnp.int32, pack.shape, 1)
    own_lane = lax.broadcasted_iota(jnp.int32, (experts, pack.shape[1]), 0) == lax.broadcasted_iota(
        jnp.int32, (experts, pack.shape[1]), 1
    )
    packed_rows = lax.dot_general(
        router[...], own_lane.astype(bf16), (((0,), (0,)), ((), ())), preferred_element_type=f32
    )
    for i, line in enumerate((norm_attn, norm_moe)):
        packed_rows = jnp.where(lane == experts + i, as_column(line[...].astype(f32)), packed_rows)
    pack[...] = packed_rows.astype(bf16)
    gains[...] = low_gains[...].astype(f32)
    chosen[...] = hits
    kept[...] = (slot_map >= 0.0).astype(f32)
    SM[c] = slot_map
    greet_all(z_peers + f_peers + [sibling, greet])

    def pieces(target):
        kv = (target * KEY_VALUE_HEADS) // C
        q_cols = pl.ds(pl.multiple_of(target * head_width, 128), head_width)
        kv_cols = pl.ds(pl.multiple_of(kv * HEAD_DIM, 128), HEAD_DIM)
        mine = W.at[s, c, f]
        return [
            (wq.at[:, q_cols], mine.at[:, pl.ds(0, head_width)]),
            (wk.at[:, kv_cols], mine.at[:, pl.ds(head_width, HEAD_DIM)]),
            (wv.at[:, kv_cols], mine.at[:, pl.ds(head_width + HEAD_DIM, HEAD_DIM)]),
            (pack, PK.at[s, c, f]),
        ]

    def token_rows(at):
        return X.at[pl.ds(pl.multiple_of(at * rows, 16), rows)]

    own = [
        pltpu.make_async_copy(src, dst, local.at[i])
        for i, (src, dst) in enumerate(pieces(c) + [(tokens, token_rows(c)), (cot, G.at[c])])
    ]
    z_copies = [
        remote(src, dst, zsend.at[i, k], zrecv.at[i, k], peer)
        for k, peer in enumerate(z_peers)
        for i, (src, dst) in enumerate(pieces(peer[1]))
    ]
    slot_copies = [
        remote(SM.at[c], SM.at[c], zsend.at[4, k], zrecv.at[4, k], peer)
        for k, peer in enumerate(z_peers)
    ]
    x_line = Line(tokens, token_rows, xrs, xrr, xls, xlr)
    g_line = Line(cot, lambda at: G.at[at], grs, grr, gls, glr)
    out_copy = remote(wo, WO.at[out_dst[0], f], wsend.at[0], wrecv.at[0], out_dst)
    out_stay = pltpu.make_async_copy(wo, WO.at[s, f], wsend.at[1])
    for copy in own + z_copies + slot_copies:
        copy.start()
    x_line.start()
    pl.when(moves)(out_copy.start)
    pl.when(stays)(out_stay.start)

    where = lax.broadcasted_iota(jnp.int32, (1, length), 1)
    where_col = lax.broadcasted_iota(jnp.int32, (length, 1), 0)
    stretch_rows = rows // 2

    def position(at):
        total = jnp.zeros_like(at)
        for j in range(2 * C):
            base = order[j] * stretch_rows - j * stretch_rows
            total = jnp.where(at // stretch_rows == j, at + base, total)
        return total

    pos_row[...] = position(where)
    pos_col[...] = position(where_col)
    angles = pos_col[...].astype(f32) * frequency[...]
    cosine[...] = jnp.cos(angles)
    turned = jnp.sin(angles)
    sine[...] = jnp.where(
        lax.broadcasted_iota(jnp.int32, turned.shape, 1) < HEAD_DIM // 2, -turned, turned
    )

    for copy in own[:5] + z_copies:
        copy.wait()

    def weight_block(index, at):
        return (W.at[s, :, at], PK.at[s, :, at], WO.at[s, at])[index]

    f_copies = [
        [
            remote(weight_block(i, f), weight_block(i, f), fsend.at[i, k], frecv.at[i, k], peer)
            for k, peer in enumerate(f_peers)
        ]
        for i in range(3)
    ]

    def to_sibling(i, k):
        at = lax.rem(f + F - k, F)
        return remote(weight_block(i, at), weight_block(i, at), csend.at[i, k], crecv.at[i, k], sibling)

    c_copies = [[to_sibling(i, k) for k in range(F)] for i in range(3)]
    for i in range(2):
        for copy in f_copies[i] + c_copies[i][:1]:
            copy.start()
    x_line.hop(1)
    pl.when(moves)(out_copy.wait)
    pl.when(stays)(out_stay.wait)
    for copy in f_copies[2] + c_copies[2][:1]:
        copy.start()
    for h in range(2, C - 1):
        x_line.hop(h)
    g_line.start()
    for k in range(F - 1):
        for i in range(2):
            f_copies[i][k].wait_recv()
            c_copies[i][k + 1].start()
    for copy in slot_copies:
        copy.wait()
    at = lax.broadcasted_iota(jnp.int32, (wide, Q * packed), 1) // packed
    expert = (at // F * C + c) * F + lax.rem(at, F)
    spread = (lax.broadcasted_iota(jnp.int32, (wide, Q * packed), 0) == expert).astype(bf16)
    slot_rows = SM[...].reshape(length, wide).astype(bf16)
    by_token = jnp.dot(slot_rows, spread, preferred_element_type=f32)
    base = (lax.broadcasted_iota(jnp.int32, by_token.shape, 0) // rows * capacity).astype(f32)
    number = lax.rem(lax.broadcasted_iota(jnp.int32, by_token.shape, 1), packed).astype(f32)
    select_t[...] = jnp.where(
        jnp.logical_and(by_token >= 0.0, by_token + base == number), 1.0, 0.0
    ).astype(bf16)
    at = lax.broadcasted_iota(jnp.int32, (Q, wide), 0)
    expert = (at // F * C + c) * F + lax.rem(at, F)
    spread = (lax.broadcasted_iota(jnp.int32, (Q, wide), 1) == expert).astype(bf16)
    by_slot = lax.dot_general(
        spread, slot_rows, (((1,), (1,)), ((), ())), preferred_element_type=f32
    )
    base = (where // rows * capacity).astype(f32)
    by_slot = jnp.where(by_slot >= 0.0, by_slot + base, -1.0)
    number = lax.broadcasted_iota(jnp.int32, (packed, length), 0).astype(f32)
    for p in range(Q):
        select[p * packed : (p + 1) * packed, :] = jnp.where(
            number == by_slot[p : p + 1, :], 1.0, 0.0
        ).astype(bf16)

    x_line.hop(C - 1)
    for i in range(2):
        for copy in c_copies[i]:
            copy.wait()
    saves = [
        pltpu.make_async_copy(X, X_out, save.at[0]),
        pltpu.make_async_copy(W, W_out, save.at[1]),
        pltpu.make_async_copy(WO, WO_out, save.at[2]),
    ]
    saves[0].start()
    saves[1].start()
    across = lax.broadcasted_iota(jnp.int32, (HEAD_DIM, HEAD_DIM), 0)
    diagonal = across == lax.broadcasted_iota(jnp.int32, (HEAD_DIM, HEAD_DIM), 1)
    flat = PK[...].reshape(width, PK.shape[-1]).astype(f32)
    for j in range(width // HEAD_DIM):
        part = slice(j * HEAD_DIM, (j + 1) * HEAD_DIM)
        for i, row in enumerate((gain_attn, gain_moe)):
            line = flat[part, experts + i : experts + i + 1]
            row[:, part] = jnp.sum(jnp.where(diagonal, line, 0.0), axis=0, keepdims=True)

    def norm_rows(i, carry):
        part = pl.ds(i * 64, 64)
        unit, _ = rms_unit(X[part, :].astype(f32))
        xn[part, :] = (unit * gain_attn[...]).astype(bf16)
        return carry

    lax.fori_loop(0, length // 64, norm_rows, 0)

    def weights(cols):
        return W[:, :, :, :, cols].reshape(width, 2 * HEAD_DIM)

    kv = jnp.dot(xn[...], weights(pl.ds(head_width, 2 * HEAD_DIM)), preferred_element_type=f32)
    k_out[...] = kv[:, :HEAD_DIM]
    v[...] = kv[:, HEAD_DIM:].astype(bf16)
    unit, _ = rms_unit(k_out[...])
    kr[...] = half_turn(unit * gains[1:2, :], cosine[...], sine[...]).astype(bf16)

    def head_pair(i, carry):
        cols = pl.ds(pl.multiple_of(i * 2 * HEAD_DIM, 2 * HEAD_DIM), 2 * HEAD_DIM)
        both = jnp.dot(xn[...], weights(cols), preferred_element_type=f32)
        q[:, cols] = both
        for half in range(2):
            lanes = pl.ds(pl.multiple_of((2 * i + half) * HEAD_DIM, HEAD_DIM), HEAD_DIM)
            for part in range(length // block):
                at = slice(part * block, (part + 1) * block)
                unit, _ = rms_unit(both[at, half * HEAD_DIM : (half + 1) * HEAD_DIM])
                qr = half_turn(unit * gains[0:1, :], cosine[at, :], sine[at, :]).astype(bf16)
                probs = score_block(qr, kr[...], pos_col[at, :], pos_row[...])
                mixed[at, lanes] = jnp.dot(
                    probs.astype(bf16), v[...], preferred_element_type=f32
                ).astype(bf16)
        return carry

    pairs = head_width // (2 * HEAD_DIM)
    half_way = pairs // 2
    g_line.hop(1)
    lax.fori_loop(0, half_way, head_pair, 0)
    for k in range(F - 1):
        f_copies[2][k].wait_recv()
        c_copies[2][k + 1].start()
    for h in range(2, C - 1):
        g_line.hop(h)
    lax.fori_loop(half_way, pairs, head_pair, 0)
    for copy in c_copies[2]:
        copy.wait()
    saves[2].start()

    def project(j, carry):
        cols = pl.ds(pl.multiple_of(j * 256, 256), 256)
        out[:, cols] = jnp.dot(
            mixed[...], WO[:, :, :, cols].reshape(head_width, 256), preferred_element_type=f32
        ).astype(bf16)
        return carry

    lax.fori_loop(0, width // 256, project, 0)

    def turn(j, carry):
        cols = pl.ds(pl.multiple_of(j * 256, 256), 256)
        xnt[cols, :] = xn[:, cols].T
        return carry

    lax.fori_loop(0, width // 256, turn, 0)
    g_line.hop(C - 1)
    x_line.finish()
    g_line.finish()
    for line in f_copies:
        for copy in line:
            copy.wait_send()
    for copy in saves + own[5:]:
        copy.wait()


def front(
    capacity, packed, order, ids, slot_ids, tokens, wq, wk, wv, wo, router, norm_attn, norm_moe, cot, gains
):
    S, C, F = sizes()
    Q = S * F
    rows, width = tokens.shape
    length = C * rows
    shard = wq.shape[0]
    head_width = wq.shape[1] // C
    experts = router.shape[0]
    wide = round_up(experts, 128)
    frequency = np.power(rope_base, -np.arange(HEAD_DIM // 2) * 2.0 / HEAD_DIM)
    frequency = jnp.asarray(np.tile(frequency, 2)[None].astype(np.float32))
    block = min(length, 512)
    sds = jax.ShapeDtypeStruct
    V = pltpu.VMEM
    vm = pl.BlockSpec(memory_space=pltpu.VMEM)
    w_shape = (S, C, F, shard, head_width + 2 * HEAD_DIM)
    wo_shape = (S, F) + wo.shape
    pack_block = (shard, round_up(experts + 2, 128))
    pack_shape = (S, C, F) + pack_block
    return pl.pallas_call(
        functools.partial(front_kernel, block, capacity, packed, experts),
        out_shape=[
            sds((length, width), bf16),
            sds(w_shape, bf16),
            sds(wo_shape, bf16),
            sds(pack_shape, bf16),
            sds((C, rows, wide), f32),
            sds((C, rows, width), bf16),
            sds((length, width), bf16),
            sds((length, head_width), f32),
            sds((length, HEAD_DIM), f32),
            sds((length, HEAD_DIM), bf16),
            sds((length, head_width), bf16),
            sds((width, length), bf16),
            sds((1, width), f32),
            sds((1, width), f32),
            sds(gains.shape, f32),
            sds((length, HEAD_DIM), f32),
            sds((length, HEAD_DIM), f32),
            sds((length, 1), jnp.int32),
            sds((1, length), jnp.int32),
            sds((Q * packed, length), bf16),
            sds((length, Q * packed), bf16),
            sds((rows, wide), f32),
            sds((rows, wide), f32),
        ],
        in_specs=[pl.BlockSpec(memory_space=pltpu.SMEM), vm, vm] + [ANY] * 5 + [vm] * 3 + [ANY, vm, vm],
        out_specs=[ANY, ANY, ANY, vm, vm, ANY] + [vm] * 17,
        scratch_shapes=[
            V((length, width), bf16),
            V(w_shape, bf16),
            V(wo_shape, bf16),
            V((length, width), bf16),
            V((length, HEAD_DIM), bf16),
            V(pack_block, bf16),
            DMA((6,)), DMA((3,)),
            DMA((5, C - 1)), DMA((5, C - 1)),
            DMA((3, F - 1)), DMA((3, F - 1)),
            DMA((3, F)), DMA((3, F)),
            DMA((2,)), DMA((1,)),
        ]
        + line_sems(C)
        + line_sems(C),
        name="gather_and_attend",
        compiler_params=params(1, 60 * 2**20),
    )(order, ids, slot_ids, tokens, wq, wk, wv, wo, router, norm_attn, norm_moe, cot, gains, frequency)


CHUNKS = 4


def columns(width, j):
    step = width // CHUNKS
    return pl.ds(j * step, step)


def three_parts(line):
    high = line.astype(bf16).astype(f32)
    rest = line - high
    middle = rest.astype(bf16).astype(f32)
    row = lax.broadcasted_iota(jnp.int32, (16, line.shape[1]), 0)
    rows = jnp.where(row == 0, high, jnp.where(row == 1, middle, jnp.where(row == 2, rest - middle, 0.0)))
    return rows.astype(bf16)


def halves(total):
    return total // 2


def dispatch_kernel(
    packed, out_part, G_in, tokens, pack, gain, chosen, kept, select, w_gate, w_up, w_down,
    buffer_out, gbuf, wrow, h1, xm, gates, hidden_out, dgp_out, dup_out, dgr,
    OP, RB, XM, SL, WM, WS, G, SG, buffer, WG, WU, WD, gp, up, gw, dup,
    local, load, saved, osend, orecv, gsend, grecv, xsend, xrecv, msend, mrecv, bsend, brecv, wsend, wrecv,
):
    S, C, F = sizes()
    s, c, f = place()
    Q = S * F
    q = s * F + f
    rows, width = tokens.shape
    total_rows = Q * packed
    half = halves(total_rows)
    z_peers = z_neighbours()
    p_at, p_peers = plane_neighbours()
    loads = [
        pltpu.make_async_copy(G_in, G, load.at[0]),
        pltpu.make_async_copy(w_down.at[0], WD, load.at[1]),
        pltpu.make_async_copy(w_gate.at[0], WG, load.at[2]),
        pltpu.make_async_copy(w_up.at[0], WU, load.at[3]),
    ]
    for copy in loads:
        copy.start()
    greet_all(z_peers + p_peers)
    mine = pl.ds(pl.multiple_of(q * packed, 16), packed)
    own_rows = pl.ds(pl.multiple_of(c * rows, 16), rows)
    right = (s, lax.rem(c + 1, C), f)
    left = (s, lax.rem(c + C - 1, C), f)

    def rightward(t):
        return remote(OP.at[t], RB.at[t], osend.at[0, t], orecv.at[0, t], right)

    def leftward(t):
        return remote(OP.at[t], RB.at[jnp.where(c - 1 == t, C, t)], osend.at[1, t], orecv.at[1, t], left)

    def merge(t, way):
        remote(OP.at[t], RB.at[t], osend.at[way, t], orecv.at[way, t], left).wait_recv()

        def add(j, carry):
            part = pl.ds(j * 32, 32)
            OP[t, part, :] = (OP[t, part, :].astype(f32) + RB[t, part, :].astype(f32)).astype(bf16)
            return carry

        lax.fori_loop(0, rows // 32, add, 0)

    def pass_on(step):
        t_right = C - 1 + c - step
        t_left = step - (C - 1 - c)

        @pl.when((t_right > c) & (t_right < C) & (c > 0))
        def _():
            merge(t_right, 0)
            rightward(t_right).start()

        @pl.when((t_left >= 0) & (t_left < c) & (c < C - 1))
        def _():
            merge(t_left, 1)
            leftward(t_left).start()

    fetch = pltpu.make_async_copy(out_part, OP, local.at[0])
    fetch.start()
    fetch.wait()

    @pl.when(c == 0)
    def _():
        for t in range(C - 1, 0, -1):
            rightward(t).start()

    @pl.when(c == C - 1)
    def _():
        for t in range(C - 1):
            leftward(t).start()

    loads[0].wait()

    def grad_slots(p):
        at = pl.ds(pl.multiple_of(p * packed, 16), packed)

        def body(j, carry):
            cols = pl.ds(pl.multiple_of(j * 512, 512), 512)
            SG[at, cols] = jnp.dot(select[at, :], G[:, cols], preferred_element_type=f32).astype(bf16)
            return carry

        lax.fori_loop(0, width // 512, body, 0)

    later = []
    for k, peer in enumerate(p_peers):
        theirs = pl.ds(pl.multiple_of(p_at[k] * packed, 16), packed)
        later.append(remote(SG.at[theirs], gbuf.at[mine], gsend.at[k], grecv.at[k], peer))
        grad_slots(p_at[k])
        later[-1].start()
    grad_slots(q)
    later.append(pltpu.make_async_copy(SG.at[mine], gbuf.at[mine], local.at[1]))
    later[-1].start()
    for step in range(1, C - 1):
        pass_on(step)

    @pl.when(c > 0)
    def _():
        remote(OP.at[0], RB.at[c], osend.at[0, c], orecv.at[0, c], left).wait_recv()

    @pl.when(c < C - 1)
    def _():
        remote(OP.at[0], RB.at[C], osend.at[1, c], orecv.at[1, c], right).wait_recv()


    def head_rows(i, carry):
        part = pl.ds(i * 32, 32)
        total = tokens[part, :].astype(f32) + OP[c, part, :].astype(f32)
        total += jnp.where(c > 0, RB[c, part, :].astype(f32), 0.0)
        total += jnp.where(c < C - 1, RB[C, part, :].astype(f32), 0.0)
        h1[part, :] = total
        unit, _ = rms_unit(total)
        normed = (unit * gain[...]).astype(bf16)
        xm[part, :] = normed
        XM[pl.ds(pl.multiple_of(c * rows + i * 32, 16), 32), :] = normed
        return carry

    lax.fori_loop(0, rows // 32, head_rows, 0)
    chunks = []
    for j in range(CHUNKS):
        piece = XM.at[own_rows, columns(width, j)]
        chunks.append(
            [remote(piece, piece, xsend.at[j, k], xrecv.at[j, k], peer) for k, peer in enumerate(z_peers)]
        )
    for copy in chunks[0]:
        copy.start()
    logits = jnp.dot(xm[...], pack[...], preferred_element_type=f32)[:, : chosen.shape[1]]
    logits = jnp.where(chosen[...] > 0.0, logits, -jnp.inf)
    power = jnp.exp(logits - jnp.max(logits, axis=-1, keepdims=True))
    gates[...] = power / jnp.sum(power, axis=-1, keepdims=True)
    WM[own_rows, :] = gates[...] * kept[...]
    row = []
    for k, peer in enumerate(z_peers):
        piece = WM.at[own_rows, :]
        row.append(remote(piece, piece, msend.at[k], mrecv.at[k], peer))
        row[-1].start()
    for line in chunks[1:]:
        for copy in line:
            copy.start()
    sent = []
    for j in range(CHUNKS):
        cols = columns(width, j)
        for copy in chunks[j]:
            copy.wait_recv()

        def slots(i, carry):
            at = pl.ds(pl.multiple_of(i * half, 16), half)
            SL[at, cols] = jnp.dot(select[at, :], XM[:, cols], preferred_element_type=f32).astype(bf16)
            return carry

        lax.fori_loop(0, 2, slots, 0)
        line = []
        for k, peer in enumerate(p_peers):
            theirs = pl.ds(pl.multiple_of(p_at[k] * packed, 16), packed)
            line.append(
                remote(SL.at[theirs, cols], buffer.at[mine, cols], bsend.at[j, k], brecv.at[j, k], peer)
            )
        line.append(pltpu.make_async_copy(SL.at[mine, cols], buffer.at[mine, cols], local.at[4 + j]))
        for copy in line:
            copy.start()
        sent.append(line)
        if j == 0:
            for copy in row:
                copy.wait_recv()
            WS[...] = jnp.zeros_like(WS)

            place_of = lax.broadcasted_iota(jnp.int32, (Q, WM.shape[1]), 0)
            expert = (place_of // F * C + c) * F + lax.rem(place_of, F)
            spread = (lax.broadcasted_iota(jnp.int32, expert.shape, 1) == expert).astype(f32)
            lines = lax.dot_general(
                spread, WM[...], (((1,), (1,)), ((), ())),
                precision=lax.Precision.HIGHEST, preferred_element_type=f32,
            )
            for p in range(Q):
                line = lax.dot_general(
                    three_parts(lines[p : p + 1, :]), select[p * packed : (p + 1) * packed, :],
                    (((1,), (1,)), ((), ())), preferred_element_type=f32,
                )
                WS[p, :, pl.ds(0, packed)] = jnp.broadcast_to(
                    jnp.sum(line, axis=0, keepdims=True), (8, packed)
                )
            scales = [
                remote(WS.at[p_at[k]], wrow.at[q], wsend.at[k], wrecv.at[k], peer)
                for k, peer in enumerate(p_peers)
            ]
            scales.append(pltpu.make_async_copy(WS.at[q], wrow.at[q], local.at[2]))
            for copy in scales:
                copy.start()
        if j == CHUNKS - 2:
            for copy in later + loads[1:]:
                copy.wait()
            reload = pltpu.make_async_copy(gbuf, SG, local.at[3])
            reload.start()
            reload.wait()

            def through_down(i, carry):
                at = pl.ds(pl.multiple_of(i * half, 16), half)
                gw[at, :] = lax.dot_general(
                    SG[at, :], WD[...], (((1,), (1,)), ((), ())), preferred_element_type=f32
                )
                return carry

            lax.fori_loop(0, 2, through_down, 0)
    for j in range(CHUNKS - 1):
        cols = columns(width, j)
        for copy in sent[j]:
            copy.wait()

        def project(i, carry):
            at = pl.ds(pl.multiple_of(i * half, 16), half)
            part = buffer[at, cols]
            one = jnp.dot(part, WG[cols, :], preferred_element_type=f32)
            two = jnp.dot(part, WU[cols, :], preferred_element_type=f32)
            gp[at, :] = one if j == 0 else gp[at, :] + one
            up[at, :] = two if j == 0 else up[at, :] + two
            return carry

        lax.fori_loop(0, 2, project, 0)
    for copy in scales:
        copy.wait()
    diagonal = lax.broadcasted_iota(jnp.int32, (packed, packed), 0) == lax.broadcasted_iota(
        jnp.int32, (packed, packed), 1
    )
    dgr[...] = jnp.zeros_like(dgr)
    cols = columns(width, CHUNKS - 1)
    inner = dup.shape[-1]
    hidden, dgp = SG.at[:, pl.ds(0, inner)], SG.at[:, pl.ds(inner, inner)]

    def saves_of(p):
        at = pl.ds(pl.multiple_of(p * packed, 16), packed)
        pairs = ((buffer, buffer_out), (hidden, hidden_out), (dgp, dgp_out), (dup, dup_out))
        return [
            pltpu.make_async_copy(src.at[at], dst.at[at], saved.at[i, p])
            for i, (src, dst) in enumerate(pairs)
        ]

    def expert_rows(p):
        at = pl.ds(pl.multiple_of(p * packed, 16), packed)
        part = buffer[at, cols]
        gate_pre = gp[at, :] + jnp.dot(part, WG[cols, :], preferred_element_type=f32)
        up_pre = up[at, :] + jnp.dot(part, WU[cols, :], preferred_element_type=f32)
        back = gw[at, :]
        scale = jnp.sum(
            jnp.where(diagonal, wrow[p, 0:1, pl.ds(0, packed)], 0.0), axis=1, keepdims=True
        )
        sigmoid = jax.nn.sigmoid(gate_pre)
        silu = gate_pre * sigmoid
        low = (silu * up_pre).astype(bf16)
        hidden[at, :] = (scale * low.astype(f32)).astype(bf16)
        dgate = jnp.sum(back * low.astype(f32), axis=-1, keepdims=True)
        line = jnp.sum(jnp.where(diagonal, dgate, 0.0), axis=0, keepdims=True)
        dgr[p, :, pl.ds(0, packed)] = jnp.broadcast_to(line, (8, packed))
        dhid = scale * back
        dgp[at, :] = (dhid * up_pre * sigmoid * (1.0 + gate_pre * (1.0 - sigmoid))).astype(bf16)
        dup[at, :] = (dhid * silu).astype(bf16)
        for copy in saves_of(p):
            copy.start()

    sent[CHUNKS - 1][Q - 1].wait()
    expert_rows(q)

    def arrival(k, carry):
        p = lax.rem(q + Q - 1 - k, Q)
        at = pl.ds(pl.multiple_of(p * packed, 16), packed)
        came = (p // F, c, lax.rem(p, F))
        remote(
            SL.at[at, cols], buffer.at[at, cols], bsend.at[CHUNKS - 1, k], brecv.at[CHUNKS - 1, k], came
        ).wait_recv()
        expert_rows(p)
        return carry

    lax.fori_loop(0, Q - 1, arrival, 0)
    for copy in sent[CHUNKS - 1][: Q - 1]:
        copy.wait_send()
    for line in chunks + [row]:
        for copy in line:
            copy.wait_send()

    @pl.when(c < C - 1)
    def _():
        def body(t, carry):
            rightward(t).wait_send()
            return carry

        lax.fori_loop(c + 1, C, body, 0)

    @pl.when(c > 0)
    def _():
        def body(t, carry):
            leftward(t).wait_send()
            return carry

        lax.fori_loop(0, c, body, 0)

    for p in range(Q):
        for copy in saves_of(p):
            copy.wait()


def dispatch(packed, out_part, G, tokens, pack, gain, chosen, kept, select, w_gate, w_up, w_down):
    S, C, F = sizes()
    Q = S * F
    rows, width = tokens.shape
    inner = w_gate.shape[-1]
    lanes = round_up(packed, 128)
    wide = chosen.shape[1]
    V = pltpu.VMEM
    sds = jax.ShapeDtypeStruct
    vm = pl.BlockSpec(memory_space=pltpu.VMEM)
    slots = Q * packed
    return pl.pallas_call(
        functools.partial(dispatch_kernel, packed),
        out_shape=[
            sds((slots, width), bf16),
            sds((slots, width), bf16),
            sds((Q, 8, lanes), f32),
            sds((rows, width), f32),
            sds((rows, width), bf16),
            sds((rows, wide), f32),
            sds((slots, inner), bf16),
            sds((slots, inner), bf16),
            sds((slots, inner), bf16),
            sds((Q, 8, lanes), f32),
        ],
        in_specs=[ANY, ANY] + [vm] * 6 + [ANY] * 3,
        out_specs=[ANY, ANY, vm, vm, vm, vm, ANY, ANY, ANY, vm],
        scratch_shapes=[
            V((C, rows, width), bf16),
            V((C + 1, rows, width), bf16),
            V((C * rows, width), bf16),
            V((slots, width), bf16),
            V((C * rows, wide), f32),
            V((Q, 8, lanes), f32),
            V((C * rows, width), bf16),
            V((slots, width), bf16),
            V((slots, width), bf16),
            V((width, inner), bf16), V((width, inner), bf16), V((inner, width), bf16),
            V((slots, inner), f32), V((slots, inner), f32), V((slots, inner), f32),
            V((slots, inner), bf16),
            DMA((4 + CHUNKS,)),
            DMA((4,)),
            DMA((4, Q)),
            DMA((2, C)), DMA((2, C)),
            DMA((Q - 1,)), DMA((Q - 1,)),
            DMA((CHUNKS, C - 1)), DMA((CHUNKS, C - 1)),
            DMA((C - 1,)), DMA((C - 1,)),
            DMA((CHUNKS, Q - 1)), DMA((CHUNKS, Q - 1)),
            DMA((Q - 1,)), DMA((Q - 1,)),
        ],
        name="dispatch_rows",
        compiler_params=params(3, 62 * 2**20),
    )(out_part, G, tokens, pack, gain, chosen, kept, select, w_gate, w_up, w_down)


def return_kernel(
    packed, experts, dgr, select, select_t, gates, pack, h1, gain, cot, xm, hidden, dgp, dup,
    w_gate, w_up, w_down,
    DA, y_part, dh1, small,
    RD, YB, PART, RX, DG, DGP, RG, DL, din, wy, WG, WU, WD, dlog, gnorm,
    local, load, dsend, drecv, gsend, grecv, ysend, yrecv, xsend, xrecv, msend, mrecv, *asems,
):
    S, C, F = sizes()
    s, c, f = place()
    Q = S * F
    q = s * F + f
    rows, width = h1.shape
    z_peers = z_neighbours()
    p_at, p_peers = plane_neighbours()
    loads = []
    for j in range(CHUNKS):
        cols = columns(width, j)
        loads.append(
            [
                pltpu.make_async_copy(w_gate.at[0, cols], WG.at[cols], load.at[0, j]),
                pltpu.make_async_copy(w_up.at[0, cols], WU.at[cols], load.at[1, j]),
            ]
        )
    load_down = pltpu.make_async_copy(w_down.at[0], WD, load.at[2, 0])
    for line in loads:
        for copy in line:
            copy.start()
    load_down.start()
    greet_all(z_peers + p_peers)
    half = halves(Q * packed)
    mine = pl.ds(pl.multiple_of(q * packed, 16), packed)
    theirs = [pl.ds(pl.multiple_of(at * packed, 16), packed) for at in p_at]
    inner_products = [
        remote(dgr.at[p_at[k]], DG.at[q], gsend.at[k], grecv.at[k], peer)
        for k, peer in enumerate(p_peers)
    ]
    inner_products.append(pltpu.make_async_copy(dgr.at[q], DG.at[q], local.at[0]))
    for copy in inner_products:
        copy.start()
    chunks = []
    for j in range(CHUNKS):
        cols = columns(width, j)
        for copy in loads[j]:
            copy.wait()

        def expert_in(i, carry):
            at = pl.ds(pl.multiple_of(i * half, 16), half)
            across = (((1,), (1,)), ((), ()))
            total = lax.dot_general(dgp[at, :], WG[cols, :], across, preferred_element_type=f32)
            total += lax.dot_general(dup[at, :], WU[cols, :], across, preferred_element_type=f32)
            din[at, cols] = total.astype(bf16)
            return carry

        lax.fori_loop(0, 2, expert_in, 0)
        line = [
            remote(din.at[theirs[k], cols], RD.at[mine, cols], dsend.at[j, k], drecv.at[j, k], peer)
            for k, peer in enumerate(p_peers)
        ]
        line.append(pltpu.make_async_copy(din.at[mine, cols], RD.at[mine, cols], local.at[2 + j]))
        for copy in line:
            copy.start()
        chunks.append(line)
    load_down.wait()
    def expert_out(i, carry):
        at = pl.ds(pl.multiple_of(i * half, 16), half)

        def body(j, carry):
            cols = pl.ds(pl.multiple_of(j * 512, 512), 512)
            y = jnp.dot(hidden[at, :], WD[:, cols], preferred_element_type=f32)
            wy[at, cols] = y.astype(bf16)
            return carry

        return lax.fori_loop(0, width // 512, body, carry)

    lax.fori_loop(0, 2, expert_out, 0)
    sums = []
    for j in range(CHUNKS):
        cols = columns(width, j)
        for copy in chunks[j]:
            copy.wait()

        def combine(i, carry):
            lanes = pl.ds(pl.multiple_of(j * (width // CHUNKS) + i * 256, 256), 256)
            PART[:, lanes] = jnp.dot(
                select_t[...], RD[:, lanes], preferred_element_type=f32
            ).astype(bf16)
            return carry

        lax.fori_loop(0, width // CHUNKS // 256, combine, 0)
        for k, peer in enumerate(z_peers):
            src = PART.at[pl.ds(pl.multiple_of(peer[1] * rows, 16), rows), cols]
            sums.append(remote(src, RX.at[k, :, cols], xsend.at[j, k], xrecv.at[j, k], peer))
            sums[-1].start()
    ys = [
        remote(wy.at[theirs[k]], YB.at[mine], ysend.at[k], yrecv.at[k], peer)
        for k, peer in enumerate(p_peers)
    ]
    ys.append(pltpu.make_async_copy(wy.at[mine], YB.at[mine], local.at[1]))
    for copy in ys:
        copy.start()
    for copy in inner_products:
        copy.wait()
    wide = gates.shape[1]
    place_of = lax.broadcasted_iota(jnp.int32, (Q, wide), 0)
    expert = (place_of // F * C + c) * F + lax.rem(place_of, F)
    spread = (lax.broadcasted_iota(jnp.int32, (Q, wide), 1) == expert).astype(f32)

    for p in range(Q):
        at = pl.ds(p * packed, packed)
        line = jnp.dot(
            three_parts(DG[p, 0:1, pl.ds(0, packed)]), select[at, :], preferred_element_type=f32
        )
        DL[pl.ds(p, 1), :] = jnp.sum(line, axis=0, keepdims=True)
    DGP[...] = lax.dot_general(
        DL[...], spread, (((0,), (0,)), ((), ())),
        precision=lax.Precision.HIGHEST, preferred_element_type=f32,
    ).reshape(DGP.shape)
    more = []
    for k, peer in enumerate(z_peers):
        more.append(remote(DGP.at[peer[1]], RG.at[k], msend.at[k], mrecv.at[k], peer))
        more[-1].start()
    for copy in more:
        copy.wait()
    total = DGP[c]
    for k in range(C - 1):
        total = total + RG[k]
    dlogits = gates[...] * (total - jnp.sum(gates[...] * total, axis=-1, keepdims=True))
    dlog[...] = dlogits.astype(bf16)
    gnorm[...] = jnp.zeros_like(gnorm)
    for copy in sums:
        copy.wait()

    def head_rows(i, carry):
        part = pl.ds(i * 32, 32)
        mine_part = pl.ds(pl.multiple_of(c * rows + i * 32, 16), 32)
        dxm = PART[mine_part, :].astype(f32)
        for k in range(C - 1):
            dxm = dxm + RX[k, part, :].astype(f32)
        dxm = dxm + lax.dot_general(
            dlog[part, :], pack[:, pl.ds(0, wide)], (((1,), (1,)), ((), ())), preferred_element_type=f32
        )
        unit, factor = rms_unit(h1[part, :])
        gnorm[...] += jnp.sum(dxm * unit, axis=0, keepdims=True)
        grad = cot[part, :].astype(f32) + norm_backward(dxm, unit, factor, gain[...])
        dh1[part, :] = grad
        RX[0, part, :] = grad.astype(bf16)
        return carry

    lax.fori_loop(0, rows // 32, head_rows, 0)
    keep = pltpu.make_async_copy(RX.at[0], DA.at[c], local.at[2 + CHUNKS])
    keep.start()
    line = Line(RX.at[0], lambda at: DA.at[at], *asems)
    line.start()
    for h in range(1, C - 1):
        line.hop(h)
    square = lax.broadcasted_iota(jnp.int32, (HEAD_DIM, HEAD_DIM), 0) == lax.broadcasted_iota(
        jnp.int32, (HEAD_DIM, HEAD_DIM), 1
    )
    small[...] = jnp.zeros_like(small)

    def small_rows(i, carry):
        at = pl.ds(pl.multiple_of(i * HEAD_DIM, HEAD_DIM), HEAD_DIM)
        router_part = lax.dot_general(
            xm[:, at], dlog[...], (((0,), (0,)), ((), ())), preferred_element_type=f32
        )
        column = jnp.sum(jnp.where(square, gnorm[:, at], 0.0), axis=1, keepdims=True)
        if wide > experts:
            lane = lax.broadcasted_iota(jnp.int32, router_part.shape, 1)
            small[at, :] = jnp.where(lane == experts, column, router_part).astype(bf16)
        else:
            small[at, pl.ds(0, wide)] = router_part.astype(bf16)
            lane = lax.broadcasted_iota(jnp.int32, (HEAD_DIM, HEAD_DIM), 1)
            small[at, pl.ds(wide, HEAD_DIM)] = jnp.where(lane == 0, column, 0.0).astype(bf16)
        return carry

    lax.fori_loop(0, width // HEAD_DIM, small_rows, 0)
    for copy in ys:
        copy.wait()

    def combine_y(i, carry):
        lanes = pl.ds(pl.multiple_of(i * 256, 256), 256)
        y_part[:, lanes] = jnp.dot(
            select_t[...], YB[:, lanes], preferred_element_type=f32
        ).astype(bf16)
        return carry

    lax.fori_loop(0, width // 256, combine_y, 0)
    line.hop(C - 1)
    line.finish()
    keep.wait()


def give_back(
    packed, experts, dgr, select, select_t, gates, pack, h1, gain, cot, xm, hidden, dgp, dup, w_gate, w_up, w_down
):
    S, C, F = sizes()
    Q = S * F
    rows, width = h1.shape
    wide = gates.shape[1]
    inner = w_gate.shape[-1]
    V = pltpu.VMEM
    sds = jax.ShapeDtypeStruct
    vm = pl.BlockSpec(memory_space=pltpu.VMEM)
    return pl.pallas_call(
        functools.partial(return_kernel, packed, experts),
        out_shape=[
            sds((C, rows, width), bf16),
            sds((C * rows, width), bf16),
            sds((rows, width), f32),
            sds(pack.shape, bf16),
        ],
        in_specs=[vm] * 12 + [ANY] * 3,
        out_specs=[ANY] + [vm] * 3,
        scratch_shapes=[
            V((Q * packed, width), bf16),
            V((Q * packed, width), bf16),
            V((C * rows, width), bf16),
            V((C - 1, rows, width), bf16),
            V(dgr.shape, f32),
            V((C, rows, wide), f32),
            V((C - 1, rows, wide), f32),
            V((Q, C * rows), f32),
            V((Q * packed, width), bf16),
            V((Q * packed, width), bf16),
            V((width, inner), bf16), V((width, inner), bf16), V((inner, width), bf16),
            V((rows, wide), bf16),
            V((1, width), f32),
            DMA((3 + CHUNKS,)),
            DMA((3, CHUNKS)),
            DMA((CHUNKS, Q - 1)), DMA((CHUNKS, Q - 1)),
            DMA((Q - 1,)), DMA((Q - 1,)),
            DMA((Q - 1,)), DMA((Q - 1,)),
            DMA((CHUNKS, C - 1)), DMA((CHUNKS, C - 1)),
            DMA((C - 1,)), DMA((C - 1,)),
        ]
        + line_sems(C),
        name="return_grads",
        compiler_params=params(5, 62 * 2**20),
    )(dgr, select, select_t, gates, pack, h1, gain, cot, xm, hidden, dgp, dup, w_gate, w_up, w_down)


def backward_kernel(
    block, da, w, wo, q, k, v, xnt, x, cosine, sine, pos_col, pos_row, gains, go, sp, yp,
    OH, OX, Q3, KV3, S3, T3, YP, *rest,
):
    DX = rest[: lax.axis_size("ctx")]
    (
    dxn, dxsem, kr, dkr, dv, acc, DQ, head_grad,
        GQ, Q1, Q2, QS, o_own, o_in, s_own, s_in, s_plane, s_sum, T, t_in, t_plane, t_sum,
        local, qlocal, csend, crecv, fsend, frecv, zsend, zrecv, qcs, qcr, qfs, qfr, qzs, qzr, ysend, yrecv,
    ) = rest[lax.axis_size("ctx") :]
    S, C, F = sizes()
    s, c, f = place()
    step = pl.program_id(0)
    units = GQ.shape[0]
    pairs = units - 1
    length, width = x.shape
    wide = 2 * HEAD_DIM
    z_peers = z_neighbours()
    f_peers = [(s, c, lax.rem(f + k, F)) for k in range(1, F)]
    sibling = (1 - s, c, f)
    cols = pl.ds(pl.multiple_of(step * wide, wide), wide)

    o_first = remote(go.at[1 - s], o_in, csend.at[0], crecv.at[0], sibling)
    t_first = remote(T, t_in, csend.at[2], crecv.at[2], sibling)
    o_load = pltpu.make_async_copy(go.at[s], o_own, local.at[0])
    half = F // 2
    mine = lax.rem(f // half, 2)
    o_saves = [
        pltpu.make_async_copy(o_own.at[pl.ds(mine * half, half)], OH, local.at[2]),
        pltpu.make_async_copy(o_own.at[pl.ds((1 - mine) * half, half)], OX, local.at[6]),
    ]
    s_first = remote(sp.at[1 - s], s_in, csend.at[1], crecv.at[1], sibling)
    s_load = pltpu.make_async_copy(sp.at[s], s_own, local.at[1])
    f_at = list(enumerate(f_peers))
    z_at = list(enumerate(z_peers))
    s_second = [remote(s_own.at[:, p[2]], s_plane.at[k], fsend.at[1, k], frecv.at[1, k], p) for k, p in f_at]
    t_second = [remote(T, t_plane.at[k], fsend.at[2, k], frecv.at[2, k], p) for k, p in f_at]
    s_third = [remote(s_sum.at[p[1]], S3.at[c], zsend.at[1, k], zrecv.at[1, k], p) for k, p in z_at]
    s_third.append(pltpu.make_async_copy(s_sum.at[c], S3.at[c], local.at[3]))
    t_third = [remote(t_sum, T3.at[c], zsend.at[2, k], zrecv.at[2, k], p) for k, p in z_at]
    t_third.append(pltpu.make_async_copy(t_sum, T3.at[c], local.at[4]))
    y_copies = [remote(yp.at[p[1]], YP.at[c], ysend.at[k], yrecv.at[k], p) for k, p in z_at]
    y_copies.append(pltpu.make_async_copy(yp.at[c], YP.at[c], local.at[5]))

    def q_first(u):
        return remote(GQ.at[u, 1 - s], Q1.at[u], qcs.at[u], qcr.at[u], sibling)

    def q_second(u):
        return [remote(GQ.at[u, s, :, p[2]], Q2.at[u, k], qfs.at[u, k], qfr.at[u, k], p) for k, p in f_at]

    def q_third(u):
        if isinstance(u, int) and u == pairs:
            landing = KV3.at[c]
        else:
            landing = Q3.at[:, pl.ds(pl.multiple_of(c * pairs * wide + u * wide, wide), wide)]
        copies = [
            remote(QS.at[u, p[1]], landing, qzs.at[u, k], qzr.at[u, k], p) for k, p in z_at
        ]
        copies.append(pltpu.make_async_copy(QS.at[u, c], landing, qlocal.at[u]))
        return copies

    def to_plane(u):
        q_first(u).wait()

        def body(i, carry):
            at = (u, s, i // F, lax.rem(i, F))
            GQ[at] = (GQ[at].astype(f32) + Q1[u, i // F, lax.rem(i, F)].astype(f32)).astype(bf16)
            return carry

        lax.fori_loop(0, C * F, body, 0)
        for copy in q_second(u):
            copy.start()

    def to_ctx(u):
        for copy in q_second(u):
            copy.wait()

        def body(i, carry):
            total = GQ[u, s, i, f].astype(f32)
            for k in range(F - 1):
                total = total + Q2[u, k, i].astype(f32)
            QS[u, i] = total.astype(bf16)
            return carry

        lax.fori_loop(0, C, body, 0)
        for copy in q_third(u):
            copy.start()

    @pl.when(step == 0)
    def _():
        greet_all(z_peers + f_peers + [sibling])
        for copy in [s_first, s_load, o_first, o_load] + y_copies:
            copy.start()
        unit, _ = rms_unit(k[...])
        kr[...] = half_turn(unit * gains[1:2, :], cosine[...], sine[...]).astype(bf16)
        dkr[...] = jnp.zeros_like(dkr)
        dv[...] = jnp.zeros_like(dv)
        head_grad[...] = jnp.zeros_like(head_grad)
        acc[...] = jnp.zeros_like(acc)

    @pl.when(step >= 1)
    def _():
        to_plane(step - 1)

    @pl.when(step == 1)
    def _():
        o_first.wait()
        o_load.wait()

        def o_body(i, carry):
            o_own[i] = (o_own[i].astype(f32) + o_in[i].astype(f32)).astype(bf16)
            return carry

        lax.fori_loop(0, F, o_body, 0)
        for copy in o_saves:
            copy.start()
        s_first.wait()
        s_load.wait()

        def s_body(i, carry):
            at = (i // F, lax.rem(i, F))
            s_own[at] = (s_own[at].astype(f32) + s_in[at].astype(f32)).astype(bf16)
            return carry

        lax.fori_loop(0, C * F, s_body, 0)
        for copy in s_second:
            copy.start()

    @pl.when(step >= 2)
    def _():
        to_ctx(step - 2)

    @pl.when(step == 2)
    def _():
        for copy in s_second:
            copy.wait()

        def s_body(i, carry):
            total = s_own[i, f].astype(f32)
            for k in range(F - 1):
                total = total + s_plane[k, i].astype(f32)
            s_sum[i] = total.astype(bf16)
            return carry

        lax.fori_loop(0, C, s_body, 0)
        for copy in s_third:
            copy.start()

    @pl.when(step < pairs)
    def _():
        dm = lax.dot_general(
            da[...], wo[cols, :], (((1,), (1,)), ((), ())), preferred_element_type=f32
        ).astype(bf16)
        for half in range(2):
            lanes = slice(half * HEAD_DIM, (half + 1) * HEAD_DIM)
            for part in range(length // block):
                rows = slice(part * block, (part + 1) * block)
                unit, factor = rms_unit(q[rows, lanes])
                cos, sin = cosine[rows, :], sine[rows, :]
                qr = half_turn(unit * gains[0:1, :], cos, sin).astype(bf16)
                keys = kr[...]
                probs = score_block(qr, keys, pos_col[rows, :], pos_row[...])
                dmh = dm[rows, lanes]
                dprobs = lax.dot_general(
                    dmh, v[...], (((1,), (1,)), ((), ())), preferred_element_type=f32
                )
                delta = jnp.sum(probs * dprobs, axis=-1, keepdims=True)
                dscores = (probs * (dprobs - delta)).astype(bf16)
                dqr = jnp.dot(dscores, keys, preferred_element_type=f32) * (HEAD_DIM**-0.5)
                rows_in = (((0,), (0,)), ((), ()))
                dkr[...] += lax.dot_general(dscores, qr, rows_in, preferred_element_type=f32) * (
                    HEAD_DIM**-0.5
                )
                dv[...] += lax.dot_general(
                    probs.astype(bf16), dmh, rows_in, preferred_element_type=f32
                )
                dqs = half_turn(dqr, cos, -sin)
                head_grad[0:1, :] += jnp.sum(dqs * unit, axis=0, keepdims=True)
                DQ[rows, lanes] = norm_backward(dqs, unit, factor, gains[0:1, :]).astype(bf16)

    @pl.when(step == pairs)
    def _():
        unit, factor = rms_unit(k[...])
        dks = half_turn(dkr[...], cosine[...], -sine[...])
        head_grad[1:2, :] += jnp.sum(dks * unit, axis=0, keepdims=True)
        DQ[:, :HEAD_DIM] = norm_backward(dks, unit, factor, gains[1:2, :]).astype(bf16)
        DQ[:, HEAD_DIM:] = dv[...].astype(bf16)

    def weight_rows(i, carry):
        part = F * GQ.shape[4]
        rows = pl.ds(pl.multiple_of(i * part, 16), part)
        piece = jnp.dot(xnt[rows, :], DQ[...], preferred_element_type=f32)
        GQ[step, i // C, lax.rem(i, C)] = piece.astype(bf16).reshape(GQ.shape[3:])
        return carry

    lax.fori_loop(0, S * C, weight_rows, 0)
    q_first(step).start()
    for j in range(4):
        part = pl.ds(j * (width // 4), width // 4)
        acc[:, part] += lax.dot_general(
            DQ[...], w[part, cols], (((1,), (1,)), ((), ())), preferred_element_type=f32
        )

    @pl.when(step == pairs)
    def _():
        to_ctx(pairs - 1)
        to_plane(pairs)
        rows_of = width // HEAD_DIM
        total = jnp.zeros((1, width), f32)

        def finish(i, total):
            rows = pl.ds(i * 64, 64)
            unit, _ = rms_unit(x[rows, :].astype(f32))
            term = acc[rows, :]
            dxn[rows, :] = term.astype(bf16)
            return total + jnp.sum(term * unit, axis=0, keepdims=True)

        total = lax.fori_loop(0, length // 64, finish, total)
        rows = length // C
        x_saves = [
            pltpu.make_async_copy(
                dxn.at[pl.ds(pl.multiple_of(lax.rem(c + i, C) * rows, 16), rows)], DX[i], dxsem.at[i]
            )
            for i in range(C)
        ]
        for copy in x_saves:
            copy.start()
        for r in range(rows_of):
            T[r : r + 1, :] = total[:, r * HEAD_DIM : (r + 1) * HEAD_DIM]
        T[rows_of:, :] = head_grad[...]
        t_first.start()
        t_first.wait()
        T[...] = T[...] + t_in[...]
        for copy in t_second:
            copy.start()
        to_ctx(pairs)
        for copy in t_second:
            copy.wait()
        order = []
        for g in range(F):
            term = jnp.zeros_like(T)
            for k in range(F - 1):
                came = lax.rem(f + F - (k + 1), F)
                term = term + jnp.where(came == g, t_plane[k], 0.0)
            order.append(term + jnp.where(f == g, T[...], 0.0))
        total = order[0]
        for term in order[1:]:
            total = total + term
        t_sum[...] = total
        for copy in t_third:
            copy.start()
        for copy in s_third + y_copies + o_saves + t_third + x_saves:
            copy.wait()
        for u in range(units):
            for copy in q_third(u):
                copy.wait()


def backward(da, w, wo, q, k, v, xnt, x, cosine, sine, pos_col, pos_row, gains, go, sp, yp):
    S, C, F = sizes()
    length, width = x.shape
    head_width = wo.shape[0]
    pairs = head_width // (2 * HEAD_DIM)
    units = pairs + 1
    shard = sp.shape[3]
    block = min(length, 512)
    wide = 2 * HEAD_DIM
    once = pl.Buffered(buffer_count=1)
    whole = lambda array: pl.BlockSpec(array.shape, lambda i: (0, 0), pipeline_mode=once)
    sds = jax.ShapeDtypeStruct
    V = pltpu.VMEM
    q_block, o_block, s_block = (shard, wide), go.shape[2:], sp.shape[3:]
    t_block = (width // HEAD_DIM + 8, HEAD_DIM)
    return pl.pallas_call(
        functools.partial(backward_kernel, block),
        out_shape=[
            sds((F // 2,) + o_block, bf16),
            sds((F // 2,) + o_block, bf16),
            sds((shard, C * head_width), bf16),
            sds((C, shard, wide), bf16),
            sds((C,) + s_block, bf16),
            sds((C,) + t_block, f32),
            sds(yp.shape, bf16),
        ]
        + [sds((length // C, width), bf16)] * C,
        grid=(units,),
        in_specs=[whole(da), whole(w), whole(wo)]
        + [pl.BlockSpec((length, wide), lambda i: (0, jnp.minimum(i, pairs - 1)))]
        + [whole(array) for array in (k, v, xnt, x, cosine, sine, pos_col, pos_row, gains)]
        + [ANY] * 3,
        out_specs=[ANY] * (7 + C),
        scratch_shapes=[
            V((length, width), bf16), DMA((C,)),
            V((length, HEAD_DIM), bf16), V((length, HEAD_DIM), f32), V((length, HEAD_DIM), f32),
            V((length, width), f32), V((length, wide), bf16), V((8, HEAD_DIM), f32),
            V((units, S, C, F) + q_block, bf16), V((units, C, F) + q_block, bf16),
            V((units, F - 1, C) + q_block, bf16), V((units, C) + q_block, bf16),
            V((F,) + o_block, bf16), V((F,) + o_block, bf16),
            V((C, F) + s_block, bf16), V((C, F) + s_block, bf16), V((F - 1, C) + s_block, bf16), V((C,) + s_block, bf16),
            V(t_block, f32), V(t_block, f32), V((F - 1,) + t_block, f32), V(t_block, f32),
            DMA((7,)), DMA((units,)),
            DMA((3,)), DMA((3,)), DMA((3, F - 1)), DMA((3, F - 1)), DMA((3, C - 1)), DMA((3, C - 1)),
            DMA((units,)), DMA((units,)), DMA((units, F - 1)), DMA((units, F - 1)),
            DMA((units, C - 1)), DMA((units, C - 1)), DMA((C - 1,)), DMA((C - 1,)),
        ],
        name="attention_backward",
        compiler_params=params(7, 60 * 2**20),
    )(da, w, wo, q, k, v, xnt, x, cosine, sine, pos_col, pos_row, gains, go, sp, yp)


def dot(left, right):
    return jnp.dot(left, right, preferred_element_type=f32)


def contract_rows(left, right):
    return lax.dot_general(left, right, (((0,), (0,)), ((), ())), preferred_element_type=f32)


def times_transpose(left, right):
    return lax.dot_general(left, right, (((1,), (1,)), ((), ())), preferred_element_type=f32)


def on_device(
    tokens,
    stretch_order,
    expert_ids,
    slot_index,
    norm_attn,
    head_gains,
    w_query,
    w_key,
    w_value,
    w_out,
    norm_moe,
    w_router,
    w_gate,
    w_up,
    w_down,
    cotangent,
):
    S, C, F = sizes()
    Q = S * F
    seq_at, ctx_at, fsdp_at = place()
    rows, width = tokens.shape[1:]
    length = C * rows
    experts = w_router.shape[1]
    capacity = rows * TOP // (Q * C) + 1
    packed = round_up(C * capacity, 16)
    lanes = round_up(packed, 128)
    head_width = w_query.shape[1] // C
    shard = w_router.shape[0]
    pack_width = round_up(experts + 2, 128)
    (
        X, W, WO, PK, _, G, out_part, q, k, v, mixed, xnt, gain_attn, gain_moe, gains,
        cosine, sine, pos_col, pos_row, select, select_t, chosen, kept_map,
    ) = front(
        capacity, packed, stretch_order, expert_ids[0].T, slot_index[0].T,
        tokens[0], w_query, w_key, w_value, w_out, w_router.T, norm_attn[None], norm_moe[None],
        cotangent[0], head_gains,
    )
    W = W.reshape(width, head_width + 2 * HEAD_DIM)
    WO = WO.reshape(head_width, width)
    PK = PK.reshape(width, pack_width)
    buffer, slot_grad, _, h1, xm, gates, hidden, dgp, dup, slot_dgate = dispatch(
        packed, out_part.reshape(C, rows, width), G.reshape(length, width), tokens[0], PK, gain_moe,
        chosen, kept_map, select, w_gate, w_up, w_down,
    )
    DA, y_part, dh1, small = give_back(
        packed, experts, slot_dgate, select, select_t, gates, PK, h1, gain_moe, cotangent[0],
        xm, hidden, dgp, dup, w_gate, w_up, w_down,
    )
    DA = DA.reshape(length, width)
    grad_out_part = contract_rows(mixed, DA).astype(bf16)
    out_parts = grad_out_part.reshape(S, F, head_width // Q, width)

    def part_of(parts, at):
        return lax.dynamic_index_in_dim(parts, at, 0, keepdims=False)

    out_half, out_other, query_sum, kv_sums, small_sums, tiny_sums, y_parts, *dxn_parts = backward(
        DA, W, WO, q, k, v, xnt, X, cosine, sine, pos_col, pos_row, gains,
        out_parts,
        small.reshape(S, C, F, shard, pack_width),
        y_part.reshape(C, rows, width),
    )
    dxn = dxn_parts[0].astype(f32)
    for i in range(1, C):
        dxn += lax.ppermute(dxn_parts[i], "ctx", [(j, (j + i) % C) for j in range(C)]).astype(f32)
    out_sum, bit = out_half, F // 2
    while True:
        came = lax.ppermute(out_other, "fsdp", [(i, i ^ bit) for i in range(F)])
        out_sum = (out_sum.astype(f32) + came.astype(f32)).astype(bf16)
        bit //= 2
        if not bit:
            break
        mine = lax.rem(fsdp_at // bit, 2)
        parts = out_sum.reshape((2, bit) + out_sum.shape[1:])
        out_sum, out_other = part_of(parts, mine), part_of(parts, 1 - mine)
    out_sum = out_sum[0]
    turn = [(i * C + j, j * S + i) for i in range(S) for j in range(C)]
    o_sum = lax.ppermute(out_sum, ("seq", "ctx"), turn)
    grad_wgate = contract_rows(buffer, dgp)
    grad_wup = contract_rows(buffer, dup)
    grad_wdown = contract_rows(hidden, slot_grad)
    layer_out = (h1 + jnp.sum(y_parts.astype(f32), axis=0)).astype(bf16)
    unit, factor = rms_unit(tokens[0].astype(f32))
    grad_tokens = (dh1 + norm_backward(dxn, unit, factor, gain_attn)).astype(bf16)
    grad_query = query_sum.astype(f32)

    def key_columns(block):
        pieces = block.astype(f32).reshape(KEY_VALUE_HEADS, C // KEY_VALUE_HEADS, shard, HEAD_DIM).sum(axis=1)
        return pieces.transpose(1, 0, 2).reshape(shard, KEY_VALUE_HEADS * HEAD_DIM)

    grad_key = key_columns(kv_sums[:, :, :HEAD_DIM])
    grad_value = key_columns(kv_sums[:, :, HEAD_DIM:])
    small_sum = jnp.sum(small_sums.astype(f32), axis=0)
    tiny_sum = jnp.sum(tiny_sums, axis=0)
    tiny_rows = width // HEAD_DIM
    device = (seq_at * C + ctx_at) * F + fsdp_at
    grad_norm_attn = lax.dynamic_slice_in_dim(
        tiny_sum[:tiny_rows].reshape(width), device * shard, shard
    )
    return (
        layer_out[None],
        grad_tokens[None],
        grad_norm_attn,
        tiny_sum[tiny_rows : tiny_rows + 2],
        grad_query,
        grad_key,
        grad_value,
        o_sum.astype(f32),
        small_sum[:, experts],
        small_sum[:, :experts],
        grad_wgate[None],
        grad_wup[None],
        grad_wdown[None],
    )


def solution(mesh):
    rows = P(("seq", "fsdp"), "ctx", None)
    vector = P(AXES)
    matrix = P(AXES, None)
    cube = P(AXES, None, None)
    return jax.shard_map(
        on_device,
        mesh=mesh,
        in_specs=(
            rows, P(), rows, rows, vector, P(), matrix, matrix, matrix, matrix,
            vector, matrix, cube, cube, cube, rows,
        ),
        out_specs=(
            rows, rows, vector, P(), matrix, matrix, matrix, matrix, vector, matrix,
            cube, cube, cube,
        ),
        check_vma=False,
    )
```

```python
import functools

import jax
import jax.numpy as jnp
import numpy as np
from jax import lax
from jax.experimental import pallas as pl
from jax.experimental.pallas import tpu as pltpu
from jax.sharding import PartitionSpec as P

QUERY_HEADS = 32
KEY_VALUE_HEADS = 4
HEAD_DIM = 128
TOP = 8
AXES = ("seq", "ctx", "fsdp")
MESH = pl.DeviceIdType.MESH
epsilon = 1e-06
rope_base = 1000000.0
VMEM_LIMIT = 56 * 2**20
f32 = jnp.float32
bf16 = jnp.bfloat16


def round_up(value, step):
    return (value + step - 1) // step * step


def place():
    return tuple(lax.axis_index(name) for name in AXES)


def sizes():
    return tuple(lax.axis_size(name) for name in AXES)


def signal(device):
    pl.semaphore_signal(
        pltpu.get_barrier_semaphore(), inc=1, device_id=device, device_id_type=MESH
    )


def remote(src, dst, send, recv, device):
    return pltpu.make_async_remote_copy(
        src_ref=src,
        dst_ref=dst,
        send_sem=send,
        recv_sem=recv,
        device_id=device,
        device_id_type=MESH,
    )


def params(cid, limit=VMEM_LIMIT):
    return pltpu.CompilerParams(
        collective_id=cid, has_side_effects=True, vmem_limit_bytes=limit
    )


ANY = pl.BlockSpec(memory_space=pl.ANY)
DMA = pltpu.SemaphoreType.DMA


def rms_unit(rows):
    factor = lax.rsqrt(jnp.mean(rows * rows, axis=-1, keepdims=True) + epsilon)
    return rows * factor, factor


def norm_backward(grad_scaled, normed, factor, gain):
    grad_normed = grad_scaled * gain
    inner = jnp.mean(grad_normed * normed, axis=-1, keepdims=True)
    return factor * (grad_normed - normed * inner)


def half_turn(rows, cosine, sine):
    return rows * cosine + pltpu.roll(rows, HEAD_DIM // 2, 1) * sine


def score_block(qr, kr, pos_col, pos_row):
    scores = lax.dot_general(
        qr, kr, (((1,), (1,)), ((), ())), preferred_element_type=f32
    ) * (HEAD_DIM**-0.5)
    scores = jnp.where(pos_col >= pos_row, scores, -jnp.inf)
    peak = jnp.max(scores, axis=-1, keepdims=True)
    weight = jnp.exp(scores - peak)
    return weight * (1.0 / jnp.sum(weight, axis=-1, keepdims=True))


def z_neighbours():
    _, C, _ = sizes()
    s, c, f = place()
    return [(s, lax.rem(c + k, C), f) for k in range(1, C)]


def plane_neighbours():
    S, _, F = sizes()
    s, c, f = place()
    Q = S * F
    at = [lax.rem(s * F + f + k, Q) for k in range(1, Q)]
    return at, [(q // F, c, lax.rem(q, F)) for q in at]


def greet_all(peers):
    for peer in peers:
        signal(peer)
    pl.semaphore_wait(pltpu.get_barrier_semaphore(), len(peers))


class Line:
    def __init__(self, own, block, rsend, rrecv, lsend, lrecv):
        s, self.c, f = place()
        self.C = lax.axis_size("ctx")
        self.own, self.block = own, block
        self.sems = (rsend, rrecv, lsend, lrecv)
        self.right = (s, lax.rem(self.c + 1, self.C), f)
        self.left = (s, lax.rem(self.c + self.C - 1, self.C), f)

    def copy(self, rightward, h):
        origin = self.c - h if rightward else self.c + h
        src = self.own if h == 0 else self.block(origin)
        send, recv = self.sems[:2] if rightward else self.sems[2:]
        return remote(
            src, self.block(origin), send.at[h], recv.at[h], self.right if rightward else self.left
        )

    def sends(self, rightward, h):
        if rightward:
            return jnp.logical_and(self.c >= h, self.c < self.C - 1)
        return jnp.logical_and(self.c + h < self.C, self.c > 0)

    def start(self):
        for way in (True, False):
            pl.when(self.sends(way, 0))(self.copy(way, 0).start)

    def hop(self, h):
        for way in (True, False):
            origin = self.c - h if way else self.c + h
            there = origin >= 0 if way else origin < self.C
            landed = remote(
                self.block(origin), self.block(origin),
                self.sems[0 if way else 2].at[h - 1], self.sems[1 if way else 3].at[h - 1],
                self.left if way else self.right,
            )
            pl.when(there)(landed.wait_recv)
            if h < self.C - 1:
                pl.when(self.sends(way, h))(self.copy(way, h).start)

    def finish(self):
        for way in (True, False):
            for h in range(self.C - 1):
                pl.when(self.sends(way, h))(self.copy(way, h).wait_send)


def line_sems(C):
    return [DMA((C - 1,)) for _ in range(4)]


def front_kernel(
    block, capacity, packed, experts,
    order, ids, slot_ids, tokens, wq, wk, wv, wo, router, norm_attn, norm_moe, cot, low_gains, frequency,
    X_out, W_out, WO_out, PK, SM, G, out_out, q_out, k_out, v, mixed_out, xnt_out, gain_attn, gain_moe, gains,
    cosine, sine, pos_col, pos_row, select_out, select_t_out, chosen, kept,
    X, W, WO, xn, kr, pack, out, q, mixed, xnt, select, select_t,
    local, save, zsend, zrecv, fsend, frecv, csend, crecv, wsend, wrecv,
    xrs, xrr, xls, xlr, grs, grr, gls, glr,
):
    S, C, F = sizes()
    s, c, f = place()
    Q = S * F
    rows, width = tokens.shape
    length = C * rows
    head_width = wq.shape[1] // C
    shard = wq.shape[0]
    wide = chosen.shape[1]
    z_peers = z_neighbours()
    f_peers = [(s, c, lax.rem(f + k, F)) for k in range(1, F)]
    sibling = (1 - s, c, f)
    pair = s * C + c
    out_dst = (lax.rem(pair, S), pair // S, f)
    pair_in = c * S + s
    out_src = (pair_in // C, lax.rem(pair_in, C), f)
    stays = jnp.logical_and(out_dst[0] == s, out_dst[1] == c)
    moves = jnp.logical_not(stays)
    greet = (
        jnp.where(stays, 1 - s, out_src[0]),
        jnp.where(stays, C - 1 - c, out_src[1]),
        f,
    )
    def as_column(line):
        size = line.shape[1]
        square = lax.broadcasted_iota(jnp.int32, (size, size), 0) == lax.broadcasted_iota(
            jnp.int32, (size, size), 1
        )
        return jnp.sum(jnp.where(square, line, 0.0), axis=1, keepdims=True)

    lane = lax.broadcasted_iota(jnp.int32, (rows, wide), 1).astype(f32)
    hits = jnp.zeros((rows, wide), f32)
    slot_map = jnp.full((rows, wide), -1.0, f32)
    for j in range(TOP):
        here = lane == as_column(ids[j : j + 1, :].astype(f32))
        slot = jnp.broadcast_to(as_column(slot_ids[j : j + 1, :].astype(f32)), (rows, wide))
        hits = jnp.where(here, 1.0, hits)
        slot_map = jnp.where(jnp.logical_and(here, slot < capacity), slot, slot_map)
    lane = lax.broadcasted_iota(jnp.int32, pack.shape, 1)
    own_lane = lax.broadcasted_iota(jnp.int32, (experts, pack.shape[1]), 0) == lax.broadcasted_iota(
        jnp.int32, (experts, pack.shape[1]), 1
    )
    packed_rows = lax.dot_general(
        router[...], own_lane.astype(bf16), (((0,), (0,)), ((), ())), preferred_element_type=f32
    )
    for i, line in enumerate((norm_attn, norm_moe)):
        packed_rows = jnp.where(lane == experts + i, as_column(line[...].astype(f32)), packed_rows)
    pack[...] = packed_rows.astype(bf16)
    gains[...] = low_gains[...].astype(f32)
    chosen[...] = hits
    kept[...] = (slot_map >= 0.0).astype(f32)
    SM[c] = slot_map
    greet_all(z_peers + f_peers + [sibling, greet])

    def pieces(target):
        kv = (target * KEY_VALUE_HEADS) // C
        q_cols = pl.ds(pl.multiple_of(target * head_width, 128), head_width)
        kv_cols = pl.ds(pl.multiple_of(kv * HEAD_DIM, 128), HEAD_DIM)
        mine = W.at[s, c, f]
        return [
            (wq.at[:, q_cols], mine.at[:, pl.ds(0, head_width)]),
            (wk.at[:, kv_cols], mine.at[:, pl.ds(head_width, HEAD_DIM)]),
            (wv.at[:, kv_cols], mine.at[:, pl.ds(head_width + HEAD_DIM, HEAD_DIM)]),
            (pack, PK.at[s, c, f]),
        ]

    def token_rows(at):
        return X.at[pl.ds(pl.multiple_of(at * rows, 16), rows)]

    own = [
        pltpu.make_async_copy(src, dst, local.at[i])
        for i, (src, dst) in enumerate(pieces(c) + [(tokens, token_rows(c)), (cot, G.at[c])])
    ]
    z_copies = [
        remote(src, dst, zsend.at[i, k], zrecv.at[i, k], peer)
        for k, peer in enumerate(z_peers)
        for i, (src, dst) in enumerate(pieces(peer[1]))
    ]
    slot_copies = [
        remote(SM.at[c], SM.at[c], zsend.at[4, k], zrecv.at[4, k], peer)
        for k, peer in enumerate(z_peers)
    ]
    x_line = Line(tokens, token_rows, xrs, xrr, xls, xlr)
    g_line = Line(cot, lambda at: G.at[at], grs, grr, gls, glr)
    out_copy = remote(wo, WO.at[out_dst[0], f], wsend.at[0], wrecv.at[0], out_dst)
    out_stay = pltpu.make_async_copy(wo, WO.at[s, f], wsend.at[1])
    for copy in own + z_copies + slot_copies:
        copy.start()
    x_line.start()
    pl.when(moves)(out_copy.start)
    pl.when(stays)(out_stay.start)

    where = lax.broadcasted_iota(jnp.int32, (1, length), 1)
    where_col = lax.broadcasted_iota(jnp.int32, (length, 1), 0)
    stretch_rows = rows // 2

    def position(at):
        total = jnp.zeros_like(at)
        for j in range(2 * C):
            base = order[j] * stretch_rows - j * stretch_rows
            total = jnp.where(at // stretch_rows == j, at + base, total)
        return total

    pos_row[...] = position(where)
    pos_col[...] = position(where_col)
    angles = pos_col[...].astype(f32) * frequency[...]
    cosine[...] = jnp.cos(angles)
    turned = jnp.sin(angles)
    sine[...] = jnp.where(
        lax.broadcasted_iota(jnp.int32, turned.shape, 1) < HEAD_DIM // 2, -turned, turned
    )

    for copy in own[:5] + z_copies:
        copy.wait()

    def weight_block(index, at):
        return (W.at[s, :, at], PK.at[s, :, at], WO.at[s, at])[index]

    f_copies = [
        [
            remote(weight_block(i, f), weight_block(i, f), fsend.at[i, k], frecv.at[i, k], peer)
            for k, peer in enumerate(f_peers)
        ]
        for i in range(3)
    ]

    def to_sibling(i, k):
        at = lax.rem(f + F - k, F)
        return remote(weight_block(i, at), weight_block(i, at), csend.at[i, k], crecv.at[i, k], sibling)

    c_copies = [[to_sibling(i, k) for k in range(F)] for i in range(3)]
    for i in range(2):
        for copy in f_copies[i] + c_copies[i][:1]:
            copy.start()
    x_line.hop(1)
    for h in range(2, C - 1):
        x_line.hop(h)
    pl.when(moves)(out_copy.wait)
    pl.when(stays)(out_stay.wait)
    for copy in f_copies[2] + c_copies[2][:1]:
        copy.start()
    for k in range(F - 1):
        for i in range(2):
            f_copies[i][k].wait_recv()
            c_copies[i][k + 1].start()
    for copy in slot_copies:
        copy.wait()
    at = lax.broadcasted_iota(jnp.int32, (wide, Q * packed), 1) // packed
    expert = (at // F * C + c) * F + lax.rem(at, F)
    spread = (lax.broadcasted_iota(jnp.int32, (wide, Q * packed), 0) == expert).astype(bf16)
    slot_rows = SM[...].reshape(length, wide).astype(bf16)
    by_token = jnp.dot(slot_rows, spread, preferred_element_type=f32)
    base = (lax.broadcasted_iota(jnp.int32, by_token.shape, 0) // rows * capacity).astype(f32)
    number = lax.rem(lax.broadcasted_iota(jnp.int32, by_token.shape, 1), packed).astype(f32)
    select_t[...] = jnp.where(
        jnp.logical_and(by_token >= 0.0, by_token + base == number), 1.0, 0.0
    ).astype(bf16)
    at = lax.broadcasted_iota(jnp.int32, (Q, wide), 0)
    expert = (at // F * C + c) * F + lax.rem(at, F)
    spread = (lax.broadcasted_iota(jnp.int32, (Q, wide), 1) == expert).astype(bf16)
    by_slot = lax.dot_general(
        spread, slot_rows, (((1,), (1,)), ((), ())), preferred_element_type=f32
    )
    base = (where // rows * capacity).astype(f32)
    by_slot = jnp.where(by_slot >= 0.0, by_slot + base, -1.0)
    number = lax.broadcasted_iota(jnp.int32, (packed, length), 0).astype(f32)
    for p in range(Q):
        select[p * packed : (p + 1) * packed, :] = jnp.where(
            number == by_slot[p : p + 1, :], 1.0, 0.0
        ).astype(bf16)

    x_line.hop(C - 1)
    g_line.start()
    for i in range(2):
        for copy in c_copies[i]:
            copy.wait()
    saves = [
        pltpu.make_async_copy(src, dst, save.at[i])
        for i, (src, dst) in enumerate(
            (
                (X, X_out), (W, W_out), (select, select_out), (select_t, select_t_out),
                (WO, WO_out), (q, q_out), (mixed, mixed_out), (out, out_out), (xnt, xnt_out),
            )
        )
    ]
    for copy in saves[:4]:
        copy.start()
    across = lax.broadcasted_iota(jnp.int32, (HEAD_DIM, HEAD_DIM), 0)
    diagonal = across == lax.broadcasted_iota(jnp.int32, (HEAD_DIM, HEAD_DIM), 1)
    flat = PK[...].reshape(width, PK.shape[-1]).astype(f32)
    for j in range(width // HEAD_DIM):
        part = slice(j * HEAD_DIM, (j + 1) * HEAD_DIM)
        for i, row in enumerate((gain_attn, gain_moe)):
            line = flat[part, experts + i : experts + i + 1]
            row[:, part] = jnp.sum(jnp.where(diagonal, line, 0.0), axis=0, keepdims=True)

    def norm_rows(i, carry):
        part = pl.ds(i * 64, 64)
        unit, _ = rms_unit(X[part, :].astype(f32))
        xn[part, :] = (unit * gain_attn[...]).astype(bf16)
        return carry

    lax.fori_loop(0, length // 64, norm_rows, 0)

    def weights(cols):
        return W[:, :, :, :, cols].reshape(width, 2 * HEAD_DIM)

    kv = jnp.dot(xn[...], weights(pl.ds(head_width, 2 * HEAD_DIM)), preferred_element_type=f32)
    k_out[...] = kv[:, :HEAD_DIM]
    v[...] = kv[:, HEAD_DIM:].astype(bf16)
    unit, _ = rms_unit(k_out[...])
    kr[...] = half_turn(unit * gains[1:2, :], cosine[...], sine[...]).astype(bf16)

    def head_pair(i, carry):
        cols = pl.ds(pl.multiple_of(i * 2 * HEAD_DIM, 2 * HEAD_DIM), 2 * HEAD_DIM)
        both = jnp.dot(xn[...], weights(cols), preferred_element_type=f32)
        q[:, cols] = both
        for half in range(2):
            lanes = pl.ds(pl.multiple_of((2 * i + half) * HEAD_DIM, HEAD_DIM), HEAD_DIM)
            for part in range(length // block):
                at = slice(part * block, (part + 1) * block)
                unit, _ = rms_unit(both[at, half * HEAD_DIM : (half + 1) * HEAD_DIM])
                qr = half_turn(unit * gains[0:1, :], cosine[at, :], sine[at, :]).astype(bf16)
                probs = score_block(qr, kr[...], pos_col[at, :], pos_row[...])
                mixed[at, lanes] = jnp.dot(
                    probs.astype(bf16), v[...], preferred_element_type=f32
                ).astype(bf16)
        return carry

    pairs = head_width // (2 * HEAD_DIM)
    half_way = pairs // 2
    hops = {}
    for h in range(1, C - 1):
        hops.setdefault(min(pairs, 1 + (h - 1) * pairs // (C - 2)), []).append(h)
    done = 0
    for stop in sorted(set(hops) | {half_way, pairs}):
        lax.fori_loop(done, stop, head_pair, 0)
        done = stop
        for h in hops.get(stop, ()):
            g_line.hop(h)
        if stop == half_way:
            for k in range(F - 1):
                f_copies[2][k].wait_recv()
                c_copies[2][k + 1].start()
    for copy in c_copies[2]:
        copy.wait()
    for copy in saves[4:7]:
        copy.start()

    def project(j, carry):
        cols = pl.ds(pl.multiple_of(j * 256, 256), 256)
        out[:, cols] = jnp.dot(
            mixed[...], WO[:, :, :, cols].reshape(head_width, 256), preferred_element_type=f32
        ).astype(bf16)
        return carry

    lax.fori_loop(0, width // 256, project, 0)
    saves[7].start()

    def turn(j, carry):
        cols = pl.ds(pl.multiple_of(j * 256, 256), 256)
        xnt[cols, :] = xn[:, cols].T
        return carry

    lax.fori_loop(0, width // 256, turn, 0)
    saves[8].start()
    g_line.hop(C - 1)
    x_line.finish()
    g_line.finish()
    for line in f_copies:
        for copy in line:
            copy.wait_send()
    for copy in saves + own[5:]:
        copy.wait()


def front(
    capacity, packed, order, ids, slot_ids, tokens, wq, wk, wv, wo, router, norm_attn, norm_moe, cot, gains
):
    S, C, F = sizes()
    Q = S * F
    rows, width = tokens.shape
    length = C * rows
    shard = wq.shape[0]
    head_width = wq.shape[1] // C
    experts = router.shape[0]
    wide = round_up(experts, 128)
    frequency = np.power(rope_base, -np.arange(HEAD_DIM // 2) * 2.0 / HEAD_DIM)
    frequency = jnp.asarray(np.tile(frequency, 2)[None].astype(np.float32))
    block = min(length, 512)
    sds = jax.ShapeDtypeStruct
    V = pltpu.VMEM
    vm = pl.BlockSpec(memory_space=pltpu.VMEM)
    w_shape = (S, C, F, shard, head_width + 2 * HEAD_DIM)
    wo_shape = (S, F) + wo.shape
    pack_block = (shard, round_up(experts + 2, 128))
    pack_shape = (S, C, F) + pack_block
    return pl.pallas_call(
        functools.partial(front_kernel, block, capacity, packed, experts),
        out_shape=[
            sds((length, width), bf16),
            sds(w_shape, bf16),
            sds(wo_shape, bf16),
            sds(pack_shape, bf16),
            sds((C, rows, wide), f32),
            sds((C, rows, width), bf16),
            sds((length, width), bf16),
            sds((length, head_width), f32),
            sds((length, HEAD_DIM), f32),
            sds((length, HEAD_DIM), bf16),
            sds((length, head_width), bf16),
            sds((width, length), bf16),
            sds((1, width), f32),
            sds((1, width), f32),
            sds(gains.shape, f32),
            sds((length, HEAD_DIM), f32),
            sds((length, HEAD_DIM), f32),
            sds((length, 1), jnp.int32),
            sds((1, length), jnp.int32),
            sds((Q * packed, length), bf16),
            sds((length, Q * packed), bf16),
            sds((rows, wide), f32),
            sds((rows, wide), f32),
        ],
        in_specs=[pl.BlockSpec(memory_space=pltpu.SMEM), vm, vm] + [ANY] * 5 + [vm] * 3 + [ANY, vm, vm],
        out_specs=[ANY] * 3 + [vm, vm] + [ANY] * 3 + [vm] * 2 + [ANY] * 2 + [vm] * 7 + [ANY] * 2 + [vm] * 2,
        scratch_shapes=[
            V((length, width), bf16),
            V(w_shape, bf16),
            V(wo_shape, bf16),
            V((length, width), bf16),
            V((length, HEAD_DIM), bf16),
            V(pack_block, bf16),
            V((length, width), bf16),
            V((length, head_width), f32),
            V((length, head_width), bf16),
            V((width, length), bf16),
            V((Q * packed, length), bf16),
            V((length, Q * packed), bf16),
            DMA((6,)), DMA((9,)),
            DMA((5, C - 1)), DMA((5, C - 1)),
            DMA((3, F - 1)), DMA((3, F - 1)),
            DMA((3, F)), DMA((3, F)),
            DMA((2,)), DMA((1,)),
        ]
        + line_sems(C)
        + line_sems(C),
        name="gather_and_attend",
        compiler_params=params(1, 60 * 2**20),
    )(order, ids, slot_ids, tokens, wq, wk, wv, wo, router, norm_attn, norm_moe, cot, gains, frequency)


CHUNKS = 8


def columns(width, j):
    step = width // CHUNKS
    return pl.ds(j * step, step)


def three_parts(line):
    high = line.astype(bf16).astype(f32)
    rest = line - high
    middle = rest.astype(bf16).astype(f32)
    row = lax.broadcasted_iota(jnp.int32, (16, line.shape[1]), 0)
    rows = jnp.where(row == 0, high, jnp.where(row == 1, middle, jnp.where(row == 2, rest - middle, 0.0)))
    return rows.astype(bf16)


def halves(total):
    return total // 2


def dispatch_kernel(
    packed, out_part, G_in, tokens, pack, gain, chosen, kept, select, w_gate, w_up, w_down,
    buffer_out, gbuf, wrow, h1, xm, gates, hidden_out, dgp_out, dup_out, dgr,
    OP, RB, XM, SL, WM, WS, G, SG, buffer, WG, WU, WD, gp, up, gw, dup,
    local, load, saved, osend, orecv, gsend, grecv, xsend, xrecv, msend, mrecv, bsend, brecv, wsend, wrecv,
):
    S, C, F = sizes()
    s, c, f = place()
    Q = S * F
    q = s * F + f
    rows, width = tokens.shape
    total_rows = Q * packed
    half = halves(total_rows)
    z_peers = z_neighbours()
    p_at, p_peers = plane_neighbours()
    loads = [
        pltpu.make_async_copy(G_in, G, load.at[0]),
        pltpu.make_async_copy(w_down.at[0], WD, load.at[1]),
        pltpu.make_async_copy(w_gate.at[0], WG, load.at[2]),
        pltpu.make_async_copy(w_up.at[0], WU, load.at[3]),
    ]
    for copy in loads:
        copy.start()
    greet_all(z_peers + p_peers)
    mine = pl.ds(pl.multiple_of(q * packed, 16), packed)
    own_rows = pl.ds(pl.multiple_of(c * rows, 16), rows)
    right = (s, lax.rem(c + 1, C), f)
    left = (s, lax.rem(c + C - 1, C), f)

    def rightward(t):
        return remote(OP.at[t], RB.at[t], osend.at[0, t], orecv.at[0, t], right)

    def leftward(t):
        return remote(OP.at[t], RB.at[jnp.where(c - 1 == t, C, t)], osend.at[1, t], orecv.at[1, t], left)

    def merge(t, way):
        remote(OP.at[t], RB.at[t], osend.at[way, t], orecv.at[way, t], left).wait_recv()

        def add(j, carry):
            part = pl.ds(j * 32, 32)
            OP[t, part, :] = (OP[t, part, :].astype(f32) + RB[t, part, :].astype(f32)).astype(bf16)
            return carry

        lax.fori_loop(0, rows // 32, add, 0)

    def pass_on(step):
        t_right = C - 1 + c - step
        t_left = step - (C - 1 - c)

        @pl.when((t_right > c) & (t_right < C) & (c > 0))
        def _():
            merge(t_right, 0)
            rightward(t_right).start()

        @pl.when((t_left >= 0) & (t_left < c) & (c < C - 1))
        def _():
            merge(t_left, 1)
            leftward(t_left).start()

    fetch = pltpu.make_async_copy(out_part, OP, local.at[0])
    fetch.start()
    fetch.wait()

    @pl.when(c == 0)
    def _():
        for t in range(C - 1, 0, -1):
            rightward(t).start()

    @pl.when(c == C - 1)
    def _():
        for t in range(C - 1):
            leftward(t).start()

    loads[0].wait()

    def grad_slots(p):
        at = pl.ds(pl.multiple_of(p * packed, 16), packed)

        def body(j, carry):
            cols = pl.ds(pl.multiple_of(j * 512, 512), 512)
            SG[at, cols] = jnp.dot(select[at, :], G[:, cols], preferred_element_type=f32).astype(bf16)
            return carry

        lax.fori_loop(0, width // 512, body, 0)

    later = []
    for k, peer in enumerate(p_peers):
        theirs = pl.ds(pl.multiple_of(p_at[k] * packed, 16), packed)
        later.append(remote(SG.at[theirs], gbuf.at[mine], gsend.at[k], grecv.at[k], peer))
        grad_slots(p_at[k])
        later[-1].start()
    grad_slots(q)
    later.append(pltpu.make_async_copy(SG.at[mine], gbuf.at[mine], local.at[1]))
    later[-1].start()
    for step in range(1, C - 1):
        pass_on(step)

    @pl.when(c > 0)
    def _():
        remote(OP.at[0], RB.at[c], osend.at[0, c], orecv.at[0, c], left).wait_recv()

    @pl.when(c < C - 1)
    def _():
        remote(OP.at[0], RB.at[C], osend.at[1, c], orecv.at[1, c], right).wait_recv()


    def head_rows(i, carry):
        part = pl.ds(i * 32, 32)
        total = tokens[part, :].astype(f32) + OP[c, part, :].astype(f32)
        total += jnp.where(c > 0, RB[c, part, :].astype(f32), 0.0)
        total += jnp.where(c < C - 1, RB[C, part, :].astype(f32), 0.0)
        h1[part, :] = total
        unit, _ = rms_unit(total)
        normed = (unit * gain[...]).astype(bf16)
        xm[part, :] = normed
        XM[pl.ds(pl.multiple_of(c * rows + i * 32, 16), 32), :] = normed
        return carry

    lax.fori_loop(0, rows // 32, head_rows, 0)
    chunks = []
    for j in range(CHUNKS):
        piece = XM.at[own_rows, columns(width, j)]
        chunks.append(
            [remote(piece, piece, xsend.at[j, k], xrecv.at[j, k], peer) for k, peer in enumerate(z_peers)]
        )
    for copy in chunks[0]:
        copy.start()
    logits = jnp.dot(xm[...], pack[...], preferred_element_type=f32)[:, : chosen.shape[1]]
    logits = jnp.where(chosen[...] > 0.0, logits, -jnp.inf)
    power = jnp.exp(logits - jnp.max(logits, axis=-1, keepdims=True))
    gates[...] = power / jnp.sum(power, axis=-1, keepdims=True)
    WM[own_rows, :] = gates[...] * kept[...]
    row = []
    for k, peer in enumerate(z_peers):
        piece = WM.at[own_rows, :]
        row.append(remote(piece, piece, msend.at[k], mrecv.at[k], peer))
        row[-1].start()
    for line in chunks[1:]:
        for copy in line:
            copy.start()
    sent = []
    for j in range(CHUNKS):
        cols = columns(width, j)
        for copy in chunks[j]:
            copy.wait_recv()

        def slots(i, carry):
            at = pl.ds(pl.multiple_of(i * half, 16), half)
            SL[at, cols] = jnp.dot(select[at, :], XM[:, cols], preferred_element_type=f32).astype(bf16)
            return carry

        lax.fori_loop(0, 2, slots, 0)
        line = []
        for k, peer in enumerate(p_peers):
            theirs = pl.ds(pl.multiple_of(p_at[k] * packed, 16), packed)
            line.append(
                remote(SL.at[theirs, cols], buffer.at[mine, cols], bsend.at[j, k], brecv.at[j, k], peer)
            )
        line.append(pltpu.make_async_copy(SL.at[mine, cols], buffer.at[mine, cols], local.at[4 + j]))
        for copy in line:
            copy.start()
        sent.append(line)
        if j == 0:
            for copy in row:
                copy.wait_recv()
            WS[...] = jnp.zeros_like(WS)

            place_of = lax.broadcasted_iota(jnp.int32, (Q, WM.shape[1]), 0)
            expert = (place_of // F * C + c) * F + lax.rem(place_of, F)
            spread = (lax.broadcasted_iota(jnp.int32, expert.shape, 1) == expert).astype(f32)
            lines = lax.dot_general(
                spread, WM[...], (((1,), (1,)), ((), ())),
                precision=lax.Precision.HIGHEST, preferred_element_type=f32,
            )
            for p in range(Q):
                line = lax.dot_general(
                    three_parts(lines[p : p + 1, :]), select[p * packed : (p + 1) * packed, :],
                    (((1,), (1,)), ((), ())), preferred_element_type=f32,
                )
                WS[p, :, pl.ds(0, packed)] = jnp.broadcast_to(
                    jnp.sum(line, axis=0, keepdims=True), (8, packed)
                )
            scales = [
                remote(WS.at[p_at[k]], wrow.at[q], wsend.at[k], wrecv.at[k], peer)
                for k, peer in enumerate(p_peers)
            ]
            scales.append(pltpu.make_async_copy(WS.at[q], wrow.at[q], local.at[2]))
            for copy in scales:
                copy.start()
        if j == CHUNKS - 2:
            for copy in later + loads[1:]:
                copy.wait()
            reload = pltpu.make_async_copy(gbuf, SG, local.at[3])
            reload.start()
            reload.wait()

            def through_down(i, carry):
                at = pl.ds(pl.multiple_of(i * half, 16), half)
                gw[at, :] = lax.dot_general(
                    SG[at, :], WD[...], (((1,), (1,)), ((), ())), preferred_element_type=f32
                )
                return carry

            lax.fori_loop(0, 2, through_down, 0)
    for j in range(CHUNKS - 1):
        cols = columns(width, j)
        for copy in sent[j]:
            copy.wait()

        def project(i, carry):
            at = pl.ds(pl.multiple_of(i * half, 16), half)
            part = buffer[at, cols]
            one = jnp.dot(part, WG[cols, :], preferred_element_type=f32)
            two = jnp.dot(part, WU[cols, :], preferred_element_type=f32)
            gp[at, :] = one if j == 0 else gp[at, :] + one
            up[at, :] = two if j == 0 else up[at, :] + two
            return carry

        lax.fori_loop(0, 2, project, 0)
    for copy in scales:
        copy.wait()
    diagonal = lax.broadcasted_iota(jnp.int32, (packed, packed), 0) == lax.broadcasted_iota(
        jnp.int32, (packed, packed), 1
    )
    dgr[...] = jnp.zeros_like(dgr)
    cols = columns(width, CHUNKS - 1)
    inner = dup.shape[-1]
    hidden, dgp = SG.at[:, pl.ds(0, inner)], SG.at[:, pl.ds(inner, inner)]

    def saves_of(p):
        at = pl.ds(pl.multiple_of(p * packed, 16), packed)
        pairs = ((buffer, buffer_out), (hidden, hidden_out), (dgp, dgp_out), (dup, dup_out))
        return [
            pltpu.make_async_copy(src.at[at], dst.at[at], saved.at[i, p])
            for i, (src, dst) in enumerate(pairs)
        ]

    def expert_rows(p):
        at = pl.ds(pl.multiple_of(p * packed, 16), packed)
        part = buffer[at, cols]
        gate_pre = gp[at, :] + jnp.dot(part, WG[cols, :], preferred_element_type=f32)
        up_pre = up[at, :] + jnp.dot(part, WU[cols, :], preferred_element_type=f32)
        back = gw[at, :]
        scale = jnp.sum(
            jnp.where(diagonal, wrow[p, 0:1, pl.ds(0, packed)], 0.0), axis=1, keepdims=True
        )
        sigmoid = jax.nn.sigmoid(gate_pre)
        silu = gate_pre * sigmoid
        low = (silu * up_pre).astype(bf16)
        hidden[at, :] = (scale * low.astype(f32)).astype(bf16)
        dgate = jnp.sum(back * low.astype(f32), axis=-1, keepdims=True)
        line = jnp.sum(jnp.where(diagonal, dgate, 0.0), axis=0, keepdims=True)
        dgr[p, :, pl.ds(0, packed)] = jnp.broadcast_to(line, (8, packed))
        dhid = scale * back
        dgp[at, :] = (dhid * up_pre * sigmoid * (1.0 + gate_pre * (1.0 - sigmoid))).astype(bf16)
        dup[at, :] = (dhid * silu).astype(bf16)
        for copy in saves_of(p):
            copy.start()

    sent[CHUNKS - 1][Q - 1].wait()
    expert_rows(q)

    def arrival(k, carry):
        p = lax.rem(q + Q - 1 - k, Q)
        at = pl.ds(pl.multiple_of(p * packed, 16), packed)
        came = (p // F, c, lax.rem(p, F))
        remote(
            SL.at[at, cols], buffer.at[at, cols], bsend.at[CHUNKS - 1, k], brecv.at[CHUNKS - 1, k], came
        ).wait_recv()
        expert_rows(p)
        return carry

    lax.fori_loop(0, Q - 1, arrival, 0)
    for copy in sent[CHUNKS - 1][: Q - 1]:
        copy.wait_send()
    for line in chunks + [row]:
        for copy in line:
            copy.wait_send()

    @pl.when(c < C - 1)
    def _():
        def body(t, carry):
            rightward(t).wait_send()
            return carry

        lax.fori_loop(c + 1, C, body, 0)

    @pl.when(c > 0)
    def _():
        def body(t, carry):
            leftward(t).wait_send()
            return carry

        lax.fori_loop(0, c, body, 0)

    for p in range(Q):
        for copy in saves_of(p):
            copy.wait()


def dispatch(packed, out_part, G, tokens, pack, gain, chosen, kept, select, w_gate, w_up, w_down):
    S, C, F = sizes()
    Q = S * F
    rows, width = tokens.shape
    inner = w_gate.shape[-1]
    lanes = round_up(packed, 128)
    wide = chosen.shape[1]
    V = pltpu.VMEM
    sds = jax.ShapeDtypeStruct
    vm = pl.BlockSpec(memory_space=pltpu.VMEM)
    slots = Q * packed
    return pl.pallas_call(
        functools.partial(dispatch_kernel, packed),
        out_shape=[
            sds((slots, width), bf16),
            sds((slots, width), bf16),
            sds((Q, 8, lanes), f32),
            sds((rows, width), f32),
            sds((rows, width), bf16),
            sds((rows, wide), f32),
            sds((slots, inner), bf16),
            sds((slots, inner), bf16),
            sds((slots, inner), bf16),
            sds((Q, 8, lanes), f32),
        ],
        in_specs=[ANY, ANY] + [vm] * 6 + [ANY] * 3,
        out_specs=[ANY, ANY, vm, vm, vm, vm, ANY, ANY, ANY, vm],
        scratch_shapes=[
            V((C, rows, width), bf16),
            V((C + 1, rows, width), bf16),
            V((C * rows, width), bf16),
            V((slots, width), bf16),
            V((C * rows, wide), f32),
            V((Q, 8, lanes), f32),
            V((C * rows, width), bf16),
            V((slots, width), bf16),
            V((slots, width), bf16),
            V((width, inner), bf16), V((width, inner), bf16), V((inner, width), bf16),
            V((slots, inner), f32), V((slots, inner), f32), V((slots, inner), f32),
            V((slots, inner), bf16),
            DMA((4 + CHUNKS,)),
            DMA((4,)),
            DMA((4, Q)),
            DMA((2, C)), DMA((2, C)),
            DMA((Q - 1,)), DMA((Q - 1,)),
            DMA((CHUNKS, C - 1)), DMA((CHUNKS, C - 1)),
            DMA((C - 1,)), DMA((C - 1,)),
            DMA((CHUNKS, Q - 1)), DMA((CHUNKS, Q - 1)),
            DMA((Q - 1,)), DMA((Q - 1,)),
        ],
        name="dispatch_rows",
        compiler_params=params(3, 62 * 2**20),
    )(out_part, G, tokens, pack, gain, chosen, kept, select, w_gate, w_up, w_down)


def return_kernel(
    packed, experts, dgr, select, select_t, gates, pack, h1, gain, cot, xm, hidden, dgp, dup,
    w_gate, w_up, w_down,
    DA, y_part, dh1, small,
    RD, YB, PART, RX, DG, DGP, RG, DL, din, wy, WG, WU, WD, dlog, gnorm, DXR,
    local, load, dsend, drecv, gsend, grecv, ysend, yrecv, xsend, xrecv, msend, mrecv, *asems,
):
    S, C, F = sizes()
    s, c, f = place()
    Q = S * F
    q = s * F + f
    rows, width = h1.shape
    z_peers = z_neighbours()
    p_at, p_peers = plane_neighbours()
    loads = []
    for j in range(CHUNKS):
        cols = columns(width, j)
        loads.append(
            [
                pltpu.make_async_copy(w_gate.at[0, cols], WG.at[cols], load.at[0, j]),
                pltpu.make_async_copy(w_up.at[0, cols], WU.at[cols], load.at[1, j]),
            ]
        )
    load_down = pltpu.make_async_copy(w_down.at[0], WD, load.at[2, 0])
    for line in loads:
        for copy in line:
            copy.start()
    load_down.start()
    greet_all(z_peers + p_peers)
    half = halves(Q * packed)
    mine = pl.ds(pl.multiple_of(q * packed, 16), packed)
    theirs = [pl.ds(pl.multiple_of(at * packed, 16), packed) for at in p_at]
    inner_products = [
        remote(dgr.at[p_at[k]], DG.at[q], gsend.at[k], grecv.at[k], peer)
        for k, peer in enumerate(p_peers)
    ]
    inner_products.append(pltpu.make_async_copy(dgr.at[q], DG.at[q], local.at[0]))
    for copy in inner_products:
        copy.start()
    chunks = []
    for j in range(CHUNKS):
        cols = columns(width, j)
        for copy in loads[j]:
            copy.wait()

        def expert_in(i, carry):
            at = pl.ds(pl.multiple_of(i * half, 16), half)
            across = (((1,), (1,)), ((), ()))
            total = lax.dot_general(dgp[at, :], WG[cols, :], across, preferred_element_type=f32)
            total += lax.dot_general(dup[at, :], WU[cols, :], across, preferred_element_type=f32)
            din[at, cols] = total.astype(bf16)
            return carry

        lax.fori_loop(0, 2, expert_in, 0)
        line = [
            remote(din.at[theirs[k], cols], RD.at[mine, cols], dsend.at[j, k], drecv.at[j, k], peer)
            for k, peer in enumerate(p_peers)
        ]
        line.append(pltpu.make_async_copy(din.at[mine, cols], RD.at[mine, cols], local.at[2 + j]))
        for copy in line:
            copy.start()
        chunks.append(line)
    load_down.wait()
    def expert_out(i, carry):
        at = pl.ds(pl.multiple_of(i * half, 16), half)

        def body(j, carry):
            cols = pl.ds(pl.multiple_of(j * 512, 512), 512)
            y = jnp.dot(hidden[at, :], WD[:, cols], preferred_element_type=f32)
            wy[at, cols] = y.astype(bf16)
            return carry

        return lax.fori_loop(0, width // 512, body, carry)

    lax.fori_loop(0, 2, expert_out, 0)
    sums = []
    for j in range(CHUNKS):
        cols = columns(width, j)
        for copy in chunks[j]:
            copy.wait()

        def combine(i, carry):
            lanes = pl.ds(pl.multiple_of(j * (width // CHUNKS) + i * 256, 256), 256)
            PART[:, lanes] = jnp.dot(
                select_t[...], RD[:, lanes], preferred_element_type=f32
            ).astype(bf16)
            return carry

        lax.fori_loop(0, width // CHUNKS // 256, combine, 0)
        for k, peer in enumerate(z_peers):
            src = PART.at[pl.ds(pl.multiple_of(peer[1] * rows, 16), rows), cols]
            sums.append(remote(src, RX.at[k, :, cols], xsend.at[j, k], xrecv.at[j, k], peer))
            sums[-1].start()
    ys = [
        remote(wy.at[theirs[k]], YB.at[mine], ysend.at[k], yrecv.at[k], peer)
        for k, peer in enumerate(p_peers)
    ]
    ys.append(pltpu.make_async_copy(wy.at[mine], YB.at[mine], local.at[1]))
    for copy in ys:
        copy.start()
    for copy in inner_products:
        copy.wait()
    wide = gates.shape[1]
    place_of = lax.broadcasted_iota(jnp.int32, (Q, wide), 0)
    expert = (place_of // F * C + c) * F + lax.rem(place_of, F)
    spread = (lax.broadcasted_iota(jnp.int32, (Q, wide), 1) == expert).astype(f32)

    for p in range(Q):
        at = pl.ds(p * packed, packed)
        line = jnp.dot(
            three_parts(DG[p, 0:1, pl.ds(0, packed)]), select[at, :], preferred_element_type=f32
        )
        DL[pl.ds(p, 1), :] = jnp.sum(line, axis=0, keepdims=True)
    DGP[...] = lax.dot_general(
        DL[...], spread, (((0,), (0,)), ((), ())),
        precision=lax.Precision.HIGHEST, preferred_element_type=f32,
    ).reshape(DGP.shape)
    more = []
    for k, peer in enumerate(z_peers):
        more.append(remote(DGP.at[peer[1]], RG.at[k], msend.at[k], mrecv.at[k], peer))
        more[-1].start()
    for copy in more:
        copy.wait()
    total = DGP[c]
    for k in range(C - 1):
        total = total + RG[k]
    dlogits = gates[...] * (total - jnp.sum(gates[...] * total, axis=-1, keepdims=True))
    dlog[...] = dlogits.astype(bf16)
    gnorm[...] = jnp.zeros_like(gnorm)
    DXR[...] = lax.dot_general(
        dlog[...], pack[:, pl.ds(0, wide)], (((1,), (1,)), ((), ())), preferred_element_type=f32
    )
    for copy in sums:
        copy.wait()

    def head_rows(i, carry):
        part = pl.ds(i * 32, 32)
        mine_part = pl.ds(pl.multiple_of(c * rows + i * 32, 16), 32)
        dxm = PART[mine_part, :].astype(f32)
        for k in range(C - 1):
            dxm = dxm + RX[k, part, :].astype(f32)
        dxm = dxm + DXR[part, :]
        unit, factor = rms_unit(h1[part, :])
        gnorm[...] += jnp.sum(dxm * unit, axis=0, keepdims=True)
        grad = cot[part, :].astype(f32) + norm_backward(dxm, unit, factor, gain[...])
        dh1[part, :] = grad
        RX[0, part, :] = grad.astype(bf16)
        return carry

    lax.fori_loop(0, rows // 32, head_rows, 0)
    keep = pltpu.make_async_copy(RX.at[0], DA.at[c], local.at[2 + CHUNKS])
    keep.start()
    line = Line(RX.at[0], lambda at: DA.at[at], *asems)
    line.start()
    for h in range(1, C - 1):
        line.hop(h)
    square = lax.broadcasted_iota(jnp.int32, (HEAD_DIM, HEAD_DIM), 0) == lax.broadcasted_iota(
        jnp.int32, (HEAD_DIM, HEAD_DIM), 1
    )
    small[...] = jnp.zeros_like(small)

    def small_rows(i, carry):
        at = pl.ds(pl.multiple_of(i * HEAD_DIM, HEAD_DIM), HEAD_DIM)
        router_part = lax.dot_general(
            xm[:, at], dlog[...], (((0,), (0,)), ((), ())), preferred_element_type=f32
        )
        column = jnp.sum(jnp.where(square, gnorm[:, at], 0.0), axis=1, keepdims=True)
        if wide > experts:
            lane = lax.broadcasted_iota(jnp.int32, router_part.shape, 1)
            small[at, :] = jnp.where(lane == experts, column, router_part).astype(bf16)
        else:
            small[at, pl.ds(0, wide)] = router_part.astype(bf16)
            lane = lax.broadcasted_iota(jnp.int32, (HEAD_DIM, HEAD_DIM), 1)
            small[at, pl.ds(wide, HEAD_DIM)] = jnp.where(lane == 0, column, 0.0).astype(bf16)
        return carry

    lax.fori_loop(0, width // HEAD_DIM, small_rows, 0)
    for copy in ys:
        copy.wait()

    def combine_y(i, carry):
        lanes = pl.ds(pl.multiple_of(i * 256, 256), 256)
        y_part[:, lanes] = jnp.dot(
            select_t[...], YB[:, lanes], preferred_element_type=f32
        ).astype(bf16)
        return carry

    lax.fori_loop(0, width // 256, combine_y, 0)
    line.hop(C - 1)
    line.finish()
    keep.wait()


def give_back(
    packed, experts, dgr, select, select_t, gates, pack, h1, gain, cot, xm, hidden, dgp, dup, w_gate, w_up, w_down
):
    S, C, F = sizes()
    Q = S * F
    rows, width = h1.shape
    wide = gates.shape[1]
    inner = w_gate.shape[-1]
    V = pltpu.VMEM
    sds = jax.ShapeDtypeStruct
    vm = pl.BlockSpec(memory_space=pltpu.VMEM)
    return pl.pallas_call(
        functools.partial(return_kernel, packed, experts),
        out_shape=[
            sds((C, rows, width), bf16),
            sds((C * rows, width), bf16),
            sds((rows, width), f32),
            sds(pack.shape, bf16),
        ],
        in_specs=[vm] * 12 + [ANY] * 3,
        out_specs=[ANY] + [vm] * 3,
        scratch_shapes=[
            V((Q * packed, width), bf16),
            V((Q * packed, width), bf16),
            V((C * rows, width), bf16),
            V((C - 1, rows, width), bf16),
            V(dgr.shape, f32),
            V((C, rows, wide), f32),
            V((C - 1, rows, wide), f32),
            V((Q, C * rows), f32),
            V((Q * packed, width), bf16),
            V((Q * packed, width), bf16),
            V((width, inner), bf16), V((width, inner), bf16), V((inner, width), bf16),
            V((rows, wide), bf16),
            V((1, width), f32),
            V((rows, width), f32),
            DMA((3 + CHUNKS,)),
            DMA((3, CHUNKS)),
            DMA((CHUNKS, Q - 1)), DMA((CHUNKS, Q - 1)),
            DMA((Q - 1,)), DMA((Q - 1,)),
            DMA((Q - 1,)), DMA((Q - 1,)),
            DMA((CHUNKS, C - 1)), DMA((CHUNKS, C - 1)),
            DMA((C - 1,)), DMA((C - 1,)),
        ]
        + line_sems(C),
        name="return_grads",
        compiler_params=params(5, 62 * 2**20),
    )(dgr, select, select_t, gates, pack, h1, gain, cot, xm, hidden, dgp, dup, w_gate, w_up, w_down)


def backward_kernel(
    block, da, w_in, wo, q, k, v, xnt_in, x_in, cosine, sine, pos_col, pos_row, gains, go, sp, yp,
    OH, OX, Q3, KV3, S3, T3, YP, *rest,
):
    DX = rest[: lax.axis_size("ctx")]
    (
    w, xnt, x, late, dxn, dxsem, kr, dkr, dv, acc, DQ, head_grad,
        GQ, Q1, Q2, QS, o_own, o_in, s_own, s_in, s_plane, s_sum, T, t_in, t_plane, t_sum,
        local, qlocal, csend, crecv, fsend, frecv, zsend, zrecv, qcs, qcr, qfs, qfr, qzs, qzr, ysend, yrecv,
    ) = rest[lax.axis_size("ctx") :]
    S, C, F = sizes()
    s, c, f = place()
    step = pl.program_id(0)
    units = GQ.shape[0]
    pairs = units - 1
    length, width = x.shape
    wide = 2 * HEAD_DIM
    late_loads = [
        pltpu.make_async_copy(src, dst, late.at[i])
        for i, (src, dst) in enumerate(((xnt_in, xnt), (w_in, w), (x_in, x)))
    ]
    z_peers = z_neighbours()
    f_peers = [(s, c, lax.rem(f + k, F)) for k in range(1, F)]
    sibling = (1 - s, c, f)
    cols = pl.ds(pl.multiple_of(step * wide, wide), wide)

    o_first = remote(go.at[1 - s], o_in, csend.at[0], crecv.at[0], sibling)
    t_first = remote(T, t_in, csend.at[2], crecv.at[2], sibling)
    o_load = pltpu.make_async_copy(go.at[s], o_own, local.at[0])
    half = F // 2
    mine = lax.rem(f // half, 2)
    o_saves = [
        pltpu.make_async_copy(o_own.at[pl.ds(mine * half, half)], OH, local.at[2]),
        pltpu.make_async_copy(o_own.at[pl.ds((1 - mine) * half, half)], OX, local.at[6]),
    ]
    s_first = remote(sp.at[1 - s], s_in, csend.at[1], crecv.at[1], sibling)
    s_load = pltpu.make_async_copy(sp.at[s], s_own, local.at[1])
    f_at = list(enumerate(f_peers))
    z_at = list(enumerate(z_peers))
    s_second = [remote(s_own.at[:, p[2]], s_plane.at[k], fsend.at[1, k], frecv.at[1, k], p) for k, p in f_at]
    t_second = [remote(T, t_plane.at[k], fsend.at[2, k], frecv.at[2, k], p) for k, p in f_at]
    s_third = [remote(s_sum.at[p[1]], S3.at[c], zsend.at[1, k], zrecv.at[1, k], p) for k, p in z_at]
    s_third.append(pltpu.make_async_copy(s_sum.at[c], S3.at[c], local.at[3]))
    t_third = [remote(t_sum, T3.at[c], zsend.at[2, k], zrecv.at[2, k], p) for k, p in z_at]
    t_third.append(pltpu.make_async_copy(t_sum, T3.at[c], local.at[4]))
    y_copies = [remote(yp.at[p[1]], YP.at[c], ysend.at[k], yrecv.at[k], p) for k, p in z_at]
    y_copies.append(pltpu.make_async_copy(yp.at[c], YP.at[c], local.at[5]))

    def q_first(u):
        return remote(GQ.at[u, 1 - s], Q1.at[u], qcs.at[u], qcr.at[u], sibling)

    def q_second(u):
        return [remote(GQ.at[u, s, :, p[2]], Q2.at[u, k], qfs.at[u, k], qfr.at[u, k], p) for k, p in f_at]

    def q_third(u):
        if isinstance(u, int) and u == pairs:
            landing = KV3.at[c]
        else:
            landing = Q3.at[:, pl.ds(pl.multiple_of(c * pairs * wide + u * wide, wide), wide)]
        copies = [
            remote(QS.at[u, p[1]], landing, qzs.at[u, k], qzr.at[u, k], p) for k, p in z_at
        ]
        copies.append(pltpu.make_async_copy(QS.at[u, c], landing, qlocal.at[u]))
        return copies

    def to_plane(u):
        q_first(u).wait()

        def body(i, carry):
            at = (u, s, i // F, lax.rem(i, F))
            GQ[at] = (GQ[at].astype(f32) + Q1[u, i // F, lax.rem(i, F)].astype(f32)).astype(bf16)
            return carry

        lax.fori_loop(0, C * F, body, 0)
        for copy in q_second(u):
            copy.start()

    def to_ctx(u):
        for copy in q_second(u):
            copy.wait()

        def body(i, carry):
            total = GQ[u, s, i, f].astype(f32)
            for k in range(F - 1):
                total = total + Q2[u, k, i].astype(f32)
            QS[u, i] = total.astype(bf16)
            return carry

        lax.fori_loop(0, C, body, 0)
        for copy in q_third(u):
            copy.start()

    @pl.when(step == 0)
    def _():
        for copy in late_loads:
            copy.start()
        greet_all(z_peers + f_peers + [sibling])
        for copy in [s_first, s_load, o_first, o_load] + y_copies:
            copy.start()
        unit, _ = rms_unit(k[...])
        kr[...] = half_turn(unit * gains[1:2, :], cosine[...], sine[...]).astype(bf16)
        dkr[...] = jnp.zeros_like(dkr)
        dv[...] = jnp.zeros_like(dv)
        head_grad[...] = jnp.zeros_like(head_grad)
        acc[...] = jnp.zeros_like(acc)

    @pl.when(step >= 1)
    def _():
        to_plane(step - 1)

    @pl.when(step == 1)
    def _():
        o_first.wait()
        o_load.wait()

        def o_body(i, carry):
            o_own[i] = (o_own[i].astype(f32) + o_in[i].astype(f32)).astype(bf16)
            return carry

        lax.fori_loop(0, F, o_body, 0)
        for copy in o_saves:
            copy.start()
        s_first.wait()
        s_load.wait()

        def s_body(i, carry):
            at = (i // F, lax.rem(i, F))
            s_own[at] = (s_own[at].astype(f32) + s_in[at].astype(f32)).astype(bf16)
            return carry

        lax.fori_loop(0, C * F, s_body, 0)
        for copy in s_second:
            copy.start()

    @pl.when(step >= 2)
    def _():
        to_ctx(step - 2)

    @pl.when(step == 2)
    def _():
        for copy in s_second:
            copy.wait()

        def s_body(i, carry):
            total = s_own[i, f].astype(f32)
            for k in range(F - 1):
                total = total + s_plane[k, i].astype(f32)
            s_sum[i] = total.astype(bf16)
            return carry

        lax.fori_loop(0, C, s_body, 0)
        for copy in s_third:
            copy.start()

    @pl.when(step < pairs)
    def _():
        dm = lax.dot_general(
            da[...], wo[cols, :], (((1,), (1,)), ((), ())), preferred_element_type=f32
        ).astype(bf16)
        for half in range(2):
            lanes = slice(half * HEAD_DIM, (half + 1) * HEAD_DIM)
            for part in range(length // block):
                rows = slice(part * block, (part + 1) * block)
                unit, factor = rms_unit(q[rows, lanes])
                cos, sin = cosine[rows, :], sine[rows, :]
                qr = half_turn(unit * gains[0:1, :], cos, sin).astype(bf16)
                keys = kr[...]
                probs = score_block(qr, keys, pos_col[rows, :], pos_row[...])
                dmh = dm[rows, lanes]
                dprobs = lax.dot_general(
                    dmh, v[...], (((1,), (1,)), ((), ())), preferred_element_type=f32
                )
                delta = jnp.sum(probs * dprobs, axis=-1, keepdims=True)
                dscores = (probs * (dprobs - delta)).astype(bf16)
                dqr = jnp.dot(dscores, keys, preferred_element_type=f32) * (HEAD_DIM**-0.5)
                rows_in = (((0,), (0,)), ((), ()))
                dkr[...] += lax.dot_general(dscores, qr, rows_in, preferred_element_type=f32) * (
                    HEAD_DIM**-0.5
                )
                dv[...] += lax.dot_general(
                    probs.astype(bf16), dmh, rows_in, preferred_element_type=f32
                )
                dqs = half_turn(dqr, cos, -sin)
                head_grad[0:1, :] += jnp.sum(dqs * unit, axis=0, keepdims=True)
                DQ[rows, lanes] = norm_backward(dqs, unit, factor, gains[0:1, :]).astype(bf16)

    @pl.when(step == pairs)
    def _():
        unit, factor = rms_unit(k[...])
        dks = half_turn(dkr[...], cosine[...], -sine[...])
        head_grad[1:2, :] += jnp.sum(dks * unit, axis=0, keepdims=True)
        DQ[:, :HEAD_DIM] = norm_backward(dks, unit, factor, gains[1:2, :]).astype(bf16)
        DQ[:, HEAD_DIM:] = dv[...].astype(bf16)

    @pl.when(step == 0)
    def _():
        for copy in late_loads:
            copy.wait()

    def weight_rows(i, carry):
        part = F * GQ.shape[4]
        rows = pl.ds(pl.multiple_of(i * part, 16), part)
        piece = jnp.dot(xnt[rows, :], DQ[...], preferred_element_type=f32)
        GQ[step, i // C, lax.rem(i, C)] = piece.astype(bf16).reshape(GQ.shape[3:])
        return carry

    lax.fori_loop(0, S * C, weight_rows, 0)
    q_first(step).start()
    for j in range(4):
        part = pl.ds(j * (width // 4), width // 4)
        acc[:, part] += lax.dot_general(
            DQ[...], w[part, cols], (((1,), (1,)), ((), ())), preferred_element_type=f32
        )

    @pl.when(step == pairs)
    def _():
        to_ctx(pairs - 1)
        to_plane(pairs)
        rows_of = width // HEAD_DIM
        total = jnp.zeros((1, width), f32)

        def finish(i, total):
            rows = pl.ds(i * 64, 64)
            unit, _ = rms_unit(x[rows, :].astype(f32))
            term = acc[rows, :]
            dxn[rows, :] = term.astype(bf16)
            return total + jnp.sum(term * unit, axis=0, keepdims=True)

        total = lax.fori_loop(0, length // 64, finish, total)
        rows = length // C
        x_saves = [
            pltpu.make_async_copy(
                dxn.at[pl.ds(pl.multiple_of(lax.rem(c + i, C) * rows, 16), rows)], DX[i], dxsem.at[i]
            )
            for i in range(C)
        ]
        for copy in x_saves:
            copy.start()
        for r in range(rows_of):
            T[r : r + 1, :] = total[:, r * HEAD_DIM : (r + 1) * HEAD_DIM]
        T[rows_of:, :] = head_grad[...]
        t_first.start()
        t_first.wait()
        T[...] = T[...] + t_in[...]
        for copy in t_second:
            copy.start()
        to_ctx(pairs)
        for copy in t_second:
            copy.wait()
        order = []
        for g in range(F):
            term = jnp.zeros_like(T)
            for k in range(F - 1):
                came = lax.rem(f + F - (k + 1), F)
                term = term + jnp.where(came == g, t_plane[k], 0.0)
            order.append(term + jnp.where(f == g, T[...], 0.0))
        total = order[0]
        for term in order[1:]:
            total = total + term
        t_sum[...] = total
        for copy in t_third:
            copy.start()
        for copy in s_third + y_copies + o_saves + t_third + x_saves:
            copy.wait()
        for u in range(units):
            for copy in q_third(u):
                copy.wait()


def backward(da, w, wo, q, k, v, xnt, x, cosine, sine, pos_col, pos_row, gains, go, sp, yp):
    S, C, F = sizes()
    length, width = x.shape
    head_width = wo.shape[0]
    pairs = head_width // (2 * HEAD_DIM)
    units = pairs + 1
    shard = sp.shape[3]
    block = min(length, 512)
    wide = 2 * HEAD_DIM
    once = pl.Buffered(buffer_count=1)
    whole = lambda array: pl.BlockSpec(array.shape, lambda i: (0, 0), pipeline_mode=once)
    sds = jax.ShapeDtypeStruct
    V = pltpu.VMEM
    q_block, o_block, s_block = (shard, wide), go.shape[2:], sp.shape[3:]
    t_block = (width // HEAD_DIM + 8, HEAD_DIM)
    return pl.pallas_call(
        functools.partial(backward_kernel, block),
        out_shape=[
            sds((F // 2,) + o_block, bf16),
            sds((F // 2,) + o_block, bf16),
            sds((shard, C * head_width), bf16),
            sds((C, shard, wide), bf16),
            sds((C,) + s_block, bf16),
            sds((C,) + t_block, f32),
            sds(yp.shape, bf16),
        ]
        + [sds((length // C, width), bf16)] * C,
        grid=(units,),
        in_specs=[whole(da), ANY, whole(wo)]
        + [pl.BlockSpec((length, wide), lambda i: (0, jnp.minimum(i, pairs - 1)))]
        + [whole(k), whole(v), ANY, ANY]
        + [whole(array) for array in (cosine, sine, pos_col, pos_row, gains)]
        + [ANY] * 3,
        out_specs=[ANY] * (7 + C),
        scratch_shapes=[
            V(w.shape, bf16), V(xnt.shape, bf16), V(x.shape, bf16), DMA((3,)),
            V((length, width), bf16), DMA((C,)),
            V((length, HEAD_DIM), bf16), V((length, HEAD_DIM), f32), V((length, HEAD_DIM), f32),
            V((length, width), f32), V((length, wide), bf16), V((8, HEAD_DIM), f32),
            V((units, S, C, F) + q_block, bf16), V((units, C, F) + q_block, bf16),
            V((units, F - 1, C) + q_block, bf16), V((units, C) + q_block, bf16),
            V((F,) + o_block, bf16), V((F,) + o_block, bf16),
            V((C, F) + s_block, bf16), V((C, F) + s_block, bf16), V((F - 1, C) + s_block, bf16), V((C,) + s_block, bf16),
            V(t_block, f32), V(t_block, f32), V((F - 1,) + t_block, f32), V(t_block, f32),
            DMA((7,)), DMA((units,)),
            DMA((3,)), DMA((3,)), DMA((3, F - 1)), DMA((3, F - 1)), DMA((3, C - 1)), DMA((3, C - 1)),
            DMA((units,)), DMA((units,)), DMA((units, F - 1)), DMA((units, F - 1)),
            DMA((units, C - 1)), DMA((units, C - 1)), DMA((C - 1,)), DMA((C - 1,)),
        ],
        name="attention_backward",
        compiler_params=params(7, 60 * 2**20),
    )(da, w, wo, q, k, v, xnt, x, cosine, sine, pos_col, pos_row, gains, go, sp, yp)


def dot(left, right):
    return jnp.dot(left, right, preferred_element_type=f32)


def contract_rows(left, right):
    return lax.dot_general(left, right, (((0,), (0,)), ((), ())), preferred_element_type=f32)


def times_transpose(left, right):
    return lax.dot_general(left, right, (((1,), (1,)), ((), ())), preferred_element_type=f32)


def on_device(
    tokens,
    stretch_order,
    expert_ids,
    slot_index,
    norm_attn,
    head_gains,
    w_query,
    w_key,
    w_value,
    w_out,
    norm_moe,
    w_router,
    w_gate,
    w_up,
    w_down,
    cotangent,
):
    S, C, F = sizes()
    Q = S * F
    seq_at, ctx_at, fsdp_at = place()
    rows, width = tokens.shape[1:]
    length = C * rows
    experts = w_router.shape[1]
    capacity = rows * TOP // (Q * C) + 1
    packed = round_up(C * capacity, 16)
    lanes = round_up(packed, 128)
    head_width = w_query.shape[1] // C
    shard = w_router.shape[0]
    pack_width = round_up(experts + 2, 128)
    (
        X, W, WO, PK, _, G, out_part, q, k, v, mixed, xnt, gain_attn, gain_moe, gains,
        cosine, sine, pos_col, pos_row, select, select_t, chosen, kept_map,
    ) = front(
        capacity, packed, stretch_order, expert_ids[0].T, slot_index[0].T,
        tokens[0], w_query, w_key, w_value, w_out, w_router.T, norm_attn[None], norm_moe[None],
        cotangent[0], head_gains,
    )
    W = W.reshape(width, head_width + 2 * HEAD_DIM)
    WO = WO.reshape(head_width, width)
    PK = PK.reshape(width, pack_width)
    buffer, slot_grad, _, h1, xm, gates, hidden, dgp, dup, slot_dgate = dispatch(
        packed, out_part.reshape(C, rows, width), G.reshape(length, width), tokens[0], PK, gain_moe,
        chosen, kept_map, select, w_gate, w_up, w_down,
    )
    DA, y_part, dh1, small = give_back(
        packed, experts, slot_dgate, select, select_t, gates, PK, h1, gain_moe, cotangent[0],
        xm, hidden, dgp, dup, w_gate, w_up, w_down,
    )
    DA = DA.reshape(length, width)
    grad_out_part = contract_rows(mixed, DA).astype(bf16)
    out_parts = grad_out_part.reshape(S, F, head_width // Q, width)

    def part_of(parts, at):
        return lax.dynamic_index_in_dim(parts, at, 0, keepdims=False)

    out_half, out_other, query_sum, kv_sums, small_sums, tiny_sums, y_parts, *dxn_parts = backward(
        DA, W, WO, q, k, v, xnt, X, cosine, sine, pos_col, pos_row, gains,
        out_parts,
        small.reshape(S, C, F, shard, pack_width),
        y_part.reshape(C, rows, width),
    )
    dxn = dxn_parts[0].astype(f32)
    for i in range(1, C):
        dxn += lax.ppermute(dxn_parts[i], "ctx", [(j, (j + i) % C) for j in range(C)]).astype(f32)
    out_sum, bit = out_half, F // 2
    while True:
        came = lax.ppermute(out_other, "fsdp", [(i, i ^ bit) for i in range(F)])
        out_sum = (out_sum.astype(f32) + came.astype(f32)).astype(bf16)
        bit //= 2
        if not bit:
            break
        mine = lax.rem(fsdp_at // bit, 2)
        parts = out_sum.reshape((2, bit) + out_sum.shape[1:])
        out_sum, out_other = part_of(parts, mine), part_of(parts, 1 - mine)
    out_sum = out_sum[0]
    turn = [(i * C + j, j * S + i) for i in range(S) for j in range(C)]
    o_sum = lax.ppermute(out_sum, ("seq", "ctx"), turn)
    grad_wgate = contract_rows(buffer, dgp)
    grad_wup = contract_rows(buffer, dup)
    grad_wdown = contract_rows(hidden, slot_grad)
    layer_out = (h1 + jnp.sum(y_parts.astype(f32), axis=0)).astype(bf16)
    unit, factor = rms_unit(tokens[0].astype(f32))
    grad_tokens = (dh1 + norm_backward(dxn, unit, factor, gain_attn)).astype(bf16)
    grad_query = query_sum.astype(f32)

    def key_columns(block):
        pieces = block.astype(f32).reshape(KEY_VALUE_HEADS, C // KEY_VALUE_HEADS, shard, HEAD_DIM).sum(axis=1)
        return pieces.transpose(1, 0, 2).reshape(shard, KEY_VALUE_HEADS * HEAD_DIM)

    grad_key = key_columns(kv_sums[:, :, :HEAD_DIM])
    grad_value = key_columns(kv_sums[:, :, HEAD_DIM:])
    small_sum = jnp.sum(small_sums.astype(f32), axis=0)
    tiny_sum = jnp.sum(tiny_sums, axis=0)
    tiny_rows = width // HEAD_DIM
    device = (seq_at * C + ctx_at) * F + fsdp_at
    grad_norm_attn = lax.dynamic_slice_in_dim(
        tiny_sum[:tiny_rows].reshape(width), device * shard, shard
    )
    return (
        layer_out[None],
        grad_tokens[None],
        grad_norm_attn,
        tiny_sum[tiny_rows : tiny_rows + 2],
        grad_query,
        grad_key,
        grad_value,
        o_sum.astype(f32),
        small_sum[:, experts],
        small_sum[:, :experts],
        grad_wgate[None],
        grad_wup[None],
        grad_wdown[None],
    )


def solution(mesh):
    rows = P(("seq", "fsdp"), "ctx", None)
    vector = P(AXES)
    matrix = P(AXES, None)
    cube = P(AXES, None, None)
    return jax.shard_map(
        on_device,
        mesh=mesh,
        in_specs=(
            rows, P(), rows, rows, vector, P(), matrix, matrix, matrix, matrix,
            vector, matrix, cube, cube, cube, rows,
        ),
        out_specs=(
            rows, rows, vector, P(), matrix, matrix, matrix, matrix, vector, matrix,
            cube, cube, cube,
        ),
        check_vma=False,
    )
```

```python
import functools

import jax
import jax.numpy as jnp
import numpy as np
from jax import lax
from jax.experimental import pallas as pl
from jax.experimental.pallas import tpu as pltpu
from jax.sharding import PartitionSpec as P

QUERY_HEADS = 32
KEY_VALUE_HEADS = 4
HEAD_DIM = 128
TOP = 8
AXES = ("seq", "ctx", "fsdp")
MESH = pl.DeviceIdType.MESH
epsilon = 1e-06
rope_base = 1000000.0
VMEM_LIMIT = 56 * 2**20
f32 = jnp.float32
bf16 = jnp.bfloat16


def round_up(value, step):
    return (value + step - 1) // step * step


def place():
    return tuple(lax.axis_index(name) for name in AXES)


def sizes():
    return tuple(lax.axis_size(name) for name in AXES)


def signal(device):
    pl.semaphore_signal(
        pltpu.get_barrier_semaphore(), inc=1, device_id=device, device_id_type=MESH
    )


def remote(src, dst, send, recv, device):
    return pltpu.make_async_remote_copy(
        src_ref=src,
        dst_ref=dst,
        send_sem=send,
        recv_sem=recv,
        device_id=device,
        device_id_type=MESH,
    )


def params(cid, limit=VMEM_LIMIT):
    return pltpu.CompilerParams(
        collective_id=cid, has_side_effects=True, vmem_limit_bytes=limit
    )


ANY = pl.BlockSpec(memory_space=pl.ANY)
DMA = pltpu.SemaphoreType.DMA


def rms_unit(rows):
    factor = lax.rsqrt(jnp.mean(rows * rows, axis=-1, keepdims=True) + epsilon)
    return rows * factor, factor


def norm_backward(grad_scaled, normed, factor, gain):
    grad_normed = grad_scaled * gain
    inner = jnp.mean(grad_normed * normed, axis=-1, keepdims=True)
    return factor * (grad_normed - normed * inner)


def half_turn(rows, cosine, sine):
    return rows * cosine + pltpu.roll(rows, HEAD_DIM // 2, 1) * sine


def score_block(qr, kr, pos_col, pos_row):
    scores = lax.dot_general(
        qr, kr, (((1,), (1,)), ((), ())), preferred_element_type=f32
    ) * (HEAD_DIM**-0.5)
    scores = jnp.where(pos_col >= pos_row, scores, -jnp.inf)
    peak = jnp.max(scores, axis=-1, keepdims=True)
    weight = jnp.exp(scores - peak)
    return weight * (1.0 / jnp.sum(weight, axis=-1, keepdims=True))


def z_neighbours():
    _, C, _ = sizes()
    s, c, f = place()
    return [(s, lax.rem(c + k, C), f) for k in range(1, C)]


def plane_neighbours():
    S, _, F = sizes()
    s, c, f = place()
    Q = S * F
    at = [lax.rem(s * F + f + k, Q) for k in range(1, Q)]
    return at, [(q // F, c, lax.rem(q, F)) for q in at]


def greet_all(peers):
    for peer in peers:
        signal(peer)
    pl.semaphore_wait(pltpu.get_barrier_semaphore(), len(peers))


class Line:
    def __init__(self, own, block, rsend, rrecv, lsend, lrecv):
        s, self.c, f = place()
        self.C = lax.axis_size("ctx")
        self.own, self.block = own, block
        self.sems = (rsend, rrecv, lsend, lrecv)
        self.right = (s, lax.rem(self.c + 1, self.C), f)
        self.left = (s, lax.rem(self.c + self.C - 1, self.C), f)

    def copy(self, rightward, h):
        origin = self.c - h if rightward else self.c + h
        src = self.own if h == 0 else self.block(origin)
        send, recv = self.sems[:2] if rightward else self.sems[2:]
        return remote(
            src, self.block(origin), send.at[h], recv.at[h], self.right if rightward else self.left
        )

    def sends(self, rightward, h):
        if rightward:
            return jnp.logical_and(self.c >= h, self.c < self.C - 1)
        return jnp.logical_and(self.c + h < self.C, self.c > 0)

    def start(self):
        for way in (True, False):
            pl.when(self.sends(way, 0))(self.copy(way, 0).start)

    def hop(self, h):
        for way in (True, False):
            origin = self.c - h if way else self.c + h
            there = origin >= 0 if way else origin < self.C
            landed = remote(
                self.block(origin), self.block(origin),
                self.sems[0 if way else 2].at[h - 1], self.sems[1 if way else 3].at[h - 1],
                self.left if way else self.right,
            )
            pl.when(there)(landed.wait_recv)
            if h < self.C - 1:
                pl.when(self.sends(way, h))(self.copy(way, h).start)

    def finish(self):
        for way in (True, False):
            for h in range(self.C - 1):
                pl.when(self.sends(way, h))(self.copy(way, h).wait_send)


def line_sems(C):
    return [DMA((C - 1,)) for _ in range(4)]


def front_kernel(
    block, capacity, packed, experts,
    order, ids, slot_ids, tokens, wq, wk, wv, wo, router, norm_attn, norm_moe, cot, low_gains, frequency,
    X_out, W_out, WO_out, PK, SM, G, out_out, q_out, k_out, v, mixed_out, xnt_out, gain_attn, gain_moe, gains,
    cosine, sine, pos_col, pos_row, select_out, select_t_out, chosen, kept,
    X, W, WO, xn, kr, pack, out, q, mixed, xnt, select, select_t,
    local, save, zsend, zrecv, fsend, frecv, csend, crecv, wsend, wrecv,
    xrs, xrr, xls, xlr, grs, grr, gls, glr,
):
    S, C, F = sizes()
    s, c, f = place()
    Q = S * F
    rows, width = tokens.shape
    length = C * rows
    head_width = wq.shape[1] // C
    shard = wq.shape[0]
    wide = chosen.shape[1]
    z_peers = z_neighbours()
    f_peers = [(s, c, lax.rem(f + k, F)) for k in range(1, F)]
    sibling = (1 - s, c, f)
    pair = s * C + c
    out_dst = (lax.rem(pair, S), pair // S, f)
    pair_in = c * S + s
    out_src = (pair_in // C, lax.rem(pair_in, C), f)
    stays = jnp.logical_and(out_dst[0] == s, out_dst[1] == c)
    moves = jnp.logical_not(stays)
    greet = (
        jnp.where(stays, 1 - s, out_src[0]),
        jnp.where(stays, C - 1 - c, out_src[1]),
        f,
    )
    def as_column(line):
        size = line.shape[1]
        square = lax.broadcasted_iota(jnp.int32, (size, size), 0) == lax.broadcasted_iota(
            jnp.int32, (size, size), 1
        )
        return jnp.sum(jnp.where(square, line, 0.0), axis=1, keepdims=True)

    lane = lax.broadcasted_iota(jnp.int32, (rows, wide), 1).astype(f32)
    hits = jnp.zeros((rows, wide), f32)
    slot_map = jnp.full((rows, wide), -1.0, f32)
    for j in range(TOP):
        here = lane == as_column(ids[j : j + 1, :].astype(f32))
        slot = jnp.broadcast_to(as_column(slot_ids[j : j + 1, :].astype(f32)), (rows, wide))
        hits = jnp.where(here, 1.0, hits)
        slot_map = jnp.where(jnp.logical_and(here, slot < capacity), slot, slot_map)
    lane = lax.broadcasted_iota(jnp.int32, pack.shape, 1)
    own_lane = lax.broadcasted_iota(jnp.int32, (experts, pack.shape[1]), 0) == lax.broadcasted_iota(
        jnp.int32, (experts, pack.shape[1]), 1
    )
    packed_rows = lax.dot_general(
        router[...], own_lane.astype(bf16), (((0,), (0,)), ((), ())), preferred_element_type=f32
    )
    for i, line in enumerate((norm_attn, norm_moe)):
        packed_rows = jnp.where(lane == experts + i, as_column(line[...].astype(f32)), packed_rows)
    pack[...] = packed_rows.astype(bf16)
    gains[...] = low_gains[...].astype(f32)
    chosen[...] = hits
    kept[...] = (slot_map >= 0.0).astype(f32)
    SM[c] = slot_map
    greet_all(z_peers + f_peers + [sibling, greet])

    def pieces(target):
        kv = (target * KEY_VALUE_HEADS) // C
        q_cols = pl.ds(pl.multiple_of(target * head_width, 128), head_width)
        kv_cols = pl.ds(pl.multiple_of(kv * HEAD_DIM, 128), HEAD_DIM)
        mine = W.at[s, c, f]
        return [
            (wq.at[:, q_cols], mine.at[:, pl.ds(0, head_width)]),
            (wk.at[:, kv_cols], mine.at[:, pl.ds(head_width, HEAD_DIM)]),
            (wv.at[:, kv_cols], mine.at[:, pl.ds(head_width + HEAD_DIM, HEAD_DIM)]),
            (pack, PK.at[s, c, f]),
        ]

    def token_rows(at):
        return X.at[pl.ds(pl.multiple_of(at * rows, 16), rows)]

    own = [
        pltpu.make_async_copy(src, dst, local.at[i])
        for i, (src, dst) in enumerate(pieces(c) + [(tokens, token_rows(c)), (cot, G.at[c])])
    ]
    z_copies = [
        remote(src, dst, zsend.at[i, k], zrecv.at[i, k], peer)
        for k, peer in enumerate(z_peers)
        for i, (src, dst) in enumerate(pieces(peer[1]))
    ]
    slot_copies = [
        remote(SM.at[c], SM.at[c], zsend.at[4, k], zrecv.at[4, k], peer)
        for k, peer in enumerate(z_peers)
    ]
    x_line = Line(tokens, token_rows, xrs, xrr, xls, xlr)
    g_line = Line(cot, lambda at: G.at[at], grs, grr, gls, glr)
    out_copy = remote(wo, WO.at[out_dst[0], f], wsend.at[0], wrecv.at[0], out_dst)
    out_stay = pltpu.make_async_copy(wo, WO.at[s, f], wsend.at[1])
    for copy in own + z_copies + slot_copies:
        copy.start()
    x_line.start()
    pl.when(moves)(out_copy.start)
    pl.when(stays)(out_stay.start)

    where = lax.broadcasted_iota(jnp.int32, (1, length), 1)
    where_col = lax.broadcasted_iota(jnp.int32, (length, 1), 0)
    stretch_rows = rows // 2

    def position(at):
        total = jnp.zeros_like(at)
        for j in range(2 * C):
            base = order[j] * stretch_rows - j * stretch_rows
            total = jnp.where(at // stretch_rows == j, at + base, total)
        return total

    pos_row[...] = position(where)
    pos_col[...] = position(where_col)
    angles = pos_col[...].astype(f32) * frequency[...]
    cosine[...] = jnp.cos(angles)
    turned = jnp.sin(angles)
    sine[...] = jnp.where(
        lax.broadcasted_iota(jnp.int32, turned.shape, 1) < HEAD_DIM // 2, -turned, turned
    )

    for copy in own[:5] + z_copies:
        copy.wait()

    def weight_block(index, at):
        return (W.at[s, :, at], PK.at[s, :, at], WO.at[s, at])[index]

    f_copies = [
        [
            remote(weight_block(i, f), weight_block(i, f), fsend.at[i, k], frecv.at[i, k], peer)
            for k, peer in enumerate(f_peers)
        ]
        for i in range(3)
    ]

    def to_sibling(i, k):
        at = lax.rem(f + F - k, F)
        return remote(weight_block(i, at), weight_block(i, at), csend.at[i, k], crecv.at[i, k], sibling)

    c_copies = [[to_sibling(i, k) for k in range(F)] for i in range(3)]
    for i in range(2):
        for copy in f_copies[i] + c_copies[i][:1]:
            copy.start()
    x_line.hop(1)
    for h in range(2, C - 1):
        x_line.hop(h)
    pl.when(moves)(out_copy.wait)
    pl.when(stays)(out_stay.wait)
    for copy in f_copies[2] + c_copies[2][:1]:
        copy.start()
    for k in range(F - 1):
        for i in range(2):
            f_copies[i][k].wait_recv()
            c_copies[i][k + 1].start()
    for copy in slot_copies:
        copy.wait()
    at = lax.broadcasted_iota(jnp.int32, (wide, Q * packed), 1) // packed
    expert = (at // F * C + c) * F + lax.rem(at, F)
    spread = (lax.broadcasted_iota(jnp.int32, (wide, Q * packed), 0) == expert).astype(bf16)
    slot_rows = SM[...].reshape(length, wide).astype(bf16)
    by_token = jnp.dot(slot_rows, spread, preferred_element_type=f32)
    base = (lax.broadcasted_iota(jnp.int32, by_token.shape, 0) // rows * capacity).astype(f32)
    number = lax.rem(lax.broadcasted_iota(jnp.int32, by_token.shape, 1), packed).astype(f32)
    select_t[...] = jnp.where(
        jnp.logical_and(by_token >= 0.0, by_token + base == number), 1.0, 0.0
    ).astype(bf16)
    at = lax.broadcasted_iota(jnp.int32, (Q, wide), 0)
    expert = (at // F * C + c) * F + lax.rem(at, F)
    spread = (lax.broadcasted_iota(jnp.int32, (Q, wide), 1) == expert).astype(bf16)
    by_slot = lax.dot_general(
        spread, slot_rows, (((1,), (1,)), ((), ())), preferred_element_type=f32
    )
    base = (where // rows * capacity).astype(f32)
    by_slot = jnp.where(by_slot >= 0.0, by_slot + base, -1.0)
    number = lax.broadcasted_iota(jnp.int32, (packed, length), 0).astype(f32)
    for p in range(Q):
        select[p * packed : (p + 1) * packed, :] = jnp.where(
            number == by_slot[p : p + 1, :], 1.0, 0.0
        ).astype(bf16)

    x_line.hop(C - 1)
    g_line.start()
    for i in range(2):
        for copy in c_copies[i]:
            copy.wait()
    saves = [
        pltpu.make_async_copy(src, dst, save.at[i])
        for i, (src, dst) in enumerate(
            (
                (X, X_out), (W, W_out), (select, select_out), (select_t, select_t_out),
                (WO, WO_out), (q, q_out), (mixed, mixed_out), (out, out_out), (xnt, xnt_out),
            )
        )
    ]
    for copy in saves[:4]:
        copy.start()
    across = lax.broadcasted_iota(jnp.int32, (HEAD_DIM, HEAD_DIM), 0)
    diagonal = across == lax.broadcasted_iota(jnp.int32, (HEAD_DIM, HEAD_DIM), 1)
    flat = PK[...].reshape(width, PK.shape[-1]).astype(f32)
    for j in range(width // HEAD_DIM):
        part = slice(j * HEAD_DIM, (j + 1) * HEAD_DIM)
        for i, row in enumerate((gain_attn, gain_moe)):
            line = flat[part, experts + i : experts + i + 1]
            row[:, part] = jnp.sum(jnp.where(diagonal, line, 0.0), axis=0, keepdims=True)

    def norm_rows(i, carry):
        part = pl.ds(i * 64, 64)
        unit, _ = rms_unit(X[part, :].astype(f32))
        xn[part, :] = (unit * gain_attn[...]).astype(bf16)
        return carry

    lax.fori_loop(0, length // 64, norm_rows, 0)

    def weights(cols):
        return W[:, :, :, :, cols].reshape(width, 2 * HEAD_DIM)

    kv = jnp.dot(xn[...], weights(pl.ds(head_width, 2 * HEAD_DIM)), preferred_element_type=f32)
    k_out[...] = kv[:, :HEAD_DIM]
    v[...] = kv[:, HEAD_DIM:].astype(bf16)
    unit, _ = rms_unit(k_out[...])
    kr[...] = half_turn(unit * gains[1:2, :], cosine[...], sine[...]).astype(bf16)

    def head_pair(i, carry):
        cols = pl.ds(pl.multiple_of(i * 2 * HEAD_DIM, 2 * HEAD_DIM), 2 * HEAD_DIM)
        both = jnp.dot(xn[...], weights(cols), preferred_element_type=f32)
        q[:, cols] = both
        for half in range(2):
            lanes = pl.ds(pl.multiple_of((2 * i + half) * HEAD_DIM, HEAD_DIM), HEAD_DIM)
            for part in range(length // block):
                at = slice(part * block, (part + 1) * block)
                unit, _ = rms_unit(both[at, half * HEAD_DIM : (half + 1) * HEAD_DIM])
                qr = half_turn(unit * gains[0:1, :], cosine[at, :], sine[at, :]).astype(bf16)
                probs = score_block(qr, kr[...], pos_col[at, :], pos_row[...])
                mixed[at, lanes] = jnp.dot(
                    probs.astype(bf16), v[...], preferred_element_type=f32
                ).astype(bf16)
        return carry

    pairs = head_width // (2 * HEAD_DIM)
    half_way = pairs // 2
    hops = {}
    for h in range(1, C - 1):
        hops.setdefault(min(pairs, 1 + (h - 1) * pairs // (C - 2)), []).append(h)
    done = 0
    for stop in sorted(set(hops) | {half_way, pairs}):
        lax.fori_loop(done, stop, head_pair, 0)
        done = stop
        for h in hops.get(stop, ()):
            g_line.hop(h)
        if stop == half_way:
            for k in range(F - 1):
                f_copies[2][k].wait_recv()
                c_copies[2][k + 1].start()
    for copy in c_copies[2]:
        copy.wait()
    for copy in saves[4:7]:
        copy.start()

    def project(j, carry):
        cols = pl.ds(pl.multiple_of(j * 256, 256), 256)
        out[:, cols] = jnp.dot(
            mixed[...], WO[:, :, :, cols].reshape(head_width, 256), preferred_element_type=f32
        ).astype(bf16)
        return carry

    lax.fori_loop(0, width // 256, project, 0)
    saves[7].start()

    def turn(j, carry):
        cols = pl.ds(pl.multiple_of(j * 256, 256), 256)
        xnt[cols, :] = xn[:, cols].T
        return carry

    lax.fori_loop(0, width // 256, turn, 0)
    saves[8].start()
    g_line.hop(C - 1)
    x_line.finish()
    g_line.finish()
    for line in f_copies:
        for copy in line:
            copy.wait_send()
    for copy in saves + own[5:]:
        copy.wait()


def front(
    capacity, packed, order, ids, slot_ids, tokens, wq, wk, wv, wo, router, norm_attn, norm_moe, cot, gains
):
    S, C, F = sizes()
    Q = S * F
    rows, width = tokens.shape
    length = C * rows
    shard = wq.shape[0]
    head_width = wq.shape[1] // C
    experts = router.shape[0]
    wide = round_up(experts, 128)
    frequency = np.power(rope_base, -np.arange(HEAD_DIM // 2) * 2.0 / HEAD_DIM)
    frequency = jnp.asarray(np.tile(frequency, 2)[None].astype(np.float32))
    block = min(length, 512)
    sds = jax.ShapeDtypeStruct
    V = pltpu.VMEM
    vm = pl.BlockSpec(memory_space=pltpu.VMEM)
    w_shape = (S, C, F, shard, head_width + 2 * HEAD_DIM)
    wo_shape = (S, F) + wo.shape
    pack_block = (shard, round_up(experts + 2, 128))
    pack_shape = (S, C, F) + pack_block
    return pl.pallas_call(
        functools.partial(front_kernel, block, capacity, packed, experts),
        out_shape=[
            sds((length, width), bf16),
            sds(w_shape, bf16),
            sds(wo_shape, bf16),
            sds(pack_shape, bf16),
            sds((C, rows, wide), f32),
            sds((C, rows, width), bf16),
            sds((length, width), bf16),
            sds((length, head_width), f32),
            sds((length, HEAD_DIM), f32),
            sds((length, HEAD_DIM), bf16),
            sds((length, head_width), bf16),
            sds((width, length), bf16),
            sds((1, width), f32),
            sds((1, width), f32),
            sds(gains.shape, f32),
            sds((length, HEAD_DIM), f32),
            sds((length, HEAD_DIM), f32),
            sds((length, 1), jnp.int32),
            sds((1, length), jnp.int32),
            sds((Q * packed, length), bf16),
            sds((length, Q * packed), bf16),
            sds((rows, wide), f32),
            sds((rows, wide), f32),
        ],
        in_specs=[pl.BlockSpec(memory_space=pltpu.SMEM), vm, vm] + [ANY] * 5 + [vm] * 3 + [ANY, vm, vm],
        out_specs=[ANY] * 3 + [vm, vm] + [ANY] * 3 + [vm] * 2 + [ANY] * 2 + [vm] * 7 + [ANY] * 2 + [vm] * 2,
        scratch_shapes=[
            V((length, width), bf16),
            V(w_shape, bf16),
            V(wo_shape, bf16),
            V((length, width), bf16),
            V((length, HEAD_DIM), bf16),
            V(pack_block, bf16),
            V((length, width), bf16),
            V((length, head_width), f32),
            V((length, head_width), bf16),
            V((width, length), bf16),
            V((Q * packed, length), bf16),
            V((length, Q * packed), bf16),
            DMA((6,)), DMA((9,)),
            DMA((5, C - 1)), DMA((5, C - 1)),
            DMA((3, F - 1)), DMA((3, F - 1)),
            DMA((3, F)), DMA((3, F)),
            DMA((2,)), DMA((1,)),
        ]
        + line_sems(C)
        + line_sems(C),
        name="gather_and_attend",
        compiler_params=params(1, 60 * 2**20),
    )(order, ids, slot_ids, tokens, wq, wk, wv, wo, router, norm_attn, norm_moe, cot, gains, frequency)


CHUNKS = 8


def columns(width, j):
    step = width // CHUNKS
    return pl.ds(j * step, step)


def three_parts(line):
    high = line.astype(bf16).astype(f32)
    rest = line - high
    middle = rest.astype(bf16).astype(f32)
    row = lax.broadcasted_iota(jnp.int32, (16, line.shape[1]), 0)
    rows = jnp.where(row == 0, high, jnp.where(row == 1, middle, jnp.where(row == 2, rest - middle, 0.0)))
    return rows.astype(bf16)


def halves(total):
    return total // 2


def dispatch_kernel(
    packed, out_part, G_in, tokens, pack, gain, chosen, kept, select, w_gate, w_up, w_down,
    buffer_out, gbuf, wrow, h1, xm, gates, hidden_out, dgp_out, dup_out, dgr,
    OP, RB, XM, SL, WM, WS, G, SG, buffer, WG, WU, WD, gp, up, gw, dup,
    local, load, saved, osend, orecv, gsend, grecv, xsend, xrecv, msend, mrecv, bsend, brecv, wsend, wrecv,
):
    S, C, F = sizes()
    s, c, f = place()
    Q = S * F
    q = s * F + f
    rows, width = tokens.shape
    total_rows = Q * packed
    half = halves(total_rows)
    z_peers = z_neighbours()
    p_at, p_peers = plane_neighbours()
    loads = [
        pltpu.make_async_copy(G_in, G, load.at[0]),
        pltpu.make_async_copy(w_down.at[0], WD, load.at[1]),
        pltpu.make_async_copy(w_gate.at[0], WG, load.at[2]),
        pltpu.make_async_copy(w_up.at[0], WU, load.at[3]),
    ]
    for copy in loads:
        copy.start()
    greet_all(z_peers + p_peers)
    mine = pl.ds(pl.multiple_of(q * packed, 16), packed)
    own_rows = pl.ds(pl.multiple_of(c * rows, 16), rows)
    right = (s, lax.rem(c + 1, C), f)
    left = (s, lax.rem(c + C - 1, C), f)

    def rightward(t):
        return remote(OP.at[t], RB.at[t], osend.at[0, t], orecv.at[0, t], right)

    def leftward(t):
        return remote(OP.at[t], RB.at[jnp.where(c - 1 == t, C, t)], osend.at[1, t], orecv.at[1, t], left)

    def merge(t, way):
        remote(OP.at[t], RB.at[t], osend.at[way, t], orecv.at[way, t], left).wait_recv()

        def add(j, carry):
            part = pl.ds(j * 32, 32)
            OP[t, part, :] = (OP[t, part, :].astype(f32) + RB[t, part, :].astype(f32)).astype(bf16)
            return carry

        lax.fori_loop(0, rows // 32, add, 0)

    def pass_on(step):
        t_right = C - 1 + c - step
        t_left = step - (C - 1 - c)

        @pl.when((t_right > c) & (t_right < C) & (c > 0))
        def _():
            merge(t_right, 0)
            rightward(t_right).start()

        @pl.when((t_left >= 0) & (t_left < c) & (c < C - 1))
        def _():
            merge(t_left, 1)
            leftward(t_left).start()

    fetch = pltpu.make_async_copy(out_part, OP, local.at[0])
    fetch.start()
    fetch.wait()

    @pl.when(c == 0)
    def _():
        for t in range(C - 1, 0, -1):
            rightward(t).start()

    @pl.when(c == C - 1)
    def _():
        for t in range(C - 1):
            leftward(t).start()

    loads[0].wait()

    def grad_slots(p):
        at = pl.ds(pl.multiple_of(p * packed, 16), packed)

        def body(j, carry):
            cols = pl.ds(pl.multiple_of(j * 512, 512), 512)
            SG[at, cols] = jnp.dot(select[at, :], G[:, cols], preferred_element_type=f32).astype(bf16)
            return carry

        lax.fori_loop(0, width // 512, body, 0)

    later = []
    for k, peer in enumerate(p_peers):
        theirs = pl.ds(pl.multiple_of(p_at[k] * packed, 16), packed)
        later.append(remote(SG.at[theirs], gbuf.at[mine], gsend.at[k], grecv.at[k], peer))
        grad_slots(p_at[k])
        later[-1].start()
    grad_slots(q)
    later.append(pltpu.make_async_copy(SG.at[mine], gbuf.at[mine], local.at[1]))
    later[-1].start()
    for step in range(1, C - 1):
        pass_on(step)

    @pl.when(c > 0)
    def _():
        remote(OP.at[0], RB.at[c], osend.at[0, c], orecv.at[0, c], left).wait_recv()

    @pl.when(c < C - 1)
    def _():
        remote(OP.at[0], RB.at[C], osend.at[1, c], orecv.at[1, c], right).wait_recv()


    def head_rows(i, carry):
        part = pl.ds(i * 32, 32)
        total = tokens[part, :].astype(f32) + OP[c, part, :].astype(f32)
        total += jnp.where(c > 0, RB[c, part, :].astype(f32), 0.0)
        total += jnp.where(c < C - 1, RB[C, part, :].astype(f32), 0.0)
        h1[part, :] = total
        unit, _ = rms_unit(total)
        normed = (unit * gain[...]).astype(bf16)
        xm[part, :] = normed
        XM[pl.ds(pl.multiple_of(c * rows + i * 32, 16), 32), :] = normed
        return carry

    lax.fori_loop(0, rows // 32, head_rows, 0)
    chunks = []
    for j in range(CHUNKS):
        piece = XM.at[own_rows, columns(width, j)]
        chunks.append(
            [remote(piece, piece, xsend.at[j, k], xrecv.at[j, k], peer) for k, peer in enumerate(z_peers)]
        )
    for copy in chunks[0]:
        copy.start()
    logits = jnp.dot(xm[...], pack[...], preferred_element_type=f32)[:, : chosen.shape[1]]
    logits = jnp.where(chosen[...] > 0.0, logits, -jnp.inf)
    power = jnp.exp(logits - jnp.max(logits, axis=-1, keepdims=True))
    gates[...] = power / jnp.sum(power, axis=-1, keepdims=True)
    WM[own_rows, :] = gates[...] * kept[...]
    row = []
    for k, peer in enumerate(z_peers):
        piece = WM.at[own_rows, :]
        row.append(remote(piece, piece, msend.at[k], mrecv.at[k], peer))
        row[-1].start()
    for line in chunks[1:]:
        for copy in line:
            copy.start()
    sent = []
    for j in range(CHUNKS):
        cols = columns(width, j)
        for copy in chunks[j]:
            copy.wait_recv()

        def slots(i, carry):
            at = pl.ds(pl.multiple_of(i * half, 16), half)
            SL[at, cols] = jnp.dot(select[at, :], XM[:, cols], preferred_element_type=f32).astype(bf16)
            return carry

        lax.fori_loop(0, 2, slots, 0)
        line = []
        for k, peer in enumerate(p_peers):
            theirs = pl.ds(pl.multiple_of(p_at[k] * packed, 16), packed)
            line.append(
                remote(SL.at[theirs, cols], buffer.at[mine, cols], bsend.at[j, k], brecv.at[j, k], peer)
            )
        line.append(pltpu.make_async_copy(SL.at[mine, cols], buffer.at[mine, cols], local.at[4 + j]))
        for copy in line:
            copy.start()
        sent.append(line)
        if j == 0:
            for copy in row:
                copy.wait_recv()
            WS[...] = jnp.zeros_like(WS)

            place_of = lax.broadcasted_iota(jnp.int32, (Q, WM.shape[1]), 0)
            expert = (place_of // F * C + c) * F + lax.rem(place_of, F)
            spread = (lax.broadcasted_iota(jnp.int32, expert.shape, 1) == expert).astype(f32)
            lines = lax.dot_general(
                spread, WM[...], (((1,), (1,)), ((), ())),
                precision=lax.Precision.HIGHEST, preferred_element_type=f32,
            )
            for p in range(Q):
                line = lax.dot_general(
                    three_parts(lines[p : p + 1, :]), select[p * packed : (p + 1) * packed, :],
                    (((1,), (1,)), ((), ())), preferred_element_type=f32,
                )
                WS[p, :, pl.ds(0, packed)] = jnp.broadcast_to(
                    jnp.sum(line, axis=0, keepdims=True), (8, packed)
                )
            scales = [
                remote(WS.at[p_at[k]], wrow.at[q], wsend.at[k], wrecv.at[k], peer)
                for k, peer in enumerate(p_peers)
            ]
            scales.append(pltpu.make_async_copy(WS.at[q], wrow.at[q], local.at[2]))
            for copy in scales:
                copy.start()
        if j == CHUNKS - 2:
            for copy in later + loads[1:]:
                copy.wait()
            reload = pltpu.make_async_copy(gbuf, SG, local.at[3])
            reload.start()
            reload.wait()

            def through_down(i, carry):
                at = pl.ds(pl.multiple_of(i * half, 16), half)
                gw[at, :] = lax.dot_general(
                    SG[at, :], WD[...], (((1,), (1,)), ((), ())), preferred_element_type=f32
                )
                return carry

            lax.fori_loop(0, 2, through_down, 0)
    for j in range(CHUNKS - 1):
        cols = columns(width, j)
        for copy in sent[j]:
            copy.wait()

        def project(i, carry):
            at = pl.ds(pl.multiple_of(i * half, 16), half)
            part = buffer[at, cols]
            one = jnp.dot(part, WG[cols, :], preferred_element_type=f32)
            two = jnp.dot(part, WU[cols, :], preferred_element_type=f32)
            gp[at, :] = one if j == 0 else gp[at, :] + one
            up[at, :] = two if j == 0 else up[at, :] + two
            return carry

        lax.fori_loop(0, 2, project, 0)
    for copy in scales:
        copy.wait()
    diagonal = lax.broadcasted_iota(jnp.int32, (packed, packed), 0) == lax.broadcasted_iota(
        jnp.int32, (packed, packed), 1
    )
    dgr[...] = jnp.zeros_like(dgr)
    cols = columns(width, CHUNKS - 1)
    inner = dup.shape[-1]
    hidden, dgp = SG.at[:, pl.ds(0, inner)], SG.at[:, pl.ds(inner, inner)]

    def saves_of(p):
        at = pl.ds(pl.multiple_of(p * packed, 16), packed)
        pairs = ((buffer, buffer_out), (hidden, hidden_out), (dgp, dgp_out), (dup, dup_out))
        return [
            pltpu.make_async_copy(src.at[at], dst.at[at], saved.at[i, p])
            for i, (src, dst) in enumerate(pairs)
        ]

    def expert_rows(p):
        at = pl.ds(pl.multiple_of(p * packed, 16), packed)
        part = buffer[at, cols]
        gate_pre = gp[at, :] + jnp.dot(part, WG[cols, :], preferred_element_type=f32)
        up_pre = up[at, :] + jnp.dot(part, WU[cols, :], preferred_element_type=f32)
        back = gw[at, :]
        scale = jnp.sum(
            jnp.where(diagonal, wrow[p, 0:1, pl.ds(0, packed)], 0.0), axis=1, keepdims=True
        )
        sigmoid = jax.nn.sigmoid(gate_pre)
        silu = gate_pre * sigmoid
        low = (silu * up_pre).astype(bf16)
        hidden[at, :] = (scale * low.astype(f32)).astype(bf16)
        dgate = jnp.sum(back * low.astype(f32), axis=-1, keepdims=True)
        line = jnp.sum(jnp.where(diagonal, dgate, 0.0), axis=0, keepdims=True)
        dgr[p, :, pl.ds(0, packed)] = jnp.broadcast_to(line, (8, packed))
        dhid = scale * back
        dgp[at, :] = (dhid * up_pre * sigmoid * (1.0 + gate_pre * (1.0 - sigmoid))).astype(bf16)
        dup[at, :] = (dhid * silu).astype(bf16)
        for copy in saves_of(p):
            copy.start()

    sent[CHUNKS - 1][Q - 1].wait()
    expert_rows(q)

    def arrival(k, carry):
        p = lax.rem(q + Q - 1 - k, Q)
        at = pl.ds(pl.multiple_of(p * packed, 16), packed)
        came = (p // F, c, lax.rem(p, F))
        remote(
            SL.at[at, cols], buffer.at[at, cols], bsend.at[CHUNKS - 1, k], brecv.at[CHUNKS - 1, k], came
        ).wait_recv()
        expert_rows(p)
        return carry

    lax.fori_loop(0, Q - 1, arrival, 0)
    for copy in sent[CHUNKS - 1][: Q - 1]:
        copy.wait_send()
    for line in chunks + [row]:
        for copy in line:
            copy.wait_send()

    @pl.when(c < C - 1)
    def _():
        def body(t, carry):
            rightward(t).wait_send()
            return carry

        lax.fori_loop(c + 1, C, body, 0)

    @pl.when(c > 0)
    def _():
        def body(t, carry):
            leftward(t).wait_send()
            return carry

        lax.fori_loop(0, c, body, 0)

    for p in range(Q):
        for copy in saves_of(p):
            copy.wait()


def dispatch(packed, out_part, G, tokens, pack, gain, chosen, kept, select, w_gate, w_up, w_down):
    S, C, F = sizes()
    Q = S * F
    rows, width = tokens.shape
    inner = w_gate.shape[-1]
    lanes = round_up(packed, 128)
    wide = chosen.shape[1]
    V = pltpu.VMEM
    sds = jax.ShapeDtypeStruct
    vm = pl.BlockSpec(memory_space=pltpu.VMEM)
    slots = Q * packed
    return pl.pallas_call(
        functools.partial(dispatch_kernel, packed),
        out_shape=[
            sds((slots, width), bf16),
            sds((slots, width), bf16),
            sds((Q, 8, lanes), f32),
            sds((rows, width), f32),
            sds((rows, width), bf16),
            sds((rows, wide), f32),
            sds((slots, inner), bf16),
            sds((slots, inner), bf16),
            sds((slots, inner), bf16),
            sds((Q, 8, lanes), f32),
        ],
        in_specs=[ANY, ANY] + [vm] * 6 + [ANY] * 3,
        out_specs=[ANY, ANY, vm, vm, vm, vm, ANY, ANY, ANY, vm],
        scratch_shapes=[
            V((C, rows, width), bf16),
            V((C + 1, rows, width), bf16),
            V((C * rows, width), bf16),
            V((slots, width), bf16),
            V((C * rows, wide), f32),
            V((Q, 8, lanes), f32),
            V((C * rows, width), bf16),
            V((slots, width), bf16),
            V((slots, width), bf16),
            V((width, inner), bf16), V((width, inner), bf16), V((inner, width), bf16),
            V((slots, inner), f32), V((slots, inner), f32), V((slots, inner), f32),
            V((slots, inner), bf16),
            DMA((4 + CHUNKS,)),
            DMA((4,)),
            DMA((4, Q)),
            DMA((2, C)), DMA((2, C)),
            DMA((Q - 1,)), DMA((Q - 1,)),
            DMA((CHUNKS, C - 1)), DMA((CHUNKS, C - 1)),
            DMA((C - 1,)), DMA((C - 1,)),
            DMA((CHUNKS, Q - 1)), DMA((CHUNKS, Q - 1)),
            DMA((Q - 1,)), DMA((Q - 1,)),
        ],
        name="dispatch_rows",
        compiler_params=params(3, 62 * 2**20),
    )(out_part, G, tokens, pack, gain, chosen, kept, select, w_gate, w_up, w_down)


def return_kernel(
    packed, experts, dgr, gates, pack, h1, gain, cot, xm, dgp, dup,
    select_in, select_t_in, hidden_in, w_gate, w_up, w_down,
    DA, y_part, dh1, small,
    RD, YB, PART, RX, DG, DGP, RG, DL, din, wy, WG, WU, WD, dlog, gnorm, DXR, select, select_t, hidden,
    local, load, dsend, drecv, gsend, grecv, ysend, yrecv, xsend, xrecv, msend, mrecv, *asems,
):
    S, C, F = sizes()
    s, c, f = place()
    Q = S * F
    q = s * F + f
    rows, width = h1.shape
    z_peers = z_neighbours()
    p_at, p_peers = plane_neighbours()
    loads = []
    for j in range(CHUNKS):
        cols = columns(width, j)
        loads.append(
            [
                pltpu.make_async_copy(w_gate.at[0, cols], WG.at[cols], load.at[0, j]),
                pltpu.make_async_copy(w_up.at[0, cols], WU.at[cols], load.at[1, j]),
            ]
        )
    load_down = pltpu.make_async_copy(w_down.at[0], WD, load.at[2, 0])
    late = [
        pltpu.make_async_copy(hidden_in, hidden, load.at[2, 1]),
        pltpu.make_async_copy(select_t_in, select_t, load.at[2, 2]),
        pltpu.make_async_copy(select_in, select, load.at[2, 3]),
    ]
    for line in loads:
        for copy in line:
            copy.start()
    load_down.start()
    for copy in late:
        copy.start()
    greet_all(z_peers + p_peers)
    half = halves(Q * packed)
    mine = pl.ds(pl.multiple_of(q * packed, 16), packed)
    theirs = [pl.ds(pl.multiple_of(at * packed, 16), packed) for at in p_at]
    inner_products = [
        remote(dgr.at[p_at[k]], DG.at[q], gsend.at[k], grecv.at[k], peer)
        for k, peer in enumerate(p_peers)
    ]
    inner_products.append(pltpu.make_async_copy(dgr.at[q], DG.at[q], local.at[0]))
    for copy in inner_products:
        copy.start()
    chunks = []
    for j in range(CHUNKS):
        cols = columns(width, j)
        for copy in loads[j]:
            copy.wait()

        def expert_in(i, carry):
            at = pl.ds(pl.multiple_of(i * half, 16), half)
            across = (((1,), (1,)), ((), ()))
            total = lax.dot_general(dgp[at, :], WG[cols, :], across, preferred_element_type=f32)
            total += lax.dot_general(dup[at, :], WU[cols, :], across, preferred_element_type=f32)
            din[at, cols] = total.astype(bf16)
            return carry

        lax.fori_loop(0, 2, expert_in, 0)
        line = [
            remote(din.at[theirs[k], cols], RD.at[mine, cols], dsend.at[j, k], drecv.at[j, k], peer)
            for k, peer in enumerate(p_peers)
        ]
        line.append(pltpu.make_async_copy(din.at[mine, cols], RD.at[mine, cols], local.at[2 + j]))
        for copy in line:
            copy.start()
        chunks.append(line)
    load_down.wait()
    for copy in late:
        copy.wait()
    def expert_out(i, carry):
        at = pl.ds(pl.multiple_of(i * half, 16), half)

        def body(j, carry):
            cols = pl.ds(pl.multiple_of(j * 512, 512), 512)
            y = jnp.dot(hidden[at, :], WD[:, cols], preferred_element_type=f32)
            wy[at, cols] = y.astype(bf16)
            return carry

        return lax.fori_loop(0, width // 512, body, carry)

    lax.fori_loop(0, 2, expert_out, 0)
    sums = []
    for j in range(CHUNKS):
        if j == CHUNKS - 1:
            ys = []
            for jj in range(2):
                cols = pl.ds(jj * (width // 2), width // 2)
                line = [
                    remote(wy.at[theirs[k], cols], YB.at[mine, cols], ysend.at[jj, k], yrecv.at[jj, k], peer)
                    for k, peer in enumerate(p_peers)
                ]
                line.append(pltpu.make_async_copy(wy.at[mine, cols], YB.at[mine, cols], local.at[(1, 2 + CHUNKS + 1)[jj]]))
                for copy in line:
                    copy.start()
                ys.append(line)
        cols = columns(width, j)
        for copy in chunks[j]:
            copy.wait()

        def combine(i, carry):
            lanes = pl.ds(pl.multiple_of(j * (width // CHUNKS) + i * 256, 256), 256)
            PART[:, lanes] = jnp.dot(
                select_t[...], RD[:, lanes], preferred_element_type=f32
            ).astype(bf16)
            return carry

        lax.fori_loop(0, width // CHUNKS // 256, combine, 0)
        for k, peer in enumerate(z_peers):
            src = PART.at[pl.ds(pl.multiple_of(peer[1] * rows, 16), rows), cols]
            sums.append(remote(src, RX.at[k, :, cols], xsend.at[j, k], xrecv.at[j, k], peer))
            sums[-1].start()
    for copy in inner_products:
        copy.wait()
    wide = gates.shape[1]
    place_of = lax.broadcasted_iota(jnp.int32, (Q, wide), 0)
    expert = (place_of // F * C + c) * F + lax.rem(place_of, F)
    spread = (lax.broadcasted_iota(jnp.int32, (Q, wide), 1) == expert).astype(f32)

    for p in range(Q):
        at = pl.ds(p * packed, packed)
        line = jnp.dot(
            three_parts(DG[p, 0:1, pl.ds(0, packed)]), select[at, :], preferred_element_type=f32
        )
        DL[pl.ds(p, 1), :] = jnp.sum(line, axis=0, keepdims=True)
    DGP[...] = lax.dot_general(
        DL[...], spread, (((0,), (0,)), ((), ())),
        precision=lax.Precision.HIGHEST, preferred_element_type=f32,
    ).reshape(DGP.shape)
    more = []
    for k, peer in enumerate(z_peers):
        more.append(remote(DGP.at[peer[1]], RG.at[k], msend.at[k], mrecv.at[k], peer))
        more[-1].start()
    for copy in more:
        copy.wait()
    total = DGP[c]
    for k in range(C - 1):
        total = total + RG[k]
    dlogits = gates[...] * (total - jnp.sum(gates[...] * total, axis=-1, keepdims=True))
    dlog[...] = dlogits.astype(bf16)
    gnorm[...] = jnp.zeros_like(gnorm)
    DXR[...] = lax.dot_general(
        dlog[...], pack[:, pl.ds(0, wide)], (((1,), (1,)), ((), ())), preferred_element_type=f32
    )
    for copy in sums:
        copy.wait()

    def head_rows(i, carry):
        part = pl.ds(i * 32, 32)
        mine_part = pl.ds(pl.multiple_of(c * rows + i * 32, 16), 32)
        dxm = PART[mine_part, :].astype(f32)
        for k in range(C - 1):
            dxm = dxm + RX[k, part, :].astype(f32)
        dxm = dxm + DXR[part, :]
        unit, factor = rms_unit(h1[part, :])
        gnorm[...] += jnp.sum(dxm * unit, axis=0, keepdims=True)
        grad = cot[part, :].astype(f32) + norm_backward(dxm, unit, factor, gain[...])
        dh1[part, :] = grad
        RX[0, part, :] = grad.astype(bf16)
        return carry

    lax.fori_loop(0, rows // 32, head_rows, 0)
    keep = pltpu.make_async_copy(RX.at[0], DA.at[c], local.at[2 + CHUNKS])
    keep.start()
    line = Line(RX.at[0], lambda at: DA.at[at], *asems)
    line.start()
    for h in range(1, C - 1):
        line.hop(h)
    square = lax.broadcasted_iota(jnp.int32, (HEAD_DIM, HEAD_DIM), 0) == lax.broadcasted_iota(
        jnp.int32, (HEAD_DIM, HEAD_DIM), 1
    )
    small[...] = jnp.zeros_like(small)

    def small_rows(i, carry):
        at = pl.ds(pl.multiple_of(i * HEAD_DIM, HEAD_DIM), HEAD_DIM)
        router_part = lax.dot_general(
            xm[:, at], dlog[...], (((0,), (0,)), ((), ())), preferred_element_type=f32
        )
        column = jnp.sum(jnp.where(square, gnorm[:, at], 0.0), axis=1, keepdims=True)
        if wide > experts:
            lane = lax.broadcasted_iota(jnp.int32, router_part.shape, 1)
            small[at, :] = jnp.where(lane == experts, column, router_part).astype(bf16)
        else:
            small[at, pl.ds(0, wide)] = router_part.astype(bf16)
            lane = lax.broadcasted_iota(jnp.int32, (HEAD_DIM, HEAD_DIM), 1)
            small[at, pl.ds(wide, HEAD_DIM)] = jnp.where(lane == 0, column, 0.0).astype(bf16)
        return carry

    lax.fori_loop(0, width // HEAD_DIM, small_rows, 0)

    def combine_y(i, carry):
        lanes = pl.ds(pl.multiple_of(i * 256, 256), 256)
        y_part[:, lanes] = jnp.dot(
            select_t[...], YB[:, lanes], preferred_element_type=f32
        ).astype(bf16)
        return carry

    for j in range(2):
        for copy in ys[j]:
            copy.wait()
        lax.fori_loop(j * (width // 512), (j + 1) * (width // 512), combine_y, 0)
    line.hop(C - 1)
    line.finish()
    keep.wait()


def give_back(
    packed, experts, dgr, select, select_t, gates, pack, h1, gain, cot, xm, hidden, dgp, dup, w_gate, w_up, w_down
):
    S, C, F = sizes()
    Q = S * F
    rows, width = h1.shape
    wide = gates.shape[1]
    inner = w_gate.shape[-1]
    V = pltpu.VMEM
    sds = jax.ShapeDtypeStruct
    vm = pl.BlockSpec(memory_space=pltpu.VMEM)
    return pl.pallas_call(
        functools.partial(return_kernel, packed, experts),
        out_shape=[
            sds((C, rows, width), bf16),
            sds((C * rows, width), bf16),
            sds((rows, width), f32),
            sds(pack.shape, bf16),
        ],
        in_specs=[vm] * 9 + [ANY] * 6,
        out_specs=[ANY] + [vm] * 3,
        scratch_shapes=[
            V((Q * packed, width), bf16),
            V((Q * packed, width), bf16),
            V((C * rows, width), bf16),
            V((C - 1, rows, width), bf16),
            V(dgr.shape, f32),
            V((C, rows, wide), f32),
            V((C - 1, rows, wide), f32),
            V((Q, C * rows), f32),
            V((Q * packed, width), bf16),
            V((Q * packed, width), bf16),
            V((width, inner), bf16), V((width, inner), bf16), V((inner, width), bf16),
            V((rows, wide), bf16),
            V((1, width), f32),
            V((rows, width), f32),
            V(select.shape, bf16), V(select_t.shape, bf16), V(hidden.shape, bf16),
            DMA((4 + CHUNKS,)),
            DMA((3, CHUNKS)),
            DMA((CHUNKS, Q - 1)), DMA((CHUNKS, Q - 1)),
            DMA((Q - 1,)), DMA((Q - 1,)),
            DMA((2, Q - 1)), DMA((2, Q - 1)),
            DMA((CHUNKS, C - 1)), DMA((CHUNKS, C - 1)),
            DMA((C - 1,)), DMA((C - 1,)),
        ]
        + line_sems(C),
        name="return_grads",
        compiler_params=params(5, 62 * 2**20),
    )(dgr, gates, pack, h1, gain, cot, xm, dgp, dup, select, select_t, hidden, w_gate, w_up, w_down)


def backward_kernel(
    block, da, w_in, wo, q, k, v, xnt_in, x_in, cosine, sine, pos_col, pos_row, gains, go, sp, yp,
    OH, OX, Q3, KV3, S3, T3, YP, *rest,
):
    DX = rest[: lax.axis_size("ctx")]
    (
    w, xnt, x, late, dxn, dxsem, kr, dkr, dv, acc, DQ, head_grad,
        GQ, Q1, Q2, QS, o_own, o_in, s_own, s_in, s_plane, s_sum, T, t_in, t_plane, t_sum,
        local, qlocal, csend, crecv, fsend, frecv, zsend, zrecv, qcs, qcr, qfs, qfr, qzs, qzr, ysend, yrecv,
    ) = rest[lax.axis_size("ctx") :]
    S, C, F = sizes()
    s, c, f = place()
    step = pl.program_id(0)
    units = GQ.shape[0]
    pairs = units - 1
    length, width = x.shape
    wide = 2 * HEAD_DIM
    late_loads = [
        pltpu.make_async_copy(src, dst, late.at[i])
        for i, (src, dst) in enumerate(((xnt_in, xnt), (w_in, w), (x_in, x)))
    ]
    z_peers = z_neighbours()
    f_peers = [(s, c, lax.rem(f + k, F)) for k in range(1, F)]
    sibling = (1 - s, c, f)
    cols = pl.ds(pl.multiple_of(step * wide, wide), wide)

    o_first = remote(go.at[1 - s], o_in, csend.at[0], crecv.at[0], sibling)
    t_first = remote(T, t_in, csend.at[2], crecv.at[2], sibling)
    o_load = pltpu.make_async_copy(go.at[s], o_own, local.at[0])
    half = F // 2
    mine = lax.rem(f // half, 2)
    o_saves = [
        pltpu.make_async_copy(o_own.at[pl.ds(mine * half, half)], OH, local.at[2]),
        pltpu.make_async_copy(o_own.at[pl.ds((1 - mine) * half, half)], OX, local.at[6]),
    ]
    s_first = remote(sp.at[1 - s], s_in, csend.at[1], crecv.at[1], sibling)
    s_load = pltpu.make_async_copy(sp.at[s], s_own, local.at[1])
    f_at = list(enumerate(f_peers))
    z_at = list(enumerate(z_peers))
    s_second = [remote(s_own.at[:, p[2]], s_plane.at[k], fsend.at[1, k], frecv.at[1, k], p) for k, p in f_at]
    t_second = [remote(T, t_plane.at[k], fsend.at[2, k], frecv.at[2, k], p) for k, p in f_at]
    s_third = [remote(s_sum.at[p[1]], S3.at[c], zsend.at[1, k], zrecv.at[1, k], p) for k, p in z_at]
    s_third.append(pltpu.make_async_copy(s_sum.at[c], S3.at[c], local.at[3]))
    t_third = [remote(t_sum, T3.at[c], zsend.at[2, k], zrecv.at[2, k], p) for k, p in z_at]
    t_third.append(pltpu.make_async_copy(t_sum, T3.at[c], local.at[4]))
    y_copies = [remote(yp.at[p[1]], YP.at[c], ysend.at[k], yrecv.at[k], p) for k, p in z_at]
    y_copies.append(pltpu.make_async_copy(yp.at[c], YP.at[c], local.at[5]))

    def q_first(u):
        return remote(GQ.at[u, 1 - s], Q1.at[u], qcs.at[u], qcr.at[u], sibling)

    def q_second(u):
        return [remote(GQ.at[u, s, :, p[2]], Q2.at[u, k], qfs.at[u, k], qfr.at[u, k], p) for k, p in f_at]

    def q_third(u):
        if isinstance(u, int) and u == pairs:
            landing = KV3.at[c]
        else:
            landing = Q3.at[:, pl.ds(pl.multiple_of(c * pairs * wide + u * wide, wide), wide)]
        copies = [
            remote(QS.at[u, p[1]], landing, qzs.at[u, k], qzr.at[u, k], p) for k, p in z_at
        ]
        copies.append(pltpu.make_async_copy(QS.at[u, c], landing, qlocal.at[u]))
        return copies

    def to_plane(u):
        q_first(u).wait()

        def body(i, carry):
            at = (u, s, i // F, lax.rem(i, F))
            GQ[at] = (GQ[at].astype(f32) + Q1[u, i // F, lax.rem(i, F)].astype(f32)).astype(bf16)
            return carry

        lax.fori_loop(0, C * F, body, 0)
        for copy in q_second(u):
            copy.start()

    def to_ctx(u):
        for copy in q_second(u):
            copy.wait()

        def body(i, carry):
            total = GQ[u, s, i, f].astype(f32)
            for k in range(F - 1):
                total = total + Q2[u, k, i].astype(f32)
            QS[u, i] = total.astype(bf16)
            return carry

        lax.fori_loop(0, C, body, 0)
        for copy in q_third(u):
            copy.start()

    @pl.when(step == 0)
    def _():
        for copy in late_loads:
            copy.start()
        greet_all(z_peers + f_peers + [sibling])
        for copy in [s_first, s_load, o_first, o_load] + y_copies:
            copy.start()
        unit, _ = rms_unit(k[...])
        kr[...] = half_turn(unit * gains[1:2, :], cosine[...], sine[...]).astype(bf16)
        dkr[...] = jnp.zeros_like(dkr)
        dv[...] = jnp.zeros_like(dv)
        head_grad[...] = jnp.zeros_like(head_grad)
        acc[...] = jnp.zeros_like(acc)

    @pl.when(step >= 1)
    def _():
        to_plane(step - 1)

    @pl.when(step == 1)
    def _():
        o_first.wait()
        o_load.wait()

        def o_body(i, carry):
            o_own[i] = (o_own[i].astype(f32) + o_in[i].astype(f32)).astype(bf16)
            return carry

        lax.fori_loop(0, F, o_body, 0)
        for copy in o_saves:
            copy.start()
        s_first.wait()
        s_load.wait()

        def s_body(i, carry):
            at = (i // F, lax.rem(i, F))
            s_own[at] = (s_own[at].astype(f32) + s_in[at].astype(f32)).astype(bf16)
            return carry

        lax.fori_loop(0, C * F, s_body, 0)
        for copy in s_second:
            copy.start()

    @pl.when(step >= 2)
    def _():
        to_ctx(step - 2)

    @pl.when(step == 2)
    def _():
        for copy in s_second:
            copy.wait()

        def s_body(i, carry):
            total = s_own[i, f].astype(f32)
            for k in range(F - 1):
                total = total + s_plane[k, i].astype(f32)
            s_sum[i] = total.astype(bf16)
            return carry

        lax.fori_loop(0, C, s_body, 0)
        for copy in s_third:
            copy.start()

    @pl.when(step < pairs)
    def _():
        dm = lax.dot_general(
            da[...], wo[cols, :], (((1,), (1,)), ((), ())), preferred_element_type=f32
        ).astype(bf16)
        for half in range(2):
            lanes = slice(half * HEAD_DIM, (half + 1) * HEAD_DIM)
            for part in range(length // block):
                rows = slice(part * block, (part + 1) * block)
                unit, factor = rms_unit(q[rows, lanes])
                cos, sin = cosine[rows, :], sine[rows, :]
                qr = half_turn(unit * gains[0:1, :], cos, sin).astype(bf16)
                keys = kr[...]
                probs = score_block(qr, keys, pos_col[rows, :], pos_row[...])
                dmh = dm[rows, lanes]
                dprobs = lax.dot_general(
                    dmh, v[...], (((1,), (1,)), ((), ())), preferred_element_type=f32
                )
                delta = jnp.sum(probs * dprobs, axis=-1, keepdims=True)
                dscores = (probs * (dprobs - delta)).astype(bf16)
                dqr = jnp.dot(dscores, keys, preferred_element_type=f32) * (HEAD_DIM**-0.5)
                rows_in = (((0,), (0,)), ((), ()))
                dkr[...] += lax.dot_general(dscores, qr, rows_in, preferred_element_type=f32) * (
                    HEAD_DIM**-0.5
                )
                dv[...] += lax.dot_general(
                    probs.astype(bf16), dmh, rows_in, preferred_element_type=f32
                )
                dqs = half_turn(dqr, cos, -sin)
                head_grad[0:1, :] += jnp.sum(dqs * unit, axis=0, keepdims=True)
                DQ[rows, lanes] = norm_backward(dqs, unit, factor, gains[0:1, :]).astype(bf16)

    @pl.when(step == pairs)
    def _():
        unit, factor = rms_unit(k[...])
        dks = half_turn(dkr[...], cosine[...], -sine[...])
        head_grad[1:2, :] += jnp.sum(dks * unit, axis=0, keepdims=True)
        DQ[:, :HEAD_DIM] = norm_backward(dks, unit, factor, gains[1:2, :]).astype(bf16)
        DQ[:, HEAD_DIM:] = dv[...].astype(bf16)

    @pl.when(step == 0)
    def _():
        for copy in late_loads:
            copy.wait()

    def weight_rows(i, carry):
        part = F * GQ.shape[4]
        rows = pl.ds(pl.multiple_of(i * part, 16), part)
        piece = jnp.dot(xnt[rows, :], DQ[...], preferred_element_type=f32)
        GQ[step, i // C, lax.rem(i, C)] = piece.astype(bf16).reshape(GQ.shape[3:])
        return carry

    lax.fori_loop(0, S * C, weight_rows, 0)
    q_first(step).start()
    for j in range(4):
        part = pl.ds(j * (width // 4), width // 4)
        acc[:, part] += lax.dot_general(
            DQ[...], w[part, cols], (((1,), (1,)), ((), ())), preferred_element_type=f32
        )

    @pl.when(step == pairs)
    def _():
        to_ctx(pairs - 1)
        to_plane(pairs)
        rows_of = width // HEAD_DIM
        total = jnp.zeros((1, width), f32)

        def finish(i, total):
            rows = pl.ds(i * 64, 64)
            unit, _ = rms_unit(x[rows, :].astype(f32))
            term = acc[rows, :]
            dxn[rows, :] = term.astype(bf16)
            return total + jnp.sum(term * unit, axis=0, keepdims=True)

        total = lax.fori_loop(0, length // 64, finish, total)
        rows = length // C
        x_saves = [
            pltpu.make_async_copy(
                dxn.at[pl.ds(pl.multiple_of(lax.rem(c + i, C) * rows, 16), rows)], DX[i], dxsem.at[i]
            )
            for i in range(C)
        ]
        for copy in x_saves:
            copy.start()
        for r in range(rows_of):
            T[r : r + 1, :] = total[:, r * HEAD_DIM : (r + 1) * HEAD_DIM]
        T[rows_of:, :] = head_grad[...]
        t_first.start()
        t_first.wait()
        T[...] = T[...] + t_in[...]
        for copy in t_second:
            copy.start()
        to_ctx(pairs)
        for copy in t_second:
            copy.wait()
        order = []
        for g in range(F):
            term = jnp.zeros_like(T)
            for k in range(F - 1):
                came = lax.rem(f + F - (k + 1), F)
                term = term + jnp.where(came == g, t_plane[k], 0.0)
            order.append(term + jnp.where(f == g, T[...], 0.0))
        total = order[0]
        for term in order[1:]:
            total = total + term
        t_sum[...] = total
        for copy in t_third:
            copy.start()
        for copy in s_third + y_copies + o_saves + t_third + x_saves:
            copy.wait()
        for u in range(units):
            for copy in q_third(u):
                copy.wait()


def backward(da, w, wo, q, k, v, xnt, x, cosine, sine, pos_col, pos_row, gains, go, sp, yp):
    S, C, F = sizes()
    length, width = x.shape
    head_width = wo.shape[0]
    pairs = head_width // (2 * HEAD_DIM)
    units = pairs + 1
    shard = sp.shape[3]
    block = min(length, 512)
    wide = 2 * HEAD_DIM
    once = pl.Buffered(buffer_count=1)
    whole = lambda array: pl.BlockSpec(array.shape, lambda i: (0, 0), pipeline_mode=once)
    sds = jax.ShapeDtypeStruct
    V = pltpu.VMEM
    q_block, o_block, s_block = (shard, wide), go.shape[2:], sp.shape[3:]
    t_block = (width // HEAD_DIM + 8, HEAD_DIM)
    return pl.pallas_call(
        functools.partial(backward_kernel, block),
        out_shape=[
            sds((F // 2,) + o_block, bf16),
            sds((F // 2,) + o_block, bf16),
            sds((shard, C * head_width), bf16),
            sds((C, shard, wide), bf16),
            sds((C,) + s_block, bf16),
            sds((C,) + t_block, f32),
            sds(yp.shape, bf16),
        ]
        + [sds((length // C, width), bf16)] * C,
        grid=(units,),
        in_specs=[whole(da), ANY, whole(wo)]
        + [pl.BlockSpec((length, wide), lambda i: (0, jnp.minimum(i, pairs - 1)))]
        + [whole(k), whole(v), ANY, ANY]
        + [whole(array) for array in (cosine, sine, pos_col, pos_row, gains)]
        + [ANY] * 3,
        out_specs=[ANY] * (7 + C),
        scratch_shapes=[
            V(w.shape, bf16), V(xnt.shape, bf16), V(x.shape, bf16), DMA((3,)),
            V((length, width), bf16), DMA((C,)),
            V((length, HEAD_DIM), bf16), V((length, HEAD_DIM), f32), V((length, HEAD_DIM), f32),
            V((length, width), f32), V((length, wide), bf16), V((8, HEAD_DIM), f32),
            V((units, S, C, F) + q_block, bf16), V((units, C, F) + q_block, bf16),
            V((units, F - 1, C) + q_block, bf16), V((units, C) + q_block, bf16),
            V((F,) + o_block, bf16), V((F,) + o_block, bf16),
            V((C, F) + s_block, bf16), V((C, F) + s_block, bf16), V((F - 1, C) + s_block, bf16), V((C,) + s_block, bf16),
            V(t_block, f32), V(t_block, f32), V((F - 1,) + t_block, f32), V(t_block, f32),
            DMA((7,)), DMA((units,)),
            DMA((3,)), DMA((3,)), DMA((3, F - 1)), DMA((3, F - 1)), DMA((3, C - 1)), DMA((3, C - 1)),
            DMA((units,)), DMA((units,)), DMA((units, F - 1)), DMA((units, F - 1)),
            DMA((units, C - 1)), DMA((units, C - 1)), DMA((C - 1,)), DMA((C - 1,)),
        ],
        name="attention_backward",
        compiler_params=params(7, 60 * 2**20),
    )(da, w, wo, q, k, v, xnt, x, cosine, sine, pos_col, pos_row, gains, go, sp, yp)


def dot(left, right):
    return jnp.dot(left, right, preferred_element_type=f32)


def contract_rows(left, right):
    return lax.dot_general(left, right, (((0,), (0,)), ((), ())), preferred_element_type=f32)


def times_transpose(left, right):
    return lax.dot_general(left, right, (((1,), (1,)), ((), ())), preferred_element_type=f32)


def on_device(
    tokens,
    stretch_order,
    expert_ids,
    slot_index,
    norm_attn,
    head_gains,
    w_query,
    w_key,
    w_value,
    w_out,
    norm_moe,
    w_router,
    w_gate,
    w_up,
    w_down,
    cotangent,
):
    S, C, F = sizes()
    Q = S * F
    seq_at, ctx_at, fsdp_at = place()
    rows, width = tokens.shape[1:]
    length = C * rows
    experts = w_router.shape[1]
    capacity = rows * TOP // (Q * C) + 1
    packed = round_up(C * capacity, 16)
    lanes = round_up(packed, 128)
    head_width = w_query.shape[1] // C
    shard = w_router.shape[0]
    pack_width = round_up(experts + 2, 128)
    (
        X, W, WO, PK, _, G, out_part, q, k, v, mixed, xnt, gain_attn, gain_moe, gains,
        cosine, sine, pos_col, pos_row, select, select_t, chosen, kept_map,
    ) = front(
        capacity, packed, stretch_order, expert_ids[0].T, slot_index[0].T,
        tokens[0], w_query, w_key, w_value, w_out, w_router.T, norm_attn[None], norm_moe[None],
        cotangent[0], head_gains,
    )
    W = W.reshape(width, head_width + 2 * HEAD_DIM)
    WO = WO.reshape(head_width, width)
    PK = PK.reshape(width, pack_width)
    buffer, slot_grad, _, h1, xm, gates, hidden, dgp, dup, slot_dgate = dispatch(
        packed, out_part.reshape(C, rows, width), G.reshape(length, width), tokens[0], PK, gain_moe,
        chosen, kept_map, select, w_gate, w_up, w_down,
    )
    DA, y_part, dh1, small = give_back(
        packed, experts, slot_dgate, select, select_t, gates, PK, h1, gain_moe, cotangent[0],
        xm, hidden, dgp, dup, w_gate, w_up, w_down,
    )
    DA = DA.reshape(length, width)
    grad_out_part = contract_rows(mixed, DA).astype(bf16)
    out_parts = grad_out_part.reshape(S, F, head_width // Q, width)

    def part_of(parts, at):
        return lax.dynamic_index_in_dim(parts, at, 0, keepdims=False)

    out_half, out_other, query_sum, kv_sums, small_sums, tiny_sums, y_parts, *dxn_parts = backward(
        DA, W, WO, q, k, v, xnt, X, cosine, sine, pos_col, pos_row, gains,
        out_parts,
        small.reshape(S, C, F, shard, pack_width),
        y_part.reshape(C, rows, width),
    )
    dxn = dxn_parts[0].astype(f32)
    for i in range(1, C):
        dxn += lax.ppermute(dxn_parts[i], "ctx", [(j, (j + i) % C) for j in range(C)]).astype(f32)
    out_sum, bit = out_half, F // 2
    while True:
        came = lax.ppermute(out_other, "fsdp", [(i, i ^ bit) for i in range(F)])
        out_sum = (out_sum.astype(f32) + came.astype(f32)).astype(bf16)
        bit //= 2
        if not bit:
            break
        mine = lax.rem(fsdp_at // bit, 2)
        parts = out_sum.reshape((2, bit) + out_sum.shape[1:])
        out_sum, out_other = part_of(parts, mine), part_of(parts, 1 - mine)
    out_sum = out_sum[0]
    turn = [(i * C + j, j * S + i) for i in range(S) for j in range(C)]
    o_sum = lax.ppermute(out_sum, ("seq", "ctx"), turn)
    grad_wgate = contract_rows(buffer, dgp)
    grad_wup = contract_rows(buffer, dup)
    grad_wdown = contract_rows(hidden, slot_grad)
    layer_out = (h1 + jnp.sum(y_parts.astype(f32), axis=0)).astype(bf16)
    unit, factor = rms_unit(tokens[0].astype(f32))
    grad_tokens = (dh1 + norm_backward(dxn, unit, factor, gain_attn)).astype(bf16)
    grad_query = query_sum.astype(f32)

    def key_columns(block):
        pieces = block.astype(f32).reshape(KEY_VALUE_HEADS, C // KEY_VALUE_HEADS, shard, HEAD_DIM).sum(axis=1)
        return pieces.transpose(1, 0, 2).reshape(shard, KEY_VALUE_HEADS * HEAD_DIM)

    grad_key = key_columns(kv_sums[:, :, :HEAD_DIM])
    grad_value = key_columns(kv_sums[:, :, HEAD_DIM:])
    small_sum = jnp.sum(small_sums.astype(f32), axis=0)
    tiny_sum = jnp.sum(tiny_sums, axis=0)
    tiny_rows = width // HEAD_DIM
    device = (seq_at * C + ctx_at) * F + fsdp_at
    grad_norm_attn = lax.dynamic_slice_in_dim(
        tiny_sum[:tiny_rows].reshape(width), device * shard, shard
    )
    return (
        layer_out[None],
        grad_tokens[None],
        grad_norm_attn,
        tiny_sum[tiny_rows : tiny_rows + 2],
        grad_query,
        grad_key,
        grad_value,
        o_sum.astype(f32),
        small_sum[:, experts],
        small_sum[:, :experts],
        grad_wgate[None],
        grad_wup[None],
        grad_wdown[None],
    )


def solution(mesh):
    rows = P(("seq", "fsdp"), "ctx", None)
    vector = P(AXES)
    matrix = P(AXES, None)
    cube = P(AXES, None, None)
    return jax.shard_map(
        on_device,
        mesh=mesh,
        in_specs=(
            rows, P(), rows, rows, vector, P(), matrix, matrix, matrix, matrix,
            vector, matrix, cube, cube, cube, rows,
        ),
        out_specs=(
            rows, rows, vector, P(), matrix, matrix, matrix, matrix, vector, matrix,
            cube, cube, cube,
        ),
        check_vma=False,
    )
```

```python
import functools

import jax
import jax.numpy as jnp
import numpy as np
from jax import lax
from jax.experimental import pallas as pl
from jax.experimental.pallas import tpu as pltpu
from jax.sharding import PartitionSpec as P

QUERY_HEADS = 32
KEY_VALUE_HEADS = 4
HEAD_DIM = 128
TOP = 8
AXES = ("seq", "ctx", "fsdp")
MESH = pl.DeviceIdType.MESH
epsilon = 1e-06
rope_base = 1000000.0
VMEM_LIMIT = 56 * 2**20
f32 = jnp.float32
bf16 = jnp.bfloat16


def round_up(value, step):
    return (value + step - 1) // step * step


def place():
    return tuple(lax.axis_index(name) for name in AXES)


def sizes():
    return tuple(lax.axis_size(name) for name in AXES)


def signal(device):
    pl.semaphore_signal(
        pltpu.get_barrier_semaphore(), inc=1, device_id=device, device_id_type=MESH
    )


def remote(src, dst, send, recv, device):
    return pltpu.make_async_remote_copy(
        src_ref=src,
        dst_ref=dst,
        send_sem=send,
        recv_sem=recv,
        device_id=device,
        device_id_type=MESH,
    )


def params(cid, limit=VMEM_LIMIT):
    return pltpu.CompilerParams(
        collective_id=cid, has_side_effects=True, vmem_limit_bytes=limit
    )


ANY = pl.BlockSpec(memory_space=pl.ANY)
DMA = pltpu.SemaphoreType.DMA


def rms_unit(rows):
    factor = lax.rsqrt(jnp.mean(rows * rows, axis=-1, keepdims=True) + epsilon)
    return rows * factor, factor


def norm_backward(grad_scaled, normed, factor, gain):
    grad_normed = grad_scaled * gain
    inner = jnp.mean(grad_normed * normed, axis=-1, keepdims=True)
    return factor * (grad_normed - normed * inner)


def half_turn(rows, cosine, sine):
    return rows * cosine + pltpu.roll(rows, HEAD_DIM // 2, 1) * sine


def score_block(qr, kr, pos_col, pos_row):
    scores = lax.dot_general(
        qr, kr, (((1,), (1,)), ((), ())), preferred_element_type=f32
    ) * (HEAD_DIM**-0.5)
    scores = jnp.where(pos_col >= pos_row, scores, -jnp.inf)
    peak = jnp.max(scores, axis=-1, keepdims=True)
    weight = jnp.exp(scores - peak)
    return weight * (1.0 / jnp.sum(weight, axis=-1, keepdims=True))


def z_neighbours():
    _, C, _ = sizes()
    s, c, f = place()
    return [(s, lax.rem(c + k, C), f) for k in range(1, C)]


def plane_neighbours():
    S, _, F = sizes()
    s, c, f = place()
    Q = S * F
    at = [lax.rem(s * F + f + k, Q) for k in range(1, Q)]
    return at, [(q // F, c, lax.rem(q, F)) for q in at]


def greet_all(peers):
    for peer in peers:
        signal(peer)
    pl.semaphore_wait(pltpu.get_barrier_semaphore(), len(peers))


class Line:
    def __init__(self, own, block, rsend, rrecv, lsend, lrecv):
        s, self.c, f = place()
        self.C = lax.axis_size("ctx")
        self.own, self.block = own, block
        self.sems = (rsend, rrecv, lsend, lrecv)
        self.right = (s, lax.rem(self.c + 1, self.C), f)
        self.left = (s, lax.rem(self.c + self.C - 1, self.C), f)

    def copy(self, rightward, h):
        origin = self.c - h if rightward else self.c + h
        src = self.own if h == 0 else self.block(origin)
        send, recv = self.sems[:2] if rightward else self.sems[2:]
        return remote(
            src, self.block(origin), send.at[h], recv.at[h], self.right if rightward else self.left
        )

    def sends(self, rightward, h):
        if rightward:
            return jnp.logical_and(self.c >= h, self.c < self.C - 1)
        return jnp.logical_and(self.c + h < self.C, self.c > 0)

    def start(self):
        for way in (True, False):
            pl.when(self.sends(way, 0))(self.copy(way, 0).start)

    def hop(self, h):
        for way in (True, False):
            origin = self.c - h if way else self.c + h
            there = origin >= 0 if way else origin < self.C
            landed = remote(
                self.block(origin), self.block(origin),
                self.sems[0 if way else 2].at[h - 1], self.sems[1 if way else 3].at[h - 1],
                self.left if way else self.right,
            )
            pl.when(there)(landed.wait_recv)
            if h < self.C - 1:
                pl.when(self.sends(way, h))(self.copy(way, h).start)

    def finish(self):
        for way in (True, False):
            for h in range(self.C - 1):
                pl.when(self.sends(way, h))(self.copy(way, h).wait_send)


def line_sems(C):
    return [DMA((C - 1,)) for _ in range(4)]


def front_kernel(
    block, capacity, packed, experts,
    order, ids, slot_ids, tokens, wq, wk, wv, wo, router, norm_attn, norm_moe, cot, low_gains, frequency,
    X_out, W_out, WO_out, PK, SM, G, out_out, q_out, k_out, v, mixed_t, xnt_out, gain_attn, gain_moe, gains,
    cosine, sine, pos_col, pos_row, select_out, select_t_out, chosen, kept,
    X, W, WO, xn, kr, pack, out, q, mixed, xnt, select, select_t,
    local, save, zsend, zrecv, fsend, frecv, csend, crecv, wsend, wrecv,
    xrs, xrr, xls, xlr, grs, grr, gls, glr,
):
    S, C, F = sizes()
    s, c, f = place()
    Q = S * F
    rows, width = tokens.shape
    length = C * rows
    head_width = wq.shape[1] // C
    shard = wq.shape[0]
    wide = chosen.shape[1]
    z_peers = z_neighbours()
    f_peers = [(s, c, lax.rem(f + k, F)) for k in range(1, F)]
    sibling = (1 - s, c, f)
    pair = s * C + c
    out_dst = (lax.rem(pair, S), pair // S, f)
    pair_in = c * S + s
    out_src = (pair_in // C, lax.rem(pair_in, C), f)
    stays = jnp.logical_and(out_dst[0] == s, out_dst[1] == c)
    moves = jnp.logical_not(stays)
    greet = (
        jnp.where(stays, 1 - s, out_src[0]),
        jnp.where(stays, C - 1 - c, out_src[1]),
        f,
    )
    def as_column(line):
        size = line.shape[1]
        square = lax.broadcasted_iota(jnp.int32, (size, size), 0) == lax.broadcasted_iota(
            jnp.int32, (size, size), 1
        )
        return jnp.sum(jnp.where(square, line, 0.0), axis=1, keepdims=True)

    lane = lax.broadcasted_iota(jnp.int32, (rows, wide), 1).astype(f32)
    hits = jnp.zeros((rows, wide), f32)
    slot_map = jnp.full((rows, wide), -1.0, f32)
    for j in range(TOP):
        here = lane == as_column(ids[j : j + 1, :].astype(f32))
        slot = jnp.broadcast_to(as_column(slot_ids[j : j + 1, :].astype(f32)), (rows, wide))
        hits = jnp.where(here, 1.0, hits)
        slot_map = jnp.where(jnp.logical_and(here, slot < capacity), slot, slot_map)
    lane = lax.broadcasted_iota(jnp.int32, pack.shape, 1)
    own_lane = lax.broadcasted_iota(jnp.int32, (experts, pack.shape[1]), 0) == lax.broadcasted_iota(
        jnp.int32, (experts, pack.shape[1]), 1
    )
    packed_rows = lax.dot_general(
        router[...], own_lane.astype(bf16), (((0,), (0,)), ((), ())), preferred_element_type=f32
    )
    for i, line in enumerate((norm_attn, norm_moe)):
        packed_rows = jnp.where(lane == experts + i, as_column(line[...].astype(f32)), packed_rows)
    pack[...] = packed_rows.astype(bf16)
    gains[...] = low_gains[...].astype(f32)
    chosen[...] = hits
    kept[...] = (slot_map >= 0.0).astype(f32)
    SM[c] = slot_map
    greet_all(z_peers + f_peers + [sibling, greet])

    def pieces(target):
        kv = (target * KEY_VALUE_HEADS) // C
        q_cols = pl.ds(pl.multiple_of(target * head_width, 128), head_width)
        kv_cols = pl.ds(pl.multiple_of(kv * HEAD_DIM, 128), HEAD_DIM)
        mine = W.at[s, c, f]
        return [
            (wq.at[:, q_cols], mine.at[:, pl.ds(0, head_width)]),
            (wk.at[:, kv_cols], mine.at[:, pl.ds(head_width, HEAD_DIM)]),
            (wv.at[:, kv_cols], mine.at[:, pl.ds(head_width + HEAD_DIM, HEAD_DIM)]),
            (pack, PK.at[s, c, f]),
        ]

    def token_rows(at):
        return X.at[pl.ds(pl.multiple_of(at * rows, 16), rows)]

    own = [
        pltpu.make_async_copy(src, dst, local.at[i])
        for i, (src, dst) in enumerate(pieces(c) + [(tokens, token_rows(c)), (cot, G.at[c])])
    ]
    z_copies = [
        remote(src, dst, zsend.at[i, k], zrecv.at[i, k], peer)
        for k, peer in enumerate(z_peers)
        for i, (src, dst) in enumerate(pieces(peer[1]))
    ]
    slot_copies = [
        remote(SM.at[c], SM.at[c], zsend.at[4, k], zrecv.at[4, k], peer)
        for k, peer in enumerate(z_peers)
    ]
    x_line = Line(tokens, token_rows, xrs, xrr, xls, xlr)
    g_line = Line(cot, lambda at: G.at[at], grs, grr, gls, glr)
    out_copy = remote(wo, WO.at[out_dst[0], f], wsend.at[0], wrecv.at[0], out_dst)
    out_stay = pltpu.make_async_copy(wo, WO.at[s, f], wsend.at[1])
    for copy in own + z_copies + slot_copies:
        copy.start()
    x_line.start()
    pl.when(moves)(out_copy.start)
    pl.when(stays)(out_stay.start)

    where = lax.broadcasted_iota(jnp.int32, (1, length), 1)
    where_col = lax.broadcasted_iota(jnp.int32, (length, 1), 0)
    stretch_rows = rows // 2

    def position(at):
        total = jnp.zeros_like(at)
        for j in range(2 * C):
            base = order[j] * stretch_rows - j * stretch_rows
            total = jnp.where(at // stretch_rows == j, at + base, total)
        return total

    pos_row[...] = position(where)
    pos_col[...] = position(where_col)
    angles = pos_col[...].astype(f32) * frequency[...]
    cosine[...] = jnp.cos(angles)
    turned = jnp.sin(angles)
    sine[...] = jnp.where(
        lax.broadcasted_iota(jnp.int32, turned.shape, 1) < HEAD_DIM // 2, -turned, turned
    )

    for copy in own[:5] + z_copies:
        copy.wait()

    def weight_block(index, at):
        return (W.at[s, :, at], PK.at[s, :, at], WO.at[s, at])[index]

    f_copies = [
        [
            remote(weight_block(i, f), weight_block(i, f), fsend.at[i, k], frecv.at[i, k], peer)
            for k, peer in enumerate(f_peers)
        ]
        for i in range(3)
    ]

    def to_sibling(i, k):
        at = lax.rem(f + F - k, F)
        return remote(weight_block(i, at), weight_block(i, at), csend.at[i, k], crecv.at[i, k], sibling)

    c_copies = [[to_sibling(i, k) for k in range(F)] for i in range(3)]
    for i in range(2):
        for copy in f_copies[i] + c_copies[i][:1]:
            copy.start()
    x_line.hop(1)
    for h in range(2, C - 1):
        x_line.hop(h)
    pl.when(moves)(out_copy.wait)
    pl.when(stays)(out_stay.wait)
    for copy in f_copies[2] + c_copies[2][:1]:
        copy.start()
    for k in range(F - 1):
        for i in range(2):
            f_copies[i][k].wait_recv()
            c_copies[i][k + 1].start()
    for copy in slot_copies:
        copy.wait()
    at = lax.broadcasted_iota(jnp.int32, (wide, Q * packed), 1) // packed
    expert = (at // F * C + c) * F + lax.rem(at, F)
    spread = (lax.broadcasted_iota(jnp.int32, (wide, Q * packed), 0) == expert).astype(bf16)
    slot_rows = SM[...].reshape(length, wide).astype(bf16)
    by_token = jnp.dot(slot_rows, spread, preferred_element_type=f32)
    base = (lax.broadcasted_iota(jnp.int32, by_token.shape, 0) // rows * capacity).astype(f32)
    number = lax.rem(lax.broadcasted_iota(jnp.int32, by_token.shape, 1), packed).astype(f32)
    select_t[...] = jnp.where(
        jnp.logical_and(by_token >= 0.0, by_token + base == number), 1.0, 0.0
    ).astype(bf16)
    at = lax.broadcasted_iota(jnp.int32, (Q, wide), 0)
    expert = (at // F * C + c) * F + lax.rem(at, F)
    spread = (lax.broadcasted_iota(jnp.int32, (Q, wide), 1) == expert).astype(bf16)
    by_slot = lax.dot_general(
        spread, slot_rows, (((1,), (1,)), ((), ())), preferred_element_type=f32
    )
    base = (where // rows * capacity).astype(f32)
    by_slot = jnp.where(by_slot >= 0.0, by_slot + base, -1.0)
    number = lax.broadcasted_iota(jnp.int32, (packed, length), 0).astype(f32)
    for p in range(Q):
        select[p * packed : (p + 1) * packed, :] = jnp.where(
            number == by_slot[p : p + 1, :], 1.0, 0.0
        ).astype(bf16)

    x_line.hop(C - 1)
    g_line.start()
    for i in range(2):
        for copy in c_copies[i]:
            copy.wait()
    saves = [
        pltpu.make_async_copy(src, dst, save.at[i])
        for i, (src, dst) in enumerate(
            (
                (X, X_out), (W, W_out), (select, select_out), (select_t, select_t_out),
                (WO, WO_out), (q, q_out), (out, out_out), (xnt, xnt_out),
            )
        )
    ]
    for copy in saves[:4]:
        copy.start()
    across = lax.broadcasted_iota(jnp.int32, (HEAD_DIM, HEAD_DIM), 0)
    diagonal = across == lax.broadcasted_iota(jnp.int32, (HEAD_DIM, HEAD_DIM), 1)
    flat = PK[...].reshape(width, PK.shape[-1]).astype(f32)
    for j in range(width // HEAD_DIM):
        part = slice(j * HEAD_DIM, (j + 1) * HEAD_DIM)
        for i, row in enumerate((gain_attn, gain_moe)):
            line = flat[part, experts + i : experts + i + 1]
            row[:, part] = jnp.sum(jnp.where(diagonal, line, 0.0), axis=0, keepdims=True)

    def norm_rows(i, carry):
        part = pl.ds(i * 64, 64)
        unit, _ = rms_unit(X[part, :].astype(f32))
        xn[part, :] = (unit * gain_attn[...]).astype(bf16)
        return carry

    lax.fori_loop(0, length // 64, norm_rows, 0)

    def weights(cols):
        return W[:, :, :, :, cols].reshape(width, 2 * HEAD_DIM)

    kv = jnp.dot(xn[...], weights(pl.ds(head_width, 2 * HEAD_DIM)), preferred_element_type=f32)
    k_out[...] = kv[:, :HEAD_DIM]
    v[...] = kv[:, HEAD_DIM:].astype(bf16)
    unit, _ = rms_unit(k_out[...])
    kr[...] = half_turn(unit * gains[1:2, :], cosine[...], sine[...]).astype(bf16)

    def head_pair(i, carry):
        cols = pl.ds(pl.multiple_of(i * 2 * HEAD_DIM, 2 * HEAD_DIM), 2 * HEAD_DIM)
        both = jnp.dot(xn[...], weights(cols), preferred_element_type=f32)
        q[:, cols] = both
        for half in range(2):
            lanes = pl.ds(pl.multiple_of((2 * i + half) * HEAD_DIM, HEAD_DIM), HEAD_DIM)
            for part in range(length // block):
                at = slice(part * block, (part + 1) * block)
                unit, _ = rms_unit(both[at, half * HEAD_DIM : (half + 1) * HEAD_DIM])
                qr = half_turn(unit * gains[0:1, :], cosine[at, :], sine[at, :]).astype(bf16)
                probs = score_block(qr, kr[...], pos_col[at, :], pos_row[...])
                mixed[at, lanes] = jnp.dot(
                    probs.astype(bf16), v[...], preferred_element_type=f32
                ).astype(bf16)
        return carry

    pairs = head_width // (2 * HEAD_DIM)
    half_way = pairs // 2
    hops = {}
    for h in range(1, C - 1):
        hops.setdefault(min(pairs, 1 + (h - 1) * pairs // (C - 2)), []).append(h)
    done = 0
    for stop in sorted(set(hops) | {half_way, pairs}):
        lax.fori_loop(done, stop, head_pair, 0)
        done = stop
        for h in hops.get(stop, ()):
            g_line.hop(h)
        if stop == half_way:
            for k in range(F - 1):
                f_copies[2][k].wait_recv()
                c_copies[2][k + 1].start()
    for copy in c_copies[2]:
        copy.wait()
    for copy in saves[4:6]:
        copy.start()

    def project(j, carry):
        cols = pl.ds(pl.multiple_of(j * 256, 256), 256)
        out[:, cols] = jnp.dot(
            mixed[...], WO[:, :, :, cols].reshape(head_width, 256), preferred_element_type=f32
        ).astype(bf16)
        return carry

    lax.fori_loop(0, width // 256, project, 0)
    saves[6].start()

    def turn(j, carry):
        cols = pl.ds(pl.multiple_of(j * 256, 256), 256)
        xnt[cols, :] = xn[:, cols].T
        return carry

    lax.fori_loop(0, width // 256, turn, 0)
    saves[7].start()

    def turn_mixed(j, carry):
        cols = pl.ds(pl.multiple_of(j * 256, 256), 256)
        mixed_t[cols, :] = mixed[:, cols].T
        return carry

    lax.fori_loop(0, head_width // 256, turn_mixed, 0)
    g_line.hop(C - 1)
    x_line.finish()
    g_line.finish()
    for line in f_copies:
        for copy in line:
            copy.wait_send()
    for copy in saves + own[5:]:
        copy.wait()


def front(
    capacity, packed, order, ids, slot_ids, tokens, wq, wk, wv, wo, router, norm_attn, norm_moe, cot, gains
):
    S, C, F = sizes()
    Q = S * F
    rows, width = tokens.shape
    length = C * rows
    shard = wq.shape[0]
    head_width = wq.shape[1] // C
    experts = router.shape[0]
    wide = round_up(experts, 128)
    frequency = np.power(rope_base, -np.arange(HEAD_DIM // 2) * 2.0 / HEAD_DIM)
    frequency = jnp.asarray(np.tile(frequency, 2)[None].astype(np.float32))
    block = min(length, 512)
    sds = jax.ShapeDtypeStruct
    V = pltpu.VMEM
    vm = pl.BlockSpec(memory_space=pltpu.VMEM)
    w_shape = (S, C, F, shard, head_width + 2 * HEAD_DIM)
    wo_shape = (S, F) + wo.shape
    pack_block = (shard, round_up(experts + 2, 128))
    pack_shape = (S, C, F) + pack_block
    return pl.pallas_call(
        functools.partial(front_kernel, block, capacity, packed, experts),
        out_shape=[
            sds((length, width), bf16),
            sds(w_shape, bf16),
            sds(wo_shape, bf16),
            sds(pack_shape, bf16),
            sds((C, rows, wide), f32),
            sds((C, rows, width), bf16),
            sds((length, width), bf16),
            sds((length, head_width), f32),
            sds((length, HEAD_DIM), f32),
            sds((length, HEAD_DIM), bf16),
            sds((head_width, length), bf16),
            sds((width, length), bf16),
            sds((1, width), f32),
            sds((1, width), f32),
            sds(gains.shape, f32),
            sds((length, HEAD_DIM), f32),
            sds((length, HEAD_DIM), f32),
            sds((length, 1), jnp.int32),
            sds((1, length), jnp.int32),
            sds((Q * packed, length), bf16),
            sds((length, Q * packed), bf16),
            sds((rows, wide), f32),
            sds((rows, wide), f32),
        ],
        in_specs=[pl.BlockSpec(memory_space=pltpu.SMEM), vm, vm] + [ANY] * 5 + [vm] * 3 + [ANY, vm, vm],
        out_specs=[ANY] * 3 + [vm, vm] + [ANY] * 3 + [vm] * 3 + [ANY] + [vm] * 7 + [ANY] * 2 + [vm] * 2,
        scratch_shapes=[
            V((length, width), bf16),
            V(w_shape, bf16),
            V(wo_shape, bf16),
            V((length, width), bf16),
            V((length, HEAD_DIM), bf16),
            V(pack_block, bf16),
            V((length, width), bf16),
            V((length, head_width), f32),
            V((length, head_width), bf16),
            V((width, length), bf16),
            V((Q * packed, length), bf16),
            V((length, Q * packed), bf16),
            DMA((6,)), DMA((9,)),
            DMA((5, C - 1)), DMA((5, C - 1)),
            DMA((3, F - 1)), DMA((3, F - 1)),
            DMA((3, F)), DMA((3, F)),
            DMA((2,)), DMA((1,)),
        ]
        + line_sems(C)
        + line_sems(C),
        name="gather_and_attend",
        compiler_params=params(1, 60 * 2**20),
    )(order, ids, slot_ids, tokens, wq, wk, wv, wo, router, norm_attn, norm_moe, cot, gains, frequency)


CHUNKS = 8


def columns(width, j):
    step = width // CHUNKS
    return pl.ds(j * step, step)


def three_parts(line):
    high = line.astype(bf16).astype(f32)
    rest = line - high
    middle = rest.astype(bf16).astype(f32)
    row = lax.broadcasted_iota(jnp.int32, (16, line.shape[1]), 0)
    rows = jnp.where(row == 0, high, jnp.where(row == 1, middle, jnp.where(row == 2, rest - middle, 0.0)))
    return rows.astype(bf16)


def halves(total):
    return total // 2


def dispatch_kernel(
    packed, out_part, G_in, tokens, pack, gain, chosen, kept, select, w_gate, w_up, w_down,
    buffer_out, gbuf, wrow, h1, xm, gates, hidden_out, dgp_out, dup_out, dgr,
    OP, RB, XM, SL, WM, WS, G, SG, buffer, WG, WU, WD, gp, up, gw, dup,
    local, load, saved, osend, orecv, gsend, grecv, xsend, xrecv, msend, mrecv, bsend, brecv, wsend, wrecv,
):
    S, C, F = sizes()
    s, c, f = place()
    Q = S * F
    q = s * F + f
    rows, width = tokens.shape
    total_rows = Q * packed
    half = halves(total_rows)
    z_peers = z_neighbours()
    p_at, p_peers = plane_neighbours()
    loads = [
        pltpu.make_async_copy(G_in, G, load.at[0]),
        pltpu.make_async_copy(w_down.at[0], WD, load.at[1]),
        pltpu.make_async_copy(w_gate.at[0], WG, load.at[2]),
        pltpu.make_async_copy(w_up.at[0], WU, load.at[3]),
    ]
    for copy in loads:
        copy.start()
    greet_all(z_peers + p_peers)
    mine = pl.ds(pl.multiple_of(q * packed, 16), packed)
    own_rows = pl.ds(pl.multiple_of(c * rows, 16), rows)
    right = (s, lax.rem(c + 1, C), f)
    left = (s, lax.rem(c + C - 1, C), f)

    def rightward(t):
        return remote(OP.at[t], RB.at[t], osend.at[0, t], orecv.at[0, t], right)

    def leftward(t):
        return remote(OP.at[t], RB.at[jnp.where(c - 1 == t, C, t)], osend.at[1, t], orecv.at[1, t], left)

    def merge(t, way):
        remote(OP.at[t], RB.at[t], osend.at[way, t], orecv.at[way, t], left).wait_recv()

        def add(j, carry):
            part = pl.ds(j * 32, 32)
            OP[t, part, :] = (OP[t, part, :].astype(f32) + RB[t, part, :].astype(f32)).astype(bf16)
            return carry

        lax.fori_loop(0, rows // 32, add, 0)

    def pass_on(step):
        t_right = C - 1 + c - step
        t_left = step - (C - 1 - c)

        @pl.when((t_right > c) & (t_right < C) & (c > 0))
        def _():
            merge(t_right, 0)
            rightward(t_right).start()

        @pl.when((t_left >= 0) & (t_left < c) & (c < C - 1))
        def _():
            merge(t_left, 1)
            leftward(t_left).start()

    fetch = pltpu.make_async_copy(out_part, OP, local.at[0])
    fetch.start()
    fetch.wait()

    @pl.when(c == 0)
    def _():
        for t in range(C - 1, 0, -1):
            rightward(t).start()

    @pl.when(c == C - 1)
    def _():
        for t in range(C - 1):
            leftward(t).start()

    loads[0].wait()

    def grad_slots(p):
        at = pl.ds(pl.multiple_of(p * packed, 16), packed)

        def body(j, carry):
            cols = pl.ds(pl.multiple_of(j * 512, 512), 512)
            SG[at, cols] = jnp.dot(select[at, :], G[:, cols], preferred_element_type=f32).astype(bf16)
            return carry

        lax.fori_loop(0, width // 512, body, 0)

    later = []
    for k, peer in enumerate(p_peers):
        theirs = pl.ds(pl.multiple_of(p_at[k] * packed, 16), packed)
        later.append(remote(SG.at[theirs], gbuf.at[mine], gsend.at[k], grecv.at[k], peer))
        grad_slots(p_at[k])
        later[-1].start()
    grad_slots(q)
    later.append(pltpu.make_async_copy(SG.at[mine], gbuf.at[mine], local.at[1]))
    later[-1].start()
    for step in range(1, C - 1):
        pass_on(step)

    @pl.when(c > 0)
    def _():
        remote(OP.at[0], RB.at[c], osend.at[0, c], orecv.at[0, c], left).wait_recv()

    @pl.when(c < C - 1)
    def _():
        remote(OP.at[0], RB.at[C], osend.at[1, c], orecv.at[1, c], right).wait_recv()


    def head_rows(i, carry):
        part = pl.ds(i * 32, 32)
        total = tokens[part, :].astype(f32) + OP[c, part, :].astype(f32)
        total += jnp.where(c > 0, RB[c, part, :].astype(f32), 0.0)
        total += jnp.where(c < C - 1, RB[C, part, :].astype(f32), 0.0)
        h1[part, :] = total
        unit, _ = rms_unit(total)
        normed = (unit * gain[...]).astype(bf16)
        xm[part, :] = normed
        XM[pl.ds(pl.multiple_of(c * rows + i * 32, 16), 32), :] = normed
        return carry

    lax.fori_loop(0, rows // 32, head_rows, 0)
    chunks = []
    for j in range(CHUNKS):
        piece = XM.at[own_rows, columns(width, j)]
        chunks.append(
            [remote(piece, piece, xsend.at[j, k], xrecv.at[j, k], peer) for k, peer in enumerate(z_peers)]
        )
    for copy in chunks[0]:
        copy.start()
    logits = jnp.dot(xm[...], pack[...], preferred_element_type=f32)[:, : chosen.shape[1]]
    logits = jnp.where(chosen[...] > 0.0, logits, -jnp.inf)
    power = jnp.exp(logits - jnp.max(logits, axis=-1, keepdims=True))
    gates[...] = power / jnp.sum(power, axis=-1, keepdims=True)
    WM[own_rows, :] = gates[...] * kept[...]
    row = []
    for k, peer in enumerate(z_peers):
        piece = WM.at[own_rows, :]
        row.append(remote(piece, piece, msend.at[k], mrecv.at[k], peer))
        row[-1].start()
    for line in chunks[1:]:
        for copy in line:
            copy.start()
    sent = []
    for j in range(CHUNKS):
        cols = columns(width, j)
        for copy in chunks[j]:
            copy.wait_recv()

        def slots(i, carry):
            at = pl.ds(pl.multiple_of(i * half, 16), half)
            SL[at, cols] = jnp.dot(select[at, :], XM[:, cols], preferred_element_type=f32).astype(bf16)
            return carry

        lax.fori_loop(0, 2, slots, 0)
        line = []
        for k, peer in enumerate(p_peers):
            theirs = pl.ds(pl.multiple_of(p_at[k] * packed, 16), packed)
            line.append(
                remote(SL.at[theirs, cols], buffer.at[mine, cols], bsend.at[j, k], brecv.at[j, k], peer)
            )
        line.append(pltpu.make_async_copy(SL.at[mine, cols], buffer.at[mine, cols], local.at[4 + j]))
        for copy in line:
            copy.start()
        sent.append(line)
        if j == 0:
            for copy in row:
                copy.wait_recv()
            WS[...] = jnp.zeros_like(WS)

            place_of = lax.broadcasted_iota(jnp.int32, (Q, WM.shape[1]), 0)
            expert = (place_of // F * C + c) * F + lax.rem(place_of, F)
            spread = (lax.broadcasted_iota(jnp.int32, expert.shape, 1) == expert).astype(f32)
            lines = lax.dot_general(
                spread, WM[...], (((1,), (1,)), ((), ())),
                precision=lax.Precision.HIGHEST, preferred_element_type=f32,
            )
            for p in range(Q):
                line = lax.dot_general(
                    three_parts(lines[p : p + 1, :]), select[p * packed : (p + 1) * packed, :],
                    (((1,), (1,)), ((), ())), preferred_element_type=f32,
                )
                WS[p, :, pl.ds(0, packed)] = jnp.broadcast_to(
                    jnp.sum(line, axis=0, keepdims=True), (8, packed)
                )
            scales = [
                remote(WS.at[p_at[k]], wrow.at[q], wsend.at[k], wrecv.at[k], peer)
                for k, peer in enumerate(p_peers)
            ]
            scales.append(pltpu.make_async_copy(WS.at[q], wrow.at[q], local.at[2]))
            for copy in scales:
                copy.start()
        if j == CHUNKS - 2:
            for copy in later + loads[1:]:
                copy.wait()
            reload = pltpu.make_async_copy(gbuf, SG, local.at[3])
            reload.start()
            reload.wait()

            def through_down(i, carry):
                at = pl.ds(pl.multiple_of(i * half, 16), half)
                gw[at, :] = lax.dot_general(
                    SG[at, :], WD[...], (((1,), (1,)), ((), ())), preferred_element_type=f32
                )
                return carry

            lax.fori_loop(0, 2, through_down, 0)
    for j in range(CHUNKS - 1):
        cols = columns(width, j)
        for copy in sent[j]:
            copy.wait()

        def project(i, carry):
            at = pl.ds(pl.multiple_of(i * half, 16), half)
            part = buffer[at, cols]
            one = jnp.dot(part, WG[cols, :], preferred_element_type=f32)
            two = jnp.dot(part, WU[cols, :], preferred_element_type=f32)
            gp[at, :] = one if j == 0 else gp[at, :] + one
            up[at, :] = two if j == 0 else up[at, :] + two
            return carry

        lax.fori_loop(0, 2, project, 0)
    for copy in scales:
        copy.wait()
    diagonal = lax.broadcasted_iota(jnp.int32, (packed, packed), 0) == lax.broadcasted_iota(
        jnp.int32, (packed, packed), 1
    )
    dgr[...] = jnp.zeros_like(dgr)
    cols = columns(width, CHUNKS - 1)
    inner = dup.shape[-1]
    hidden, dgp = SG.at[:, pl.ds(0, inner)], SG.at[:, pl.ds(inner, inner)]

    def saves_of(p):
        at = pl.ds(pl.multiple_of(p * packed, 16), packed)
        pairs = ((buffer, buffer_out), (hidden, hidden_out), (dgp, dgp_out), (dup, dup_out))
        return [
            pltpu.make_async_copy(src.at[at], dst.at[at], saved.at[i, p])
            for i, (src, dst) in enumerate(pairs)
        ]

    def expert_rows(p):
        at = pl.ds(pl.multiple_of(p * packed, 16), packed)
        part = buffer[at, cols]
        gate_pre = gp[at, :] + jnp.dot(part, WG[cols, :], preferred_element_type=f32)
        up_pre = up[at, :] + jnp.dot(part, WU[cols, :], preferred_element_type=f32)
        back = gw[at, :]
        scale = jnp.sum(
            jnp.where(diagonal, wrow[p, 0:1, pl.ds(0, packed)], 0.0), axis=1, keepdims=True
        )
        sigmoid = jax.nn.sigmoid(gate_pre)
        silu = gate_pre * sigmoid
        low = (silu * up_pre).astype(bf16)
        hidden[at, :] = (scale * low.astype(f32)).astype(bf16)
        dgate = jnp.sum(back * low.astype(f32), axis=-1, keepdims=True)
        line = jnp.sum(jnp.where(diagonal, dgate, 0.0), axis=0, keepdims=True)
        dgr[p, :, pl.ds(0, packed)] = jnp.broadcast_to(line, (8, packed))
        dhid = scale * back
        dgp[at, :] = (dhid * up_pre * sigmoid * (1.0 + gate_pre * (1.0 - sigmoid))).astype(bf16)
        dup[at, :] = (dhid * silu).astype(bf16)
        for copy in saves_of(p):
            copy.start()

    sent[CHUNKS - 1][Q - 1].wait()
    expert_rows(q)

    def arrival(k, carry):
        p = lax.rem(q + Q - 1 - k, Q)
        at = pl.ds(pl.multiple_of(p * packed, 16), packed)
        came = (p // F, c, lax.rem(p, F))
        remote(
            SL.at[at, cols], buffer.at[at, cols], bsend.at[CHUNKS - 1, k], brecv.at[CHUNKS - 1, k], came
        ).wait_recv()
        expert_rows(p)
        return carry

    lax.fori_loop(0, Q - 1, arrival, 0)
    for copy in sent[CHUNKS - 1][: Q - 1]:
        copy.wait_send()
    for line in chunks + [row]:
        for copy in line:
            copy.wait_send()

    @pl.when(c < C - 1)
    def _():
        def body(t, carry):
            rightward(t).wait_send()
            return carry

        lax.fori_loop(c + 1, C, body, 0)

    @pl.when(c > 0)
    def _():
        def body(t, carry):
            leftward(t).wait_send()
            return carry

        lax.fori_loop(0, c, body, 0)

    for p in range(Q):
        for copy in saves_of(p):
            copy.wait()


def dispatch(packed, out_part, G, tokens, pack, gain, chosen, kept, select, w_gate, w_up, w_down):
    S, C, F = sizes()
    Q = S * F
    rows, width = tokens.shape
    inner = w_gate.shape[-1]
    lanes = round_up(packed, 128)
    wide = chosen.shape[1]
    V = pltpu.VMEM
    sds = jax.ShapeDtypeStruct
    vm = pl.BlockSpec(memory_space=pltpu.VMEM)
    slots = Q * packed
    return pl.pallas_call(
        functools.partial(dispatch_kernel, packed),
        out_shape=[
            sds((slots, width), bf16),
            sds((slots, width), bf16),
            sds((Q, 8, lanes), f32),
            sds((rows, width), f32),
            sds((rows, width), bf16),
            sds((rows, wide), f32),
            sds((slots, inner), bf16),
            sds((slots, inner), bf16),
            sds((slots, inner), bf16),
            sds((Q, 8, lanes), f32),
        ],
        in_specs=[ANY, ANY] + [vm] * 6 + [ANY] * 3,
        out_specs=[ANY, ANY, vm, vm, vm, vm, ANY, ANY, ANY, vm],
        scratch_shapes=[
            V((C, rows, width), bf16),
            V((C + 1, rows, width), bf16),
            V((C * rows, width), bf16),
            V((slots, width), bf16),
            V((C * rows, wide), f32),
            V((Q, 8, lanes), f32),
            V((C * rows, width), bf16),
            V((slots, width), bf16),
            V((slots, width), bf16),
            V((width, inner), bf16), V((width, inner), bf16), V((inner, width), bf16),
            V((slots, inner), f32), V((slots, inner), f32), V((slots, inner), f32),
            V((slots, inner), bf16),
            DMA((4 + CHUNKS,)),
            DMA((4,)),
            DMA((4, Q)),
            DMA((2, C)), DMA((2, C)),
            DMA((Q - 1,)), DMA((Q - 1,)),
            DMA((CHUNKS, C - 1)), DMA((CHUNKS, C - 1)),
            DMA((C - 1,)), DMA((C - 1,)),
            DMA((CHUNKS, Q - 1)), DMA((CHUNKS, Q - 1)),
            DMA((Q - 1,)), DMA((Q - 1,)),
        ],
        name="dispatch_rows",
        compiler_params=params(3, 62 * 2**20),
    )(out_part, G, tokens, pack, gain, chosen, kept, select, w_gate, w_up, w_down)


def return_kernel(
    packed, experts, dgr, gates, pack, h1, gain, cot, xm, dgp, dup,
    select_in, select_t_in, hidden_in, w_gate, w_up, w_down,
    DA, y_part, dh1, small,
    RD, YB, PART, RX, DG, DGP, RG, DL, din, wy, WG, WU, WD, dlog, gnorm, DXR, select, select_t, hidden,
    local, load, dsend, drecv, gsend, grecv, ysend, yrecv, xsend, xrecv, msend, mrecv, *asems,
):
    S, C, F = sizes()
    s, c, f = place()
    Q = S * F
    q = s * F + f
    rows, width = h1.shape
    z_peers = z_neighbours()
    p_at, p_peers = plane_neighbours()
    loads = []
    for j in range(CHUNKS):
        cols = columns(width, j)
        loads.append(
            [
                pltpu.make_async_copy(w_gate.at[0, cols], WG.at[cols], load.at[0, j]),
                pltpu.make_async_copy(w_up.at[0, cols], WU.at[cols], load.at[1, j]),
            ]
        )
    load_down = pltpu.make_async_copy(w_down.at[0], WD, load.at[2, 0])
    late = [
        pltpu.make_async_copy(hidden_in, hidden, load.at[2, 1]),
        pltpu.make_async_copy(select_t_in, select_t, load.at[2, 2]),
        pltpu.make_async_copy(select_in, select, load.at[2, 3]),
    ]
    for line in loads:
        for copy in line:
            copy.start()
    load_down.start()
    for copy in late:
        copy.start()
    greet_all(z_peers + p_peers)
    half = halves(Q * packed)
    mine = pl.ds(pl.multiple_of(q * packed, 16), packed)
    theirs = [pl.ds(pl.multiple_of(at * packed, 16), packed) for at in p_at]
    inner_products = [
        remote(dgr.at[p_at[k]], DG.at[q], gsend.at[k], grecv.at[k], peer)
        for k, peer in enumerate(p_peers)
    ]
    inner_products.append(pltpu.make_async_copy(dgr.at[q], DG.at[q], local.at[0]))
    for copy in inner_products:
        copy.start()
    chunks = []
    for j in range(CHUNKS):
        cols = columns(width, j)
        for copy in loads[j]:
            copy.wait()

        def expert_in(i, carry):
            at = pl.ds(pl.multiple_of(i * half, 16), half)
            across = (((1,), (1,)), ((), ()))
            total = lax.dot_general(dgp[at, :], WG[cols, :], across, preferred_element_type=f32)
            total += lax.dot_general(dup[at, :], WU[cols, :], across, preferred_element_type=f32)
            din[at, cols] = total.astype(bf16)
            return carry

        lax.fori_loop(0, 2, expert_in, 0)
        line = [
            remote(din.at[theirs[k], cols], RD.at[mine, cols], dsend.at[j, k], drecv.at[j, k], peer)
            for k, peer in enumerate(p_peers)
        ]
        line.append(pltpu.make_async_copy(din.at[mine, cols], RD.at[mine, cols], local.at[2 + j]))
        for copy in line:
            copy.start()
        chunks.append(line)
    load_down.wait()
    for copy in late:
        copy.wait()
    def expert_out(i, carry):
        at = pl.ds(pl.multiple_of(i * half, 16), half)

        def body(j, carry):
            cols = pl.ds(pl.multiple_of(j * 512, 512), 512)
            y = jnp.dot(hidden[at, :], WD[:, cols], preferred_element_type=f32)
            wy[at, cols] = y.astype(bf16)
            return carry

        return lax.fori_loop(0, width // 512, body, carry)

    lax.fori_loop(0, 2, expert_out, 0)
    sums = []
    for j in range(CHUNKS):
        if j == CHUNKS - 1:
            ys = []
            for jj in range(2):
                cols = pl.ds(jj * (width // 2), width // 2)
                line = [
                    remote(wy.at[theirs[k], cols], YB.at[mine, cols], ysend.at[jj, k], yrecv.at[jj, k], peer)
                    for k, peer in enumerate(p_peers)
                ]
                line.append(pltpu.make_async_copy(wy.at[mine, cols], YB.at[mine, cols], local.at[(1, 2 + CHUNKS + 1)[jj]]))
                for copy in line:
                    copy.start()
                ys.append(line)
        cols = columns(width, j)
        for copy in chunks[j]:
            copy.wait()

        def combine(i, carry):
            lanes = pl.ds(pl.multiple_of(j * (width // CHUNKS) + i * 256, 256), 256)
            PART[:, lanes] = jnp.dot(
                select_t[...], RD[:, lanes], preferred_element_type=f32
            ).astype(bf16)
            return carry

        lax.fori_loop(0, width // CHUNKS // 256, combine, 0)
        for k, peer in enumerate(z_peers):
            src = PART.at[pl.ds(pl.multiple_of(peer[1] * rows, 16), rows), cols]
            sums.append(remote(src, RX.at[k, :, cols], xsend.at[j, k], xrecv.at[j, k], peer))
            sums[-1].start()
    for copy in inner_products:
        copy.wait()
    wide = gates.shape[1]
    place_of = lax.broadcasted_iota(jnp.int32, (Q, wide), 0)
    expert = (place_of // F * C + c) * F + lax.rem(place_of, F)
    spread = (lax.broadcasted_iota(jnp.int32, (Q, wide), 1) == expert).astype(f32)

    for p in range(Q):
        at = pl.ds(p * packed, packed)
        line = jnp.dot(
            three_parts(DG[p, 0:1, pl.ds(0, packed)]), select[at, :], preferred_element_type=f32
        )
        DL[pl.ds(p, 1), :] = jnp.sum(line, axis=0, keepdims=True)
    DGP[...] = lax.dot_general(
        DL[...], spread, (((0,), (0,)), ((), ())),
        precision=lax.Precision.HIGHEST, preferred_element_type=f32,
    ).reshape(DGP.shape)
    more = []
    for k, peer in enumerate(z_peers):
        more.append(remote(DGP.at[peer[1]], RG.at[k], msend.at[k], mrecv.at[k], peer))
        more[-1].start()
    for copy in more:
        copy.wait()
    total = DGP[c]
    for k in range(C - 1):
        total = total + RG[k]
    dlogits = gates[...] * (total - jnp.sum(gates[...] * total, axis=-1, keepdims=True))
    dlog[...] = dlogits.astype(bf16)
    gnorm[...] = jnp.zeros_like(gnorm)
    DXR[...] = lax.dot_general(
        dlog[...], pack[:, pl.ds(0, wide)], (((1,), (1,)), ((), ())), preferred_element_type=f32
    )
    for copy in sums:
        copy.wait()

    def head_rows(i, carry):
        part = pl.ds(i * 32, 32)
        mine_part = pl.ds(pl.multiple_of(c * rows + i * 32, 16), 32)
        dxm = PART[mine_part, :].astype(f32)
        for k in range(C - 1):
            dxm = dxm + RX[k, part, :].astype(f32)
        dxm = dxm + DXR[part, :]
        unit, factor = rms_unit(h1[part, :])
        gnorm[...] += jnp.sum(dxm * unit, axis=0, keepdims=True)
        grad = cot[part, :].astype(f32) + norm_backward(dxm, unit, factor, gain[...])
        dh1[part, :] = grad
        RX[0, part, :] = grad.astype(bf16)
        return carry

    lax.fori_loop(0, rows // 32, head_rows, 0)
    keep = pltpu.make_async_copy(RX.at[0], DA.at[c], local.at[2 + CHUNKS])
    keep.start()
    line = Line(RX.at[0], lambda at: DA.at[at], *asems)
    line.start()
    for h in range(1, C - 1):
        line.hop(h)
    square = lax.broadcasted_iota(jnp.int32, (HEAD_DIM, HEAD_DIM), 0) == lax.broadcasted_iota(
        jnp.int32, (HEAD_DIM, HEAD_DIM), 1
    )
    small[...] = jnp.zeros_like(small)

    def small_rows(i, carry):
        at = pl.ds(pl.multiple_of(i * HEAD_DIM, HEAD_DIM), HEAD_DIM)
        router_part = lax.dot_general(
            xm[:, at], dlog[...], (((0,), (0,)), ((), ())), preferred_element_type=f32
        )
        column = jnp.sum(jnp.where(square, gnorm[:, at], 0.0), axis=1, keepdims=True)
        if wide > experts:
            lane = lax.broadcasted_iota(jnp.int32, router_part.shape, 1)
            small[at, :] = jnp.where(lane == experts, column, router_part).astype(bf16)
        else:
            small[at, pl.ds(0, wide)] = router_part.astype(bf16)
            lane = lax.broadcasted_iota(jnp.int32, (HEAD_DIM, HEAD_DIM), 1)
            small[at, pl.ds(wide, HEAD_DIM)] = jnp.where(lane == 0, column, 0.0).astype(bf16)
        return carry

    lax.fori_loop(0, width // HEAD_DIM, small_rows, 0)

    def combine_y(i, carry):
        lanes = pl.ds(pl.multiple_of(i * 256, 256), 256)
        y_part[:, lanes] = jnp.dot(
            select_t[...], YB[:, lanes], preferred_element_type=f32
        ).astype(bf16)
        return carry

    for j in range(2):
        for copy in ys[j]:
            copy.wait()
        lax.fori_loop(j * (width // 512), (j + 1) * (width // 512), combine_y, 0)
    line.hop(C - 1)
    line.finish()
    keep.wait()


def give_back(
    packed, experts, dgr, select, select_t, gates, pack, h1, gain, cot, xm, hidden, dgp, dup, w_gate, w_up, w_down
):
    S, C, F = sizes()
    Q = S * F
    rows, width = h1.shape
    wide = gates.shape[1]
    inner = w_gate.shape[-1]
    V = pltpu.VMEM
    sds = jax.ShapeDtypeStruct
    vm = pl.BlockSpec(memory_space=pltpu.VMEM)
    return pl.pallas_call(
        functools.partial(return_kernel, packed, experts),
        out_shape=[
            sds((C, rows, width), bf16),
            sds((C * rows, width), bf16),
            sds((rows, width), f32),
            sds(pack.shape, bf16),
        ],
        in_specs=[vm] * 9 + [ANY] * 6,
        out_specs=[ANY] + [vm] * 3,
        scratch_shapes=[
            V((Q * packed, width), bf16),
            V((Q * packed, width), bf16),
            V((C * rows, width), bf16),
            V((C - 1, rows, width), bf16),
            V(dgr.shape, f32),
            V((C, rows, wide), f32),
            V((C - 1, rows, wide), f32),
            V((Q, C * rows), f32),
            V((Q * packed, width), bf16),
            V((Q * packed, width), bf16),
            V((width, inner), bf16), V((width, inner), bf16), V((inner, width), bf16),
            V((rows, wide), bf16),
            V((1, width), f32),
            V((rows, width), f32),
            V(select.shape, bf16), V(select_t.shape, bf16), V(hidden.shape, bf16),
            DMA((4 + CHUNKS,)),
            DMA((3, CHUNKS)),
            DMA((CHUNKS, Q - 1)), DMA((CHUNKS, Q - 1)),
            DMA((Q - 1,)), DMA((Q - 1,)),
            DMA((2, Q - 1)), DMA((2, Q - 1)),
            DMA((CHUNKS, C - 1)), DMA((CHUNKS, C - 1)),
            DMA((C - 1,)), DMA((C - 1,)),
        ]
        + line_sems(C),
        name="return_grads",
        compiler_params=params(5, 62 * 2**20),
    )(dgr, gates, pack, h1, gain, cot, xm, dgp, dup, select, select_t, hidden, w_gate, w_up, w_down)


def backward_kernel(
    block, da, w_in, wo, q, k, v, xnt_in, x_in, cosine, sine, pos_col, pos_row, gains, mixed_t, sp, yp,
    OH, OX, Q3, KV3, S3, T3, YP, *rest,
):
    DX = rest[: lax.axis_size("ctx")]
    (
    w, xnt, x, late, dxn, dxsem, kr, dkr, dv, acc, DQ, head_grad,
        GQ, Q1, Q2, QS, GO, o_in, s_own, s_in, s_plane, s_sum, T, t_in, t_plane, t_sum,
        local, qlocal, csend, crecv, fsend, frecv, zsend, zrecv, qcs, qcr, qfs, qfr, qzs, qzr, ysend, yrecv,
    ) = rest[lax.axis_size("ctx") :]
    S, C, F = sizes()
    s, c, f = place()
    step = pl.program_id(0)
    units = GQ.shape[0]
    pairs = units - 1
    length, width = x.shape
    wide = 2 * HEAD_DIM
    late_loads = [
        pltpu.make_async_copy(src, dst, late.at[i])
        for i, (src, dst) in enumerate(((xnt_in, xnt), (w_in, w), (x_in, x)))
    ]
    z_peers = z_neighbours()
    f_peers = [(s, c, lax.rem(f + k, F)) for k in range(1, F)]
    sibling = (1 - s, c, f)
    cols = pl.ds(pl.multiple_of(step * wide, wide), wide)

    o_own = GO.at[s]
    o_first = remote(GO.at[1 - s], o_in, csend.at[0], crecv.at[0], sibling)
    t_first = remote(T, t_in, csend.at[2], crecv.at[2], sibling)
    half = F // 2
    mine = lax.rem(f // half, 2)
    o_saves = [
        pltpu.make_async_copy(o_own.at[pl.ds(mine * half, half)], OH, local.at[2]),
        pltpu.make_async_copy(o_own.at[pl.ds((1 - mine) * half, half)], OX, local.at[6]),
    ]
    s_first = remote(sp.at[1 - s], s_in, csend.at[1], crecv.at[1], sibling)
    s_load = pltpu.make_async_copy(sp.at[s], s_own, local.at[1])
    f_at = list(enumerate(f_peers))
    z_at = list(enumerate(z_peers))
    s_second = [remote(s_own.at[:, p[2]], s_plane.at[k], fsend.at[1, k], frecv.at[1, k], p) for k, p in f_at]
    t_second = [remote(T, t_plane.at[k], fsend.at[2, k], frecv.at[2, k], p) for k, p in f_at]
    s_third = [remote(s_sum.at[p[1]], S3.at[c], zsend.at[1, k], zrecv.at[1, k], p) for k, p in z_at]
    s_third.append(pltpu.make_async_copy(s_sum.at[c], S3.at[c], local.at[3]))
    t_third = [remote(t_sum, T3.at[c], zsend.at[2, k], zrecv.at[2, k], p) for k, p in z_at]
    t_third.append(pltpu.make_async_copy(t_sum, T3.at[c], local.at[4]))
    y_copies = [remote(yp.at[p[1]], YP.at[c], ysend.at[k], yrecv.at[k], p) for k, p in z_at]
    y_copies.append(pltpu.make_async_copy(yp.at[c], YP.at[c], local.at[5]))

    def q_first(u):
        return remote(GQ.at[u, 1 - s], Q1.at[u], qcs.at[u], qcr.at[u], sibling)

    def q_second(u):
        return [remote(GQ.at[u, s, :, p[2]], Q2.at[u, k], qfs.at[u, k], qfr.at[u, k], p) for k, p in f_at]

    def q_third(u):
        if isinstance(u, int) and u == pairs:
            landing = KV3.at[c]
        else:
            landing = Q3.at[:, pl.ds(pl.multiple_of(c * pairs * wide + u * wide, wide), wide)]
        copies = [
            remote(QS.at[u, p[1]], landing, qzs.at[u, k], qzr.at[u, k], p) for k, p in z_at
        ]
        copies.append(pltpu.make_async_copy(QS.at[u, c], landing, qlocal.at[u]))
        return copies

    def to_plane(u):
        q_first(u).wait()

        def body(i, carry):
            at = (u, s, i // F, lax.rem(i, F))
            GQ[at] = (GQ[at].astype(f32) + Q1[u, i // F, lax.rem(i, F)].astype(f32)).astype(bf16)
            return carry

        lax.fori_loop(0, C * F, body, 0)
        for copy in q_second(u):
            copy.start()

    def to_ctx(u):
        for copy in q_second(u):
            copy.wait()

        def body(i, carry):
            total = GQ[u, s, i, f].astype(f32)
            for k in range(F - 1):
                total = total + Q2[u, k, i].astype(f32)
            QS[u, i] = total.astype(bf16)
            return carry

        lax.fori_loop(0, C, body, 0)
        for copy in q_third(u):
            copy.start()

    @pl.when(step == 0)
    def _():
        for copy in late_loads:
            copy.start()
        greet_all(z_peers + f_peers + [sibling])
        for copy in [s_first, s_load] + y_copies:
            copy.start()

        def out_rows(i, carry):
            at, j = i // 4, lax.rem(i, 4)
            part = mixed_t.shape[0] // S
            rows = pl.ds(pl.multiple_of(at * part, 16), part)
            lanes = pl.ds(pl.multiple_of(j * (width // 4), width // 4), width // 4)
            piece = jnp.dot(mixed_t[rows, :], da[:, lanes], preferred_element_type=f32)
            GO[at, :, :, lanes] = piece.astype(bf16).reshape(F, part // F, width // 4)
            return carry

        lax.fori_loop(0, S * 4, out_rows, 0)
        o_first.start()
        unit, _ = rms_unit(k[...])
        kr[...] = half_turn(unit * gains[1:2, :], cosine[...], sine[...]).astype(bf16)
        dkr[...] = jnp.zeros_like(dkr)
        dv[...] = jnp.zeros_like(dv)
        head_grad[...] = jnp.zeros_like(head_grad)
        acc[...] = jnp.zeros_like(acc)

    @pl.when(step >= 1)
    def _():
        to_plane(step - 1)

    @pl.when(step == 1)
    def _():
        o_first.wait()

        def o_body(i, carry):
            o_own[i] = (o_own[i].astype(f32) + o_in[i].astype(f32)).astype(bf16)
            return carry

        lax.fori_loop(0, F, o_body, 0)
        for copy in o_saves:
            copy.start()
        s_first.wait()
        s_load.wait()

        def s_body(i, carry):
            at = (i // F, lax.rem(i, F))
            s_own[at] = (s_own[at].astype(f32) + s_in[at].astype(f32)).astype(bf16)
            return carry

        lax.fori_loop(0, C * F, s_body, 0)
        for copy in s_second:
            copy.start()

    @pl.when(step >= 2)
    def _():
        to_ctx(step - 2)

    @pl.when(step == 2)
    def _():
        for copy in s_second:
            copy.wait()

        def s_body(i, carry):
            total = s_own[i, f].astype(f32)
            for k in range(F - 1):
                total = total + s_plane[k, i].astype(f32)
            s_sum[i] = total.astype(bf16)
            return carry

        lax.fori_loop(0, C, s_body, 0)
        for copy in s_third:
            copy.start()

    @pl.when(step < pairs)
    def _():
        dm = lax.dot_general(
            da[...], wo[cols, :], (((1,), (1,)), ((), ())), preferred_element_type=f32
        ).astype(bf16)
        for half in range(2):
            lanes = slice(half * HEAD_DIM, (half + 1) * HEAD_DIM)
            for part in range(length // block):
                rows = slice(part * block, (part + 1) * block)
                unit, factor = rms_unit(q[rows, lanes])
                cos, sin = cosine[rows, :], sine[rows, :]
                qr = half_turn(unit * gains[0:1, :], cos, sin).astype(bf16)
                keys = kr[...]
                probs = score_block(qr, keys, pos_col[rows, :], pos_row[...])
                dmh = dm[rows, lanes]
                dprobs = lax.dot_general(
                    dmh, v[...], (((1,), (1,)), ((), ())), preferred_element_type=f32
                )
                delta = jnp.sum(probs * dprobs, axis=-1, keepdims=True)
                dscores = (probs * (dprobs - delta)).astype(bf16)
                dqr = jnp.dot(dscores, keys, preferred_element_type=f32) * (HEAD_DIM**-0.5)
                rows_in = (((0,), (0,)), ((), ()))
                dkr[...] += lax.dot_general(dscores, qr, rows_in, preferred_element_type=f32) * (
                    HEAD_DIM**-0.5
                )
                dv[...] += lax.dot_general(
                    probs.astype(bf16), dmh, rows_in, preferred_element_type=f32
                )
                dqs = half_turn(dqr, cos, -sin)
                head_grad[0:1, :] += jnp.sum(dqs * unit, axis=0, keepdims=True)
                DQ[rows, lanes] = norm_backward(dqs, unit, factor, gains[0:1, :]).astype(bf16)

    @pl.when(step == pairs)
    def _():
        unit, factor = rms_unit(k[...])
        dks = half_turn(dkr[...], cosine[...], -sine[...])
        head_grad[1:2, :] += jnp.sum(dks * unit, axis=0, keepdims=True)
        DQ[:, :HEAD_DIM] = norm_backward(dks, unit, factor, gains[1:2, :]).astype(bf16)
        DQ[:, HEAD_DIM:] = dv[...].astype(bf16)

    @pl.when(step == 0)
    def _():
        for copy in late_loads:
            copy.wait()

    def weight_rows(i, carry):
        part = F * GQ.shape[4]
        rows = pl.ds(pl.multiple_of(i * part, 16), part)
        piece = jnp.dot(xnt[rows, :], DQ[...], preferred_element_type=f32)
        GQ[step, i // C, lax.rem(i, C)] = piece.astype(bf16).reshape(GQ.shape[3:])
        return carry

    lax.fori_loop(0, S * C, weight_rows, 0)
    q_first(step).start()
    for j in range(4):
        part = pl.ds(j * (width // 4), width // 4)
        acc[:, part] += lax.dot_general(
            DQ[...], w[part, cols], (((1,), (1,)), ((), ())), preferred_element_type=f32
        )

    @pl.when(step == pairs)
    def _():
        to_ctx(pairs - 1)
        to_plane(pairs)
        rows_of = width // HEAD_DIM
        total = jnp.zeros((1, width), f32)

        def finish(i, total):
            rows = pl.ds(i * 64, 64)
            unit, _ = rms_unit(x[rows, :].astype(f32))
            term = acc[rows, :]
            dxn[rows, :] = term.astype(bf16)
            return total + jnp.sum(term * unit, axis=0, keepdims=True)

        total = lax.fori_loop(0, length // 64, finish, total)
        rows = length // C
        x_saves = [
            pltpu.make_async_copy(
                dxn.at[pl.ds(pl.multiple_of(lax.rem(c + i, C) * rows, 16), rows)], DX[i], dxsem.at[i]
            )
            for i in range(C)
        ]
        for copy in x_saves:
            copy.start()
        for r in range(rows_of):
            T[r : r + 1, :] = total[:, r * HEAD_DIM : (r + 1) * HEAD_DIM]
        T[rows_of:, :] = head_grad[...]
        t_first.start()
        t_first.wait()
        T[...] = T[...] + t_in[...]
        for copy in t_second:
            copy.start()
        to_ctx(pairs)
        for copy in t_second:
            copy.wait()
        order = []
        for g in range(F):
            term = jnp.zeros_like(T)
            for k in range(F - 1):
                came = lax.rem(f + F - (k + 1), F)
                term = term + jnp.where(came == g, t_plane[k], 0.0)
            order.append(term + jnp.where(f == g, T[...], 0.0))
        total = order[0]
        for term in order[1:]:
            total = total + term
        t_sum[...] = total
        for copy in t_third:
            copy.start()
        for copy in s_third + y_copies + o_saves + t_third + x_saves:
            copy.wait()
        for u in range(units):
            for copy in q_third(u):
                copy.wait()


def backward(da, w, wo, q, k, v, xnt, x, cosine, sine, pos_col, pos_row, gains, mixed_t, sp, yp):
    S, C, F = sizes()
    length, width = x.shape
    head_width = wo.shape[0]
    pairs = head_width // (2 * HEAD_DIM)
    units = pairs + 1
    shard = sp.shape[3]
    block = min(length, 512)
    wide = 2 * HEAD_DIM
    once = pl.Buffered(buffer_count=1)
    whole = lambda array: pl.BlockSpec(array.shape, lambda i: (0, 0), pipeline_mode=once)
    sds = jax.ShapeDtypeStruct
    V = pltpu.VMEM
    q_block, o_block, s_block = (shard, wide), (head_width // (S * F), width), sp.shape[3:]
    t_block = (width // HEAD_DIM + 8, HEAD_DIM)
    return pl.pallas_call(
        functools.partial(backward_kernel, block),
        out_shape=[
            sds((F // 2,) + o_block, bf16),
            sds((F // 2,) + o_block, bf16),
            sds((shard, C * head_width), bf16),
            sds((C, shard, wide), bf16),
            sds((C,) + s_block, bf16),
            sds((C,) + t_block, f32),
            sds(yp.shape, bf16),
        ]
        + [sds((length // C, width), bf16)] * C,
        grid=(units,),
        in_specs=[whole(da), ANY, whole(wo)]
        + [pl.BlockSpec((length, wide), lambda i: (0, jnp.minimum(i, pairs - 1)))]
        + [whole(k), whole(v), ANY, ANY]
        + [whole(array) for array in (cosine, sine, pos_col, pos_row, gains, mixed_t)]
        + [ANY] * 2,
        out_specs=[ANY] * (7 + C),
        scratch_shapes=[
            V(w.shape, bf16), V(xnt.shape, bf16), V(x.shape, bf16), DMA((3,)),
            V((length, width), bf16), DMA((C,)),
            V((length, HEAD_DIM), bf16), V((length, HEAD_DIM), f32), V((length, HEAD_DIM), f32),
            V((length, width), f32), V((length, wide), bf16), V((8, HEAD_DIM), f32),
            V((units, S, C, F) + q_block, bf16), V((units, C, F) + q_block, bf16),
            V((units, F - 1, C) + q_block, bf16), V((units, C) + q_block, bf16),
            V((S, F) + o_block, bf16), V((F,) + o_block, bf16),
            V((C, F) + s_block, bf16), V((C, F) + s_block, bf16), V((F - 1, C) + s_block, bf16), V((C,) + s_block, bf16),
            V(t_block, f32), V(t_block, f32), V((F - 1,) + t_block, f32), V(t_block, f32),
            DMA((7,)), DMA((units,)),
            DMA((3,)), DMA((3,)), DMA((3, F - 1)), DMA((3, F - 1)), DMA((3, C - 1)), DMA((3, C - 1)),
            DMA((units,)), DMA((units,)), DMA((units, F - 1)), DMA((units, F - 1)),
            DMA((units, C - 1)), DMA((units, C - 1)), DMA((C - 1,)), DMA((C - 1,)),
        ],
        name="attention_backward",
        compiler_params=params(7, 60 * 2**20),
    )(da, w, wo, q, k, v, xnt, x, cosine, sine, pos_col, pos_row, gains, mixed_t, sp, yp)


def dot(left, right):
    return jnp.dot(left, right, preferred_element_type=f32)


def contract_rows(left, right):
    return lax.dot_general(left, right, (((0,), (0,)), ((), ())), preferred_element_type=f32)


def times_transpose(left, right):
    return lax.dot_general(left, right, (((1,), (1,)), ((), ())), preferred_element_type=f32)


def on_device(
    tokens,
    stretch_order,
    expert_ids,
    slot_index,
    norm_attn,
    head_gains,
    w_query,
    w_key,
    w_value,
    w_out,
    norm_moe,
    w_router,
    w_gate,
    w_up,
    w_down,
    cotangent,
):
    S, C, F = sizes()
    Q = S * F
    seq_at, ctx_at, fsdp_at = place()
    rows, width = tokens.shape[1:]
    length = C * rows
    experts = w_router.shape[1]
    capacity = rows * TOP // (Q * C) + 1
    packed = round_up(C * capacity, 16)
    lanes = round_up(packed, 128)
    head_width = w_query.shape[1] // C
    shard = w_router.shape[0]
    pack_width = round_up(experts + 2, 128)
    (
        X, W, WO, PK, _, G, out_part, q, k, v, mixed_t, xnt, gain_attn, gain_moe, gains,
        cosine, sine, pos_col, pos_row, select, select_t, chosen, kept_map,
    ) = front(
        capacity, packed, stretch_order, expert_ids[0].T, slot_index[0].T,
        tokens[0], w_query, w_key, w_value, w_out, w_router.T, norm_attn[None], norm_moe[None],
        cotangent[0], head_gains,
    )
    W = W.reshape(width, head_width + 2 * HEAD_DIM)
    WO = WO.reshape(head_width, width)
    PK = PK.reshape(width, pack_width)
    buffer, slot_grad, _, h1, xm, gates, hidden, dgp, dup, slot_dgate = dispatch(
        packed, out_part.reshape(C, rows, width), G.reshape(length, width), tokens[0], PK, gain_moe,
        chosen, kept_map, select, w_gate, w_up, w_down,
    )
    DA, y_part, dh1, small = give_back(
        packed, experts, slot_dgate, select, select_t, gates, PK, h1, gain_moe, cotangent[0],
        xm, hidden, dgp, dup, w_gate, w_up, w_down,
    )
    DA = DA.reshape(length, width)

    def part_of(parts, at):
        return lax.dynamic_index_in_dim(parts, at, 0, keepdims=False)

    out_half, out_other, query_sum, kv_sums, small_sums, tiny_sums, y_parts, *dxn_parts = backward(
        DA, W, WO, q, k, v, xnt, X, cosine, sine, pos_col, pos_row, gains,
        mixed_t,
        small.reshape(S, C, F, shard, pack_width),
        y_part.reshape(C, rows, width),
    )
    dxn = dxn_parts[0].astype(f32)
    for i in range(1, C):
        dxn += lax.ppermute(dxn_parts[i], "ctx", [(j, (j + i) % C) for j in range(C)]).astype(f32)
    out_sum, bit = out_half, F // 2
    while True:
        came = lax.ppermute(out_other, "fsdp", [(i, i ^ bit) for i in range(F)])
        out_sum = (out_sum.astype(f32) + came.astype(f32)).astype(bf16)
        bit //= 2
        if not bit:
            break
        mine = lax.rem(fsdp_at // bit, 2)
        parts = out_sum.reshape((2, bit) + out_sum.shape[1:])
        out_sum, out_other = part_of(parts, mine), part_of(parts, 1 - mine)
    out_sum = out_sum[0]
    turn = [(i * C + j, j * S + i) for i in range(S) for j in range(C)]
    o_sum = lax.ppermute(out_sum, ("seq", "ctx"), turn)
    grad_wgate = contract_rows(buffer, dgp)
    grad_wup = contract_rows(buffer, dup)
    grad_wdown = contract_rows(hidden, slot_grad)
    layer_out = (h1 + jnp.sum(y_parts.astype(f32), axis=0)).astype(bf16)
    unit, factor = rms_unit(tokens[0].astype(f32))
    grad_tokens = (dh1 + norm_backward(dxn, unit, factor, gain_attn)).astype(bf16)
    grad_query = query_sum.astype(f32)

    def key_columns(block):
        pieces = block.astype(f32).reshape(KEY_VALUE_HEADS, C // KEY_VALUE_HEADS, shard, HEAD_DIM).sum(axis=1)
        return pieces.transpose(1, 0, 2).reshape(shard, KEY_VALUE_HEADS * HEAD_DIM)

    grad_key = key_columns(kv_sums[:, :, :HEAD_DIM])
    grad_value = key_columns(kv_sums[:, :, HEAD_DIM:])
    small_sum = jnp.sum(small_sums.astype(f32), axis=0)
    tiny_sum = jnp.sum(tiny_sums, axis=0)
    tiny_rows = width // HEAD_DIM
    device = (seq_at * C + ctx_at) * F + fsdp_at
    grad_norm_attn = lax.dynamic_slice_in_dim(
        tiny_sum[:tiny_rows].reshape(width), device * shard, shard
    )
    return (
        layer_out[None],
        grad_tokens[None],
        grad_norm_attn,
        tiny_sum[tiny_rows : tiny_rows + 2],
        grad_query,
        grad_key,
        grad_value,
        o_sum.astype(f32),
        small_sum[:, experts],
        small_sum[:, :experts],
        grad_wgate[None],
        grad_wup[None],
        grad_wdown[None],
    )


def solution(mesh):
    rows = P(("seq", "fsdp"), "ctx", None)
    vector = P(AXES)
    matrix = P(AXES, None)
    cube = P(AXES, None, None)
    return jax.shard_map(
        on_device,
        mesh=mesh,
        in_specs=(
            rows, P(), rows, rows, vector, P(), matrix, matrix, matrix, matrix,
            vector, matrix, cube, cube, cube, rows,
        ),
        out_specs=(
            rows, rows, vector, P(), matrix, matrix, matrix, matrix, vector, matrix,
            cube, cube, cube,
        ),
        check_vma=False,
    )
```

```python
import functools

import jax
import jax.numpy as jnp
import numpy as np
from jax import lax
from jax.experimental import pallas as pl
from jax.experimental.pallas import tpu as pltpu
from jax.sharding import PartitionSpec as P

QUERY_HEADS = 32
KEY_VALUE_HEADS = 4
HEAD_DIM = 128
TOP = 8
AXES = ("seq", "ctx", "fsdp")
MESH = pl.DeviceIdType.MESH
epsilon = 1e-06
rope_base = 1000000.0
VMEM_LIMIT = 56 * 2**20
f32 = jnp.float32
bf16 = jnp.bfloat16


def round_up(value, step):
    return (value + step - 1) // step * step


def place():
    return tuple(lax.axis_index(name) for name in AXES)


def sizes():
    return tuple(lax.axis_size(name) for name in AXES)


def signal(device):
    pl.semaphore_signal(
        pltpu.get_barrier_semaphore(), inc=1, device_id=device, device_id_type=MESH
    )


def remote(src, dst, send, recv, device):
    return pltpu.make_async_remote_copy(
        src_ref=src,
        dst_ref=dst,
        send_sem=send,
        recv_sem=recv,
        device_id=device,
        device_id_type=MESH,
    )


def params(cid, limit=VMEM_LIMIT):
    return pltpu.CompilerParams(
        collective_id=cid, has_side_effects=True, vmem_limit_bytes=limit
    )


ANY = pl.BlockSpec(memory_space=pl.ANY)
DMA = pltpu.SemaphoreType.DMA


def rms_unit(rows):
    factor = lax.rsqrt(jnp.mean(rows * rows, axis=-1, keepdims=True) + epsilon)
    return rows * factor, factor


def norm_backward(grad_scaled, normed, factor, gain):
    grad_normed = grad_scaled * gain
    inner = jnp.mean(grad_normed * normed, axis=-1, keepdims=True)
    return factor * (grad_normed - normed * inner)


def half_turn(rows, cosine, sine):
    return rows * cosine + pltpu.roll(rows, HEAD_DIM // 2, 1) * sine


def score_block(qr, kr, pos_col, pos_row):
    scores = lax.dot_general(
        qr, kr, (((1,), (1,)), ((), ())), preferred_element_type=f32
    ) * (HEAD_DIM**-0.5)
    scores = jnp.where(pos_col >= pos_row, scores, -jnp.inf)
    peak = jnp.max(scores, axis=-1, keepdims=True)
    weight = jnp.exp(scores - peak)
    return weight * (1.0 / jnp.sum(weight, axis=-1, keepdims=True))


def z_neighbours():
    _, C, _ = sizes()
    s, c, f = place()
    return [(s, lax.rem(c + k, C), f) for k in range(1, C)]


def plane_neighbours():
    S, _, F = sizes()
    s, c, f = place()
    Q = S * F
    at = [lax.rem(s * F + f + k, Q) for k in range(1, Q)]
    return at, [(q // F, c, lax.rem(q, F)) for q in at]


def greet_all(peers):
    for peer in peers:
        signal(peer)
    pl.semaphore_wait(pltpu.get_barrier_semaphore(), len(peers))


class Line:
    def __init__(self, own, block, rsend, rrecv, lsend, lrecv):
        s, self.c, f = place()
        self.C = lax.axis_size("ctx")
        self.own, self.block = own, block
        self.sems = (rsend, rrecv, lsend, lrecv)
        self.right = (s, lax.rem(self.c + 1, self.C), f)
        self.left = (s, lax.rem(self.c + self.C - 1, self.C), f)

    def copy(self, rightward, h):
        origin = self.c - h if rightward else self.c + h
        src = self.own if h == 0 else self.block(origin)
        send, recv = self.sems[:2] if rightward else self.sems[2:]
        return remote(
            src, self.block(origin), send.at[h], recv.at[h], self.right if rightward else self.left
        )

    def sends(self, rightward, h):
        if rightward:
            return jnp.logical_and(self.c >= h, self.c < self.C - 1)
        return jnp.logical_and(self.c + h < self.C, self.c > 0)

    def start(self):
        for way in (True, False):
            pl.when(self.sends(way, 0))(self.copy(way, 0).start)

    def hop(self, h):
        for way in (True, False):
            origin = self.c - h if way else self.c + h
            there = origin >= 0 if way else origin < self.C
            landed = remote(
                self.block(origin), self.block(origin),
                self.sems[0 if way else 2].at[h - 1], self.sems[1 if way else 3].at[h - 1],
                self.left if way else self.right,
            )
            pl.when(there)(landed.wait_recv)
            if h < self.C - 1:
                pl.when(self.sends(way, h))(self.copy(way, h).start)

    def finish(self):
        for way in (True, False):
            for h in range(self.C - 1):
                pl.when(self.sends(way, h))(self.copy(way, h).wait_send)


def line_sems(C):
    return [DMA((C - 1,)) for _ in range(4)]


def front_kernel(
    block, capacity, packed, experts,
    order, ids, slot_ids, tokens, wq, wk, wv, wo, router, norm_attn, norm_moe, cot, low_gains, frequency,
    X_out, W_out, WO_out, PK, SM, G, out_out, q_out, k_out, v, mixed_t, xnt_out, gain_attn, gain_moe, gains,
    cosine, sine, pos_col, pos_row, select_out, select_t_out, chosen, kept,
    X, W, WO, xn, kr, pack, out, q, mixed, xnt, select, select_t,
    local, save, zsend, zrecv, fsend, frecv, csend, crecv, wsend, wrecv,
    xrs, xrr, xls, xlr, grs, grr, gls, glr,
):
    S, C, F = sizes()
    s, c, f = place()
    Q = S * F
    rows, width = tokens.shape
    length = C * rows
    head_width = wq.shape[1] // C
    shard = wq.shape[0]
    wide = chosen.shape[1]
    z_peers = z_neighbours()
    f_peers = [(s, c, lax.rem(f + k, F)) for k in range(1, F)]
    sibling = (1 - s, c, f)
    pair = s * C + c
    out_dst = (lax.rem(pair, S), pair // S, f)
    pair_in = c * S + s
    out_src = (pair_in // C, lax.rem(pair_in, C), f)
    stays = jnp.logical_and(out_dst[0] == s, out_dst[1] == c)
    moves = jnp.logical_not(stays)
    greet = (
        jnp.where(stays, 1 - s, out_src[0]),
        jnp.where(stays, C - 1 - c, out_src[1]),
        f,
    )
    def as_column(line):
        size = line.shape[1]
        square = lax.broadcasted_iota(jnp.int32, (size, size), 0) == lax.broadcasted_iota(
            jnp.int32, (size, size), 1
        )
        return jnp.sum(jnp.where(square, line, 0.0), axis=1, keepdims=True)

    lane = lax.broadcasted_iota(jnp.int32, (rows, wide), 1).astype(f32)
    hits = jnp.zeros((rows, wide), f32)
    slot_map = jnp.full((rows, wide), -1.0, f32)
    for j in range(TOP):
        here = lane == as_column(ids[j : j + 1, :].astype(f32))
        slot = jnp.broadcast_to(as_column(slot_ids[j : j + 1, :].astype(f32)), (rows, wide))
        hits = jnp.where(here, 1.0, hits)
        slot_map = jnp.where(jnp.logical_and(here, slot < capacity), slot, slot_map)
    lane = lax.broadcasted_iota(jnp.int32, pack.shape, 1)
    own_lane = lax.broadcasted_iota(jnp.int32, (experts, pack.shape[1]), 0) == lax.broadcasted_iota(
        jnp.int32, (experts, pack.shape[1]), 1
    )
    packed_rows = lax.dot_general(
        router[...], own_lane.astype(bf16), (((0,), (0,)), ((), ())), preferred_element_type=f32
    )
    for i, line in enumerate((norm_attn, norm_moe)):
        packed_rows = jnp.where(lane == experts + i, as_column(line[...].astype(f32)), packed_rows)
    pack[...] = packed_rows.astype(bf16)
    gains[...] = low_gains[...].astype(f32)
    chosen[...] = hits
    kept[...] = (slot_map >= 0.0).astype(f32)
    SM[c] = slot_map
    greet_all(z_peers + f_peers + [sibling, greet])

    def pieces(target):
        kv = (target * KEY_VALUE_HEADS) // C
        q_cols = pl.ds(pl.multiple_of(target * head_width, 128), head_width)
        kv_cols = pl.ds(pl.multiple_of(kv * HEAD_DIM, 128), HEAD_DIM)
        mine = W.at[s, c, f]
        return [
            (wq.at[:, q_cols], mine.at[:, pl.ds(0, head_width)]),
            (wk.at[:, kv_cols], mine.at[:, pl.ds(head_width, HEAD_DIM)]),
            (wv.at[:, kv_cols], mine.at[:, pl.ds(head_width + HEAD_DIM, HEAD_DIM)]),
            (pack, PK.at[s, c, f]),
        ]

    def token_rows(at):
        return X.at[pl.ds(pl.multiple_of(at * rows, 16), rows)]

    own = [
        pltpu.make_async_copy(src, dst, local.at[i])
        for i, (src, dst) in enumerate(pieces(c) + [(tokens, token_rows(c)), (cot, G.at[c])])
    ]
    z_copies = [
        remote(src, dst, zsend.at[i, k], zrecv.at[i, k], peer)
        for k, peer in enumerate(z_peers)
        for i, (src, dst) in enumerate(pieces(peer[1]))
    ]
    slot_copies = [
        remote(SM.at[c], SM.at[c], zsend.at[4, k], zrecv.at[4, k], peer)
        for k, peer in enumerate(z_peers)
    ]
    x_line = Line(tokens, token_rows, xrs, xrr, xls, xlr)
    g_line = Line(cot, lambda at: G.at[at], grs, grr, gls, glr)
    out_copy = remote(wo, WO.at[out_dst[0], f], wsend.at[0], wrecv.at[0], out_dst)
    out_stay = pltpu.make_async_copy(wo, WO.at[s, f], wsend.at[1])
    for copy in own + z_copies + slot_copies:
        copy.start()
    x_line.start()
    pl.when(moves)(out_copy.start)
    pl.when(stays)(out_stay.start)

    where = lax.broadcasted_iota(jnp.int32, (1, length), 1)
    where_col = lax.broadcasted_iota(jnp.int32, (length, 1), 0)
    stretch_rows = rows // 2

    def position(at):
        total = jnp.zeros_like(at)
        for j in range(2 * C):
            base = order[j] * stretch_rows - j * stretch_rows
            total = jnp.where(at // stretch_rows == j, at + base, total)
        return total

    pos_row[...] = position(where)
    pos_col[...] = position(where_col)
    angles = pos_col[...].astype(f32) * frequency[...]
    cosine[...] = jnp.cos(angles)
    turned = jnp.sin(angles)
    sine[...] = jnp.where(
        lax.broadcasted_iota(jnp.int32, turned.shape, 1) < HEAD_DIM // 2, -turned, turned
    )

    for copy in own[:5] + z_copies:
        copy.wait()

    def weight_block(index, at):
        return (W.at[s, :, at], PK.at[s, :, at], WO.at[s, at])[index]

    f_copies = [
        [
            remote(weight_block(i, f), weight_block(i, f), fsend.at[i, k], frecv.at[i, k], peer)
            for k, peer in enumerate(f_peers)
        ]
        for i in range(3)
    ]

    def to_sibling(i, k):
        at = lax.rem(f + F - k, F)
        return remote(weight_block(i, at), weight_block(i, at), csend.at[i, k], crecv.at[i, k], sibling)

    c_copies = [[to_sibling(i, k) for k in range(F)] for i in range(3)]
    for i in range(2):
        for copy in f_copies[i] + c_copies[i][:1]:
            copy.start()
    x_line.hop(1)
    for h in range(2, C - 1):
        x_line.hop(h)
    pl.when(moves)(out_copy.wait)
    pl.when(stays)(out_stay.wait)
    for copy in f_copies[2] + c_copies[2][:1]:
        copy.start()
    for k in range(F - 1):
        for i in range(2):
            f_copies[i][k].wait_recv()
            c_copies[i][k + 1].start()
    for copy in slot_copies:
        copy.wait()
    at = lax.broadcasted_iota(jnp.int32, (wide, Q * packed), 1) // packed
    expert = (at // F * C + c) * F + lax.rem(at, F)
    spread = (lax.broadcasted_iota(jnp.int32, (wide, Q * packed), 0) == expert).astype(bf16)
    slot_rows = SM[...].reshape(length, wide).astype(bf16)
    by_token = jnp.dot(slot_rows, spread, preferred_element_type=f32)
    base = (lax.broadcasted_iota(jnp.int32, by_token.shape, 0) // rows * capacity).astype(f32)
    number = lax.rem(lax.broadcasted_iota(jnp.int32, by_token.shape, 1), packed).astype(f32)
    select_t[...] = jnp.where(
        jnp.logical_and(by_token >= 0.0, by_token + base == number), 1.0, 0.0
    ).astype(bf16)
    at = lax.broadcasted_iota(jnp.int32, (Q, wide), 0)
    expert = (at // F * C + c) * F + lax.rem(at, F)
    spread = (lax.broadcasted_iota(jnp.int32, (Q, wide), 1) == expert).astype(bf16)
    by_slot = lax.dot_general(
        spread, slot_rows, (((1,), (1,)), ((), ())), preferred_element_type=f32
    )
    base = (where // rows * capacity).astype(f32)
    by_slot = jnp.where(by_slot >= 0.0, by_slot + base, -1.0)
    number = lax.broadcasted_iota(jnp.int32, (packed, length), 0).astype(f32)
    for p in range(Q):
        select[p * packed : (p + 1) * packed, :] = jnp.where(
            number == by_slot[p : p + 1, :], 1.0, 0.0
        ).astype(bf16)

    x_line.hop(C - 1)
    g_line.start()
    for i in range(2):
        for copy in c_copies[i]:
            copy.wait()
    saves = [
        pltpu.make_async_copy(src, dst, save.at[i])
        for i, (src, dst) in enumerate(
            (
                (X, X_out), (W, W_out), (select, select_out), (select_t, select_t_out),
                (WO, WO_out), (q, q_out), (out, out_out), (xnt, xnt_out),
            )
        )
    ]
    for copy in saves[:4]:
        copy.start()
    across = lax.broadcasted_iota(jnp.int32, (HEAD_DIM, HEAD_DIM), 0)
    diagonal = across == lax.broadcasted_iota(jnp.int32, (HEAD_DIM, HEAD_DIM), 1)
    flat = PK[...].reshape(width, PK.shape[-1]).astype(f32)
    for j in range(width // HEAD_DIM):
        part = slice(j * HEAD_DIM, (j + 1) * HEAD_DIM)
        for i, row in enumerate((gain_attn, gain_moe)):
            line = flat[part, experts + i : experts + i + 1]
            row[:, part] = jnp.sum(jnp.where(diagonal, line, 0.0), axis=0, keepdims=True)

    def norm_rows(i, carry):
        part = pl.ds(i * 64, 64)
        unit, _ = rms_unit(X[part, :].astype(f32))
        xn[part, :] = (unit * gain_attn[...]).astype(bf16)
        return carry

    lax.fori_loop(0, length // 64, norm_rows, 0)

    def weights(cols):
        return W[:, :, :, :, cols].reshape(width, 2 * HEAD_DIM)

    kv = jnp.dot(xn[...], weights(pl.ds(head_width, 2 * HEAD_DIM)), preferred_element_type=f32)
    k_out[...] = kv[:, :HEAD_DIM]
    v[...] = kv[:, HEAD_DIM:].astype(bf16)
    unit, _ = rms_unit(k_out[...])
    kr[...] = half_turn(unit * gains[1:2, :], cosine[...], sine[...]).astype(bf16)

    def head_pair(i, carry):
        cols = pl.ds(pl.multiple_of(i * 2 * HEAD_DIM, 2 * HEAD_DIM), 2 * HEAD_DIM)
        both = jnp.dot(xn[...], weights(cols), preferred_element_type=f32)
        q[:, cols] = both
        for half in range(2):
            lanes = pl.ds(pl.multiple_of((2 * i + half) * HEAD_DIM, HEAD_DIM), HEAD_DIM)
            for part in range(length // block):
                at = slice(part * block, (part + 1) * block)
                unit, _ = rms_unit(both[at, half * HEAD_DIM : (half + 1) * HEAD_DIM])
                qr = half_turn(unit * gains[0:1, :], cosine[at, :], sine[at, :]).astype(bf16)
                probs = score_block(qr, kr[...], pos_col[at, :], pos_row[...])
                mixed[at, lanes] = jnp.dot(
                    probs.astype(bf16), v[...], preferred_element_type=f32
                ).astype(bf16)
        return carry

    pairs = head_width // (2 * HEAD_DIM)
    half_way = pairs // 2
    hops = {}
    for h in range(1, C - 1):
        hops.setdefault(min(pairs, 1 + (h - 1) * pairs // (C - 2)), []).append(h)
    done = 0
    for stop in sorted(set(hops) | {half_way, pairs}):
        lax.fori_loop(done, stop, head_pair, 0)
        done = stop
        for h in hops.get(stop, ()):
            g_line.hop(h)
        if stop == half_way:
            for k in range(F - 1):
                f_copies[2][k].wait_recv()
                c_copies[2][k + 1].start()
    for copy in c_copies[2]:
        copy.wait()
    for copy in saves[4:6]:
        copy.start()

    def project(j, carry):
        cols = pl.ds(pl.multiple_of(j * 256, 256), 256)
        out[:, cols] = jnp.dot(
            mixed[...], WO[:, :, :, cols].reshape(head_width, 256), preferred_element_type=f32
        ).astype(bf16)
        return carry

    lax.fori_loop(0, width // 256, project, 0)
    saves[6].start()

    def turn(j, carry):
        cols = pl.ds(pl.multiple_of(j * 256, 256), 256)
        xnt[cols, :] = xn[:, cols].T
        return carry

    lax.fori_loop(0, width // 256, turn, 0)
    saves[7].start()

    def turn_mixed(j, carry):
        cols = pl.ds(pl.multiple_of(j * 256, 256), 256)
        mixed_t[cols, :] = mixed[:, cols].T
        return carry

    lax.fori_loop(0, head_width // 256, turn_mixed, 0)
    g_line.hop(C - 1)
    x_line.finish()
    g_line.finish()
    for line in f_copies:
        for copy in line:
            copy.wait_send()
    for copy in saves + own[5:]:
        copy.wait()


def front(
    capacity, packed, order, ids, slot_ids, tokens, wq, wk, wv, wo, router, norm_attn, norm_moe, cot, gains
):
    S, C, F = sizes()
    Q = S * F
    rows, width = tokens.shape
    length = C * rows
    shard = wq.shape[0]
    head_width = wq.shape[1] // C
    experts = router.shape[0]
    wide = round_up(experts, 128)
    frequency = np.power(rope_base, -np.arange(HEAD_DIM // 2) * 2.0 / HEAD_DIM)
    frequency = jnp.asarray(np.tile(frequency, 2)[None].astype(np.float32))
    block = min(length, 512)
    sds = jax.ShapeDtypeStruct
    V = pltpu.VMEM
    vm = pl.BlockSpec(memory_space=pltpu.VMEM)
    w_shape = (S, C, F, shard, head_width + 2 * HEAD_DIM)
    wo_shape = (S, F) + wo.shape
    pack_block = (shard, round_up(experts + 2, 128))
    pack_shape = (S, C, F) + pack_block
    return pl.pallas_call(
        functools.partial(front_kernel, block, capacity, packed, experts),
        out_shape=[
            sds((length, width), bf16),
            sds(w_shape, bf16),
            sds(wo_shape, bf16),
            sds(pack_shape, bf16),
            sds((C, rows, wide), f32),
            sds((C, rows, width), bf16),
            sds((length, width), bf16),
            sds((length, head_width), f32),
            sds((length, HEAD_DIM), f32),
            sds((length, HEAD_DIM), bf16),
            sds((head_width, length), bf16),
            sds((width, length), bf16),
            sds((1, width), f32),
            sds((1, width), f32),
            sds(gains.shape, f32),
            sds((length, HEAD_DIM), f32),
            sds((length, HEAD_DIM), f32),
            sds((length, 1), jnp.int32),
            sds((1, length), jnp.int32),
            sds((Q * packed, length), bf16),
            sds((length, Q * packed), bf16),
            sds((rows, wide), f32),
            sds((rows, wide), f32),
        ],
        in_specs=[pl.BlockSpec(memory_space=pltpu.SMEM), vm, vm] + [ANY] * 5 + [vm] * 3 + [ANY, vm, vm],
        out_specs=[ANY] * 3 + [vm, vm] + [ANY] * 3 + [vm] * 3 + [ANY] + [vm] * 7 + [ANY] * 2 + [vm] * 2,
        scratch_shapes=[
            V((length, width), bf16),
            V(w_shape, bf16),
            V(wo_shape, bf16),
            V((length, width), bf16),
            V((length, HEAD_DIM), bf16),
            V(pack_block, bf16),
            V((length, width), bf16),
            V((length, head_width), f32),
            V((length, head_width), bf16),
            V((width, length), bf16),
            V((Q * packed, length), bf16),
            V((length, Q * packed), bf16),
            DMA((6,)), DMA((9,)),
            DMA((5, C - 1)), DMA((5, C - 1)),
            DMA((3, F - 1)), DMA((3, F - 1)),
            DMA((3, F)), DMA((3, F)),
            DMA((2,)), DMA((1,)),
        ]
        + line_sems(C)
        + line_sems(C),
        name="gather_and_attend",
        compiler_params=params(1, 60 * 2**20),
    )(order, ids, slot_ids, tokens, wq, wk, wv, wo, router, norm_attn, norm_moe, cot, gains, frequency)


CHUNKS = 8


def columns(width, j):
    step = width // CHUNKS
    return pl.ds(j * step, step)


def three_parts(line):
    high = line.astype(bf16).astype(f32)
    rest = line - high
    middle = rest.astype(bf16).astype(f32)
    row = lax.broadcasted_iota(jnp.int32, (16, line.shape[1]), 0)
    rows = jnp.where(row == 0, high, jnp.where(row == 1, middle, jnp.where(row == 2, rest - middle, 0.0)))
    return rows.astype(bf16)


def halves(total):
    return total // 2


def dispatch_kernel(
    packed, out_part, G_in, tokens, pack, gain, chosen, kept, select, w_gate, w_up, w_down,
    buffer_out, gbuf, wrow, h1, xm, gates, hidden_out, dgp_out, dup_out, dgr,
    OP, RB, XM, SL, WM, WS, G, SG, buffer, WG, WU, WD, gp, up, gw, dup,
    local, load, saved, osend, orecv, gsend, grecv, xsend, xrecv, msend, mrecv, bsend, brecv, wsend, wrecv,
):
    S, C, F = sizes()
    s, c, f = place()
    Q = S * F
    q = s * F + f
    rows, width = tokens.shape
    total_rows = Q * packed
    half = halves(total_rows)
    z_peers = z_neighbours()
    p_at, p_peers = plane_neighbours()
    loads = [
        pltpu.make_async_copy(G_in, G, load.at[0]),
        pltpu.make_async_copy(w_down.at[0], WD, load.at[1]),
        pltpu.make_async_copy(w_gate.at[0], WG, load.at[2]),
        pltpu.make_async_copy(w_up.at[0], WU, load.at[3]),
    ]
    for copy in loads:
        copy.start()
    greet_all(z_peers + p_peers)
    mine = pl.ds(pl.multiple_of(q * packed, 16), packed)
    own_rows = pl.ds(pl.multiple_of(c * rows, 16), rows)
    right = (s, lax.rem(c + 1, C), f)
    left = (s, lax.rem(c + C - 1, C), f)

    def rightward(t):
        return remote(OP.at[t], RB.at[t], osend.at[0, t], orecv.at[0, t], right)

    def leftward(t):
        return remote(OP.at[t], RB.at[jnp.where(c - 1 == t, C, t)], osend.at[1, t], orecv.at[1, t], left)

    def merge(t, way):
        remote(OP.at[t], RB.at[t], osend.at[way, t], orecv.at[way, t], left).wait_recv()

        def add(j, carry):
            part = pl.ds(j * 32, 32)
            OP[t, part, :] = (OP[t, part, :].astype(f32) + RB[t, part, :].astype(f32)).astype(bf16)
            return carry

        lax.fori_loop(0, rows // 32, add, 0)

    def pass_on(step):
        t_right = C - 1 + c - step
        t_left = step - (C - 1 - c)

        @pl.when((t_right > c) & (t_right < C) & (c > 0))
        def _():
            merge(t_right, 0)
            rightward(t_right).start()

        @pl.when((t_left >= 0) & (t_left < c) & (c < C - 1))
        def _():
            merge(t_left, 1)
            leftward(t_left).start()

    fetch = pltpu.make_async_copy(out_part, OP, local.at[0])
    fetch.start()
    fetch.wait()

    @pl.when(c == 0)
    def _():
        for t in range(C - 1, 0, -1):
            rightward(t).start()

    @pl.when(c == C - 1)
    def _():
        for t in range(C - 1):
            leftward(t).start()

    loads[0].wait()

    def grad_slots(p):
        at = pl.ds(pl.multiple_of(p * packed, 16), packed)

        def body(j, carry):
            cols = pl.ds(pl.multiple_of(j * 512, 512), 512)
            SG[at, cols] = jnp.dot(select[at, :], G[:, cols], preferred_element_type=f32).astype(bf16)
            return carry

        lax.fori_loop(0, width // 512, body, 0)

    later = []
    for k, peer in enumerate(p_peers):
        theirs = pl.ds(pl.multiple_of(p_at[k] * packed, 16), packed)
        later.append(remote(SG.at[theirs], gbuf.at[mine], gsend.at[k], grecv.at[k], peer))
        grad_slots(p_at[k])
        later[-1].start()
    grad_slots(q)
    later.append(pltpu.make_async_copy(SG.at[mine], gbuf.at[mine], local.at[1]))
    later[-1].start()
    for step in range(1, C - 1):
        pass_on(step)

    @pl.when(c > 0)
    def _():
        remote(OP.at[0], RB.at[c], osend.at[0, c], orecv.at[0, c], left).wait_recv()

    @pl.when(c < C - 1)
    def _():
        remote(OP.at[0], RB.at[C], osend.at[1, c], orecv.at[1, c], right).wait_recv()


    def head_rows(i, carry):
        part = pl.ds(i * 32, 32)
        total = tokens[part, :].astype(f32) + OP[c, part, :].astype(f32)
        total += jnp.where(c > 0, RB[c, part, :].astype(f32), 0.0)
        total += jnp.where(c < C - 1, RB[C, part, :].astype(f32), 0.0)
        h1[part, :] = total
        unit, _ = rms_unit(total)
        normed = (unit * gain[...]).astype(bf16)
        xm[part, :] = normed
        XM[pl.ds(pl.multiple_of(c * rows + i * 32, 16), 32), :] = normed
        return carry

    lax.fori_loop(0, rows // 32, head_rows, 0)
    chunks = []
    for j in range(CHUNKS):
        piece = XM.at[own_rows, columns(width, j)]
        chunks.append(
            [remote(piece, piece, xsend.at[j, k], xrecv.at[j, k], peer) for k, peer in enumerate(z_peers)]
        )
    for copy in chunks[0]:
        copy.start()
    logits = jnp.dot(xm[...], pack[...], preferred_element_type=f32)[:, : chosen.shape[1]]
    logits = jnp.where(chosen[...] > 0.0, logits, -jnp.inf)
    power = jnp.exp(logits - jnp.max(logits, axis=-1, keepdims=True))
    gates[...] = power / jnp.sum(power, axis=-1, keepdims=True)
    WM[own_rows, :] = gates[...] * kept[...]
    row = []
    for k, peer in enumerate(z_peers):
        piece = WM.at[own_rows, :]
        row.append(remote(piece, piece, msend.at[k], mrecv.at[k], peer))
        row[-1].start()
    for line in chunks[1:]:
        for copy in line:
            copy.start()
    sent = []
    for j in range(CHUNKS):
        cols = columns(width, j)
        for copy in chunks[j]:
            copy.wait_recv()

        def slots(i, carry):
            at = pl.ds(pl.multiple_of(i * half, 16), half)
            SL[at, cols] = jnp.dot(select[at, :], XM[:, cols], preferred_element_type=f32).astype(bf16)
            return carry

        lax.fori_loop(0, 2, slots, 0)
        line = []
        for k, peer in enumerate(p_peers):
            theirs = pl.ds(pl.multiple_of(p_at[k] * packed, 16), packed)
            line.append(
                remote(SL.at[theirs, cols], buffer.at[mine, cols], bsend.at[j, k], brecv.at[j, k], peer)
            )
        line.append(pltpu.make_async_copy(SL.at[mine, cols], buffer.at[mine, cols], local.at[4 + j]))
        for copy in line:
            copy.start()
        sent.append(line)
        if j == 0:
            for copy in row:
                copy.wait_recv()
            WS[...] = jnp.zeros_like(WS)

            place_of = lax.broadcasted_iota(jnp.int32, (Q, WM.shape[1]), 0)
            expert = (place_of // F * C + c) * F + lax.rem(place_of, F)
            spread = (lax.broadcasted_iota(jnp.int32, expert.shape, 1) == expert).astype(f32)
            lines = lax.dot_general(
                spread, WM[...], (((1,), (1,)), ((), ())),
                precision=lax.Precision.HIGHEST, preferred_element_type=f32,
            )
            for p in range(Q):
                line = lax.dot_general(
                    three_parts(lines[p : p + 1, :]), select[p * packed : (p + 1) * packed, :],
                    (((1,), (1,)), ((), ())), preferred_element_type=f32,
                )
                WS[p, :, pl.ds(0, packed)] = jnp.broadcast_to(
                    jnp.sum(line, axis=0, keepdims=True), (8, packed)
                )
            scales = [
                remote(WS.at[p_at[k]], wrow.at[q], wsend.at[k], wrecv.at[k], peer)
                for k, peer in enumerate(p_peers)
            ]
            scales.append(pltpu.make_async_copy(WS.at[q], wrow.at[q], local.at[2]))
            for copy in scales:
                copy.start()
        if j == CHUNKS - 2:
            for copy in later + loads[1:]:
                copy.wait()
            reload = pltpu.make_async_copy(gbuf, SG, local.at[3])
            reload.start()
            reload.wait()

            def through_down(i, carry):
                at = pl.ds(pl.multiple_of(i * half, 16), half)
                gw[at, :] = lax.dot_general(
                    SG[at, :], WD[...], (((1,), (1,)), ((), ())), preferred_element_type=f32
                )
                return carry

            lax.fori_loop(0, 2, through_down, 0)
    for j in range(CHUNKS - 1):
        cols = columns(width, j)
        for copy in sent[j]:
            copy.wait()

        def project(i, carry):
            at = pl.ds(pl.multiple_of(i * half, 16), half)
            part = buffer[at, cols]
            one = jnp.dot(part, WG[cols, :], preferred_element_type=f32)
            two = jnp.dot(part, WU[cols, :], preferred_element_type=f32)
            gp[at, :] = one if j == 0 else gp[at, :] + one
            up[at, :] = two if j == 0 else up[at, :] + two
            return carry

        lax.fori_loop(0, 2, project, 0)
    for copy in scales:
        copy.wait()
    diagonal = lax.broadcasted_iota(jnp.int32, (packed, packed), 0) == lax.broadcasted_iota(
        jnp.int32, (packed, packed), 1
    )
    dgr[...] = jnp.zeros_like(dgr)
    cols = columns(width, CHUNKS - 1)
    inner = dup.shape[-1]
    hidden, dgp = SG.at[:, pl.ds(0, inner)], SG.at[:, pl.ds(inner, inner)]

    def saves_of(p):
        at = pl.ds(pl.multiple_of(p * packed, 16), packed)
        pairs = ((buffer, buffer_out), (hidden, hidden_out), (dgp, dgp_out), (dup, dup_out))
        return [
            pltpu.make_async_copy(src.at[at], dst.at[at], saved.at[i, p])
            for i, (src, dst) in enumerate(pairs)
        ]

    def expert_rows(p):
        at = pl.ds(pl.multiple_of(p * packed, 16), packed)
        part = buffer[at, cols]
        gate_pre = gp[at, :] + jnp.dot(part, WG[cols, :], preferred_element_type=f32)
        up_pre = up[at, :] + jnp.dot(part, WU[cols, :], preferred_element_type=f32)
        back = gw[at, :]
        scale = jnp.sum(
            jnp.where(diagonal, wrow[p, 0:1, pl.ds(0, packed)], 0.0), axis=1, keepdims=True
        )
        sigmoid = jax.nn.sigmoid(gate_pre)
        silu = gate_pre * sigmoid
        low = (silu * up_pre).astype(bf16)
        hidden[at, :] = (scale * low.astype(f32)).astype(bf16)
        dgate = jnp.sum(back * low.astype(f32), axis=-1, keepdims=True)
        line = jnp.sum(jnp.where(diagonal, dgate, 0.0), axis=0, keepdims=True)
        dgr[p, :, pl.ds(0, packed)] = jnp.broadcast_to(line, (8, packed))
        dhid = scale * back
        dgp[at, :] = (dhid * up_pre * sigmoid * (1.0 + gate_pre * (1.0 - sigmoid))).astype(bf16)
        dup[at, :] = (dhid * silu).astype(bf16)
        for copy in saves_of(p):
            copy.start()

    sent[CHUNKS - 1][Q - 1].wait()
    expert_rows(q)

    def arrival(k, carry):
        p = lax.rem(q + Q - 1 - k, Q)
        at = pl.ds(pl.multiple_of(p * packed, 16), packed)
        came = (p // F, c, lax.rem(p, F))
        remote(
            SL.at[at, cols], buffer.at[at, cols], bsend.at[CHUNKS - 1, k], brecv.at[CHUNKS - 1, k], came
        ).wait_recv()
        expert_rows(p)
        return carry

    lax.fori_loop(0, Q - 1, arrival, 0)
    for copy in sent[CHUNKS - 1][: Q - 1]:
        copy.wait_send()
    for line in chunks + [row]:
        for copy in line:
            copy.wait_send()

    @pl.when(c < C - 1)
    def _():
        def body(t, carry):
            rightward(t).wait_send()
            return carry

        lax.fori_loop(c + 1, C, body, 0)

    @pl.when(c > 0)
    def _():
        def body(t, carry):
            leftward(t).wait_send()
            return carry

        lax.fori_loop(0, c, body, 0)

    for p in range(Q):
        for copy in saves_of(p):
            copy.wait()


def dispatch(packed, out_part, G, tokens, pack, gain, chosen, kept, select, w_gate, w_up, w_down):
    S, C, F = sizes()
    Q = S * F
    rows, width = tokens.shape
    inner = w_gate.shape[-1]
    lanes = round_up(packed, 128)
    wide = chosen.shape[1]
    V = pltpu.VMEM
    sds = jax.ShapeDtypeStruct
    vm = pl.BlockSpec(memory_space=pltpu.VMEM)
    slots = Q * packed
    return pl.pallas_call(
        functools.partial(dispatch_kernel, packed),
        out_shape=[
            sds((slots, width), bf16),
            sds((slots, width), bf16),
            sds((Q, 8, lanes), f32),
            sds((rows, width), f32),
            sds((rows, width), bf16),
            sds((rows, wide), f32),
            sds((slots, inner), bf16),
            sds((slots, inner), bf16),
            sds((slots, inner), bf16),
            sds((Q, 8, lanes), f32),
        ],
        in_specs=[ANY, ANY] + [vm] * 6 + [ANY] * 3,
        out_specs=[ANY, ANY, vm, vm, vm, vm, ANY, ANY, ANY, vm],
        scratch_shapes=[
            V((C, rows, width), bf16),
            V((C + 1, rows, width), bf16),
            V((C * rows, width), bf16),
            V((slots, width), bf16),
            V((C * rows, wide), f32),
            V((Q, 8, lanes), f32),
            V((C * rows, width), bf16),
            V((slots, width), bf16),
            V((slots, width), bf16),
            V((width, inner), bf16), V((width, inner), bf16), V((inner, width), bf16),
            V((slots, inner), f32), V((slots, inner), f32), V((slots, inner), f32),
            V((slots, inner), bf16),
            DMA((4 + CHUNKS,)),
            DMA((4,)),
            DMA((4, Q)),
            DMA((2, C)), DMA((2, C)),
            DMA((Q - 1,)), DMA((Q - 1,)),
            DMA((CHUNKS, C - 1)), DMA((CHUNKS, C - 1)),
            DMA((C - 1,)), DMA((C - 1,)),
            DMA((CHUNKS, Q - 1)), DMA((CHUNKS, Q - 1)),
            DMA((Q - 1,)), DMA((Q - 1,)),
        ],
        name="dispatch_rows",
        compiler_params=params(3, 62 * 2**20),
    )(out_part, G, tokens, pack, gain, chosen, kept, select, w_gate, w_up, w_down)


def return_kernel(
    packed, experts, dgr, gates, pack, h1, gain, cot, xm, dgp, dup,
    select_in, select_t_in, hidden_in, w_gate, w_up, w_down,
    DA, y_part, dh1, small,
    RD, YB, PART, RX, DG, DGP, RG, DL, din, wy, WG, WU, WD, dlog, gnorm, DXR, select, select_t, hidden,
    local, load, dsend, drecv, gsend, grecv, ysend, yrecv, xsend, xrecv, msend, mrecv, *asems,
):
    S, C, F = sizes()
    s, c, f = place()
    Q = S * F
    q = s * F + f
    rows, width = h1.shape
    z_peers = z_neighbours()
    p_at, p_peers = plane_neighbours()
    loads = []
    for j in range(CHUNKS):
        cols = columns(width, j)
        loads.append(
            [
                pltpu.make_async_copy(w_gate.at[0, cols], WG.at[cols], load.at[0, j]),
                pltpu.make_async_copy(w_up.at[0, cols], WU.at[cols], load.at[1, j]),
            ]
        )
    load_down = pltpu.make_async_copy(w_down.at[0], WD, load.at[2, 0])
    late = [
        pltpu.make_async_copy(hidden_in, hidden, load.at[2, 1]),
        pltpu.make_async_copy(select_t_in, select_t, load.at[2, 2]),
        pltpu.make_async_copy(select_in, select, load.at[2, 3]),
    ]
    for line in loads:
        for copy in line:
            copy.start()
    load_down.start()
    for copy in late:
        copy.start()
    greet_all(z_peers + p_peers)
    half = halves(Q * packed)
    mine = pl.ds(pl.multiple_of(q * packed, 16), packed)
    theirs = [pl.ds(pl.multiple_of(at * packed, 16), packed) for at in p_at]
    inner_products = [
        remote(dgr.at[p_at[k]], DG.at[q], gsend.at[k], grecv.at[k], peer)
        for k, peer in enumerate(p_peers)
    ]
    inner_products.append(pltpu.make_async_copy(dgr.at[q], DG.at[q], local.at[0]))
    for copy in inner_products:
        copy.start()
    chunks = []
    for j in range(CHUNKS):
        cols = columns(width, j)
        for copy in loads[j]:
            copy.wait()

        def expert_in(i, carry):
            at = pl.ds(pl.multiple_of(i * half, 16), half)
            across = (((1,), (1,)), ((), ()))
            total = lax.dot_general(dgp[at, :], WG[cols, :], across, preferred_element_type=f32)
            total += lax.dot_general(dup[at, :], WU[cols, :], across, preferred_element_type=f32)
            din[at, cols] = total.astype(bf16)
            return carry

        lax.fori_loop(0, 2, expert_in, 0)
        line = [
            remote(din.at[theirs[k], cols], RD.at[mine, cols], dsend.at[j, k], drecv.at[j, k], peer)
            for k, peer in enumerate(p_peers)
        ]
        line.append(pltpu.make_async_copy(din.at[mine, cols], RD.at[mine, cols], local.at[2 + j]))
        for copy in line:
            copy.start()
        chunks.append(line)
    load_down.wait()
    for copy in late:
        copy.wait()
    def expert_out(i, carry):
        at = pl.ds(pl.multiple_of(i * half, 16), half)

        def body(j, carry):
            cols = pl.ds(pl.multiple_of(j * 512, 512), 512)
            y = jnp.dot(hidden[at, :], WD[:, cols], preferred_element_type=f32)
            wy[at, cols] = y.astype(bf16)
            return carry

        return lax.fori_loop(0, width // 512, body, carry)

    lax.fori_loop(0, 2, expert_out, 0)
    sums = []
    for j in range(CHUNKS):
        if j == CHUNKS - 1:
            ys = []
            for jj in range(2):
                cols = pl.ds(jj * (width // 2), width // 2)
                line = [
                    remote(wy.at[theirs[k], cols], YB.at[mine, cols], ysend.at[jj, k], yrecv.at[jj, k], peer)
                    for k, peer in enumerate(p_peers)
                ]
                line.append(pltpu.make_async_copy(wy.at[mine, cols], YB.at[mine, cols], local.at[(1, 2 + CHUNKS + 1)[jj]]))
                for copy in line:
                    copy.start()
                ys.append(line)
        cols = columns(width, j)
        for copy in chunks[j]:
            copy.wait()

        def combine(i, carry):
            lanes = pl.ds(pl.multiple_of(j * (width // CHUNKS) + i * 256, 256), 256)
            PART[:, lanes] = jnp.dot(
                select_t[...], RD[:, lanes], preferred_element_type=f32
            ).astype(bf16)
            return carry

        lax.fori_loop(0, width // CHUNKS // 256, combine, 0)
        for k, peer in enumerate(z_peers):
            src = PART.at[pl.ds(pl.multiple_of(peer[1] * rows, 16), rows), cols]
            sums.append(remote(src, RX.at[k, :, cols], xsend.at[j, k], xrecv.at[j, k], peer))
            sums[-1].start()
    for copy in inner_products:
        copy.wait()
    wide = gates.shape[1]
    place_of = lax.broadcasted_iota(jnp.int32, (Q, wide), 0)
    expert = (place_of // F * C + c) * F + lax.rem(place_of, F)
    spread = (lax.broadcasted_iota(jnp.int32, (Q, wide), 1) == expert).astype(f32)

    for p in range(Q):
        at = pl.ds(p * packed, packed)
        line = jnp.dot(
            three_parts(DG[p, 0:1, pl.ds(0, packed)]), select[at, :], preferred_element_type=f32
        )
        DL[pl.ds(p, 1), :] = jnp.sum(line, axis=0, keepdims=True)
    DGP[...] = lax.dot_general(
        DL[...], spread, (((0,), (0,)), ((), ())),
        precision=lax.Precision.HIGHEST, preferred_element_type=f32,
    ).reshape(DGP.shape)
    more = []
    for k, peer in enumerate(z_peers):
        more.append(remote(DGP.at[peer[1]], RG.at[k], msend.at[k], mrecv.at[k], peer))
        more[-1].start()
    for copy in more:
        copy.wait()
    total = DGP[c]
    for k in range(C - 1):
        total = total + RG[k]
    dlogits = gates[...] * (total - jnp.sum(gates[...] * total, axis=-1, keepdims=True))
    dlog[...] = dlogits.astype(bf16)
    gnorm[...] = jnp.zeros_like(gnorm)
    DXR[...] = lax.dot_general(
        dlog[...], pack[:, pl.ds(0, wide)], (((1,), (1,)), ((), ())), preferred_element_type=f32
    )
    for copy in sums:
        copy.wait()

    def head_rows(i, carry):
        part = pl.ds(i * 32, 32)
        mine_part = pl.ds(pl.multiple_of(c * rows + i * 32, 16), 32)
        dxm = PART[mine_part, :].astype(f32)
        for k in range(C - 1):
            dxm = dxm + RX[k, part, :].astype(f32)
        dxm = dxm + DXR[part, :]
        unit, factor = rms_unit(h1[part, :])
        gnorm[...] += jnp.sum(dxm * unit, axis=0, keepdims=True)
        grad = cot[part, :].astype(f32) + norm_backward(dxm, unit, factor, gain[...])
        dh1[part, :] = grad
        RX[0, part, :] = grad.astype(bf16)
        return carry

    lax.fori_loop(0, rows // 32, head_rows, 0)
    keep = pltpu.make_async_copy(RX.at[0], DA.at[c], local.at[2 + CHUNKS])
    keep.start()
    line = Line(RX.at[0], lambda at: DA.at[at], *asems)
    line.start()
    for h in range(1, C - 1):
        line.hop(h)
    square = lax.broadcasted_iota(jnp.int32, (HEAD_DIM, HEAD_DIM), 0) == lax.broadcasted_iota(
        jnp.int32, (HEAD_DIM, HEAD_DIM), 1
    )
    small[...] = jnp.zeros_like(small)

    def small_rows(i, carry):
        at = pl.ds(pl.multiple_of(i * HEAD_DIM, HEAD_DIM), HEAD_DIM)
        router_part = lax.dot_general(
            xm[:, at], dlog[...], (((0,), (0,)), ((), ())), preferred_element_type=f32
        )
        column = jnp.sum(jnp.where(square, gnorm[:, at], 0.0), axis=1, keepdims=True)
        if wide > experts:
            lane = lax.broadcasted_iota(jnp.int32, router_part.shape, 1)
            small[at, :] = jnp.where(lane == experts, column, router_part).astype(bf16)
        else:
            small[at, pl.ds(0, wide)] = router_part.astype(bf16)
            lane = lax.broadcasted_iota(jnp.int32, (HEAD_DIM, HEAD_DIM), 1)
            small[at, pl.ds(wide, HEAD_DIM)] = jnp.where(lane == 0, column, 0.0).astype(bf16)
        return carry

    lax.fori_loop(0, width // HEAD_DIM, small_rows, 0)

    def combine_y(i, carry):
        lanes = pl.ds(pl.multiple_of(i * 256, 256), 256)
        y_part[:, lanes] = jnp.dot(
            select_t[...], YB[:, lanes], preferred_element_type=f32
        ).astype(bf16)
        return carry

    for j in range(2):
        for copy in ys[j]:
            copy.wait()
        lax.fori_loop(j * (width // 512), (j + 1) * (width // 512), combine_y, 0)
    line.hop(C - 1)
    line.finish()
    keep.wait()


def give_back(
    packed, experts, dgr, select, select_t, gates, pack, h1, gain, cot, xm, hidden, dgp, dup, w_gate, w_up, w_down
):
    S, C, F = sizes()
    Q = S * F
    rows, width = h1.shape
    wide = gates.shape[1]
    inner = w_gate.shape[-1]
    V = pltpu.VMEM
    sds = jax.ShapeDtypeStruct
    vm = pl.BlockSpec(memory_space=pltpu.VMEM)
    return pl.pallas_call(
        functools.partial(return_kernel, packed, experts),
        out_shape=[
            sds((C, rows, width), bf16),
            sds((C * rows, width), bf16),
            sds((rows, width), f32),
            sds(pack.shape, bf16),
        ],
        in_specs=[vm] * 9 + [ANY] * 6,
        out_specs=[ANY] + [vm] * 3,
        scratch_shapes=[
            V((Q * packed, width), bf16),
            V((Q * packed, width), bf16),
            V((C * rows, width), bf16),
            V((C - 1, rows, width), bf16),
            V(dgr.shape, f32),
            V((C, rows, wide), f32),
            V((C - 1, rows, wide), f32),
            V((Q, C * rows), f32),
            V((Q * packed, width), bf16),
            V((Q * packed, width), bf16),
            V((width, inner), bf16), V((width, inner), bf16), V((inner, width), bf16),
            V((rows, wide), bf16),
            V((1, width), f32),
            V((rows, width), f32),
            V(select.shape, bf16), V(select_t.shape, bf16), V(hidden.shape, bf16),
            DMA((4 + CHUNKS,)),
            DMA((3, CHUNKS)),
            DMA((CHUNKS, Q - 1)), DMA((CHUNKS, Q - 1)),
            DMA((Q - 1,)), DMA((Q - 1,)),
            DMA((2, Q - 1)), DMA((2, Q - 1)),
            DMA((CHUNKS, C - 1)), DMA((CHUNKS, C - 1)),
            DMA((C - 1,)), DMA((C - 1,)),
        ]
        + line_sems(C),
        name="return_grads",
        compiler_params=params(5, 62 * 2**20),
    )(dgr, gates, pack, h1, gain, cot, xm, dgp, dup, select, select_t, hidden, w_gate, w_up, w_down)


def backward_kernel(
    block, da, w_in, wo, q, k, v, xnt_in, x_in, cosine, sine, pos_col, pos_row, gains, mixed_t, sp, yp,
    OH, OX, Q3, KV3, S3, T3, YP, *rest,
):
    DX = rest[: lax.axis_size("ctx")]
    (
    w, xnt, x, late, dxn, dxsem, kr, dkr, dv, acc, DQ, head_grad,
        GQ, Q1, Q2, QS, GO, o_in, s_own, s_in, s_plane, s_sum, T, t_in, t_plane, t_sum,
        local, qlocal, csend, crecv, fsend, frecv, zsend, zrecv, qcs, qcr, qfs, qfr, qzs, qzr, ysend, yrecv,
    ) = rest[lax.axis_size("ctx") :]
    S, C, F = sizes()
    s, c, f = place()
    step = pl.program_id(0)
    units = GQ.shape[0]
    pairs = units - 1
    length, width = x.shape
    wide = 2 * HEAD_DIM
    late_loads = [
        pltpu.make_async_copy(src, dst, late.at[i])
        for i, (src, dst) in enumerate(((xnt_in, xnt), (w_in, w), (x_in, x)))
    ]
    z_peers = z_neighbours()
    f_peers = [(s, c, lax.rem(f + k, F)) for k in range(1, F)]
    sibling = (1 - s, c, f)
    cols = pl.ds(pl.multiple_of(step * wide, wide), wide)

    o_own = GO.at[s]
    o_first = remote(GO.at[1 - s], o_in, csend.at[0], crecv.at[0], sibling)
    t_first = remote(T, t_in, csend.at[2], crecv.at[2], sibling)
    half = F // 2
    mine = lax.rem(f // half, 2)
    o_saves = [
        pltpu.make_async_copy(o_own.at[pl.ds(mine * half, half)], OH, local.at[2]),
        pltpu.make_async_copy(o_own.at[pl.ds((1 - mine) * half, half)], OX, local.at[6]),
    ]
    s_first = remote(sp.at[1 - s], s_in, csend.at[1], crecv.at[1], sibling)
    s_load = pltpu.make_async_copy(sp.at[s], s_own, local.at[1])
    f_at = list(enumerate(f_peers))
    z_at = list(enumerate(z_peers))
    s_second = [remote(s_own.at[:, p[2]], s_plane.at[k], fsend.at[1, k], frecv.at[1, k], p) for k, p in f_at]
    t_second = [remote(T, t_plane.at[k], fsend.at[2, k], frecv.at[2, k], p) for k, p in f_at]
    s_third = [remote(s_sum.at[p[1]], S3.at[c], zsend.at[1, k], zrecv.at[1, k], p) for k, p in z_at]
    s_third.append(pltpu.make_async_copy(s_sum.at[c], S3.at[c], local.at[3]))
    t_third = [remote(t_sum, T3.at[c], zsend.at[2, k], zrecv.at[2, k], p) for k, p in z_at]
    t_third.append(pltpu.make_async_copy(t_sum, T3.at[c], local.at[4]))
    y_copies = [remote(yp.at[p[1]], YP.at[c], ysend.at[k], yrecv.at[k], p) for k, p in z_at]
    y_copies.append(pltpu.make_async_copy(yp.at[c], YP.at[c], local.at[5]))

    def q_first(u):
        return remote(GQ.at[u, 1 - s], Q1.at[u], qcs.at[u], qcr.at[u], sibling)

    def q_second(u):
        return [remote(GQ.at[u, s, :, p[2]], Q2.at[u, k], qfs.at[u, k], qfr.at[u, k], p) for k, p in f_at]

    def q_third(u):
        if isinstance(u, int) and u == pairs:
            landing = KV3.at[c]
        else:
            landing = Q3.at[:, pl.ds(pl.multiple_of(c * pairs * wide + u * wide, wide), wide)]
        copies = [
            remote(QS.at[u, p[1]], landing, qzs.at[u, k], qzr.at[u, k], p) for k, p in z_at
        ]
        copies.append(pltpu.make_async_copy(QS.at[u, c], landing, qlocal.at[u]))
        return copies

    def to_plane(u):
        q_first(u).wait()

        def body(i, carry):
            at = (u, s, i // F, lax.rem(i, F))
            GQ[at] = (GQ[at].astype(f32) + Q1[u, i // F, lax.rem(i, F)].astype(f32)).astype(bf16)
            return carry

        lax.fori_loop(0, C * F, body, 0)
        for copy in q_second(u):
            copy.start()

    def to_ctx(u):
        for copy in q_second(u):
            copy.wait()

        def body(i, carry):
            total = GQ[u, s, i, f].astype(f32)
            for k in range(F - 1):
                total = total + Q2[u, k, i].astype(f32)
            QS[u, i] = total.astype(bf16)
            return carry

        lax.fori_loop(0, C, body, 0)
        for copy in q_third(u):
            copy.start()

    @pl.when(step == 0)
    def _():
        for copy in late_loads:
            copy.start()
        greet_all(z_peers + f_peers + [sibling])
        for copy in [s_first, s_load] + y_copies:
            copy.start()

        def out_rows(i, carry):
            at, j = i // 4, lax.rem(i, 4)
            part = mixed_t.shape[0] // S
            rows = pl.ds(pl.multiple_of(at * part, 16), part)
            lanes = pl.ds(pl.multiple_of(j * (width // 4), width // 4), width // 4)
            piece = jnp.dot(mixed_t[rows, :], da[:, lanes], preferred_element_type=f32)
            GO[at, :, :, lanes] = piece.astype(bf16).reshape(F, part // F, width // 4)
            return carry

        lax.fori_loop(0, S * 4, out_rows, 0)
        o_first.start()
        unit, _ = rms_unit(k[...])
        kr[...] = half_turn(unit * gains[1:2, :], cosine[...], sine[...]).astype(bf16)
        dkr[...] = jnp.zeros_like(dkr)
        dv[...] = jnp.zeros_like(dv)
        head_grad[...] = jnp.zeros_like(head_grad)
        acc[...] = jnp.zeros_like(acc)

    @pl.when(step >= 1)
    def _():
        to_plane(step - 1)

    @pl.when(step == 1)
    def _():
        o_first.wait()

        def o_body(i, carry):
            o_own[i] = (o_own[i].astype(f32) + o_in[i].astype(f32)).astype(bf16)
            return carry

        lax.fori_loop(0, F, o_body, 0)
        for copy in o_saves:
            copy.start()
        s_first.wait()
        s_load.wait()

        def s_body(i, carry):
            at = (i // F, lax.rem(i, F))
            s_own[at] = (s_own[at].astype(f32) + s_in[at].astype(f32)).astype(bf16)
            return carry

        lax.fori_loop(0, C * F, s_body, 0)
        for copy in s_second:
            copy.start()

    @pl.when(step >= 2)
    def _():
        to_ctx(step - 2)

    @pl.when(step == 2)
    def _():
        for copy in s_second:
            copy.wait()

        def s_body(i, carry):
            total = s_own[i, f].astype(f32)
            for k in range(F - 1):
                total = total + s_plane[k, i].astype(f32)
            s_sum[i] = total.astype(bf16)
            return carry

        lax.fori_loop(0, C, s_body, 0)
        for copy in s_third:
            copy.start()

    @pl.when(step < pairs)
    def _():
        dm = lax.dot_general(
            da[...], wo[cols, :], (((1,), (1,)), ((), ())), preferred_element_type=f32
        ).astype(bf16)
        for half in range(2):
            lanes = slice(half * HEAD_DIM, (half + 1) * HEAD_DIM)
            for part in range(length // block):
                rows = slice(part * block, (part + 1) * block)
                unit, factor = rms_unit(q[rows, lanes])
                cos, sin = cosine[rows, :], sine[rows, :]
                qr = half_turn(unit * gains[0:1, :], cos, sin).astype(bf16)
                keys = kr[...]
                probs = score_block(qr, keys, pos_col[rows, :], pos_row[...])
                dmh = dm[rows, lanes]
                dprobs = lax.dot_general(
                    dmh, v[...], (((1,), (1,)), ((), ())), preferred_element_type=f32
                )
                delta = jnp.sum(probs * dprobs, axis=-1, keepdims=True)
                dscores = (probs * (dprobs - delta)).astype(bf16)
                dqr = jnp.dot(dscores, keys, preferred_element_type=f32) * (HEAD_DIM**-0.5)
                rows_in = (((0,), (0,)), ((), ()))
                dkr[...] += lax.dot_general(dscores, qr, rows_in, preferred_element_type=f32) * (
                    HEAD_DIM**-0.5
                )
                dv[...] += lax.dot_general(
                    probs.astype(bf16), dmh, rows_in, preferred_element_type=f32
                )
                dqs = half_turn(dqr, cos, -sin)
                head_grad[0:1, :] += jnp.sum(dqs * unit, axis=0, keepdims=True)
                DQ[rows, lanes] = norm_backward(dqs, unit, factor, gains[0:1, :]).astype(bf16)

    @pl.when(step == pairs)
    def _():
        unit, factor = rms_unit(k[...])
        dks = half_turn(dkr[...], cosine[...], -sine[...])
        head_grad[1:2, :] += jnp.sum(dks * unit, axis=0, keepdims=True)
        DQ[:, :HEAD_DIM] = norm_backward(dks, unit, factor, gains[1:2, :]).astype(bf16)
        DQ[:, HEAD_DIM:] = dv[...].astype(bf16)

    @pl.when(step == 0)
    def _():
        for copy in late_loads:
            copy.wait()

    def weight_rows(i, carry):
        part = F * GQ.shape[4]
        rows = pl.ds(pl.multiple_of(i * part, 16), part)
        piece = jnp.dot(xnt[rows, :], DQ[...], preferred_element_type=f32)
        GQ[step, i // C, lax.rem(i, C)] = piece.astype(bf16).reshape(GQ.shape[3:])
        return carry

    lax.fori_loop(0, S * C, weight_rows, 0)
    q_first(step).start()
    for j in range(4):
        part = pl.ds(j * (width // 4), width // 4)
        acc[:, part] += lax.dot_general(
            DQ[...], w[part, cols], (((1,), (1,)), ((), ())), preferred_element_type=f32
        )

    @pl.when(step == pairs)
    def _():
        to_ctx(pairs - 1)
        to_plane(pairs)
        rows_of = width // HEAD_DIM
        total = jnp.zeros((1, width), f32)

        def finish(i, total):
            rows = pl.ds(i * 64, 64)
            unit, _ = rms_unit(x[rows, :].astype(f32))
            term = acc[rows, :]
            dxn[rows, :] = term.astype(bf16)
            return total + jnp.sum(term * unit, axis=0, keepdims=True)

        total = lax.fori_loop(0, length // 64, finish, total)
        rows = length // C
        x_saves = [
            pltpu.make_async_copy(
                dxn.at[pl.ds(pl.multiple_of(lax.rem(c + i, C) * rows, 16), rows)], DX[i], dxsem.at[i]
            )
            for i in range(C)
        ]
        for copy in x_saves:
            copy.start()
        for r in range(rows_of):
            T[r : r + 1, :] = total[:, r * HEAD_DIM : (r + 1) * HEAD_DIM]
        T[rows_of:, :] = head_grad[...]
        t_first.start()
        t_first.wait()
        T[...] = T[...] + t_in[...]
        for copy in t_second:
            copy.start()
        to_ctx(pairs)
        for copy in t_second:
            copy.wait()
        order = []
        for g in range(F):
            term = jnp.zeros_like(T)
            for k in range(F - 1):
                came = lax.rem(f + F - (k + 1), F)
                term = term + jnp.where(came == g, t_plane[k], 0.0)
            order.append(term + jnp.where(f == g, T[...], 0.0))
        total = order[0]
        for term in order[1:]:
            total = total + term
        t_sum[...] = total
        for copy in t_third:
            copy.start()
        for copy in s_third + y_copies + o_saves + t_third + x_saves:
            copy.wait()
        for u in range(units):
            for copy in q_third(u):
                copy.wait()


def backward(da, w, wo, q, k, v, xnt, x, cosine, sine, pos_col, pos_row, gains, mixed_t, sp, yp):
    S, C, F = sizes()
    length, width = x.shape
    head_width = wo.shape[0]
    pairs = head_width // (2 * HEAD_DIM)
    units = pairs + 1
    shard = sp.shape[3]
    block = min(length, 512)
    wide = 2 * HEAD_DIM
    once = pl.Buffered(buffer_count=1)
    whole = lambda array: pl.BlockSpec(array.shape, lambda i: (0, 0), pipeline_mode=once)
    sds = jax.ShapeDtypeStruct
    V = pltpu.VMEM
    q_block, o_block, s_block = (shard, wide), (head_width // (S * F), width), sp.shape[3:]
    t_block = (width // HEAD_DIM + 8, HEAD_DIM)
    return pl.pallas_call(
        functools.partial(backward_kernel, block),
        out_shape=[
            sds((F // 2,) + o_block, bf16),
            sds((F // 2,) + o_block, bf16),
            sds((shard, C * head_width), bf16),
            sds((C, shard, wide), bf16),
            sds((C,) + s_block, bf16),
            sds((C,) + t_block, f32),
            sds(yp.shape, bf16),
        ]
        + [sds((length // C, width), bf16)] * C,
        grid=(units,),
        in_specs=[whole(da), ANY, whole(wo)]
        + [pl.BlockSpec((length, wide), lambda i: (0, jnp.minimum(i, pairs - 1)))]
        + [whole(k), whole(v), ANY, ANY]
        + [whole(array) for array in (cosine, sine, pos_col, pos_row, gains, mixed_t)]
        + [ANY] * 2,
        out_specs=[ANY] * (7 + C),
        scratch_shapes=[
            V(w.shape, bf16), V(xnt.shape, bf16), V(x.shape, bf16), DMA((3,)),
            V((length, width), bf16), DMA((C,)),
            V((length, HEAD_DIM), bf16), V((length, HEAD_DIM), f32), V((length, HEAD_DIM), f32),
            V((length, width), f32), V((length, wide), bf16), V((8, HEAD_DIM), f32),
            V((units, S, C, F) + q_block, bf16), V((units, C, F) + q_block, bf16),
            V((units, F - 1, C) + q_block, bf16), V((units, C) + q_block, bf16),
            V((S, F) + o_block, bf16), V((F,) + o_block, bf16),
            V((C, F) + s_block, bf16), V((C, F) + s_block, bf16), V((F - 1, C) + s_block, bf16), V((C,) + s_block, bf16),
            V(t_block, f32), V(t_block, f32), V((F - 1,) + t_block, f32), V(t_block, f32),
            DMA((7,)), DMA((units,)),
            DMA((3,)), DMA((3,)), DMA((3, F - 1)), DMA((3, F - 1)), DMA((3, C - 1)), DMA((3, C - 1)),
            DMA((units,)), DMA((units,)), DMA((units, F - 1)), DMA((units, F - 1)),
            DMA((units, C - 1)), DMA((units, C - 1)), DMA((C - 1,)), DMA((C - 1,)),
        ],
        name="attention_backward",
        compiler_params=params(7, 60 * 2**20),
    )(da, w, wo, q, k, v, xnt, x, cosine, sine, pos_col, pos_row, gains, mixed_t, sp, yp)


def dot(left, right):
    return jnp.dot(left, right, preferred_element_type=f32)


def contract_rows(left, right):
    return lax.dot_general(left, right, (((0,), (0,)), ((), ())), preferred_element_type=f32)


def times_transpose(left, right):
    return lax.dot_general(left, right, (((1,), (1,)), ((), ())), preferred_element_type=f32)


def on_device(
    tokens,
    stretch_order,
    expert_ids,
    slot_index,
    norm_attn,
    head_gains,
    w_query,
    w_key,
    w_value,
    w_out,
    norm_moe,
    w_router,
    w_gate,
    w_up,
    w_down,
    cotangent,
):
    S, C, F = sizes()
    Q = S * F
    seq_at, ctx_at, fsdp_at = place()
    rows, width = tokens.shape[1:]
    length = C * rows
    experts = w_router.shape[1]
    capacity = rows * TOP // (Q * C) + 1
    packed = round_up(C * capacity, 16)
    lanes = round_up(packed, 128)
    head_width = w_query.shape[1] // C
    shard = w_router.shape[0]
    pack_width = round_up(experts + 2, 128)
    (
        X, W, WO, PK, _, G, out_part, q, k, v, mixed_t, xnt, gain_attn, gain_moe, gains,
        cosine, sine, pos_col, pos_row, select, select_t, chosen, kept_map,
    ) = front(
        capacity, packed, stretch_order, expert_ids[0].T, slot_index[0].T,
        tokens[0], w_query, w_key, w_value, w_out, w_router.T, norm_attn[None], norm_moe[None],
        cotangent[0], head_gains,
    )
    W = W.reshape(width, head_width + 2 * HEAD_DIM)
    WO = WO.reshape(head_width, width)
    PK = PK.reshape(width, pack_width)
    buffer, slot_grad, _, h1, xm, gates, hidden, dgp, dup, slot_dgate = dispatch(
        packed, out_part.reshape(C, rows, width), G.reshape(length, width), tokens[0], PK, gain_moe,
        chosen, kept_map, select, w_gate, w_up, w_down,
    )
    DA, y_part, dh1, small = give_back(
        packed, experts, slot_dgate, select, select_t, gates, PK, h1, gain_moe, cotangent[0],
        xm, hidden, dgp, dup, w_gate, w_up, w_down,
    )
    DA = DA.reshape(length, width)

    def part_of(parts, at):
        return lax.dynamic_index_in_dim(parts, at, 0, keepdims=False)

    out_half, out_other, query_sum, kv_sums, small_sums, tiny_sums, y_parts, *dxn_parts = backward(
        DA, W, WO, q, k, v, xnt, X, cosine, sine, pos_col, pos_row, gains,
        mixed_t,
        small.reshape(S, C, F, shard, pack_width),
        y_part.reshape(C, rows, width),
    )
    dxn = dxn_parts[0].astype(f32)
    for i in range(1, C):
        dxn += lax.ppermute(dxn_parts[i], "ctx", [(j, (j + i) % C) for j in range(C)]).astype(f32)
    out_sum, bit = out_half, F // 2
    while True:
        came = lax.ppermute(out_other, "fsdp", [(i, i ^ bit) for i in range(F)])
        out_sum = (out_sum.astype(f32) + came.astype(f32)).astype(bf16)
        bit //= 2
        if not bit:
            break
        out_sum, hidden, slot_grad = lax.optimization_barrier((out_sum, hidden, slot_grad))
        mine = lax.rem(fsdp_at // bit, 2)
        parts = out_sum.reshape((2, bit) + out_sum.shape[1:])
        out_sum, out_other = part_of(parts, mine), part_of(parts, 1 - mine)
    out_sum = out_sum[0]
    turn = [(i * C + j, j * S + i) for i in range(S) for j in range(C)]
    o_sum = lax.ppermute(out_sum, ("seq", "ctx"), turn)
    grad_wgate = contract_rows(buffer, dgp)
    grad_wup = contract_rows(buffer, dup)
    grad_wdown = contract_rows(hidden, slot_grad)
    layer_out = (h1 + jnp.sum(y_parts.astype(f32), axis=0)).astype(bf16)
    unit, factor = rms_unit(tokens[0].astype(f32))
    grad_tokens = (dh1 + norm_backward(dxn, unit, factor, gain_attn)).astype(bf16)
    grad_query = query_sum.astype(f32)

    def key_columns(block):
        pieces = block.astype(f32).reshape(KEY_VALUE_HEADS, C // KEY_VALUE_HEADS, shard, HEAD_DIM).sum(axis=1)
        return pieces.transpose(1, 0, 2).reshape(shard, KEY_VALUE_HEADS * HEAD_DIM)

    grad_key = key_columns(kv_sums[:, :, :HEAD_DIM])
    grad_value = key_columns(kv_sums[:, :, HEAD_DIM:])
    small_sum = jnp.sum(small_sums.astype(f32), axis=0)
    tiny_sum = jnp.sum(tiny_sums, axis=0)
    tiny_rows = width // HEAD_DIM
    device = (seq_at * C + ctx_at) * F + fsdp_at
    grad_norm_attn = lax.dynamic_slice_in_dim(
        tiny_sum[:tiny_rows].reshape(width), device * shard, shard
    )
    return (
        layer_out[None],
        grad_tokens[None],
        grad_norm_attn,
        tiny_sum[tiny_rows : tiny_rows + 2],
        grad_query,
        grad_key,
        grad_value,
        o_sum.astype(f32),
        small_sum[:, experts],
        small_sum[:, :experts],
        grad_wgate[None],
        grad_wup[None],
        grad_wdown[None],
    )


def solution(mesh):
    rows = P(("seq", "fsdp"), "ctx", None)
    vector = P(AXES)
    matrix = P(AXES, None)
    cube = P(AXES, None, None)
    return jax.shard_map(
        on_device,
        mesh=mesh,
        in_specs=(
            rows, P(), rows, rows, vector, P(), matrix, matrix, matrix, matrix,
            vector, matrix, cube, cube, cube, rows,
        ),
        out_specs=(
            rows, rows, vector, P(), matrix, matrix, matrix, matrix, vector, matrix,
            cube, cube, cube,
        ),
        check_vma=False,
    )
```
